32 devices in a mesh: dp: 16 (over z, x, core), tp: 2 (over y).
Axes of the slice: x: 2, y: 2, z: 4, core: 2. Of those that a mesh axis runs over, the one named last changes fastest.
Arguments:
- tokens: bfloat16 [65536, 768], P('dp'), may hold values from -6 to 6
- long_lengths: int32 [32], P('dp'), may hold values from 256 to 1024, as said below
- short_lengths: int32 [128], P('dp'), may hold values from 64 to 256, as said below
- ln1_gain: bfloat16 [768], replicated, may hold values from 0.25 to 1.75
- ln1_bias: bfloat16 [768], replicated, may hold values from -2 to 2
- w_query: bfloat16 [768, 768], P(None, 'tp'), may hold values from -0.21875 to 0.21875
- b_query: bfloat16 [768], P('tp'), may hold values from -2 to 2
- w_key: bfloat16 [768, 768], P(None, 'tp'), may hold values from -0.21875 to 0.21875
- w_value: bfloat16 [768, 768], P(None, 'tp'), may hold values from -0.21875 to 0.21875
- b_value: bfloat16 [768], P('tp'), may hold values from -2 to 2
- w_out: bfloat16 [768, 768], P('tp'), may hold values from -3 to 3
- b_out: bfloat16 [768], replicated, may hold values from -2 to 2
- ln2_gain: bfloat16 [768], replicated, may hold values from 0.25 to 1.75
- ln2_bias: bfloat16 [768], replicated, may hold values from -2 to 2
- w_up: bfloat16 [768, 3072], P(None, 'tp'), may hold values from -0.21875 to 0.21875
- b_up: bfloat16 [3072], P('tp'), may hold values from -2 to 2
- w_down: bfloat16 [3072, 768], P('tp'), may hold values from -0.109375 to 0.109375
- b_down: bfloat16 [768], replicated, may hold values from -2 to 2
- cotangent: bfloat16 [65536, 768], P(('dp', 'tp')), may hold values from -6 to 6
Outputs:
- output: bfloat16 [65536, 768], P(('dp', 'tp'))
- grad_tokens: float32 [65536, 768], P(('dp', 'tp'))
- grad_ln1_gain: float32 [768], replicated
- grad_ln1_bias: float32 [768], replicated
- grad_w_query: float32 [768, 768], P(None, 'tp')
- grad_b_query: float32 [768], P('tp')
- grad_w_key: float32 [768, 768], P(None, 'tp')
- grad_w_value: float32 [768, 768], P(None, 'tp')
- grad_b_value: float32 [768], P('tp')
- grad_w_out: float32 [768, 768], P('tp')
- grad_b_out: float32 [768], replicated
- grad_ln2_gain: float32 [768], replicated
- grad_ln2_bias: float32 [768], replicated
- grad_w_up: float32 [768, 3072], P(None, 'tp')
- grad_b_up: float32 [3072], P('tp')
- grad_w_down: float32 [3072, 768], P('tp')
- grad_b_down: float32 [768], replicated
The draws below stay inside these ranges and needn't reach their ends.
Inputs may be any that keep to these rules, and one draw needn't show every extreme that they name: `long_lengths`: valid tokens of each high-resolution image; keys at or after it are masked. `short_lengths`: valid tokens of each low-resolution image; keys at or after it are masked.
All inputs are finite; a program needn't handle non-finite values.
Results may differ from the reference program's by a relative error of at most 0.012.
The reference program's roundings to bfloat16 on the way count: a program that leaves them out, or rounds other values in their place, can miss the bound.
Values may be sent and summed in bfloat16 or wider, within the bound.
A program may use at most 320 MiB of HBM per device.

```python
import jax
import jax.numpy as jnp
from jax import lax

D = 768
HEADS = 16
HEAD_DIM = 48
FF = 3072
LEN_L = 1024
LEN_S = 256
LONG_DEV = 2
SHORT_DEV = 8
TOK_DEV = 4096
TOKENS = 65536
QW = 768
LONG_IMGS = 32
SHORT_IMGS = 128
N_DP = 16


def ragged_lengths(key, image_count, seq_len):
    drawn = jax.random.randint(key, (image_count,), seq_len // 4, seq_len + 1, dtype=jnp.int32)
    drawn = drawn.at[0].set(seq_len)
    return drawn.at[1].set(seq_len // 4)


def draw_long_lengths(key, part):
    key = jax.random.fold_in(key, 11)
    return ragged_lengths(key, LONG_IMGS, LEN_L)


def draw_short_lengths(key, part):
    key = jax.random.fold_in(key, 23)
    return ragged_lengths(key, SHORT_IMGS, LEN_S)


def block_scale(own_key, dims, shards, least, largest):
    def one(position, shards_of):
        heights = jax.random.uniform(jax.random.fold_in(jax.random.fold_in(own_key, 6), position), (shards_of,), jnp.float32, least / len(shards), largest / len(shards))
        return jnp.repeat(jnp.exp(heights), dims[position] // shards_of).reshape((-1,) + (1,) * (len(dims) - position - 1))

    loudness = one(*shards[0])
    for cut in shards[1:]:
        loudness = loudness * one(*cut)
    return loudness


def scatter_about(key, dims, deviation, most, cuts=(), held_as=jnp.bfloat16):
    array = deviation * jax.random.normal(key, dims, jnp.float32)
    if cuts:
        array = array * block_scale(key, dims, cuts, -0.22, 0.18)
    return jnp.clip(array, -most, most).astype(held_as)


def setup_inputs(seed: int = 0) -> dict:
    splits = jax.random.split(jax.random.key(seed), 20)
    return {
        "tokens": scatter_about(splits[0], (TOKENS, D), 1.0, 6.0, ((0, 16),)),
        "long_lengths": draw_long_lengths(jax.random.fold_in(splits[19], 71), 0),
        "short_lengths": draw_short_lengths(jax.random.fold_in(splits[19], 71), 0),
        "ln1_gain": jnp.clip(1.0 + 0.15 * jax.random.normal(splits[3], (D,), jnp.float32), 0.25, 1.75).astype(jnp.bfloat16),
        "ln1_bias": scatter_about(splits[4], (D,), 0.3, 2.0),
        "w_query": scatter_about(splits[5], (D, QW), D ** -0.5, 0.21875, ((1, 2),)),
        "b_query": scatter_about(splits[6], (QW,), 0.3, 2.0, ((0, 2),)),
        "w_key": scatter_about(splits[7], (D, QW), D ** -0.5, 0.21875, ((1, 2),)),
        "w_value": scatter_about(splits[8], (D, QW), D ** -0.5, 0.21875, ((1, 2),)),
        "b_value": scatter_about(splits[9], (QW,), 0.3, 2.0, ((0, 2),)),
        "w_out": scatter_about(splits[10], (QW, D), 4 ** -0.5, 3.0, ((0, 2),)),
        "b_out": scatter_about(splits[11], (D,), 0.3, 2.0),
        "ln2_gain": jnp.clip(1.0 + 0.15 * jax.random.normal(splits[12], (D,), jnp.float32), 0.25, 1.75).astype(jnp.bfloat16),
        "ln2_bias": scatter_about(splits[13], (D,), 0.3, 2.0),
        "w_up": scatter_about(splits[14], (D, FF), D ** -0.5, 0.21875, ((1, 2),)),
        "b_up": scatter_about(splits[15], (FF,), 0.3, 2.0, ((0, 2),)),
        "w_down": scatter_about(splits[16], (FF, D), FF ** -0.5, 0.109375, ((0, 2),)),
        "b_down": scatter_about(splits[17], (D,), 0.3, 2.0),
        "cotangent": scatter_about(splits[18], (TOKENS, D), 1.0, 6.0, ((0, 32),)),
    }


@jax.custom_vjp
def low(v):
    return lax.optimization_barrier(v.astype(jnp.bfloat16)).astype(jnp.float32)

@jax.custom_vjp
def low_back(v):
    return v

def low_keep(v):
    return (low(v), None)

def low_pass(kept, grad):
    return (grad,)

def back_keep(v):
    return (v, None)

def back_low(kept, grad):
    return (low(grad),)
low.defvjp(low_keep, low_pass)
low_back.defvjp(back_keep, back_low)

def matmul(left, right):
    return jnp.dot(left, right, precision=lax.Precision.HIGHEST)

def layer_norm(values, gain, shift):
    center = values - lax.optimization_barrier(jnp.mean(values, axis=-1, keepdims=True))
    spread = lax.optimization_barrier(jnp.mean(center * center, axis=-1, keepdims=True))
    return center * lax.rsqrt(spread + 1e-06) * gain + shift

def attend(queries, key_rows, value_rows, length):
    seq_len = queries.shape[0]
    scores = low_back(jnp.einsum('qhd,khd->hqk', queries, key_rows, precision=lax.Precision.HIGHEST) * HEAD_DIM ** (-0.5))
    keep = jnp.arange(seq_len, dtype=jnp.int32) < length
    scores = jnp.where(keep[None, None, :], scores, -1e+30)
    row_top = lax.optimization_barrier(jnp.max(scores, axis=-1, keepdims=True))
    exp_terms = jnp.exp(scores - row_top)
    probs = exp_terms / lax.optimization_barrier(jnp.sum(exp_terms, axis=-1, keepdims=True))
    return jnp.einsum('hqk,khd->qhd', low(probs), value_rows, precision=lax.Precision.HIGHEST)

def group_attention(queries, key_rows, value_rows, lengths, seq_len):
    image_count = lengths.shape[0]
    block_shape = (image_count, seq_len, HEADS, HEAD_DIM)
    checked = jax.checkpoint(attend)
    mixed = lax.map(lambda block: checked(block[0], block[1], block[2], block[3]), (queries.reshape(block_shape), key_rows.reshape(block_shape), value_rows.reshape(block_shape), lengths))
    return mixed.reshape(image_count * seq_len, HEADS * HEAD_DIM)

def layer(values, long_len, short_len, params):
    gain_one, shift_one, w_query, b_query, w_key, w_value, b_value, w_out, b_out, gain_two, shift_two, w_up, b_up, w_down, b_down = params
    normed_in = low(layer_norm(values, gain_one, shift_one))
    queries = low(low_back(matmul(normed_in, w_query) + b_query))
    key_rows = low(low_back(matmul(normed_in, w_key)))
    value_rows = low(low_back(matmul(normed_in, w_value) + b_value))
    split = long_len.shape[0] * LEN_L
    long_part = group_attention(queries[:split], key_rows[:split], value_rows[:split], long_len, LEN_L)
    short_part = group_attention(queries[split:], key_rows[split:], value_rows[split:], short_len, LEN_S)
    attended = low(low_back(jnp.concatenate([long_part, short_part], axis=0)))
    resid = values + low_back(matmul(attended, w_out)) + b_out
    normed_mid = low(layer_norm(resid, gain_two, shift_two))
    pre_up = low_back(matmul(normed_mid, w_up) + b_up)
    activ = low(jax.nn.gelu(pre_up, approximate=False))
    return resid + low_back(matmul(activ, w_down)) + b_down

def reference(tokens, long_lengths, short_lengths, ln1_gain, ln1_bias, w_query, b_query, w_key, w_value, b_value, w_out, b_out, ln2_gain, ln2_bias, w_up, b_up, w_down, b_down, cotangent):
    params = tuple((item.astype(jnp.float32) for item in (ln1_gain, ln1_bias, w_query, b_query, w_key, w_value, b_value, w_out, b_out, ln2_gain, ln2_bias, w_up, b_up, w_down, b_down)))
    blocks = tokens.astype(jnp.float32).reshape(N_DP, TOK_DEV, D)
    cot_blocks = cotangent.astype(jnp.float32).reshape(N_DP, TOK_DEV, D)
    long_blocks = long_lengths.reshape(N_DP, LONG_DEV)
    short_blocks = short_lengths.reshape(N_DP, SHORT_DEV)

    def one_block(totals, block):
        values, long_len, short_len, grad_out = block
        result, backward = jax.vjp(lambda inner, weights: layer(inner, long_len, short_len, weights), values, params)
        grad_values, grad_params = backward(grad_out)
        totals = tuple((total + part for total, part in zip(totals, grad_params)))
        return (totals, (result.astype(jnp.bfloat16), grad_values))
    start = tuple((jnp.zeros(item.shape, jnp.float32) for item in params))
    totals, (results, grads) = lax.scan(one_block, start, (blocks, long_blocks, short_blocks, cot_blocks))
    return (results.reshape(TOKENS, D), grads.reshape(TOKENS, D), totals[0], totals[1], totals[2], totals[3], totals[4], totals[5], totals[6], totals[7], totals[8], totals[9], totals[10], totals[11], totals[12], totals[13], totals[14])
```

```python
import functools
import math

import jax
import jax.numpy as jnp
from jax import lax
from jax.experimental import pallas as pl
from jax.experimental.pallas import tpu as pltpu
from jax.sharding import PartitionSpec as P

HEAD_DIM = 48
LEN_L = 1024
LEN_S = 256
F32 = jnp.float32
BF16 = jnp.bfloat16
LOG2E = math.log2(math.e)
SCALE = HEAD_DIM ** (-0.5)
VMEM_LIMIT = 58 << 20
HEAD_GROUP = 2


def contract(left, right, left_dim, right_dim):
    return lax.dot_general(
        left, right, (((left_dim,), (right_dim,)), ((), ())), preferred_element_type=F32
    )


def params():
    return pltpu.CompilerParams(vmem_limit_bytes=VMEM_LIMIT)


def cost(flops, bytes_accessed, transcendentals=0):
    return pl.CostEstimate(
        flops=int(flops), bytes_accessed=int(bytes_accessed), transcendentals=int(transcendentals)
    )


def whole(shape):
    zeros = (0,) * len(shape)
    return pl.BlockSpec(shape, lambda *_: zeros)


def norm_parts(values):
    center = values - jnp.mean(values, axis=-1, keepdims=True)
    inv = lax.rsqrt(jnp.mean(center * center, axis=-1, keepdims=True) + 1e-06)
    return center * inv, inv


def norm_back(hat, inv, grad_hat):
    mean_grad = jnp.mean(grad_hat, axis=-1, keepdims=True)
    mean_both = jnp.mean(grad_hat * hat, axis=-1, keepdims=True)
    return inv * (grad_hat - mean_grad - hat * mean_both)


def project_norm_kernel(rank_ref, tok_ref, gain_ref, shift_ref, w_ref, b_ref, x_ref, qkv_ref):
    hat, _ = norm_parts(tok_ref[...].astype(F32))
    normed = (hat * gain_ref[...] + shift_ref[...]).astype(BF16)
    x_ref[...] = normed
    qkv_ref[...] = (contract(w_ref[...], normed, 0, 1) + b_ref[...]).astype(BF16)


def project_kernel(x_ref, w_ref, b_ref, qkv_ref):
    qkv_ref[...] = (contract(w_ref[...], x_ref[...], 0, 1) + b_ref[...]).astype(BF16)


def own_row_block(per_part):
    def index(i, rank_ref):
        part = i // per_part
        return (part * 2 * per_part + rank_ref[0] * per_part + i % per_part, 0)

    return index


def project_norm(rank, tokens, gain, shift, w_cat, b_col, rows, block):
    width, out = w_cat.shape
    per_part = LEN_L // block
    return pl.pallas_call(
        project_norm_kernel,
        grid_spec=pltpu.PrefetchScalarGridSpec(
            num_scalar_prefetch=1,
            grid=(rows // block,),
            in_specs=[
                pl.BlockSpec((block, width), own_row_block(per_part)),
                whole((1, width)),
                whole((1, width)),
                whole((width, out)),
                whole((out, 1)),
            ],
            out_specs=[
                pl.BlockSpec((block, width), lambda i, _: (i, 0)),
                pl.BlockSpec((out, block), lambda i, _: (0, i)),
            ],
        ),
        out_shape=[
            jax.ShapeDtypeStruct((rows, width), BF16),
            jax.ShapeDtypeStruct((out, rows), BF16),
        ],
        compiler_params=params(),
        cost_estimate=cost(2 * rows * width * out, 4 * rows * width + 2 * out * rows),
        name="project_norm",
    )(rank, tokens, gain, shift, w_cat, b_col)


def project(normed, w_cat, b_col, block):
    rows, width = normed.shape
    out = w_cat.shape[1]
    return pl.pallas_call(
        project_kernel,
        grid=(rows // block,),
        in_specs=[
            pl.BlockSpec((block, width), lambda i: (i, 0)),
            whole((width, out)),
            whole((out, 1)),
        ],
        out_specs=pl.BlockSpec((out, block), lambda i: (0, i)),
        out_shape=jax.ShapeDtypeStruct((out, rows), BF16),
        compiler_params=params(),
        cost_estimate=cost(2 * rows * width * out, 2 * rows * width + 2 * out * rows),
        name="project",
    )(normed, w_cat, b_col)


def three_terms(value):
    high = value.astype(BF16).astype(F32)
    rest = value - high
    mid = rest.astype(BF16).astype(F32)
    return [high, mid, rest - mid]


def extra_rows(rows, count):
    at = lax.broadcasted_iota(jnp.int32, (16, count), 0)
    out = jnp.zeros((16, count), F32)
    for place, row in enumerate(rows):
        out = jnp.where(at == place, row, out)
    return out.astype(BF16)


def mask_row(length, count):
    at = lax.broadcasted_iota(jnp.int32, (1, count), 1)
    return jnp.where(at < length, 0.0, -1e30).astype(F32)


def scaled_query(query):
    wide = query.astype(F32) * (SCALE * LOG2E)
    high = wide.astype(BF16)
    return [high, (wide - high.astype(F32)).astype(BF16)]


def attend_forward_kernel(long_ref, short_ref, qkv_ref, out_ref, log_ref, *, block):
    heads = qkv_ref.shape[1]
    work = []
    for head in range(heads):
        work += [(head, 0, LEN_L, long_ref[0], at, block) for at in range(0, LEN_L, block)]
        for image in range(short_ref.shape[0]):
            work.append((head, LEN_L + image * LEN_S, LEN_S, short_ref[image], 0, LEN_S))

    def scores(item):
        head, start, count, length, at, size = item
        keys = qkv_ref[1, head, :, start : start + count]
        key_rows = jnp.concatenate([keys, keys, extra_rows([mask_row(length, count)], count)], 0)
        query = scaled_query(qkv_ref[0, head, :, start + at : start + at + size])
        query_rows = jnp.concatenate([*query, jnp.ones((16, size), BF16)], 0)
        return contract(key_rows, query_rows, 0, 0)

    def finish(item, score):
        head, start, count, length, at, size = item
        here = slice(start + at, start + at + size)
        values = qkv_ref[2, head, :, start : start + count]
        value_rows = jnp.concatenate([values, jnp.ones((16, count), BF16)], 0)
        top = jnp.max(score, axis=0, keepdims=True)
        weights = jnp.exp2(score - top).astype(BF16)
        mixed = contract(value_rows, weights, 1, 0)
        total = mixed[HEAD_DIM : HEAD_DIM + 1]
        out_ref[head, :, here] = (mixed[:HEAD_DIM] * (1.0 / total)).astype(BF16)
        log_ref[head, :, here] = top + jnp.log2(total)

    score = scores(work[0])
    for place, item in enumerate(work):
        later = scores(work[place + 1]) if place + 1 < len(work) else None
        finish(item, score)
        score = later


def attend_forward(long_len, short_len, qkv, block=1024):
    _, heads, _, rows = qkv.shape
    group = HEAD_GROUP
    pairs = heads * (LEN_L**2 + short_len.shape[0] * LEN_S**2)
    return pl.pallas_call(
        functools.partial(attend_forward_kernel, block=block),
        grid_spec=pltpu.PrefetchScalarGridSpec(
            num_scalar_prefetch=2,
            grid=(heads // group,),
            in_specs=[pl.BlockSpec((3, group, HEAD_DIM, rows), lambda h, *_: (0, h, 0, 0))],
            out_specs=[
                pl.BlockSpec((group, HEAD_DIM, rows), lambda h, *_: (h, 0, 0)),
                pl.BlockSpec((group, 1, rows), lambda h, *_: (h, 0, 0)),
            ],
        ),
        out_shape=[
            jax.ShapeDtypeStruct((heads, HEAD_DIM, rows), BF16),
            jax.ShapeDtypeStruct((heads, 1, rows), F32),
        ],
        compiler_params=params(),
        cost_estimate=cost(pairs * 2 * 512, 8 * heads * HEAD_DIM * rows, pairs),
        name="attend_forward",
    )(long_len, short_len, qkv)


def attend_backward_kernel(
    long_ref, short_ref, qkv_ref, out_ref, log_ref, grad_ref, dqkv_ref, *, block
):
    for head in range(qkv_ref.shape[1]):
        images = [(0, LEN_L, long_ref[0], block)]
        for image in range(short_ref.shape[0]):
            images.append((LEN_L + image * LEN_S, LEN_S, short_ref[image], LEN_S))
        for start, count, length, size in images:
            every = slice(start, start + count)
            keys = qkv_ref[1, head, :, every]
            values = qkv_ref[2, head, :, every]
            ones = jnp.ones((1, count), F32)
            key_rows = jnp.concatenate(
                [keys, keys, extra_rows([ones, ones, ones, mask_row(length, count)], count)], 0
            )
            value_rows = jnp.concatenate([values, extra_rows([ones, ones, ones], count)], 0)
            grad_values = grad_keys = None
            for at in range(start, start + count, size):
                here = slice(at, at + size)
                query = qkv_ref[0, head, :, here]
                grads = grad_ref[head, :, here]
                inner = jnp.sum(
                    grads.astype(F32) * out_ref[head, :, here].astype(F32), axis=0, keepdims=True
                )
                terms = three_terms(-log_ref[head, :, here]) + [jnp.ones((1, size), F32)]
                query_rows = jnp.concatenate([*scaled_query(query), extra_rows(terms, size)], 0)
                grad_rows = jnp.concatenate([grads, extra_rows(three_terms(-inner), size)], 0)
                score = contract(query_rows, key_rows, 0, 0)
                grad_probs = contract(grad_rows, value_rows, 0, 0)
                probs = jnp.exp2(score)
                grad_score = (probs * grad_probs).astype(BF16)
                part_values = contract(grads, probs.astype(BF16), 1, 0)
                part_keys = contract(query, grad_score, 1, 0)
                grad_values = part_values if grad_values is None else grad_values + part_values
                grad_keys = part_keys if grad_keys is None else grad_keys + part_keys
                dqkv_ref[0, head, :, here] = (contract(keys, grad_score, 1, 1) * SCALE).astype(BF16)
            dqkv_ref[1, head, :, every] = (grad_keys * SCALE).astype(BF16)
            dqkv_ref[2, head, :, every] = grad_values.astype(BF16)


def attend_backward(long_len, short_len, qkv, out, log_total, grads, block=256):
    _, heads, _, rows = qkv.shape
    group = HEAD_GROUP
    pairs = heads * (LEN_L**2 + short_len.shape[0] * LEN_S**2)
    all_three = pl.BlockSpec((3, group, HEAD_DIM, rows), lambda h, *_: (0, h, 0, 0))
    one = pl.BlockSpec((group, HEAD_DIM, rows), lambda h, *_: (h, 0, 0))
    return pl.pallas_call(
        functools.partial(attend_backward_kernel, block=block),
        grid_spec=pltpu.PrefetchScalarGridSpec(
            num_scalar_prefetch=2,
            grid=(heads // group,),
            in_specs=[all_three, one, pl.BlockSpec((group, 1, rows), lambda h, *_: (h, 0, 0)), one],
            out_specs=all_three,
        ),
        out_shape=jax.ShapeDtypeStruct(qkv.shape, BF16),
        compiler_params=params(),
        cost_estimate=cost(pairs * 5 * 512, 16 * heads * HEAD_DIM * rows, pairs),
        name="attend_backward",
    )(long_len, short_len, qkv, out, log_total, grads)


def middle_kernel(
    rank_ref, tok_ref, own_ref, other_ref, w_ref, b_ref, gain_ref, shift_ref, resid_ref, mid_ref
):
    attended = jnp.concatenate([own_ref[...], other_ref[...]], 0)
    resid = tok_ref[...].astype(F32) + contract(attended, w_ref[...], 0, 0) + b_ref[...]
    resid_ref[...] = resid
    hat, _ = norm_parts(resid)
    mid_ref[...] = (hat * gain_ref[...] + shift_ref[...]).astype(BF16)


def middle(rank, tokens, own, other, w_out, b_out, gain, shift, block):
    half, rows = own.shape
    width = w_out.shape[1]
    columns = pl.BlockSpec((half, block), lambda i, _: (0, i))
    out_rows = pl.BlockSpec((block, width), lambda i, _: (i, 0))
    return pl.pallas_call(
        middle_kernel,
        grid_spec=pltpu.PrefetchScalarGridSpec(
            num_scalar_prefetch=1,
            grid=(rows // block,),
            in_specs=[
                pl.BlockSpec((block, width), own_row_block(LEN_L // block)),
                columns,
                columns,
                whole((2 * half, width)),
                whole((1, width)),
                whole((1, width)),
                whole((1, width)),
            ],
            out_specs=[out_rows, out_rows],
        ),
        out_shape=[
            jax.ShapeDtypeStruct((rows, width), F32),
            jax.ShapeDtypeStruct((rows, width), BF16),
        ],
        compiler_params=params(),
        cost_estimate=cost(4 * rows * width * half, 12 * rows * width),
        name="middle",
    )(rank, tokens, own, other, w_out, b_out, gain, shift)


ERFC_TERMS = (0.254829592, -0.284496736, 1.421413741, -1.453152027, 1.061405429)
ERFC_SLOPE = 0.3275911


def gelu_and_slope(value):
    bell = jnp.exp2(value * value * (-0.5 * LOG2E))
    base = 1.0 + jnp.abs(value) * (ERFC_SLOPE * math.sqrt(0.5))
    ratio = 1.0 / base
    poly = ERFC_TERMS[4] * 0.5
    for term in ERFC_TERMS[3::-1]:
        poly = poly * ratio + term * 0.5
    tail = poly * ratio * bell
    below = jnp.where(value < 0.0, tail, 1.0 - tail)
    return value * below, below + value * bell * (1.0 / math.sqrt(2.0 * math.pi))


def feed_kernel(
    mid_ref, grad_ref, up_ref, b_ref, down_ref, sum_ref, gmid_ref, dup_ref, ddown_ref, db_ref,
    act_ref, gpre_ref, *, chunk,
):
    @pl.when(pl.program_id(0) == 0)
    def _():
        sum_ref[...] = jnp.zeros_like(sum_ref)
        gmid_ref[...] = jnp.zeros_like(gmid_ref)

    rows = mid_ref.shape[0]
    up, down, bias = up_ref[...], down_ref[...], b_ref[...]

    def products(at):
        here = slice(at, at + chunk)
        return (
            contract(mid_ref[here], up, 1, 0) + bias,
            contract(grad_ref[here], down, 1, 1),
        )

    now = products(0)
    db = None
    for at in range(0, rows, chunk):
        here = slice(at, at + chunk)
        later = products(at + chunk) if at + chunk < rows else None
        value, slope = gelu_and_slope(now[0])
        act = value.astype(BF16)
        gpre = (slope * now[1]).astype(BF16)
        act_ref[here] = act
        gpre_ref[here] = gpre
        part = jnp.sum(gpre.astype(F32), axis=0, keepdims=True)
        db = part if db is None else db + part
        sum_ref[here] += contract(act, down, 1, 0)
        gmid_ref[here] += contract(gpre, up, 1, 1)
        now = later
    db_ref[...] = db
    ddown_ref[...] = contract(act_ref[...], grad_ref[...], 0, 0).astype(BF16)
    dup_ref[...] = contract(mid_ref[...], gpre_ref[...], 0, 0).astype(BF16)


def feed(mid, grads, w_up, b_up, w_down, block=512, chunk=512):
    rows, width = mid.shape
    hidden = w_up.shape[1]
    return pl.pallas_call(
        functools.partial(feed_kernel, chunk=chunk),
        grid=(hidden // block,),
        in_specs=[
            whole((rows, width)),
            whole((rows, width)),
            pl.BlockSpec((width, block), lambda j: (0, j)),
            pl.BlockSpec((1, block), lambda j: (0, j)),
            pl.BlockSpec((block, width), lambda j: (j, 0)),
        ],
        out_specs=[
            whole((rows, width)),
            whole((rows, width)),
            pl.BlockSpec((width, block), lambda j: (0, j)),
            pl.BlockSpec((block, width), lambda j: (j, 0)),
            pl.BlockSpec((1, block), lambda j: (0, j)),
        ],
        out_shape=[
            jax.ShapeDtypeStruct((rows, width), F32),
            jax.ShapeDtypeStruct((rows, width), F32),
            jax.ShapeDtypeStruct((width, hidden), BF16),
            jax.ShapeDtypeStruct((hidden, width), BF16),
            jax.ShapeDtypeStruct((1, hidden), F32),
        ],
        scratch_shapes=[pltpu.VMEM((rows, block), BF16), pltpu.VMEM((rows, block), BF16)],
        compiler_params=params(),
        cost_estimate=cost(12 * rows * width * hidden, 20 * rows * width, 2 * rows * hidden),
        name="feed",
    )(mid, grads, w_up, b_up, w_down)


def branch_kernel(
    resid_ref, sum1_ref, sum2_ref, gmid1_ref, gmid2_ref, grad_ref, gain_ref, bdown_ref, w_ref,
    own_ref, other_ref, out_ref, gresid_ref, gown_ref, gother_ref, dw_ref, small_ref,
):
    @pl.when(pl.program_id(0) == 0)
    def _():
        dw_ref[...] = jnp.zeros_like(dw_ref)
        small_ref[...] = jnp.zeros_like(small_ref)

    resid = resid_ref[...]
    grads = grad_ref[...].astype(F32)
    out_ref[...] = (resid + sum1_ref[...] + sum2_ref[...] + bdown_ref[...]).astype(BF16)
    gmid = gmid1_ref[...] + gmid2_ref[...]
    hat, inv = norm_parts(resid)
    gresid = grads + norm_back(hat, inv, gmid * gain_ref[...])
    gresid_ref[...] = gresid
    branch = gresid.astype(BF16)
    gatt = contract(w_ref[...], branch, 1, 1).astype(BF16)
    half = own_ref.shape[0]
    gown_ref[...] = gatt[:half]
    gother_ref[...] = gatt[half:]
    attended = jnp.concatenate([own_ref[...], other_ref[...]], 0)
    dw_ref[...] += contract(attended, branch, 1, 0)
    small_ref[0:1] += jnp.sum(gmid * hat, axis=0, keepdims=True)
    small_ref[1:2] += jnp.sum(gmid, axis=0, keepdims=True)
    small_ref[2:3] += jnp.sum(gresid, axis=0, keepdims=True)
    small_ref[3:4] += jnp.sum(grads, axis=0, keepdims=True)


def branch(resid, sums, gmids, grads, gain, b_down, w_out, own, other, block):
    rows, width = resid.shape
    half = own.shape[0]
    by_row = pl.BlockSpec((block, width), lambda i: (i, 0))
    columns = pl.BlockSpec((half, block), lambda i: (0, i))
    return pl.pallas_call(
        branch_kernel,
        grid=(rows // block,),
        in_specs=[by_row] * 6
        + [whole((1, width)), whole((1, width)), whole((2 * half, width)), columns, columns],
        out_specs=[by_row, by_row, columns, columns, whole((2 * half, width)), whole((8, width))],
        out_shape=[
            jax.ShapeDtypeStruct((rows, width), BF16),
            jax.ShapeDtypeStruct((rows, width), F32),
            jax.ShapeDtypeStruct((half, rows), BF16),
            jax.ShapeDtypeStruct((half, rows), BF16),
            jax.ShapeDtypeStruct((2 * half, width), F32),
            jax.ShapeDtypeStruct((8, width), F32),
        ],
        compiler_params=params(),
        cost_estimate=cost(8 * rows * width * half, 32 * rows * width),
        name="branch",
    )(resid, *sums, *gmids, grads, gain, b_down, w_out, own, other)


def back_first_kernel(x_ref, d_ref, w_ref, gin_ref, dw_ref, db_ref, acc_ref):
    @pl.when(pl.program_id(0) == 0)
    def _():
        acc_ref[...] = jnp.zeros_like(acc_ref)
        db_ref[...] = jnp.zeros_like(db_ref)

    gin_ref[...] = contract(d_ref[...], w_ref[...], 0, 1)
    acc_ref[...] += contract(x_ref[...], d_ref[...], 0, 1)
    db_ref[...] += jnp.sum(d_ref[...].astype(F32), axis=1, keepdims=True)

    @pl.when(pl.program_id(0) == pl.num_programs(0) - 1)
    def _():
        dw_ref[...] = acc_ref[...].astype(BF16)


def back_first(normed, dqkv, w_cat, block):
    rows, width = normed.shape
    out = w_cat.shape[1]
    by_row = pl.BlockSpec((block, width), lambda i: (i, 0))
    return pl.pallas_call(
        back_first_kernel,
        grid=(rows // block,),
        in_specs=[by_row, pl.BlockSpec((out, block), lambda i: (0, i)), whole((width, out))],
        out_specs=[by_row, whole((width, out)), whole((out, 1))],
        out_shape=[
            jax.ShapeDtypeStruct((rows, width), F32),
            jax.ShapeDtypeStruct((width, out), BF16),
            jax.ShapeDtypeStruct((out, 1), F32),
        ],
        scratch_shapes=[pltpu.VMEM((width, out), F32)],
        compiler_params=params(),
        cost_estimate=cost(4 * rows * width * out, 10 * rows * width),
        name="back_first",
    )(normed, dqkv, w_cat)


def back_last_kernel(
    rank_ref, tok_ref, x_ref, d_ref, w_ref, gin_ref, gresid_ref, gain_ref,
    gtok_ref, dw_ref, db_ref, small_ref, acc_ref,
):
    @pl.when(pl.program_id(0) == 0)
    def _():
        acc_ref[...] = jnp.zeros_like(acc_ref)
        db_ref[...] = jnp.zeros_like(db_ref)
        small_ref[...] = jnp.zeros_like(small_ref)

    gin = gin_ref[...] + contract(d_ref[...], w_ref[...], 0, 1)
    acc_ref[...] += contract(x_ref[...], d_ref[...], 0, 1)
    db_ref[...] += jnp.sum(d_ref[...].astype(F32), axis=1, keepdims=True)
    hat, inv = norm_parts(tok_ref[...].astype(F32))
    gtok_ref[...] = gresid_ref[...] + norm_back(hat, inv, gin * gain_ref[...])
    small_ref[0:1] += jnp.sum(gin * hat, axis=0, keepdims=True)
    small_ref[1:2] += jnp.sum(gin, axis=0, keepdims=True)

    @pl.when(pl.program_id(0) == pl.num_programs(0) - 1)
    def _():
        dw_ref[...] = acc_ref[...].astype(BF16)


def back_last(rank, tokens, normed, dqkv, w_cat, gin, gresid, gain, block):
    rows, width = normed.shape
    out = w_cat.shape[1]
    by_row = pl.BlockSpec((block, width), lambda i, _: (i, 0))
    return pl.pallas_call(
        back_last_kernel,
        grid_spec=pltpu.PrefetchScalarGridSpec(
            num_scalar_prefetch=1,
            grid=(rows // block,),
            in_specs=[
                pl.BlockSpec((block, width), own_row_block(LEN_L // block)),
                by_row,
                pl.BlockSpec((out, block), lambda i, _: (0, i)),
                whole((width, out)),
                by_row,
                by_row,
                whole((1, width)),
            ],
            out_specs=[by_row, whole((width, out)), whole((out, 1)), whole((8, width))],
            scratch_shapes=[pltpu.VMEM((width, out), F32)],
        ),
        out_shape=[
            jax.ShapeDtypeStruct((rows, width), F32),
            jax.ShapeDtypeStruct((width, out), BF16),
            jax.ShapeDtypeStruct((out, 1), F32),
            jax.ShapeDtypeStruct((8, width), F32),
        ],
        compiler_params=params(),
        cost_estimate=cost(4 * rows * width * out, 16 * rows * width),
        name="back_last",
    )(rank, tokens, normed, dqkv, w_cat, gin, gresid, gain)


def swap_tp(array):
    return lax.ppermute(array, "tp", [(0, 1), (1, 0)])


def swap_dp(array, bit):
    count = lax.axis_size("dp")
    return lax.ppermute(array, "dp", [(i, i ^ bit) for i in range(count)])


def dp_bit(bit):
    return (lax.axis_index("dp") & bit) != 0


def joined(mine, theirs, second):
    return jnp.where(second, jnp.concatenate([theirs, mine], 0), jnp.concatenate([mine, theirs], 0))


def half_of(array, second):
    size = array.shape[0] // 2
    return lax.dynamic_slice_in_dim(array, jnp.where(second, size, 0), size, 0)


def fetch_other(array, bits):
    piece = array
    for bit in reversed(bits):
        piece = half_of(piece, dp_bit(bit))
    piece = swap_tp(piece)
    for bit in bits:
        piece = joined(piece, swap_dp(piece, bit), dp_bit(bit))
    return piece


def add_low(left, right):
    return (left.astype(F32) + right.astype(F32)).astype(BF16)


def sum_everywhere(own, other, stages):
    terms = [own, other]
    for stage in stages:
        if stage == "tp":
            terms = [add_low(terms[0], swap_tp(terms[1]))]
        else:
            second = dp_bit(stage)
            terms = [
                add_low(half_of(term, second), swap_dp(half_of(term, ~second), stage))
                for term in terms
            ]
    total = terms[0]
    for stage in reversed(stages):
        if stage != "tp":
            total = joined(total, swap_dp(total, stage), dp_bit(stage))
    return total.astype(F32)


def by_images(
    tokens, long_lengths, short_lengths, ln1_gain, ln1_bias, w_query, b_query, w_key, w_value,
    b_value, w_out, b_out, ln2_gain, ln2_bias, w_up, b_up, w_down, b_down, cotangent,
):
    rank = lax.axis_index("tp")
    rank_arr = jnp.reshape(rank, (1,)).astype(jnp.int32)
    second = rank == 1
    rows = tokens.shape[0] // 2
    width = tokens.shape[1]
    half = w_query.shape[1]
    heads = half // HEAD_DIM
    long_len = lax.dynamic_slice_in_dim(long_lengths, rank, 1, 0)
    shorts = short_lengths.shape[0] // 2
    short_len = lax.dynamic_slice_in_dim(short_lengths, rank * shorts, shorts, 0)
    row = lambda vector: vector.astype(F32).reshape(1, -1)
    core, xbit = 1, 2

    w_cat = jnp.concatenate([w_query, w_key, w_value], axis=1)
    w_cat2 = fetch_other(w_cat, [core, xbit])
    bias = jnp.concatenate([b_query, b_value, b_up]).astype(F32)
    bias2 = swap_tp(bias)

    def column(packed):
        return jnp.concatenate(
            [packed[:half], jnp.zeros((half,), F32), packed[half : 2 * half]]
        ).reshape(-1, 1)

    w_out2 = fetch_other(w_out, [core, xbit])
    w_up2 = fetch_other(w_up, [core, xbit])
    w_down2 = fetch_other(w_down, [core, xbit])
    kept = half_of(cotangent, second)
    got = swap_tp(half_of(cotangent, ~second))
    grads = joined(kept, got, second)

    normed, qkv = project_norm(
        rank_arr, tokens, row(ln1_gain), row(ln1_bias), w_cat, column(bias), rows, 512
    )
    parts = (3, heads, HEAD_DIM, rows)
    qkv = qkv.reshape(parts)
    att, log_total = attend_forward(long_len, short_len, qkv)
    qkv2 = project(normed, w_cat2, column(bias2), 512).reshape(parts)
    att2, log_total2 = attend_forward(long_len, short_len, qkv2)
    flat = (half, rows)
    att, att2 = att.reshape(flat), att2.reshape(flat)
    w_out_all = jnp.concatenate([w_out, w_out2], axis=0)
    resid, mid = middle(
        rank_arr, tokens, att, att2, w_out_all, row(b_out), row(ln2_gain), row(ln2_bias), 512
    )
    sum1, gmid1, dup1, ddown1, dbup1 = feed(mid, grads, w_up, row(bias[2 * half :]), w_down)
    sum2, gmid2, dup2, ddown2, dbup2 = feed(mid, grads, w_up2, row(bias2[2 * half :]), w_down2)
    out, gresid, gatt, gatt2, dwout, small2 = branch(
        resid, (sum1, sum2), (gmid1, gmid2), grads, row(ln2_gain), row(b_down), w_out_all,
        att, att2, 512,
    )
    by_head = (heads, HEAD_DIM, rows)
    zbits = [4, 8]
    grad_up = sum_everywhere(dup1, dup2, [core, xbit, *zbits, "tp"])
    dwout = dwout.astype(BF16)
    grad_down_out = sum_everywhere(
        jnp.concatenate([ddown1, dwout[:half]], 0),
        jnp.concatenate([ddown2, dwout[half:]], 0),
        [core, "tp", xbit, *zbits],
    )
    result = joined(half_of(out, second), swap_tp(half_of(out, ~second)), second)

    dqkv = attend_backward(
        long_len, short_len, qkv, att.reshape(by_head), log_total, gatt.reshape(by_head)
    ).reshape(3 * half, rows)
    gin, dw_cat, db = back_first(normed, dqkv, w_cat, 512)
    dqkv2 = attend_backward(
        long_len, short_len, qkv2, att2.reshape(by_head), log_total2, gatt2.reshape(by_head)
    ).reshape(3 * half, rows)
    gtok, dw_cat2, db2, small1 = back_last(
        rank_arr, tokens, normed, dqkv2, w_cat2, gin, gresid, row(ln1_gain), 512
    )
    grad_cat = sum_everywhere(dw_cat, dw_cat2, [core, xbit, *zbits, "tp"])
    sent = swap_tp(half_of(gtok, ~second).astype(BF16)).astype(F32)
    grad_tokens = joined(half_of(gtok, second), sent, second)

    one = jnp.concatenate([db[:half, 0], db[2 * half :, 0], dbup1[0]])
    two = jnp.concatenate([db2[:half, 0], db2[2 * half :, 0], dbup2[0]])
    ordered = joined(one, two, second)
    packed = jnp.concatenate([small1[0], small1[1], *(small2[i] for i in range(4)), ordered])
    packed = lax.psum(packed, ("dp", "tp"))
    small = packed[: 6 * width].reshape(6, width)
    mine = half_of(packed[6 * width :], second)
    hidden = w_down.shape[0]
    return (
        result,
        grad_tokens,
        small[0],
        small[1],
        grad_cat[:, :half],
        mine[:half],
        grad_cat[:, half : 2 * half],
        grad_cat[:, 2 * half :],
        mine[half : 2 * half],
        grad_down_out[hidden:],
        small[4],
        small[2],
        small[3],
        grad_up,
        mine[2 * half :],
        grad_down_out[:hidden],
        small[5],
    )


def layer_norm(values, gain, shift):
    center = values - jnp.mean(values, axis=-1, keepdims=True)
    spread = jnp.mean(center * center, axis=-1, keepdims=True)
    return center * lax.rsqrt(spread + 1e-06) * gain + shift


def dot_plain(left, right):
    return jnp.dot(left, right, preferred_element_type=jnp.float32)


def dot_rows(left, right):
    return lax.dot_general(
        left, right, (((0,), (0,)), ((), ())), preferred_element_type=jnp.float32
    )


def dot_back(left, right):
    return lax.dot_general(
        left, right, (((1,), (1,)), ((), ())), preferred_element_type=jnp.float32
    )


def group_shape(image_count, seq_len, head_count):
    per_step = math.gcd(image_count, max(1, 512 // seq_len))
    return (image_count // per_step, per_step, seq_len, head_count, HEAD_DIM)


def masked_scores(query_blk, key_blk, length_blk):
    seq_len = query_blk.shape[1]
    raw = jnp.einsum(
        "bqhd,bkhd->bhqk", query_blk, key_blk, preferred_element_type=jnp.float32
    ) * HEAD_DIM ** (-0.5)
    keep = jnp.arange(seq_len, dtype=jnp.int32)[None, :] < length_blk[:, None]
    return jnp.where(keep[:, None, None, :], raw, -1e30)


def attention_forward(queries, key_rows, value_rows, lengths, seq_len):
    image_count = lengths.shape[0]
    head_count = queries.shape[1] // HEAD_DIM
    block_shape = group_shape(image_count, seq_len, head_count)

    def one_step(block):
        query_blk, key_blk, value_blk, length_blk = block
        scores = masked_scores(query_blk, key_blk, length_blk)
        row_top = jnp.max(scores, axis=-1, keepdims=True)
        exp_terms = jnp.exp(scores - row_top)
        row_total = jnp.sum(exp_terms, axis=-1, keepdims=True)
        weights = (exp_terms / row_total).astype(jnp.bfloat16)
        mixed = jnp.einsum(
            "bhqk,bkhd->bqhd", weights, value_blk, preferred_element_type=jnp.float32
        )
        return (mixed, (row_top + jnp.log(row_total))[..., 0])

    mixed, log_total = lax.map(
        one_step,
        (
            queries.reshape(block_shape),
            key_rows.reshape(block_shape),
            value_rows.reshape(block_shape),
            lengths.reshape(block_shape[:2]),
        ),
    )
    return (mixed.reshape(image_count * seq_len, head_count * HEAD_DIM), log_total)


def attention_backward(queries, key_rows, value_rows, grads, lengths, log_total, seq_len):
    image_count = lengths.shape[0]
    head_count = queries.shape[1] // HEAD_DIM
    block_shape = group_shape(image_count, seq_len, head_count)
    scale = HEAD_DIM ** (-0.5)

    def one_step(block):
        query_blk, key_blk, value_blk, grad_blk, length_blk, total_blk = block
        scores = masked_scores(query_blk, key_blk, length_blk)
        probs = jnp.exp(scores - total_blk[..., None])
        grad_values = jnp.einsum(
            "bhqk,bqhd->bkhd",
            probs.astype(jnp.bfloat16),
            grad_blk,
            preferred_element_type=jnp.float32,
        )
        grad_probs = jnp.einsum(
            "bqhd,bkhd->bhqk", grad_blk, value_blk, preferred_element_type=jnp.float32
        )
        inner = jnp.sum(probs * grad_probs, axis=-1, keepdims=True)
        grad_scores = (probs * (grad_probs - inner)).astype(jnp.bfloat16)
        grad_queries = (
            jnp.einsum("bhqk,bkhd->bqhd", grad_scores, key_blk, preferred_element_type=jnp.float32)
            * scale
        )
        grad_keys = (
            jnp.einsum(
                "bhqk,bqhd->bkhd", grad_scores, query_blk, preferred_element_type=jnp.float32
            )
            * scale
        )
        return (grad_queries, grad_keys, grad_values)

    results = lax.map(
        one_step,
        (
            queries.reshape(block_shape),
            key_rows.reshape(block_shape),
            value_rows.reshape(block_shape),
            grads.reshape(block_shape),
            lengths.reshape(block_shape[:2]),
            log_total,
        ),
    )
    flat = (image_count * seq_len, head_count * HEAD_DIM)
    return tuple((item.reshape(flat) for item in results))


def local(
    tokens,
    long_lengths,
    short_lengths,
    ln1_gain,
    ln1_bias,
    w_query,
    b_query,
    w_key,
    w_value,
    b_value,
    w_out,
    b_out,
    ln2_gain,
    ln2_bias,
    w_up,
    b_up,
    w_down,
    b_down,
    cotangent,
):
    tp_count = lax.axis_size("tp")
    tp_rank = lax.axis_index("tp")
    row_count = tokens.shape[0]
    share = row_count // tp_count
    split = long_lengths.shape[0] * LEN_L
    gain_one = ln1_gain.astype(jnp.float32)
    shift_one = ln1_bias.astype(jnp.float32)
    gain_two = ln2_gain.astype(jnp.float32)
    shift_two = ln2_bias.astype(jnp.float32)
    normed_in = layer_norm(tokens.astype(jnp.float32), gain_one, shift_one).astype(jnp.bfloat16)
    queries = (dot_plain(normed_in, w_query) + b_query.astype(jnp.float32)).astype(jnp.bfloat16)
    key_rows = dot_plain(normed_in, w_key).astype(jnp.bfloat16)
    value_rows = (dot_plain(normed_in, w_value) + b_value.astype(jnp.float32)).astype(jnp.bfloat16)
    long_mixed, long_total = attention_forward(
        queries[:split], key_rows[:split], value_rows[:split], long_lengths, LEN_L
    )
    short_mixed, short_total = attention_forward(
        queries[split:], key_rows[split:], value_rows[split:], short_lengths, LEN_S
    )
    attended = jnp.concatenate([long_mixed, short_mixed], axis=0).astype(jnp.bfloat16)
    attn_sum = lax.psum_scatter(dot_plain(attended, w_out), "tp", scatter_dimension=0, tiled=True)
    own_tokens = lax.dynamic_slice_in_dim(tokens, tp_rank * share, share, 0).astype(jnp.float32)
    resid = own_tokens + attn_sum + b_out.astype(jnp.float32)
    normed_mid = layer_norm(resid, gain_two, shift_two).astype(jnp.bfloat16)
    grad_out = cotangent.astype(jnp.float32)
    mid_rows = lax.all_gather(normed_mid, "tp", axis=0, tiled=True)
    pre_up = dot_plain(mid_rows, w_up) + b_up.astype(jnp.float32)
    activ = jax.nn.gelu(pre_up, approximate=False).astype(jnp.bfloat16)
    ffn_sum = lax.psum_scatter(
        dot_plain(activ, w_down).astype(jnp.bfloat16), "tp", scatter_dimension=0, tiled=True
    ).astype(jnp.float32)
    result = resid + ffn_sum + b_down.astype(jnp.float32)
    grad_rows = lax.all_gather(cotangent, "tp", axis=0, tiled=True)
    grad_w_down = dot_rows(activ, grad_rows)
    grad_activ = dot_back(grad_rows, w_down)
    _, gelu_back = jax.vjp(lambda inner: jax.nn.gelu(inner, approximate=False), pre_up)
    grad_pre = gelu_back(grad_activ)[0].astype(jnp.bfloat16)
    grad_w_up = dot_rows(mid_rows, grad_pre)
    grad_b_up = jnp.sum(grad_pre.astype(jnp.float32), axis=0)
    grad_mid = lax.psum_scatter(dot_back(grad_pre, w_up), "tp", scatter_dimension=0, tiled=True)
    _, norm_two_back = jax.vjp(layer_norm, resid, gain_two, shift_two)
    grad_resid_norm, grad_gain_two, grad_shift_two = norm_two_back(grad_mid)
    grad_resid = grad_out + grad_resid_norm
    grad_b_down = jnp.sum(grad_out, axis=0)
    grad_b_out = jnp.sum(grad_resid, axis=0)
    grad_branch = lax.all_gather(grad_resid.astype(jnp.bfloat16), "tp", axis=0, tiled=True)
    grad_w_out = dot_rows(attended, grad_branch)
    grad_attended = dot_back(grad_branch, w_out).astype(jnp.bfloat16)
    long_grads = attention_backward(
        queries[:split],
        key_rows[:split],
        value_rows[:split],
        grad_attended[:split],
        long_lengths,
        long_total,
        LEN_L,
    )
    short_grads = attention_backward(
        queries[split:],
        key_rows[split:],
        value_rows[split:],
        grad_attended[split:],
        short_lengths,
        short_total,
        LEN_S,
    )
    grad_queries = jnp.concatenate([long_grads[0], short_grads[0]], axis=0).astype(jnp.bfloat16)
    grad_keys = jnp.concatenate([long_grads[1], short_grads[1]], axis=0).astype(jnp.bfloat16)
    grad_values = jnp.concatenate([long_grads[2], short_grads[2]], axis=0).astype(jnp.bfloat16)
    grad_w_query = dot_rows(normed_in, grad_queries)
    grad_b_query = jnp.sum(grad_queries.astype(jnp.float32), axis=0)
    grad_w_key = dot_rows(normed_in, grad_keys)
    grad_w_value = dot_rows(normed_in, grad_values)
    grad_b_value = jnp.sum(grad_values.astype(jnp.float32), axis=0)
    grad_in = lax.psum_scatter(
        dot_back(grad_queries, w_query)
        + dot_back(grad_keys, w_key)
        + dot_back(grad_values, w_value),
        "tp",
        scatter_dimension=0,
        tiled=True,
    )
    _, norm_one_back = jax.vjp(layer_norm, own_tokens, gain_one, shift_one)
    grad_tokens_norm, grad_gain_one, grad_shift_one = norm_one_back(grad_in)
    grad_tokens = grad_resid + grad_tokens_norm
    summed = lax.psum(
        (
            grad_w_query,
            grad_b_query,
            grad_w_key,
            grad_w_value,
            grad_b_value,
            grad_w_out,
            grad_w_up,
            grad_b_up,
            grad_w_down,
        ),
        "dp",
    )
    shared = lax.psum(
        (grad_gain_one, grad_shift_one, grad_b_out, grad_gain_two, grad_shift_two, grad_b_down),
        ("dp", "tp"),
    )
    return (
        result.astype(jnp.bfloat16),
        grad_tokens,
        shared[0],
        shared[1],
        summed[0],
        summed[1],
        summed[2],
        summed[3],
        summed[4],
        summed[5],
        shared[2],
        shared[3],
        shared[4],
        summed[6],
        summed[7],
        summed[8],
        shared[5],
    )


def pick(*arrays):
    tokens, long_lengths, short_lengths, w_query, w_up = (arrays[i] for i in (0, 1, 2, 5, 14))
    fits = (
        lax.axis_size("tp") == 2
        and lax.axis_size("dp") == 16
        and long_lengths.shape[0] == 2
        and short_lengths.shape[0] == 8
        and tokens.shape == (2 * LEN_L + 8 * LEN_S, 768)
        and w_query.shape[1] == 8 * HEAD_DIM
        and w_up.shape[1] == 1536
    )
    return by_images(*arrays) if fits else local(*arrays)


def solution(mesh):
    placed = (
        P("dp", None),
        P("dp"),
        P("dp"),
        P(),
        P(),
        P(None, "tp"),
        P("tp"),
        P(None, "tp"),
        P(None, "tp"),
        P("tp"),
        P("tp", None),
        P(),
        P(),
        P(),
        P(None, "tp"),
        P("tp"),
        P("tp", None),
        P(),
        P(("dp", "tp"), None),
    )
    return jax.shard_map(
        pick,
        mesh=mesh,
        in_specs=placed,
        out_specs=(
            P(("dp", "tp"), None),
            P(("dp", "tp"), None),
            P(),
            P(),
            P(None, "tp"),
            P("tp"),
            P(None, "tp"),
            P(None, "tp"),
            P("tp"),
            P("tp", None),
            P(),
            P(),
            P(),
            P(None, "tp"),
            P("tp"),
            P("tp", None),
            P(),
        ),
        check_vma=False,
    )
```

```python
import functools
import math

import jax
import jax.numpy as jnp
from jax import lax
from jax.experimental import pallas as pl
from jax.experimental.pallas import tpu as pltpu
from jax.sharding import PartitionSpec as P

HEAD_DIM = 48
LEN_L = 1024
LEN_S = 256
F32 = jnp.float32
BF16 = jnp.bfloat16
LOG2E = math.log2(math.e)
SCALE = HEAD_DIM ** (-0.5)
VMEM_LIMIT = 58 << 20
HEAD_GROUP = 2


def contract(left, right, left_dim, right_dim):
    return lax.dot_general(
        left, right, (((left_dim,), (right_dim,)), ((), ())), preferred_element_type=F32
    )


def params():
    return pltpu.CompilerParams(vmem_limit_bytes=VMEM_LIMIT)


def cost(flops, bytes_accessed, transcendentals=0):
    return pl.CostEstimate(
        flops=int(flops), bytes_accessed=int(bytes_accessed), transcendentals=int(transcendentals)
    )


def whole(shape):
    zeros = (0,) * len(shape)
    return pl.BlockSpec(shape, lambda *_: zeros)


def norm_parts(values):
    center = values - jnp.mean(values, axis=-1, keepdims=True)
    inv = lax.rsqrt(jnp.mean(center * center, axis=-1, keepdims=True) + 1e-06)
    return center * inv, inv


def norm_back(hat, inv, grad_hat):
    mean_grad = jnp.mean(grad_hat, axis=-1, keepdims=True)
    mean_both = jnp.mean(grad_hat * hat, axis=-1, keepdims=True)
    return inv * (grad_hat - mean_grad - hat * mean_both)


def project_norm_kernel(rank_ref, tok_ref, gain_ref, shift_ref, w_ref, b_ref, x_ref, own_ref, qkv_ref):
    hat, _ = norm_parts(tok_ref[...].astype(F32))
    normed = (hat * gain_ref[...] + shift_ref[...]).astype(BF16)
    x_ref[...] = normed
    own_ref[...] = tok_ref[...]
    qkv_ref[0] = (contract(w_ref[...], normed, 0, 1) + b_ref[...]).astype(BF16)


def project_kernel(_, x_ref, w_ref, b_ref, qkv_ref):
    qkv_ref[0] = (contract(w_ref[...], x_ref[...], 0, 1) + b_ref[...]).astype(BF16)


def own_row_block(per_part):
    def index(i, rank_ref):
        part = i // per_part
        return (part * 2 * per_part + rank_ref[0] * per_part + i % per_part, 0)

    return index


def project_norm(rank, tokens, gain, shift, w_cat, b_col, rows, block):
    width, out = w_cat.shape
    per_part = LEN_L // block
    by_row = pl.BlockSpec((block, width), lambda i, _: (i, 0))
    return pl.pallas_call(
        project_norm_kernel,
        grid_spec=pltpu.PrefetchScalarGridSpec(
            num_scalar_prefetch=1,
            grid=(rows // block,),
            in_specs=[
                pl.BlockSpec((block, width), own_row_block(per_part)),
                whole((1, width)),
                whole((1, width)),
                whole((width, out)),
                whole((out, 1)),
            ],
            out_specs=[by_row, by_row, pl.BlockSpec((1, out, block), lambda i, _: (0, 0, i))],
        ),
        out_shape=[
            jax.ShapeDtypeStruct((rows, width), BF16),
            jax.ShapeDtypeStruct((rows, width), BF16),
            jax.ShapeDtypeStruct((2, out, rows), BF16),
        ],
        compiler_params=params(),
        cost_estimate=cost(2 * rows * width * out, 4 * rows * width + 2 * out * rows),
        name="project_norm",
    )(rank, tokens, gain, shift, w_cat, b_col)


def project(both, normed, w_cat, b_col, block):
    rows, width = normed.shape
    out = w_cat.shape[1]
    return pl.pallas_call(
        project_kernel,
        grid=(rows // block,),
        in_specs=[
            pl.BlockSpec(memory_space=pl.ANY),
            pl.BlockSpec((block, width), lambda i: (i, 0)),
            whole((width, out)),
            whole((out, 1)),
        ],
        out_specs=pl.BlockSpec((1, out, block), lambda i: (1, 0, i)),
        out_shape=jax.ShapeDtypeStruct(both.shape, BF16),
        input_output_aliases={0: 0},
        compiler_params=params(),
        cost_estimate=cost(2 * rows * width * out, 2 * rows * width + 2 * out * rows),
        name="project",
    )(both, normed, w_cat, b_col)


def three_terms(value):
    high = value.astype(BF16).astype(F32)
    rest = value - high
    mid = rest.astype(BF16).astype(F32)
    return [high, mid, rest - mid]


def extra_rows(rows, count):
    at = lax.broadcasted_iota(jnp.int32, (16, count), 0)
    out = jnp.zeros((16, count), F32)
    for place, row in enumerate(rows):
        out = jnp.where(at == place, row, out)
    return out.astype(BF16)


def scaled_query(query):
    wide = query.astype(F32) * (SCALE * LOG2E)
    high = wide.astype(BF16)
    return [high, (wide - high.astype(F32)).astype(BF16)]


def attend_forward_kernel(mask_ref, qkv_ref, *refs, block):
    out_ref, log_ref = refs[-2:]
    heads, rows = qkv_ref.shape[2], qkv_ref.shape[4]
    work = []
    for head in range(heads):
        work += [(head, 0, LEN_L, at, block) for at in range(0, LEN_L, block)]
        work += [(head, start, LEN_S, 0, LEN_S) for start in range(LEN_L, rows, LEN_S)]

    def scores(item):
        head, start, count, at, size = item
        every = slice(start, start + count)
        keys = qkv_ref[0, 1, head, :, every]
        key_rows = jnp.concatenate([keys, keys, extra_rows([mask_ref[:, every]], count)], 0)
        query = scaled_query(qkv_ref[0, 0, head, :, start + at : start + at + size])
        query_rows = jnp.concatenate([*query, jnp.ones((16, size), BF16)], 0)
        return contract(key_rows, query_rows, 0, 0)

    def finish(item, score):
        head, start, count, at, size = item
        here = slice(start + at, start + at + size)
        values = qkv_ref[0, 2, head, :, start : start + count]
        value_rows = jnp.concatenate([values, jnp.ones((16, count), BF16)], 0)
        top = jnp.max(score, axis=0, keepdims=True)
        weights = jnp.exp2(score - top).astype(BF16)
        mixed = contract(value_rows, weights, 1, 0)
        total = mixed[HEAD_DIM : HEAD_DIM + 1]
        out_ref[0, head, :, here] = (mixed[:HEAD_DIM] * (1.0 / total)).astype(BF16)
        log_ref[0, head, :, here] = top + jnp.log2(total)

    score = scores(work[0])
    for place, item in enumerate(work):
        later = scores(work[place + 1]) if place + 1 < len(work) else None
        finish(item, score)
        score = later


def pair_count(heads, rows):
    return heads * (LEN_L**2 + (rows - LEN_L) * LEN_S)


def attend_forward(mask, qkv, part, earlier=(), block=1024):
    _, _, heads, _, rows = qkv.shape
    group = HEAD_GROUP
    pairs = pair_count(heads, rows)
    return pl.pallas_call(
        functools.partial(attend_forward_kernel, block=block),
        grid=(heads // group,),
        in_specs=[
            whole((1, rows)),
            pl.BlockSpec((1, 3, group, HEAD_DIM, rows), lambda h: (part, 0, h, 0, 0)),
            *(pl.BlockSpec(memory_space=pl.ANY) for _ in earlier),
        ],
        out_specs=[
            pl.BlockSpec((1, group, HEAD_DIM, rows), lambda h: (part, h, 0, 0)),
            pl.BlockSpec((1, group, 1, rows), lambda h: (part, h, 0, 0)),
        ],
        out_shape=[
            jax.ShapeDtypeStruct((2, heads, HEAD_DIM, rows), BF16),
            jax.ShapeDtypeStruct((2, heads, 1, rows), F32),
        ],
        input_output_aliases={2: 0, 3: 1} if earlier else {},
        compiler_params=params(),
        cost_estimate=cost(pairs * 2 * 512, 8 * heads * HEAD_DIM * rows, pairs),
        name="attend_forward",
    )(mask, qkv, *earlier)


class PlaneSum:
    COPIES = 10

    def __init__(self, refs):
        (self.own, self.seen, self.out, self.acc, self.from_core, self.seen_here, self.from_x,
         self.from_z, self.send, self.recv, self.local) = refs
        me = lax.axis_index("dp")
        self.core, self.x, self.z = me % 2, (me // 2) % 2, me // 4
        self.rows = self.own.shape[0]

    @staticmethod
    def buffers(shape):
        rows, width = shape
        return [
            pltpu.VMEM((rows // 2, width), BF16),
            pltpu.VMEM((rows // 2, width), BF16),
            pltpu.VMEM((rows // 2, width), BF16),
            pltpu.VMEM((rows // 4, width), BF16),
            pltpu.VMEM((3, rows // 16, width), BF16),
            pltpu.SemaphoreType.DMA((PlaneSum.COPIES,)),
            pltpu.SemaphoreType.DMA((PlaneSum.COPIES,)),
            pltpu.SemaphoreType.DMA((3,)),
        ]

    def device(self, z, x, core):
        return {"dp": (z * 2 + x) * 2 + core}

    def copy(self, source, target, place, device):
        return pltpu.make_async_remote_copy(
            src_ref=source,
            dst_ref=target,
            send_sem=self.send.at[place],
            recv_sem=self.recv.at[place],
            device_id=device,
            device_id_type=pl.DeviceIdType.MESH,
        )

    def part(self, ref, start, count):
        return ref.at[pl.ds(pl.multiple_of(start, 16), count)]

    def core_copy(self):
        half = self.rows // 2
        return self.copy(
            self.part(self.own, (1 - self.core) * half, half),
            self.from_core,
            0,
            self.device(self.z, self.x, 1 - self.core),
        )

    def local_copies(self):
        half = self.rows // 2
        return [
            pltpu.make_async_copy(
                self.part(self.own, self.core * half, half), self.acc, self.local.at[0]
            ),
            pltpu.make_async_copy(self.seen, self.seen_here, self.local.at[1]),
        ]

    def x_copy(self):
        count = self.rows // 4
        return self.copy(
            self.part(self.acc, (1 - self.x) * count, count),
            self.from_x,
            1,
            self.device(self.z, 1 - self.x, self.core),
        )

    def z_copies(self):
        count = self.rows // 16
        copies = []
        for step in (1, 2, 3):
            there = (self.z + step) % 4
            copies.append(
                self.copy(
                    self.part(self.acc, self.x * 4 * count + there * count, count),
                    self.from_z.at[step - 1],
                    1 + step,
                    self.device(there, self.x, self.core),
                )
            )
        return copies

    def piece(self):
        count = self.rows // 16
        inside = self.x * 4 * count + self.z * count
        place = self.core * 8 * count + inside
        return self.part(self.acc, inside, count), self.part(self.out, place, count)

    def keep_copy(self):
        mine, place = self.piece()
        return pltpu.make_async_copy(mine, place, self.local.at[2])

    def back_z_copies(self):
        mine, place = self.piece()
        return [
            self.copy(mine, place, 4 + step, self.device((self.z + step) % 4, self.x, self.core))
            for step in (1, 2, 3)
        ]

    def back_x_copy(self):
        count = self.rows // 4
        place = self.part(self.out, self.core * 2 * count + self.x * count, count)
        return self.copy(place, place, 8, self.device(self.z, 1 - self.x, self.core))

    def back_core_copy(self):
        count = self.rows // 2
        place = self.part(self.out, self.core * count, count)
        return self.copy(place, place, 9, self.device(self.z, self.x, 1 - self.core))

    def add(self, start, count, terms):
        tile = 48
        width = self.acc.shape[1]

        def body(i, _):
            at = pl.multiple_of(i * tile, 16)
            here = pl.ds(pl.multiple_of(start + at, 16), tile)
            total = self.acc[here, :].astype(F32)
            for term in terms:
                total = total + term[pl.ds(at, tile), :].astype(F32)
            self.acc[here, :] = total.astype(BF16)
            return 0

        lax.fori_loop(0, count // tile, body, 0)

    def begin(self):
        self.core_copy().start()
        for copy in self.local_copies():
            copy.start()

    def along_x(self):
        self.core_copy().wait()
        for copy in self.local_copies():
            copy.wait()
        self.add(0, self.rows // 2, [self.from_core, self.seen_here])
        self.x_copy().start()

    def along_z(self):
        self.x_copy().wait()
        count = self.rows // 4
        self.add(self.x * count, count, [self.from_x])
        for copy in self.z_copies():
            copy.start()

    def back_along_z(self):
        for copy in self.z_copies():
            copy.wait()
        count = self.rows // 16
        inside = self.x * 4 * count + self.z * count
        self.add(inside, count, [self.from_z.at[i] for i in range(3)])
        self.keep_copy().start()
        for copy in self.back_z_copies():
            copy.start()

    def back_along_x(self):
        self.keep_copy().wait()
        for copy in self.back_z_copies():
            copy.wait()
        self.back_x_copy().start()

    def back_to_core(self):
        self.back_x_copy().wait()
        self.back_core_copy().start()

    def end(self):
        self.back_core_copy().wait()


def greet_plane():
    me = lax.axis_index("dp")
    core, x, z = me % 2, (me // 2) % 2, me // 4
    barrier = pltpu.get_barrier_semaphore()
    others = [(z, x, 1 - core), (z, 1 - x, core)] + [((z + i) % 4, x, core) for i in (1, 2, 3)]
    for other_z, other_x, other_core in others:
        pl.semaphore_signal(
            barrier,
            inc=1,
            device_id={"dp": (other_z * 2 + other_x) * 2 + other_core},
            device_id_type=pl.DeviceIdType.MESH,
        )
    pl.semaphore_wait(barrier, len(others))


SUM_STEPS = (
    (0, 1, 5, 8, 12, 15, 15),
    (0, 4, 8, 12, 15, 15, 15),
    (0, 2, 5, 9, 12, 15, 15),
)


def attend_backward_kernel(*refs, block, sums):
    mask_ref, qkv_ref, out_ref, log_ref, grad_ref = refs[:5]
    sum_in = refs[5 : 5 + 2 * sums]
    dqkv_ref = refs[5 + 2 * sums]
    sum_out = refs[6 + 2 * sums : 6 + 3 * sums]
    scratch = refs[6 + 3 * sums :]
    each = len(scratch) // sums
    plane = [
        PlaneSum((*sum_in[2 * i : 2 * i + 2], sum_out[i], *scratch[each * i : each * (i + 1)]))
        for i in range(sums)
    ]
    step = pl.program_id(0)

    for at in sorted({at for times in SUM_STEPS for at in times[:-2]}):

        @pl.when(step == at)
        def _(at=at):
            if at == 0:
                greet_plane()
            for one, times in zip(plane, SUM_STEPS):
                for when, action in zip(
                    times[:-2],
                    (one.begin, one.along_x, one.along_z, one.back_along_z, one.back_along_x),
                ):
                    if when == at:
                        action()

    rows = qkv_ref.shape[4]
    images = [(0, LEN_L, block)] + [(at, LEN_S, LEN_S) for at in range(LEN_L, rows, LEN_S)]
    for start, count, size in images:
        every = slice(start, start + count)
        keys = qkv_ref[0, 1, 0, :, every]
        values = qkv_ref[0, 2, 0, :, every]
        ones = jnp.ones((1, count), F32)
        key_rows = jnp.concatenate(
            [keys, keys, extra_rows([ones, ones, ones, mask_ref[:, every]], count)], 0
        )
        value_rows = jnp.concatenate([values, extra_rows([ones, ones, ones], count)], 0)
        grad_values = grad_keys = None
        for at in range(start, start + count, size):
            here = slice(at, at + size)
            query = qkv_ref[0, 0, 0, :, here]
            grads = grad_ref[0, 0, :, here]
            inner = jnp.sum(
                grads.astype(F32) * out_ref[0, 0, :, here].astype(F32), axis=0, keepdims=True
            )
            terms = three_terms(-log_ref[0, 0, :, here]) + [jnp.ones((1, size), F32)]
            query_rows = jnp.concatenate([*scaled_query(query), extra_rows(terms, size)], 0)
            grad_rows = jnp.concatenate([grads, extra_rows(three_terms(-inner), size)], 0)
            score = contract(query_rows, key_rows, 0, 0)
            grad_probs = contract(grad_rows, value_rows, 0, 0)
            probs = jnp.exp2(score)
            grad_score = (probs * grad_probs).astype(BF16)
            part_values = contract(grads, probs.astype(BF16), 1, 0)
            part_keys = contract(query, grad_score, 1, 0)
            grad_values = part_values if grad_values is None else grad_values + part_values
            grad_keys = part_keys if grad_keys is None else grad_keys + part_keys
            dqkv_ref[0, 0, 0, :, here] = (contract(keys, grad_score, 1, 1) * SCALE).astype(BF16)
        dqkv_ref[0, 1, 0, :, every] = (grad_keys * SCALE).astype(BF16)
        dqkv_ref[0, 2, 0, :, every] = grad_values.astype(BF16)

    @pl.when(step == pl.num_programs(0) - 1)
    def _():
        for one in plane:
            one.back_to_core()
        for one in plane:
            one.end()


def attend_backward(mask, qkv, out, log_total, grads, terms, block=256):
    _, _, heads, _, rows = qkv.shape
    pairs = pair_count(2 * heads, rows)
    anywhere = pl.BlockSpec(memory_space=pl.ANY)
    all_three = pl.BlockSpec((1, 3, 1, HEAD_DIM, rows), lambda h: (h // heads, 0, h % heads, 0, 0))
    one = pl.BlockSpec((1, 1, HEAD_DIM, rows), lambda h: (h // heads, h % heads, 0, 0))
    row = pl.BlockSpec((1, 1, 1, rows), lambda h: (h // heads, h % heads, 0, 0))
    shapes = [own.shape for own, _ in terms]
    return pl.pallas_call(
        functools.partial(attend_backward_kernel, block=block, sums=len(terms)),
        grid=(2 * heads,),
        in_specs=[whole((1, rows)), all_three, one, row, one] + [anywhere] * (2 * len(terms)),
        out_specs=[all_three] + [anywhere] * len(terms),
        out_shape=[jax.ShapeDtypeStruct(qkv.shape, BF16)]
        + [jax.ShapeDtypeStruct(shape, BF16) for shape in shapes],
        scratch_shapes=[ref for shape in shapes for ref in PlaneSum.buffers(shape)],
        compiler_params=pltpu.CompilerParams(
            vmem_limit_bytes=VMEM_LIMIT, collective_id=0, has_side_effects=True
        ),
        cost_estimate=cost(pairs * 5 * 512, 32 * heads * HEAD_DIM * rows, pairs),
        name="attend_backward",
    )(mask, qkv, out, log_total, grads, *(array for pair in terms for array in pair))


def middle_kernel(
    tok_ref, att_ref, w_ref, b_ref, gain_ref, shift_ref, resid_ref, mid_ref
):
    resid = tok_ref[...].astype(F32) + contract(att_ref[...], w_ref[...], 0, 0) + b_ref[...]
    resid_ref[...] = resid
    hat, _ = norm_parts(resid)
    mid_ref[...] = (hat * gain_ref[...] + shift_ref[...]).astype(BF16)


def middle(tokens, attended, w_out, b_out, gain, shift, block):
    heads_width, rows = attended.shape
    width = w_out.shape[1]
    by_row = pl.BlockSpec((block, width), lambda i: (i, 0))
    return pl.pallas_call(
        middle_kernel,
        grid=(rows // block,),
        in_specs=[
            by_row,
            pl.BlockSpec((heads_width, block), lambda i: (0, i)),
            whole((heads_width, width)),
            whole((1, width)),
            whole((1, width)),
            whole((1, width)),
        ],
        out_specs=[by_row, by_row],
        out_shape=[
            jax.ShapeDtypeStruct((rows, width), F32),
            jax.ShapeDtypeStruct((rows, width), BF16),
        ],
        compiler_params=params(),
        cost_estimate=cost(2 * rows * width * heads_width, 12 * rows * width),
        name="middle",
    )(tokens, attended, w_out, b_out, gain, shift)


ERFC_TERMS = (0.254829592, -0.284496736, 1.421413741, -1.453152027, 1.061405429)
ERFC_SLOPE = 0.3275911


def gelu_and_slope(value):
    bell = jnp.exp2(value * value * (-0.5 * LOG2E))
    base = 1.0 + jnp.abs(value) * (ERFC_SLOPE * math.sqrt(0.5))
    ratio = 1.0 / base
    poly = ERFC_TERMS[4] * 0.5
    for term in ERFC_TERMS[3::-1]:
        poly = poly * ratio + term * 0.5
    tail = poly * ratio * bell
    below = jnp.where(value < 0.0, tail, 1.0 - tail)
    return value * below, below + value * bell * (1.0 / math.sqrt(2.0 * math.pi))


def feed_kernel(
    mid_ref, grad_ref, up_ref, b_ref, down_ref, sum_ref, gmid_ref, dup_ref, ddown_ref, db_ref,
    act_ref, gpre_ref, *, chunk,
):
    @pl.when(pl.program_id(0) == 0)
    def _():
        sum_ref[...] = jnp.zeros_like(sum_ref)
        gmid_ref[...] = jnp.zeros_like(gmid_ref)

    rows = mid_ref.shape[0]
    up, down, bias = up_ref[...], down_ref[...], b_ref[...]

    def products(at):
        here = slice(at, at + chunk)
        return (
            contract(mid_ref[here], up, 1, 0) + bias,
            contract(grad_ref[here], down, 1, 1),
        )

    now = products(0)
    db = None
    for at in range(0, rows, chunk):
        here = slice(at, at + chunk)
        later = products(at + chunk) if at + chunk < rows else None
        value, slope = gelu_and_slope(now[0])
        act = value.astype(BF16)
        gpre = (slope * now[1]).astype(BF16)
        act_ref[here] = act
        gpre_ref[here] = gpre
        part = jnp.sum(gpre.astype(F32), axis=0, keepdims=True)
        db = part if db is None else db + part
        sum_ref[here] += contract(act, down, 1, 0)
        gmid_ref[here] += contract(gpre, up, 1, 1)
        now = later
    db_ref[...] = db
    ddown_ref[...] = contract(act_ref[...], grad_ref[...], 0, 0).astype(BF16)
    dup_ref[...] = contract(mid_ref[...], gpre_ref[...], 0, 0).astype(BF16)


def feed(mid, grads, w_up, b_up, w_down, block=512, chunk=512):
    rows, width = mid.shape
    hidden = w_up.shape[1]
    return pl.pallas_call(
        functools.partial(feed_kernel, chunk=chunk),
        grid=(hidden // block,),
        in_specs=[
            whole((rows, width)),
            whole((rows, width)),
            pl.BlockSpec((width, block), lambda j: (0, j)),
            pl.BlockSpec((1, block), lambda j: (0, j)),
            pl.BlockSpec((block, width), lambda j: (j, 0)),
        ],
        out_specs=[
            whole((rows, width)),
            whole((rows, width)),
            pl.BlockSpec((width, block), lambda j: (0, j)),
            pl.BlockSpec((block, width), lambda j: (j, 0)),
            pl.BlockSpec((1, block), lambda j: (0, j)),
        ],
        out_shape=[
            jax.ShapeDtypeStruct((rows, width), F32),
            jax.ShapeDtypeStruct((rows, width), F32),
            jax.ShapeDtypeStruct((width, hidden), BF16),
            jax.ShapeDtypeStruct((hidden, width), BF16),
            jax.ShapeDtypeStruct((1, hidden), F32),
        ],
        scratch_shapes=[pltpu.VMEM((rows, block), BF16), pltpu.VMEM((rows, block), BF16)],
        compiler_params=params(),
        cost_estimate=cost(12 * rows * width * hidden, 20 * rows * width, 2 * rows * hidden),
        name="feed",
    )(mid, grads, w_up, b_up, w_down)


def branch_kernel(
    resid_ref, sum1_ref, sum2_ref, gmid1_ref, gmid2_ref, grad_ref, gain_ref, bdown_ref, w_ref,
    att_ref, out_ref, gresid_ref, gatt_ref, dw_own_ref, dw_other_ref, small_ref, acc_ref,
):
    @pl.when(pl.program_id(0) == 0)
    def _():
        acc_ref[...] = jnp.zeros_like(acc_ref)
        small_ref[...] = jnp.zeros_like(small_ref)

    resid = resid_ref[...]
    grads = grad_ref[...].astype(F32)
    out_ref[...] = (resid + sum1_ref[...] + sum2_ref[...] + bdown_ref[...]).astype(BF16)
    gmid = gmid1_ref[...] + gmid2_ref[...]
    hat, inv = norm_parts(resid)
    gresid = grads + norm_back(hat, inv, gmid * gain_ref[...])
    gresid_ref[...] = gresid
    branch = gresid.astype(BF16)
    gatt_ref[...] = contract(w_ref[...], branch, 1, 1).astype(BF16)
    acc_ref[...] += contract(branch, att_ref[...], 0, 1)
    small_ref[0:1] += jnp.sum(gmid * hat, axis=0, keepdims=True)
    small_ref[1:2] += jnp.sum(gmid, axis=0, keepdims=True)
    small_ref[2:3] += jnp.sum(gresid, axis=0, keepdims=True)
    small_ref[3:4] += jnp.sum(grads, axis=0, keepdims=True)

    @pl.when(pl.program_id(0) == pl.num_programs(0) - 1)
    def _():
        half = dw_own_ref.shape[1]
        dw_own_ref[...] = acc_ref[:, :half].astype(BF16)
        dw_other_ref[...] = acc_ref[:, half:].astype(BF16)


def branch(resid, sums, gmids, grads, gain, b_down, w_out, attended, block):
    rows, width = resid.shape
    heads_width = attended.shape[0]
    by_row = pl.BlockSpec((block, width), lambda i: (i, 0))
    columns = pl.BlockSpec((heads_width, block), lambda i: (0, i))
    half = (width, heads_width // 2)
    return pl.pallas_call(
        branch_kernel,
        grid=(rows // block,),
        in_specs=[by_row] * 6
        + [whole((1, width)), whole((1, width)), whole((heads_width, width)), columns],
        out_specs=[by_row, by_row, columns, whole(half), whole(half), whole((8, width))],
        out_shape=[
            jax.ShapeDtypeStruct((rows, width), BF16),
            jax.ShapeDtypeStruct((rows, width), F32),
            jax.ShapeDtypeStruct((heads_width, rows), BF16),
            jax.ShapeDtypeStruct(half, BF16),
            jax.ShapeDtypeStruct(half, BF16),
            jax.ShapeDtypeStruct((8, width), F32),
        ],
        scratch_shapes=[pltpu.VMEM((width, heads_width), F32)],
        compiler_params=params(),
        cost_estimate=cost(4 * rows * width * heads_width, 32 * rows * width),
        name="branch",
    )(resid, *sums, *gmids, grads, gain, b_down, w_out, attended)


def back_kernel(
    tok_ref, x_ref, d_ref, w_ref, w2_ref, gresid_ref, gain_ref,
    gtok_ref, dw_ref, dw2_ref, db_ref, small_ref, acc_ref,
):
    @pl.when(pl.program_id(0) == 0)
    def _():
        acc_ref[...] = jnp.zeros_like(acc_ref)
        db_ref[...] = jnp.zeros_like(db_ref)
        small_ref[...] = jnp.zeros_like(small_ref)

    gin = contract(d_ref[0], w_ref[...], 0, 1) + contract(d_ref[1], w2_ref[...], 0, 1)
    for half in (0, 1):
        acc_ref[half] += contract(x_ref[...], d_ref[half], 0, 1)
        db_ref[half] += jnp.sum(d_ref[half].astype(F32), axis=1, keepdims=True)
    hat, inv = norm_parts(tok_ref[...].astype(F32))
    gtok_ref[...] = gresid_ref[...] + norm_back(hat, inv, gin * gain_ref[...])
    small_ref[0:1] += jnp.sum(gin * hat, axis=0, keepdims=True)
    small_ref[1:2] += jnp.sum(gin, axis=0, keepdims=True)

    @pl.when(pl.program_id(0) == pl.num_programs(0) - 1)
    def _():
        dw_ref[...] = acc_ref[0].astype(BF16)
        dw2_ref[...] = acc_ref[1].astype(BF16)


def back(tokens, normed, dqkv, w_cat, w_cat2, gresid, gain, block):
    rows, width = normed.shape
    out = w_cat.shape[1]
    by_row = pl.BlockSpec((block, width), lambda i: (i, 0))
    return pl.pallas_call(
        back_kernel,
        grid=(rows // block,),
        in_specs=[
            by_row,
            by_row,
            pl.BlockSpec((2, out, block), lambda i: (0, 0, i)),
            whole((width, out)),
            whole((width, out)),
            by_row,
            whole((1, width)),
        ],
        out_specs=[
            by_row,
            whole((width, out)),
            whole((width, out)),
            whole((2, out, 1)),
            whole((8, width)),
        ],
        out_shape=[
            jax.ShapeDtypeStruct((rows, width), F32),
            jax.ShapeDtypeStruct((width, out), BF16),
            jax.ShapeDtypeStruct((width, out), BF16),
            jax.ShapeDtypeStruct((2, out, 1), F32),
            jax.ShapeDtypeStruct((8, width), F32),
        ],
        scratch_shapes=[pltpu.VMEM((2, width, out), F32)],
        compiler_params=params(),
        cost_estimate=cost(8 * rows * width * out, 16 * rows * width),
        name="back",
    )(tokens, normed, dqkv, w_cat, w_cat2, gresid, gain)


def sum_kernel(*refs):
    greet_plane()
    one = PlaneSum(refs)
    for action in (one.begin, one.along_x, one.along_z, one.back_along_z, one.back_along_x):
        action()
    one.back_to_core()
    one.end()


def plane_sum(own, seen):
    anywhere = pl.BlockSpec(memory_space=pl.ANY)
    return pl.pallas_call(
        sum_kernel,
        in_specs=[anywhere, anywhere],
        out_specs=anywhere,
        out_shape=jax.ShapeDtypeStruct(own.shape, BF16),
        scratch_shapes=PlaneSum.buffers(own.shape),
        compiler_params=pltpu.CompilerParams(
            vmem_limit_bytes=VMEM_LIMIT, collective_id=1, has_side_effects=True
        ),
        name="plane_sum",
    )(own, seen)


def swap_tp(array):
    return lax.ppermute(array, "tp", [(0, 1), (1, 0)])


def swap_dp(array, bit):
    count = lax.axis_size("dp")
    return lax.ppermute(array, "dp", [(i, i ^ bit) for i in range(count)])


def dp_bit(bit):
    return (lax.axis_index("dp") & bit) != 0


def joined(mine, theirs, second):
    return jnp.where(second, jnp.concatenate([theirs, mine], 0), jnp.concatenate([mine, theirs], 0))


def half_of(array, second):
    size = array.shape[0] // 2
    return lax.dynamic_slice_in_dim(array, jnp.where(second, size, 0), size, 0)


def fetch_other(array, bits):
    piece = array
    for bit in reversed(bits):
        piece = half_of(piece, dp_bit(bit))
    piece = swap_tp(piece)
    for bit in bits:
        piece = joined(piece, swap_dp(piece, bit), dp_bit(bit))
    return piece


def add_low(left, right):
    return (left.astype(F32) + right.astype(F32)).astype(BF16)


def partner_term(other):
    second = dp_bit(1)
    both = add_low(half_of(other, second), swap_dp(half_of(other, ~second), 1))
    return swap_tp(both)


def by_images(
    tokens, long_lengths, short_lengths, ln1_gain, ln1_bias, w_query, b_query, w_key, w_value,
    b_value, w_out, b_out, ln2_gain, ln2_bias, w_up, b_up, w_down, b_down, cotangent,
):
    rank = lax.axis_index("tp")
    rank_arr = jnp.reshape(rank, (1,)).astype(jnp.int32)
    second = rank == 1
    rows = tokens.shape[0] // 2
    width = tokens.shape[1]
    half = w_query.shape[1]
    heads = half // HEAD_DIM
    long_len = lax.dynamic_slice_in_dim(long_lengths, rank, 1, 0)
    shorts = short_lengths.shape[0] // 2
    short_len = lax.dynamic_slice_in_dim(short_lengths, rank * shorts, shorts, 0)
    valid = jnp.concatenate(
        [
            jnp.arange(LEN_L) < long_len[0],
            (jnp.arange(LEN_S)[None, :] < short_len[:, None]).reshape(-1),
        ]
    )
    mask = jnp.where(valid, 0.0, -1e30).astype(F32).reshape(1, -1)
    row = lambda vector: vector.astype(F32).reshape(1, -1)
    core, xbit = 1, 2

    w_cat = jnp.concatenate([w_query, w_key, w_value], axis=1)
    w_cat2 = fetch_other(w_cat, [core, xbit])
    bias = jnp.concatenate([b_query, b_value, b_up]).astype(F32)
    bias2 = swap_tp(bias)

    def column(packed):
        return jnp.concatenate(
            [packed[:half], jnp.zeros((half,), F32), packed[half : 2 * half]]
        ).reshape(-1, 1)

    w_out2 = fetch_other(w_out, [core, xbit])
    w_up2 = fetch_other(w_up, [core, xbit])
    w_down2 = fetch_other(w_down, [core, xbit])
    kept = half_of(cotangent, second)
    got = swap_tp(half_of(cotangent, ~second))
    grads = joined(kept, got, second)

    normed, own_tokens, qkv = project_norm(
        rank_arr, tokens, row(ln1_gain), row(ln1_bias), w_cat, column(bias), rows, 512
    )
    parts = (2, 3, heads, HEAD_DIM, rows)
    att = attend_forward(mask, qkv.reshape(parts), 0)
    qkv = project(qkv, normed, w_cat2, column(bias2), 512).reshape(parts)
    att, log_total = attend_forward(mask, qkv, 1, att)
    attended = att.reshape(2 * half, rows)
    w_out_all = jnp.concatenate([w_out, w_out2], axis=0)
    resid, mid = middle(
        own_tokens, attended, w_out_all, row(b_out), row(ln2_gain), row(ln2_bias), 512
    )
    sum2, gmid2, dup2, ddown2, dbup2 = feed(mid, grads, w_up2, row(bias2[2 * half :]), w_down2)
    seen_up, seen_down = partner_term(dup2), partner_term(ddown2)
    sum1, gmid1, dup1, ddown1, dbup1 = feed(mid, grads, w_up, row(bias[2 * half :]), w_down)
    out, gresid, gatt, dwout1, dwout2, small2 = branch(
        resid, (sum1, sum2), (gmid1, gmid2), grads, row(ln2_gain), row(b_down), w_out_all,
        attended, 512,
    )
    dqkv, grad_up, grad_down, grad_out_t = attend_backward(
        mask, qkv, att, log_total, gatt.reshape(2, heads, HEAD_DIM, rows),
        ((dup1, seen_up), (ddown1, seen_down), (dwout1, partner_term(dwout2))),
    )
    result = joined(half_of(out, second), swap_tp(half_of(out, ~second)), second)
    gtok, dw_cat, dw_cat2, db, small1 = back(
        own_tokens, normed, dqkv.reshape(2, 3 * half, rows), w_cat, w_cat2, gresid,
        row(ln1_gain), 512,
    )
    grad_cat = plane_sum(dw_cat, partner_term(dw_cat2)).astype(F32)
    sent = swap_tp(half_of(gtok, ~second).astype(BF16)).astype(F32)
    grad_tokens = joined(half_of(gtok, second), sent, second)

    one = jnp.concatenate([db[0, :half, 0], db[0, 2 * half :, 0], dbup1[0]])
    two = jnp.concatenate([db[1, :half, 0], db[1, 2 * half :, 0], dbup2[0]])
    ordered = joined(one, two, second)
    packed = jnp.concatenate([small1[0], small1[1], *(small2[i] for i in range(4)), ordered])
    packed = lax.psum(packed, ("dp", "tp"))
    small = packed[: 6 * width].reshape(6, width)
    mine = half_of(packed[6 * width :], second)
    return (
        result,
        grad_tokens,
        small[0],
        small[1],
        grad_cat[:, :half],
        mine[:half],
        grad_cat[:, half : 2 * half],
        grad_cat[:, 2 * half :],
        mine[half : 2 * half],
        grad_out_t.T.astype(F32),
        small[4],
        small[2],
        small[3],
        grad_up.astype(F32),
        mine[2 * half :],
        grad_down.astype(F32),
        small[5],
    )


def layer_norm(values, gain, shift):
    center = values - jnp.mean(values, axis=-1, keepdims=True)
    spread = jnp.mean(center * center, axis=-1, keepdims=True)
    return center * lax.rsqrt(spread + 1e-06) * gain + shift


def dot_plain(left, right):
    return jnp.dot(left, right, preferred_element_type=jnp.float32)


def dot_rows(left, right):
    return lax.dot_general(
        left, right, (((0,), (0,)), ((), ())), preferred_element_type=jnp.float32
    )


def dot_back(left, right):
    return lax.dot_general(
        left, right, (((1,), (1,)), ((), ())), preferred_element_type=jnp.float32
    )


def group_shape(image_count, seq_len, head_count):
    per_step = math.gcd(image_count, max(1, 512 // seq_len))
    return (image_count // per_step, per_step, seq_len, head_count, HEAD_DIM)


def masked_scores(query_blk, key_blk, length_blk):
    seq_len = query_blk.shape[1]
    raw = jnp.einsum(
        "bqhd,bkhd->bhqk", query_blk, key_blk, preferred_element_type=jnp.float32
    ) * HEAD_DIM ** (-0.5)
    keep = jnp.arange(seq_len, dtype=jnp.int32)[None, :] < length_blk[:, None]
    return jnp.where(keep[:, None, None, :], raw, -1e30)


def attention_forward(queries, key_rows, value_rows, lengths, seq_len):
    image_count = lengths.shape[0]
    head_count = queries.shape[1] // HEAD_DIM
    block_shape = group_shape(image_count, seq_len, head_count)

    def one_step(block):
        query_blk, key_blk, value_blk, length_blk = block
        scores = masked_scores(query_blk, key_blk, length_blk)
        row_top = jnp.max(scores, axis=-1, keepdims=True)
        exp_terms = jnp.exp(scores - row_top)
        row_total = jnp.sum(exp_terms, axis=-1, keepdims=True)
        weights = (exp_terms / row_total).astype(jnp.bfloat16)
        mixed = jnp.einsum(
            "bhqk,bkhd->bqhd", weights, value_blk, preferred_element_type=jnp.float32
        )
        return (mixed, (row_top + jnp.log(row_total))[..., 0])

    mixed, log_total = lax.map(
        one_step,
        (
            queries.reshape(block_shape),
            key_rows.reshape(block_shape),
            value_rows.reshape(block_shape),
            lengths.reshape(block_shape[:2]),
        ),
    )
    return (mixed.reshape(image_count * seq_len, head_count * HEAD_DIM), log_total)


def attention_backward(queries, key_rows, value_rows, grads, lengths, log_total, seq_len):
    image_count = lengths.shape[0]
    head_count = queries.shape[1] // HEAD_DIM
    block_shape = group_shape(image_count, seq_len, head_count)
    scale = HEAD_DIM ** (-0.5)

    def one_step(block):
        query_blk, key_blk, value_blk, grad_blk, length_blk, total_blk = block
        scores = masked_scores(query_blk, key_blk, length_blk)
        probs = jnp.exp(scores - total_blk[..., None])
        grad_values = jnp.einsum(
            "bhqk,bqhd->bkhd",
            probs.astype(jnp.bfloat16),
            grad_blk,
            preferred_element_type=jnp.float32,
        )
        grad_probs = jnp.einsum(
            "bqhd,bkhd->bhqk", grad_blk, value_blk, preferred_element_type=jnp.float32
        )
        inner = jnp.sum(probs * grad_probs, axis=-1, keepdims=True)
        grad_scores = (probs * (grad_probs - inner)).astype(jnp.bfloat16)
        grad_queries = (
            jnp.einsum("bhqk,bkhd->bqhd", grad_scores, key_blk, preferred_element_type=jnp.float32)
            * scale
        )
        grad_keys = (
            jnp.einsum(
                "bhqk,bqhd->bkhd", grad_scores, query_blk, preferred_element_type=jnp.float32
            )
            * scale
        )
        return (grad_queries, grad_keys, grad_values)

    results = lax.map(
        one_step,
        (
            queries.reshape(block_shape),
            key_rows.reshape(block_shape),
            value_rows.reshape(block_shape),
            grads.reshape(block_shape),
            lengths.reshape(block_shape[:2]),
            log_total,
        ),
    )
    flat = (image_count * seq_len, head_count * HEAD_DIM)
    return tuple((item.reshape(flat) for item in results))


def local(
    tokens,
    long_lengths,
    short_lengths,
    ln1_gain,
    ln1_bias,
    w_query,
    b_query,
    w_key,
    w_value,
    b_value,
    w_out,
    b_out,
    ln2_gain,
    ln2_bias,
    w_up,
    b_up,
    w_down,
    b_down,
    cotangent,
):
    tp_count = lax.axis_size("tp")
    tp_rank = lax.axis_index("tp")
    row_count = tokens.shape[0]
    share = row_count // tp_count
    split = long_lengths.shape[0] * LEN_L
    gain_one = ln1_gain.astype(jnp.float32)
    shift_one = ln1_bias.astype(jnp.float32)
    gain_two = ln2_gain.astype(jnp.float32)
    shift_two = ln2_bias.astype(jnp.float32)
    normed_in = layer_norm(tokens.astype(jnp.float32), gain_one, shift_one).astype(jnp.bfloat16)
    queries = (dot_plain(normed_in, w_query) + b_query.astype(jnp.float32)).astype(jnp.bfloat16)
    key_rows = dot_plain(normed_in, w_key).astype(jnp.bfloat16)
    value_rows = (dot_plain(normed_in, w_value) + b_value.astype(jnp.float32)).astype(jnp.bfloat16)
    long_mixed, long_total = attention_forward(
        queries[:split], key_rows[:split], value_rows[:split], long_lengths, LEN_L
    )
    short_mixed, short_total = attention_forward(
        queries[split:], key_rows[split:], value_rows[split:], short_lengths, LEN_S
    )
    attended = jnp.concatenate([long_mixed, short_mixed], axis=0).astype(jnp.bfloat16)
    attn_sum = lax.psum_scatter(dot_plain(attended, w_out), "tp", scatter_dimension=0, tiled=True)
    own_tokens = lax.dynamic_slice_in_dim(tokens, tp_rank * share, share, 0).astype(jnp.float32)
    resid = own_tokens + attn_sum + b_out.astype(jnp.float32)
    normed_mid = layer_norm(resid, gain_two, shift_two).astype(jnp.bfloat16)
    grad_out = cotangent.astype(jnp.float32)
    mid_rows = lax.all_gather(normed_mid, "tp", axis=0, tiled=True)
    pre_up = dot_plain(mid_rows, w_up) + b_up.astype(jnp.float32)
    activ = jax.nn.gelu(pre_up, approximate=False).astype(jnp.bfloat16)
    ffn_sum = lax.psum_scatter(
        dot_plain(activ, w_down).astype(jnp.bfloat16), "tp", scatter_dimension=0, tiled=True
    ).astype(jnp.float32)
    result = resid + ffn_sum + b_down.astype(jnp.float32)
    grad_rows = lax.all_gather(cotangent, "tp", axis=0, tiled=True)
    grad_w_down = dot_rows(activ, grad_rows)
    grad_activ = dot_back(grad_rows, w_down)
    _, gelu_back = jax.vjp(lambda inner: jax.nn.gelu(inner, approximate=False), pre_up)
    grad_pre = gelu_back(grad_activ)[0].astype(jnp.bfloat16)
    grad_w_up = dot_rows(mid_rows, grad_pre)
    grad_b_up = jnp.sum(grad_pre.astype(jnp.float32), axis=0)
    grad_mid = lax.psum_scatter(dot_back(grad_pre, w_up), "tp", scatter_dimension=0, tiled=True)
    _, norm_two_back = jax.vjp(layer_norm, resid, gain_two, shift_two)
    grad_resid_norm, grad_gain_two, grad_shift_two = norm_two_back(grad_mid)
    grad_resid = grad_out + grad_resid_norm
    grad_b_down = jnp.sum(grad_out, axis=0)
    grad_b_out = jnp.sum(grad_resid, axis=0)
    grad_branch = lax.all_gather(grad_resid.astype(jnp.bfloat16), "tp", axis=0, tiled=True)
    grad_w_out = dot_rows(attended, grad_branch)
    grad_attended = dot_back(grad_branch, w_out).astype(jnp.bfloat16)
    long_grads = attention_backward(
        queries[:split],
        key_rows[:split],
        value_rows[:split],
        grad_attended[:split],
        long_lengths,
        long_total,
        LEN_L,
    )
    short_grads = attention_backward(
        queries[split:],
        key_rows[split:],
        value_rows[split:],
        grad_attended[split:],
        short_lengths,
        short_total,
        LEN_S,
    )
    grad_queries = jnp.concatenate([long_grads[0], short_grads[0]], axis=0).astype(jnp.bfloat16)
    grad_keys = jnp.concatenate([long_grads[1], short_grads[1]], axis=0).astype(jnp.bfloat16)
    grad_values = jnp.concatenate([long_grads[2], short_grads[2]], axis=0).astype(jnp.bfloat16)
    grad_w_query = dot_rows(normed_in, grad_queries)
    grad_b_query = jnp.sum(grad_queries.astype(jnp.float32), axis=0)
    grad_w_key = dot_rows(normed_in, grad_keys)
    grad_w_value = dot_rows(normed_in, grad_values)
    grad_b_value = jnp.sum(grad_values.astype(jnp.float32), axis=0)
    grad_in = lax.psum_scatter(
        dot_back(grad_queries, w_query)
        + dot_back(grad_keys, w_key)
        + dot_back(grad_values, w_value),
        "tp",
        scatter_dimension=0,
        tiled=True,
    )
    _, norm_one_back = jax.vjp(layer_norm, own_tokens, gain_one, shift_one)
    grad_tokens_norm, grad_gain_one, grad_shift_one = norm_one_back(grad_in)
    grad_tokens = grad_resid + grad_tokens_norm
    summed = lax.psum(
        (
            grad_w_query,
            grad_b_query,
            grad_w_key,
            grad_w_value,
            grad_b_value,
            grad_w_out,
            grad_w_up,
            grad_b_up,
            grad_w_down,
        ),
        "dp",
    )
    shared = lax.psum(
        (grad_gain_one, grad_shift_one, grad_b_out, grad_gain_two, grad_shift_two, grad_b_down),
        ("dp", "tp"),
    )
    return (
        result.astype(jnp.bfloat16),
        grad_tokens,
        shared[0],
        shared[1],
        summed[0],
        summed[1],
        summed[2],
        summed[3],
        summed[4],
        summed[5],
        shared[2],
        shared[3],
        shared[4],
        summed[6],
        summed[7],
        summed[8],
        shared[5],
    )


def pick(*arrays):
    tokens, long_lengths, short_lengths, w_query, w_up = (arrays[i] for i in (0, 1, 2, 5, 14))
    fits = (
        lax.axis_size("tp") == 2
        and lax.axis_size("dp") == 16
        and long_lengths.shape[0] == 2
        and short_lengths.shape[0] == 8
        and tokens.shape == (2 * LEN_L + 8 * LEN_S, 768)
        and w_query.shape[1] == 8 * HEAD_DIM
        and w_up.shape[1] == 1536
    )
    return by_images(*arrays) if fits else local(*arrays)


def solution(mesh):
    placed = (
        P("dp", None),
        P("dp"),
        P("dp"),
        P(),
        P(),
        P(None, "tp"),
        P("tp"),
        P(None, "tp"),
        P(None, "tp"),
        P("tp"),
        P("tp", None),
        P(),
        P(),
        P(),
        P(None, "tp"),
        P("tp"),
        P("tp", None),
        P(),
        P(("dp", "tp"), None),
    )
    return jax.shard_map(
        pick,
        mesh=mesh,
        in_specs=placed,
        out_specs=(
            P(("dp", "tp"), None),
            P(("dp", "tp"), None),
            P(),
            P(),
            P(None, "tp"),
            P("tp"),
            P(None, "tp"),
            P(None, "tp"),
            P("tp"),
            P("tp", None),
            P(),
            P(),
            P(),
            P(None, "tp"),
            P("tp"),
            P("tp", None),
            P(),
        ),
        check_vma=False,
    )
```

```python
import functools
import math

import jax
import jax.numpy as jnp
from jax import lax
from jax.experimental import pallas as pl
from jax.experimental.pallas import tpu as pltpu
from jax.sharding import PartitionSpec as P

HEAD_DIM = 48
LEN_L = 1024
LEN_S = 256
F32 = jnp.float32
BF16 = jnp.bfloat16
LOG2E = math.log2(math.e)
SCALE = HEAD_DIM ** (-0.5)
VMEM_LIMIT = 58 << 20
HEAD_GROUP = 2


def contract(left, right, left_dim, right_dim):
    return lax.dot_general(
        left, right, (((left_dim,), (right_dim,)), ((), ())), preferred_element_type=F32
    )


def params():
    return pltpu.CompilerParams(vmem_limit_bytes=VMEM_LIMIT)


def cost(flops, bytes_accessed, transcendentals=0):
    return pl.CostEstimate(
        flops=int(flops), bytes_accessed=int(bytes_accessed), transcendentals=int(transcendentals)
    )


def whole(shape):
    zeros = (0,) * len(shape)
    return pl.BlockSpec(shape, lambda *_: zeros)


def norm_parts(values):
    center = values - jnp.mean(values, axis=-1, keepdims=True)
    inv = lax.rsqrt(jnp.mean(center * center, axis=-1, keepdims=True) + 1e-06)
    return center * inv, inv


def norm_back(hat, inv, grad_hat):
    mean_grad = jnp.mean(grad_hat, axis=-1, keepdims=True)
    mean_both = jnp.mean(grad_hat * hat, axis=-1, keepdims=True)
    return inv * (grad_hat - mean_grad - hat * mean_both)


def project_norm_kernel(rank_ref, tok_ref, gain_ref, shift_ref, w_ref, b_ref, x_ref, own_ref, qkv_ref):
    hat, _ = norm_parts(tok_ref[...].astype(F32))
    normed = (hat * gain_ref[...] + shift_ref[...]).astype(BF16)
    x_ref[...] = normed
    own_ref[...] = tok_ref[...]
    qkv_ref[0] = (contract(w_ref[...], normed, 0, 1) + b_ref[...]).astype(BF16)


def project_kernel(_, x_ref, w_ref, b_ref, qkv_ref):
    qkv_ref[0] = (contract(w_ref[...], x_ref[...], 0, 1) + b_ref[...]).astype(BF16)


def own_row_block(per_part):
    def index(i, rank_ref):
        part = i // per_part
        return (part * 2 * per_part + rank_ref[0] * per_part + i % per_part, 0)

    return index


def project_norm(rank, tokens, gain, shift, w_cat, b_col, rows, block):
    width, out = w_cat.shape
    per_part = LEN_L // block
    by_row = pl.BlockSpec((block, width), lambda i, _: (i, 0))
    return pl.pallas_call(
        project_norm_kernel,
        grid_spec=pltpu.PrefetchScalarGridSpec(
            num_scalar_prefetch=1,
            grid=(rows // block,),
            in_specs=[
                pl.BlockSpec((block, width), own_row_block(per_part)),
                whole((1, width)),
                whole((1, width)),
                whole((width, out)),
                whole((out, 1)),
            ],
            out_specs=[by_row, by_row, pl.BlockSpec((1, out, block), lambda i, _: (0, 0, i))],
        ),
        out_shape=[
            jax.ShapeDtypeStruct((rows, width), BF16),
            jax.ShapeDtypeStruct((rows, width), BF16),
            jax.ShapeDtypeStruct((2, out, rows), BF16),
        ],
        compiler_params=params(),
        cost_estimate=cost(2 * rows * width * out, 4 * rows * width + 2 * out * rows),
        name="project_norm",
    )(rank, tokens, gain, shift, w_cat, b_col)


def project(both, normed, w_cat, b_col, block):
    rows, width = normed.shape
    out = w_cat.shape[1]
    return pl.pallas_call(
        project_kernel,
        grid=(rows // block,),
        in_specs=[
            pl.BlockSpec(memory_space=pl.ANY),
            pl.BlockSpec((block, width), lambda i: (i, 0)),
            whole((width, out)),
            whole((out, 1)),
        ],
        out_specs=pl.BlockSpec((1, out, block), lambda i: (1, 0, i)),
        out_shape=jax.ShapeDtypeStruct(both.shape, BF16),
        input_output_aliases={0: 0},
        compiler_params=params(),
        cost_estimate=cost(2 * rows * width * out, 2 * rows * width + 2 * out * rows),
        name="project",
    )(both, normed, w_cat, b_col)


def three_terms(value):
    high = value.astype(BF16).astype(F32)
    rest = value - high
    mid = rest.astype(BF16).astype(F32)
    return [high, mid, rest - mid]


def extra_rows(rows, count):
    at = lax.broadcasted_iota(jnp.int32, (16, count), 0)
    out = jnp.zeros((16, count), F32)
    for place, row in enumerate(rows):
        out = jnp.where(at == place, row, out)
    return out.astype(BF16)


def scaled_query(query):
    wide = query.astype(F32) * (SCALE * LOG2E)
    high = wide.astype(BF16)
    return [high, (wide - high.astype(F32)).astype(BF16)]


def attend_forward_kernel(mask_ref, qkv_ref, *refs, block):
    out_ref, log_ref = refs[-2:]
    heads, rows = qkv_ref.shape[2], qkv_ref.shape[4]
    work = []
    for head in range(heads):
        work += [(head, 0, LEN_L, at, block) for at in range(0, LEN_L, block)]
        work += [(head, start, LEN_S, 0, LEN_S) for start in range(LEN_L, rows, LEN_S)]

    def scores(item):
        head, start, count, at, size = item
        every = slice(start, start + count)
        keys = qkv_ref[0, 1, head, :, every]
        key_rows = jnp.concatenate([keys, keys, extra_rows([mask_ref[:, every]], count)], 0)
        query = scaled_query(qkv_ref[0, 0, head, :, start + at : start + at + size])
        query_rows = jnp.concatenate([*query, jnp.ones((16, size), BF16)], 0)
        return contract(key_rows, query_rows, 0, 0)

    def finish(item, score):
        head, start, count, at, size = item
        here = slice(start + at, start + at + size)
        values = qkv_ref[0, 2, head, :, start : start + count]
        value_rows = jnp.concatenate([values, jnp.ones((16, count), BF16)], 0)
        top = jnp.max(score, axis=0, keepdims=True)
        weights = jnp.exp2(score - top).astype(BF16)
        mixed = contract(value_rows, weights, 1, 0)
        total = mixed[HEAD_DIM : HEAD_DIM + 1]
        out_ref[0, head, :, here] = (mixed[:HEAD_DIM] * (1.0 / total)).astype(BF16)
        log_ref[0, head, :, here] = top + jnp.log2(total)

    score = scores(work[0])
    for place, item in enumerate(work):
        later = scores(work[place + 1]) if place + 1 < len(work) else None
        finish(item, score)
        score = later


def pair_count(heads, rows):
    return heads * (LEN_L**2 + (rows - LEN_L) * LEN_S)


def attend_forward(mask, qkv, part, earlier=(), block=1024):
    _, _, heads, _, rows = qkv.shape
    group = HEAD_GROUP
    pairs = pair_count(heads, rows)
    return pl.pallas_call(
        functools.partial(attend_forward_kernel, block=block),
        grid=(heads // group,),
        in_specs=[
            whole((1, rows)),
            pl.BlockSpec((1, 3, group, HEAD_DIM, rows), lambda h: (part, 0, h, 0, 0)),
            *(pl.BlockSpec(memory_space=pl.ANY) for _ in earlier),
        ],
        out_specs=[
            pl.BlockSpec((1, group, HEAD_DIM, rows), lambda h: (part, h, 0, 0)),
            pl.BlockSpec((1, group, 1, rows), lambda h: (part, h, 0, 0)),
        ],
        out_shape=[
            jax.ShapeDtypeStruct((2, heads, HEAD_DIM, rows), BF16),
            jax.ShapeDtypeStruct((2, heads, 1, rows), F32),
        ],
        input_output_aliases={2: 0, 3: 1} if earlier else {},
        compiler_params=params(),
        cost_estimate=cost(pairs * 2 * 512, 8 * heads * HEAD_DIM * rows, pairs),
        name="attend_forward",
    )(mask, qkv, *earlier)


class Place:
    def __init__(self):
        me = lax.axis_index("dp")
        self.core, self.x, self.z = me % 2, (me // 2) % 2, me // 4
        self.rank = lax.axis_index("tp")

    def at(self, z=None, x=None, core=None):
        z = self.z if z is None else z
        x = self.x if x is None else x
        core = self.core if core is None else core
        return {"dp": (z * 2 + x) * 2 + core}

    def across_core(self):
        return self.at(core=1 - self.core)

    def across_x(self):
        return self.at(x=1 - self.x)

    def along_z(self, step):
        return self.at(z=(self.z + step) % 4)

    def partner(self):
        return {"tp": 1 - self.rank}

    def greet(self):
        barrier = pltpu.get_barrier_semaphore()
        others = [self.across_core(), self.across_x(), self.partner()]
        others += [self.along_z(step) for step in (1, 2, 3)]
        for other in others:
            pl.semaphore_signal(
                barrier, inc=1, device_id=other, device_id_type=pl.DeviceIdType.MESH
            )
        pl.semaphore_wait(barrier, len(others))


def send_to(source, target, send, recv, device):
    return pltpu.make_async_remote_copy(
        src_ref=source,
        dst_ref=target,
        send_sem=send,
        recv_sem=recv,
        device_id=device,
        device_id_type=pl.DeviceIdType.MESH,
    )


def part(ref, start, count):
    return ref.at[pl.ds(pl.multiple_of(start, 16), count)]


def add_rows(target, start, count, terms):
    tile = 48

    def body(i, _):
        at = pl.multiple_of(i * tile, 16)
        here = pl.ds(pl.multiple_of(start + at, 16), tile)
        total = target[here, :].astype(F32)
        for term in terms:
            total = total + term[pl.ds(at, tile), :].astype(F32)
        target[here, :] = total.astype(BF16)
        return 0

    lax.fori_loop(0, count // tile, body, 0)


class PlaneSum:
    def __init__(self, place, own, seen, out, refs):
        self.place, self.own, self.seen, self.out = place, own, seen, out
        (self.acc, self.seen_here, self.from_core, self.from_x, self.from_z,
         self.send, self.recv, self.local) = refs
        self.rows = own.shape[0]

    @staticmethod
    def buffers(rows, width):
        return [
            pltpu.VMEM((rows // 2, width), BF16),
            pltpu.VMEM((rows // 2, width), BF16),
            pltpu.VMEM((rows // 2, width), BF16),
            pltpu.VMEM((rows // 4, width), BF16),
            pltpu.VMEM((3, rows // 16, width), BF16),
            pltpu.SemaphoreType.DMA((10,)),
            pltpu.SemaphoreType.DMA((10,)),
            pltpu.SemaphoreType.DMA((3,)),
        ]

    def copy(self, source, target, place, device):
        return send_to(source, target, self.send.at[place], self.recv.at[place], device)

    def core_copy(self):
        half = self.rows // 2
        source = part(self.own, (1 - self.place.core) * half, half)
        return self.copy(source, self.from_core, 0, self.place.across_core())

    def local_copies(self):
        half = self.rows // 2
        source = part(self.own, self.place.core * half, half)
        copies = [pltpu.make_async_copy(source, self.acc, self.local.at[0])]
        if self.seen is not None:
            copies.append(pltpu.make_async_copy(self.seen, self.seen_here, self.local.at[1]))
        return copies

    def x_copy(self):
        count = self.rows // 4
        source = part(self.acc, (1 - self.place.x) * count, count)
        return self.copy(source, self.from_x, 1, self.place.across_x())

    def z_copies(self):
        count = self.rows // 16
        copies = []
        for step in (1, 2, 3):
            there = (self.place.z + step) % 4
            source = part(self.acc, self.place.x * 4 * count + there * count, count)
            target = self.from_z.at[step - 1]
            copies.append(self.copy(source, target, 1 + step, self.place.along_z(step)))
        return copies

    def piece(self):
        count = self.rows // 16
        inside = self.place.x * 4 * count + self.place.z * count
        return (
            part(self.acc, inside, count),
            part(self.out, self.place.core * 8 * count + inside, count),
        )

    def keep_copy(self):
        mine, there = self.piece()
        return pltpu.make_async_copy(mine, there, self.local.at[2])

    def back_z_copies(self):
        mine, there = self.piece()
        return [
            self.copy(mine, there, 4 + step, self.place.along_z(step)) for step in (1, 2, 3)
        ]

    def back_x_copy(self):
        count = self.rows // 4
        there = part(self.out, self.place.core * 2 * count + self.place.x * count, count)
        return self.copy(there, there, 8, self.place.across_x())

    def back_core_copy(self):
        count = self.rows // 2
        there = part(self.out, self.place.core * count, count)
        return self.copy(there, there, 9, self.place.across_core())

    def begin(self):
        self.core_copy().start()
        for copy in self.local_copies():
            copy.start()

    def along_x(self):
        self.core_copy().wait()
        for copy in self.local_copies():
            copy.wait()
        add_rows(self.acc, 0, self.rows // 2, [self.from_core, self.seen_here])
        self.x_copy().start()

    def along_z(self):
        self.x_copy().wait()
        count = self.rows // 4
        add_rows(self.acc, self.place.x * count, count, [self.from_x])
        for copy in self.z_copies():
            copy.start()

    def back_along_z(self):
        for copy in self.z_copies():
            copy.wait()
        count = self.rows // 16
        inside = self.place.x * 4 * count + self.place.z * count
        add_rows(self.acc, inside, count, [self.from_z.at[i] for i in range(3)])
        self.keep_copy().start()
        for copy in self.back_z_copies():
            copy.start()

    def back_along_x(self):
        self.keep_copy().wait()
        for copy in self.back_z_copies():
            copy.wait()
        self.back_x_copy().start()

    def back_to_core(self):
        self.back_x_copy().wait()
        self.back_core_copy().start()

    def end(self):
        self.back_core_copy().wait()


class PartnerTerm:
    def __init__(self, place, other, seen, refs):
        self.place, self.other, self.seen = place, other, seen
        self.from_core, self.send, self.recv = refs
        self.half = other.shape[0] // 2

    @staticmethod
    def buffers(rows, width):
        return [
            pltpu.VMEM((rows // 2, width), BF16),
            pltpu.SemaphoreType.DMA((2,)),
            pltpu.SemaphoreType.DMA((2,)),
        ]

    def core_copy(self):
        source = part(self.other, (1 - self.place.core) * self.half, self.half)
        return send_to(
            source, self.from_core, self.send.at[0], self.recv.at[0], self.place.across_core()
        )

    def partner_copy(self):
        return send_to(
            self.from_core, self.seen, self.send.at[1], self.recv.at[1], self.place.partner()
        )

    def begin(self):
        self.core_copy().start()

    def to_partner(self):
        self.core_copy().wait()
        mine = part(self.other, self.place.core * self.half, self.half)
        add_rows(self.from_core, 0, self.half, [mine])
        self.partner_copy().start()

    def end(self):
        self.partner_copy().wait()


class SmallSum:
    ROWS = 16

    def __init__(self, place, own, other, refs):
        self.place, self.own, self.other = place, own, other
        self.sums, self.got, self.send, self.recv = refs

    @staticmethod
    def buffers(width):
        rows = SmallSum.ROWS
        return [
            pltpu.VMEM((3, rows, width), F32),
            pltpu.VMEM((6, rows, width), F32),
            pltpu.SemaphoreType.DMA((6,)),
            pltpu.SemaphoreType.DMA((6,)),
        ]

    def copy(self, source, place, device):
        return send_to(source, self.got.at[place], self.send.at[place], self.recv.at[place], device)

    def partner_copy(self):
        return self.copy(self.other, 0, self.place.partner())

    def core_copy(self):
        return self.copy(self.sums.at[0], 1, self.place.across_core())

    def x_copy(self):
        return self.copy(self.sums.at[1], 2, self.place.across_x())

    def z_copies(self):
        return [
            self.copy(self.sums.at[2], 2 + step, self.place.along_z(step)) for step in (1, 2, 3)
        ]

    def begin(self):
        self.partner_copy().start()

    def over_cores(self):
        self.partner_copy().wait()
        self.sums[0] = self.own[...] + self.got[0]
        self.core_copy().start()

    def over_x(self):
        self.core_copy().wait()
        self.sums[1] = self.sums[0] + self.got[1]
        self.x_copy().start()

    def over_z(self):
        self.x_copy().wait()
        self.sums[2] = self.sums[1] + self.got[2]
        for copy in self.z_copies():
            copy.start()

    def end(self):
        for copy in self.z_copies():
            copy.wait()
        return self.sums[2] + self.got[3] + self.got[4] + self.got[5]


def middle_kernel(
    tok_ref, att_ref, w_ref, b_ref, gain_ref, shift_ref, resid_ref, mid_ref
):
    resid = tok_ref[...].astype(F32) + contract(att_ref[...], w_ref[...], 0, 0) + b_ref[...]
    resid_ref[...] = resid
    hat, _ = norm_parts(resid)
    mid_ref[...] = (hat * gain_ref[...] + shift_ref[...]).astype(BF16)


def middle(tokens, attended, w_out, b_out, gain, shift, block):
    heads_width, rows = attended.shape
    width = w_out.shape[1]
    by_row = pl.BlockSpec((block, width), lambda i: (i, 0))
    return pl.pallas_call(
        middle_kernel,
        grid=(rows // block,),
        in_specs=[
            by_row,
            pl.BlockSpec((heads_width, block), lambda i: (0, i)),
            whole((heads_width, width)),
            whole((1, width)),
            whole((1, width)),
            whole((1, width)),
        ],
        out_specs=[by_row, by_row],
        out_shape=[
            jax.ShapeDtypeStruct((rows, width), F32),
            jax.ShapeDtypeStruct((rows, width), BF16),
        ],
        compiler_params=params(),
        cost_estimate=cost(2 * rows * width * heads_width, 12 * rows * width),
        name="middle",
    )(tokens, attended, w_out, b_out, gain, shift)


ERFC_TERMS = (0.254829592, -0.284496736, 1.421413741, -1.453152027, 1.061405429)
ERFC_SLOPE = 0.3275911


def gelu_and_slope(value):
    bell = jnp.exp2(value * value * (-0.5 * LOG2E))
    base = 1.0 + jnp.abs(value) * (ERFC_SLOPE * math.sqrt(0.5))
    ratio = 1.0 / base
    poly = ERFC_TERMS[4] * 0.5
    for term in ERFC_TERMS[3::-1]:
        poly = poly * ratio + term * 0.5
    tail = poly * ratio * bell
    below = jnp.where(value < 0.0, tail, 1.0 - tail)
    return value * below, below + value * bell * (1.0 / math.sqrt(2.0 * math.pi))


def feed_kernel(
    mid_ref, grad_ref, up_ref, b_ref, down_ref, sum_ref, gmid_ref, dup_ref, ddown_ref, db_ref,
    act_ref, gpre_ref, *, chunk,
):
    @pl.when(pl.program_id(0) == 0)
    def _():
        sum_ref[...] = jnp.zeros_like(sum_ref)
        gmid_ref[...] = jnp.zeros_like(gmid_ref)

    rows = mid_ref.shape[0]
    up, down, bias = up_ref[...], down_ref[...], b_ref[...]

    def products(at):
        here = slice(at, at + chunk)
        return (
            contract(mid_ref[here], up, 1, 0) + bias,
            contract(grad_ref[here], down, 1, 1),
        )

    now = products(0)
    db = None
    for at in range(0, rows, chunk):
        here = slice(at, at + chunk)
        later = products(at + chunk) if at + chunk < rows else None
        value, slope = gelu_and_slope(now[0])
        act = value.astype(BF16)
        gpre = (slope * now[1]).astype(BF16)
        act_ref[here] = act
        gpre_ref[here] = gpre
        part = jnp.sum(gpre.astype(F32), axis=0, keepdims=True)
        db = part if db is None else db + part
        sum_ref[here] += contract(act, down, 1, 0)
        gmid_ref[here] += contract(gpre, up, 1, 1)
        now = later
    db_ref[...] = db
    ddown_ref[...] = contract(act_ref[...], grad_ref[...], 0, 0).astype(BF16)
    dup_ref[...] = contract(mid_ref[...], gpre_ref[...], 0, 0).astype(BF16)


def feed(mid, grads, w_up, b_up, w_down, block=512, chunk=512):
    rows, width = mid.shape
    hidden = w_up.shape[1]
    return pl.pallas_call(
        functools.partial(feed_kernel, chunk=chunk),
        grid=(hidden // block,),
        in_specs=[
            whole((rows, width)),
            whole((rows, width)),
            pl.BlockSpec((width, block), lambda j: (0, j)),
            pl.BlockSpec((1, block), lambda j: (0, j)),
            pl.BlockSpec((block, width), lambda j: (j, 0)),
        ],
        out_specs=[
            whole((rows, width)),
            whole((rows, width)),
            pl.BlockSpec((width, block), lambda j: (0, j)),
            pl.BlockSpec((block, width), lambda j: (j, 0)),
            pl.BlockSpec((1, block), lambda j: (0, j)),
        ],
        out_shape=[
            jax.ShapeDtypeStruct((rows, width), F32),
            jax.ShapeDtypeStruct((rows, width), F32),
            jax.ShapeDtypeStruct((width, hidden), BF16),
            jax.ShapeDtypeStruct((hidden, width), BF16),
            jax.ShapeDtypeStruct((1, hidden), F32),
        ],
        scratch_shapes=[pltpu.VMEM((rows, block), BF16), pltpu.VMEM((rows, block), BF16)],
        compiler_params=params(),
        cost_estimate=cost(12 * rows * width * hidden, 20 * rows * width, 2 * rows * hidden),
        name="feed",
    )(mid, grads, w_up, b_up, w_down)


def branch_kernel(
    resid_ref, sum1_ref, sum2_ref, gmid1_ref, gmid2_ref, grad_ref, gain_ref, bdown_ref, w_ref,
    att_ref, out_ref, gresid_ref, gatt_ref, dw_own_ref, dw_other_ref, small_ref, acc_ref,
):
    @pl.when(pl.program_id(0) == 0)
    def _():
        acc_ref[...] = jnp.zeros_like(acc_ref)
        small_ref[...] = jnp.zeros_like(small_ref)

    resid = resid_ref[...]
    grads = grad_ref[...].astype(F32)
    out_ref[...] = (resid + sum1_ref[...] + sum2_ref[...] + bdown_ref[...]).astype(BF16)
    gmid = gmid1_ref[...] + gmid2_ref[...]
    hat, inv = norm_parts(resid)
    gresid = grads + norm_back(hat, inv, gmid * gain_ref[...])
    gresid_ref[...] = gresid
    branch = gresid.astype(BF16)
    gatt_ref[...] = contract(w_ref[...], branch, 1, 1).astype(BF16)
    acc_ref[...] += contract(branch, att_ref[...], 0, 1)
    small_ref[0:1] += jnp.sum(gmid * hat, axis=0, keepdims=True)
    small_ref[1:2] += jnp.sum(gmid, axis=0, keepdims=True)
    small_ref[2:3] += jnp.sum(gresid, axis=0, keepdims=True)
    small_ref[3:4] += jnp.sum(grads, axis=0, keepdims=True)

    @pl.when(pl.program_id(0) == pl.num_programs(0) - 1)
    def _():
        half = dw_own_ref.shape[1]
        dw_own_ref[...] = acc_ref[:, :half].astype(BF16)
        dw_other_ref[...] = acc_ref[:, half:].astype(BF16)


def branch(resid, sums, gmids, grads, gain, b_down, w_out, attended, block):
    rows, width = resid.shape
    heads_width = attended.shape[0]
    by_row = pl.BlockSpec((block, width), lambda i: (i, 0))
    columns = pl.BlockSpec((heads_width, block), lambda i: (0, i))
    half = (width, heads_width // 2)
    return pl.pallas_call(
        branch_kernel,
        grid=(rows // block,),
        in_specs=[by_row] * 6
        + [whole((1, width)), whole((1, width)), whole((heads_width, width)), columns],
        out_specs=[by_row, by_row, columns, whole(half), whole(half), whole((8, width))],
        out_shape=[
            jax.ShapeDtypeStruct((rows, width), BF16),
            jax.ShapeDtypeStruct((rows, width), F32),
            jax.ShapeDtypeStruct((heads_width, rows), BF16),
            jax.ShapeDtypeStruct(half, BF16),
            jax.ShapeDtypeStruct(half, BF16),
            jax.ShapeDtypeStruct((8, width), F32),
        ],
        scratch_shapes=[pltpu.VMEM((width, heads_width), F32)],
        compiler_params=params(),
        cost_estimate=cost(4 * rows * width * heads_width, 32 * rows * width),
        name="branch",
    )(resid, *sums, *gmids, grads, gain, b_down, w_out, attended)


TAIL_BLOCK = 512
SUM_ACTIONS = ("begin", "along_x", "along_z", "back_along_z", "back_along_x", "back_to_core")
SUM_STEPS = (
    (0, 1, 3, 7, 9, 11),
    (0, 3, 5, 11, 13, 15),
    (0, 5, 9, 15, 17, 19),
    (0, 7, 13, 17, 20, 99),
    (0, 4, 6, 8, 10, 13),
    (17, 18, 20, 99, 99, 99),
)
LAST = 99


def tail_kernel(
    mask_ref, qkv_ref, att_ref, log_ref, gatt_ref, gain_ref, small2_ref, dbup1_ref, dbup2_ref,
    wout2_ref, x_hbm, w_hbm, w2_hbm, tok_hbm, gresid_hbm, up_hbm, down_hbm, wout_hbm, seen_up,
    seen_down, out_hbm,
    gtok_ref, small_ref, got_hbm, gup_hbm, gdown_hbm, gout_hbm, gcat_hbm, got_out,
    d_ref, x_ref, w_ref, tok_ref, gresid_ref, dw_ref, dw2_ref, sent_ref, own_small, other_small,
    load_sem, row_sem, tok_send, tok_recv, *scratch, heads, block,
):
    step = pl.program_id(0)
    place = Place()
    first_rows = 2 * heads + 1
    width = x_ref.shape[1]
    half = heads * HEAD_DIM
    halves = width

    groups = []
    at = 0
    for count in [8] * 6 + [3, 3, 4]:
        groups.append(scratch[at : at + count])
        at += count
    columns = lambda ref, i: ref.at[:, pl.ds(i * halves, halves)]
    rows_of = lambda ref, i, count: ref.at[pl.ds(i * count, count)]
    sums = [
        PlaneSum(place, columns(up_hbm, i), columns(seen_up, i), columns(gup_hbm, i), groups[i])
        for i in (0, 1)
    ]
    down_rows = down_hbm.shape[0] // 2
    sums += [
        PlaneSum(
            place,
            rows_of(down_hbm, i, down_rows),
            rows_of(seen_down, i, down_rows // 2),
            rows_of(gdown_hbm, i, down_rows),
            groups[2 + i],
        )
        for i in (0, 1)
    ]
    sums.append(PlaneSum(place, wout_hbm, None, gout_hbm, groups[4]))
    sums.append(PlaneSum(place, dw_ref, None, gcat_hbm, groups[5]))
    cat_term = PartnerTerm(place, dw2_ref, groups[5][1], groups[6])
    out_term = PartnerTerm(place, wout2_ref, groups[4][1], groups[7])
    small = SmallSum(place, own_small, other_small, groups[8])
    theirs = pl.ds(pl.multiple_of((1 - place.rank) * LEN_L, LEN_L), LEN_L)
    out_copy = send_to(
        out_hbm.at[theirs], got_out, tok_send.at[2], tok_recv.at[2], place.partner()
    )

    loads = [
        pltpu.make_async_copy(x_hbm, x_ref, load_sem.at[0]),
        pltpu.make_async_copy(w_hbm, w_ref.at[0], load_sem.at[1]),
        pltpu.make_async_copy(w2_hbm, w_ref.at[1], load_sem.at[2]),
    ]

    def row_start(i):
        mine = i // 2
        return ((1 - mine) * (1 - place.rank) + mine * place.rank) * LEN_L + (i % 2) * TAIL_BLOCK

    def row_loads(i):
        start = pl.ds(pl.multiple_of(row_start(i), TAIL_BLOCK), TAIL_BLOCK)
        slot = i % 2
        return [
            pltpu.make_async_copy(tok_hbm.at[start], tok_ref.at[slot], row_sem.at[slot, 0]),
            pltpu.make_async_copy(gresid_hbm.at[start], gresid_ref.at[slot], row_sem.at[slot, 1]),
        ]

    def token_copy(i):
        there = pl.ds(i * TAIL_BLOCK, TAIL_BLOCK)
        return send_to(
            sent_ref.at[there], got_hbm.at[there], tok_send.at[i], tok_recv.at[i], place.partner()
        )

    def weight_gradient(source, target):
        for i in range(3):
            here = pl.ds(i * half, half)
            product = contract(x_ref[...], d_ref[source, here, :], 0, 1)
            target[:, here] = product.astype(BF16)

    def bias_rows(source, target):
        ones = jnp.ones((16, d_ref.shape[2]), BF16)
        for i, which in ((0, 0), (1, 2)):
            row = contract(ones, d_ref[source, pl.ds(which * half, half), :], 1, 1)
            target[8:9, pl.ds(i * half, half)] = row[:1]

    last_step = first_rows + 3
    events = {}
    for one, times in zip(sums, SUM_STEPS):
        for when, action in zip(times, SUM_ACTIONS):
            events.setdefault(when, []).append(getattr(one, action))
    late = events.pop(LAST, [])

    for when in sorted(events):

        @pl.when(step == when)
        def _(when=when):
            if when == 0:
                place.greet()
                out_term.begin()
            if when == 1:
                out_term.to_partner()
                out_copy.start()
            if when == 4:
                out_term.end()
            for action in events[when]:
                action()

    @pl.when(step == 2)
    def _():
        for copy in loads:
            copy.start()

    @pl.when(step == heads)
    def _():
        for copy in loads:
            copy.wait()
        weight_gradient(1, dw2_ref)
        cat_term.begin()

    @pl.when(step == heads + 1)
    def _():
        cat_term.to_partner()
        own_small[...] = jnp.zeros_like(own_small)
        other_small[...] = jnp.zeros_like(other_small)
        bias_rows(1, other_small)

    @pl.when(step < 2 * heads)
    def _():
        back_one_head(mask_ref, qkv_ref, att_ref, log_ref, gatt_ref, d_ref, step, heads, block)

    @pl.when(step == 2 * heads)
    def _():
        for copy in row_loads(0):
            copy.start()
        cat_term.end()
        weight_gradient(0, dw_ref)
        bias_rows(0, own_small)

    for i in range(4):

        @pl.when(step == first_rows + i)
        def _(i=i):
            for copy in row_loads(i):
                copy.wait()
            if i < 3:
                for copy in row_loads(i + 1):
                    copy.start()
            here = pl.ds(pl.multiple_of(row_start(i), TAIL_BLOCK), TAIL_BLOCK)
            gin = contract(d_ref[0, :, here], w_ref[0], 0, 1)
            gin += contract(d_ref[1, :, here], w_ref[1], 0, 1)
            hat, inv = norm_parts(tok_ref[i % 2].astype(F32))
            gtok = gresid_ref[i % 2] + norm_back(hat, inv, gin * gain_ref[...])
            own_small[0:1] += jnp.sum(gin * hat, axis=0, keepdims=True)
            own_small[1:2] += jnp.sum(gin, axis=0, keepdims=True)
            if i < 2:
                sent_ref[pl.ds(i * TAIL_BLOCK, TAIL_BLOCK), :] = gtok.astype(BF16)
                token_copy(i).start()
            else:
                gtok_ref[...] = gtok

    @pl.when(step == last_step)
    def _():
        own_small[2:6] = small2_ref[0:4]
        other_small[0:2] = own_small[0:2]
        other_small[2:6] = small2_ref[0:4]
        for i in (0, 1):
            own_small[6 + i : 7 + i] = dbup1_ref[:, pl.ds(i * width, width)]
            other_small[6 + i : 7 + i] = dbup2_ref[:, pl.ds(i * width, width)]
        small.begin()
        late_steps = iter(late)
        small.over_cores()
        small.over_x()
        small.over_z()
        for action in late_steps:
            action()
        small_ref[...] = small.end()
        out_copy.wait()
        for i in (0, 1):
            token_copy(i).wait()
        for one in sums:
            one.end()


def back_one_head(mask_ref, qkv_ref, att_ref, log_ref, gatt_ref, d_ref, step, heads, block):
    rows = qkv_ref.shape[4]
    half = heads * HEAD_DIM
    source = 1 - step // heads
    head_at = pl.multiple_of((step % heads) * HEAD_DIM, HEAD_DIM)

    def store(which, columns, value):
        d_ref[source, pl.ds(which * half + head_at, HEAD_DIM), columns] = value.astype(BF16)

    images = [(0, LEN_L, block)] + [(at, LEN_S, LEN_S) for at in range(LEN_L, rows, LEN_S)]
    for start, count, size in images:
        every = slice(start, start + count)
        keys = qkv_ref[0, 1, 0, :, every]
        values = qkv_ref[0, 2, 0, :, every]
        ones = jnp.ones((1, count), F32)
        key_rows = jnp.concatenate(
            [keys, keys, extra_rows([ones, ones, ones, mask_ref[:, every]], count)], 0
        )
        value_rows = jnp.concatenate([values, extra_rows([ones, ones, ones], count)], 0)
        grad_values = grad_keys = None
        for at in range(start, start + count, size):
            here = slice(at, at + size)
            query = qkv_ref[0, 0, 0, :, here]
            grads = gatt_ref[0, 0, :, here]
            inner = jnp.sum(
                grads.astype(F32) * att_ref[0, 0, :, here].astype(F32), axis=0, keepdims=True
            )
            terms = three_terms(-log_ref[0, 0, :, here]) + [jnp.ones((1, size), F32)]
            query_rows = jnp.concatenate([*scaled_query(query), extra_rows(terms, size)], 0)
            grad_rows = jnp.concatenate([grads, extra_rows(three_terms(-inner), size)], 0)
            score = contract(query_rows, key_rows, 0, 0)
            grad_probs = contract(grad_rows, value_rows, 0, 0)
            probs = jnp.exp2(score)
            grad_score = (probs * grad_probs).astype(BF16)
            part_values = contract(grads, probs.astype(BF16), 1, 0)
            part_keys = contract(query, grad_score, 1, 0)
            grad_values = part_values if grad_values is None else grad_values + part_values
            grad_keys = part_keys if grad_keys is None else grad_keys + part_keys
            store(0, here, contract(keys, grad_score, 1, 1) * SCALE)
        store(1, every, grad_keys * SCALE)
        store(2, every, grad_values)


def tail(
    mask, qkv, att, log_total, gatt, gain, small2, dbup1, dbup2, dwout2, normed, w_cat, w_cat2,
    tokens, gresid, dup, ddown, dwout, seen_up, seen_down, out_rows, block=256,
):
    _, _, heads, _, rows = qkv.shape
    width, out = w_cat.shape
    anywhere = pl.BlockSpec(memory_space=pl.ANY)
    last = 2 * heads - 1

    def head(h):
        h = jnp.minimum(h, last)
        return 1 - h // heads, h % heads

    all_three = pl.BlockSpec(
        (1, 3, 1, HEAD_DIM, rows), lambda h: (head(h)[0], 0, head(h)[1], 0, 0)
    )
    one = pl.BlockSpec((1, 1, HEAD_DIM, rows), lambda h: (*head(h), 0, 0))
    row = pl.BlockSpec((1, 1, 1, rows), lambda h: (*head(h), 0, 0))
    sum_shapes = [(width, width)] * 4 + [dwout.shape, (width, out)]
    scratch = [
        pltpu.VMEM((2, out, rows), BF16),
        pltpu.VMEM((rows, width), BF16),
        pltpu.VMEM((2, width, out), BF16),
        pltpu.VMEM((2, TAIL_BLOCK, width), BF16),
        pltpu.VMEM((2, TAIL_BLOCK, width), F32),
        pltpu.VMEM((width, out), BF16),
        pltpu.VMEM((width, out), BF16),
        pltpu.VMEM((rows // 2, width), BF16),
        pltpu.VMEM((SmallSum.ROWS, width), F32),
        pltpu.VMEM((SmallSum.ROWS, width), F32),
        pltpu.SemaphoreType.DMA((3,)),
        pltpu.SemaphoreType.DMA((2, 2)),
        pltpu.SemaphoreType.DMA((3,)),
        pltpu.SemaphoreType.DMA((3,)),
    ]
    for shape in sum_shapes:
        scratch += PlaneSum.buffers(*shape)
    scratch += PartnerTerm.buffers(width, out) + PartnerTerm.buffers(*dwout.shape)
    scratch += SmallSum.buffers(width)
    pairs = pair_count(2 * heads, rows)
    first_rows = 2 * heads + 1
    return pl.pallas_call(
        functools.partial(tail_kernel, heads=heads, block=block),
        grid=(first_rows + 4,),
        in_specs=[
            whole((1, rows)), all_three, one, row, one, whole((1, width)), whole((8, width)),
            whole((1, 2 * width)), whole((1, 2 * width)), whole(dwout.shape),
        ]
        + [anywhere] * 11,
        out_specs=[
            pl.BlockSpec(
                (TAIL_BLOCK, width), lambda h: (jnp.maximum(h - first_rows - 2, 0), 0)
            ),
            whole((SmallSum.ROWS, width)),
        ]
        + [anywhere] * 6,
        out_shape=[
            jax.ShapeDtypeStruct((rows // 2, width), F32),
            jax.ShapeDtypeStruct((SmallSum.ROWS, width), F32),
            jax.ShapeDtypeStruct((rows // 2, width), BF16),
            jax.ShapeDtypeStruct(dup.shape, BF16),
            jax.ShapeDtypeStruct(ddown.shape, BF16),
            jax.ShapeDtypeStruct(dwout.shape, BF16),
            jax.ShapeDtypeStruct((width, out), BF16),
            jax.ShapeDtypeStruct((rows // 2, width), BF16),
        ],
        scratch_shapes=scratch,
        compiler_params=pltpu.CompilerParams(
            vmem_limit_bytes=VMEM_LIMIT, collective_id=0, has_side_effects=True
        ),
        cost_estimate=cost(pairs * 5 * 512, 32 * heads * HEAD_DIM * rows, pairs),
        name="tail",
    )(
        mask, qkv, att, log_total, gatt, gain, small2, dbup1, dbup2, dwout2, normed, w_cat, w_cat2,
        tokens, gresid, dup, ddown, dwout, seen_up, seen_down, out_rows,
    )


def swap_tp(array):
    return lax.ppermute(array, "tp", [(0, 1), (1, 0)])


def swap_dp(array, bit):
    count = lax.axis_size("dp")
    return lax.ppermute(array, "dp", [(i, i ^ bit) for i in range(count)])


def dp_bit(bit):
    return (lax.axis_index("dp") & bit) != 0


def joined(mine, theirs, second):
    return jnp.where(second, jnp.concatenate([theirs, mine], 0), jnp.concatenate([mine, theirs], 0))


def half_of(array, second):
    size = array.shape[0] // 2
    return lax.dynamic_slice_in_dim(array, jnp.where(second, size, 0), size, 0)


def fetch_other(array, bits):
    piece = array
    for bit in reversed(bits):
        piece = half_of(piece, dp_bit(bit))
    piece = swap_tp(piece)
    for bit in bits:
        piece = joined(piece, swap_dp(piece, bit), dp_bit(bit))
    return piece


def add_low(left, right):
    return (left.astype(F32) + right.astype(F32)).astype(BF16)


def over_cores(other, chunks=1):
    second = dp_bit(1)
    split = other.reshape(chunks, other.shape[0] // chunks, other.shape[1])
    half = split.shape[1] // 2
    take = lambda which: lax.dynamic_slice_in_dim(split, jnp.where(which, half, 0), half, 1)
    both = add_low(take(second), swap_dp(take(~second), 1))
    return both.reshape(-1, other.shape[1])


def by_images(
    tokens, long_lengths, short_lengths, ln1_gain, ln1_bias, w_query, b_query, w_key, w_value,
    b_value, w_out, b_out, ln2_gain, ln2_bias, w_up, b_up, w_down, b_down, cotangent,
):
    rank = lax.axis_index("tp")
    rank_arr = jnp.reshape(rank, (1,)).astype(jnp.int32)
    second = rank == 1
    rows = tokens.shape[0] // 2
    width = tokens.shape[1]
    half = w_query.shape[1]
    heads = half // HEAD_DIM
    long_len = lax.dynamic_slice_in_dim(long_lengths, rank, 1, 0)
    shorts = short_lengths.shape[0] // 2
    short_len = lax.dynamic_slice_in_dim(short_lengths, rank * shorts, shorts, 0)
    valid = jnp.concatenate(
        [
            jnp.arange(LEN_L) < long_len[0],
            (jnp.arange(LEN_S)[None, :] < short_len[:, None]).reshape(-1),
        ]
    )
    mask = jnp.where(valid, 0.0, -1e30).astype(F32).reshape(1, -1)
    row = lambda vector: vector.astype(F32).reshape(1, -1)
    core, xbit = 1, 2

    w_cat = jnp.concatenate([w_query, w_key, w_value], axis=1)
    w_cat2 = fetch_other(w_cat, [core, xbit])
    bias = jnp.concatenate([b_query, b_value, b_up]).astype(F32)
    bias2 = swap_tp(bias)

    def column(packed):
        return jnp.concatenate(
            [packed[:half], jnp.zeros((half,), F32), packed[half : 2 * half]]
        ).reshape(-1, 1)

    w_out2 = fetch_other(w_out, [core, xbit])
    w_up2 = fetch_other(w_up, [core, xbit])
    w_down2 = fetch_other(w_down, [core, xbit])
    kept = half_of(cotangent, second)
    got = swap_tp(half_of(cotangent, ~second))
    grads = joined(kept, got, second)

    normed, own_tokens, qkv = project_norm(
        rank_arr, tokens, row(ln1_gain), row(ln1_bias), w_cat, column(bias), rows, 512
    )
    parts = (2, 3, heads, HEAD_DIM, rows)
    att = attend_forward(mask, qkv.reshape(parts), 0)
    qkv = project(qkv, normed, w_cat2, column(bias2), 512).reshape(parts)
    att, log_total = attend_forward(mask, qkv, 1, att)
    attended = att.reshape(2 * half, rows)
    w_out_all = jnp.concatenate([w_out, w_out2], axis=0)
    resid, mid = middle(
        own_tokens, attended, w_out_all, row(b_out), row(ln2_gain), row(ln2_bias), 512
    )
    sum2, gmid2, dup2, ddown2, dbup2 = feed(mid, grads, w_up2, row(bias2[2 * half :]), w_down2)
    mid, both_up, both_down = lax.optimization_barrier((mid, over_cores(dup2), over_cores(ddown2, 2)))
    seen_up, seen_down = swap_tp(both_up), swap_tp(both_down)
    sum1, gmid1, dup1, ddown1, dbup1 = feed(mid, grads, w_up, row(bias[2 * half :]), w_down)
    out, gresid, gatt, dwout1, dwout2, small2 = branch(
        resid, (sum1, sum2), (gmid1, gmid2), grads, row(ln2_gain), row(b_down), w_out_all,
        attended, 512,
    )
    gtok, small, got_tok, grad_up, grad_down, grad_out_t, grad_cat, got_out = tail(
        mask, qkv, att, log_total, gatt.reshape(2, heads, HEAD_DIM, rows), row(ln1_gain), small2,
        dbup1, dbup2, dwout2, normed, w_cat, w_cat2, own_tokens, gresid, dup1, ddown1, dwout1,
        seen_up, seen_down, out,
    )
    result = joined(half_of(out, second), got_out, second)
    grad_tokens = joined(gtok, got_tok.astype(F32), second)
    grad_cat = grad_cat.astype(F32)
    return (
        result,
        grad_tokens,
        small[0],
        small[1],
        grad_cat[:, :half],
        small[8, :half],
        grad_cat[:, half : 2 * half],
        grad_cat[:, 2 * half :],
        small[8, half:],
        grad_out_t.T.astype(F32),
        small[4],
        small[2],
        small[3],
        grad_up.astype(F32),
        small[6:8].reshape(-1),
        grad_down.astype(F32),
        small[5],
    )


def layer_norm(values, gain, shift):
    center = values - jnp.mean(values, axis=-1, keepdims=True)
    spread = jnp.mean(center * center, axis=-1, keepdims=True)
    return center * lax.rsqrt(spread + 1e-06) * gain + shift


def dot_plain(left, right):
    return jnp.dot(left, right, preferred_element_type=jnp.float32)


def dot_rows(left, right):
    return lax.dot_general(
        left, right, (((0,), (0,)), ((), ())), preferred_element_type=jnp.float32
    )


def dot_back(left, right):
    return lax.dot_general(
        left, right, (((1,), (1,)), ((), ())), preferred_element_type=jnp.float32
    )


def group_shape(image_count, seq_len, head_count):
    per_step = math.gcd(image_count, max(1, 512 // seq_len))
    return (image_count // per_step, per_step, seq_len, head_count, HEAD_DIM)


def masked_scores(query_blk, key_blk, length_blk):
    seq_len = query_blk.shape[1]
    raw = jnp.einsum(
        "bqhd,bkhd->bhqk", query_blk, key_blk, preferred_element_type=jnp.float32
    ) * HEAD_DIM ** (-0.5)
    keep = jnp.arange(seq_len, dtype=jnp.int32)[None, :] < length_blk[:, None]
    return jnp.where(keep[:, None, None, :], raw, -1e30)


def attention_forward(queries, key_rows, value_rows, lengths, seq_len):
    image_count = lengths.shape[0]
    head_count = queries.shape[1] // HEAD_DIM
    block_shape = group_shape(image_count, seq_len, head_count)

    def one_step(block):
        query_blk, key_blk, value_blk, length_blk = block
        scores = masked_scores(query_blk, key_blk, length_blk)
        row_top = jnp.max(scores, axis=-1, keepdims=True)
        exp_terms = jnp.exp(scores - row_top)
        row_total = jnp.sum(exp_terms, axis=-1, keepdims=True)
        weights = (exp_terms / row_total).astype(jnp.bfloat16)
        mixed = jnp.einsum(
            "bhqk,bkhd->bqhd", weights, value_blk, preferred_element_type=jnp.float32
        )
        return (mixed, (row_top + jnp.log(row_total))[..., 0])

    mixed, log_total = lax.map(
        one_step,
        (
            queries.reshape(block_shape),
            key_rows.reshape(block_shape),
            value_rows.reshape(block_shape),
            lengths.reshape(block_shape[:2]),
        ),
    )
    return (mixed.reshape(image_count * seq_len, head_count * HEAD_DIM), log_total)


def attention_backward(queries, key_rows, value_rows, grads, lengths, log_total, seq_len):
    image_count = lengths.shape[0]
    head_count = queries.shape[1] // HEAD_DIM
    block_shape = group_shape(image_count, seq_len, head_count)
    scale = HEAD_DIM ** (-0.5)

    def one_step(block):
        query_blk, key_blk, value_blk, grad_blk, length_blk, total_blk = block
        scores = masked_scores(query_blk, key_blk, length_blk)
        probs = jnp.exp(scores - total_blk[..., None])
        grad_values = jnp.einsum(
            "bhqk,bqhd->bkhd",
            probs.astype(jnp.bfloat16),
            grad_blk,
            preferred_element_type=jnp.float32,
        )
        grad_probs = jnp.einsum(
            "bqhd,bkhd->bhqk", grad_blk, value_blk, preferred_element_type=jnp.float32
        )
        inner = jnp.sum(probs * grad_probs, axis=-1, keepdims=True)
        grad_scores = (probs * (grad_probs - inner)).astype(jnp.bfloat16)
        grad_queries = (
            jnp.einsum("bhqk,bkhd->bqhd", grad_scores, key_blk, preferred_element_type=jnp.float32)
            * scale
        )
        grad_keys = (
            jnp.einsum(
                "bhqk,bqhd->bkhd", grad_scores, query_blk, preferred_element_type=jnp.float32
            )
            * scale
        )
        return (grad_queries, grad_keys, grad_values)

    results = lax.map(
        one_step,
        (
            queries.reshape(block_shape),
            key_rows.reshape(block_shape),
            value_rows.reshape(block_shape),
            grads.reshape(block_shape),
            lengths.reshape(block_shape[:2]),
            log_total,
        ),
    )
    flat = (image_count * seq_len, head_count * HEAD_DIM)
    return tuple((item.reshape(flat) for item in results))


def local(
    tokens,
    long_lengths,
    short_lengths,
    ln1_gain,
    ln1_bias,
    w_query,
    b_query,
    w_key,
    w_value,
    b_value,
    w_out,
    b_out,
    ln2_gain,
    ln2_bias,
    w_up,
    b_up,
    w_down,
    b_down,
    cotangent,
):
    tp_count = lax.axis_size("tp")
    tp_rank = lax.axis_index("tp")
    row_count = tokens.shape[0]
    share = row_count // tp_count
    split = long_lengths.shape[0] * LEN_L
    gain_one = ln1_gain.astype(jnp.float32)
    shift_one = ln1_bias.astype(jnp.float32)
    gain_two = ln2_gain.astype(jnp.float32)
    shift_two = ln2_bias.astype(jnp.float32)
    normed_in = layer_norm(tokens.astype(jnp.float32), gain_one, shift_one).astype(jnp.bfloat16)
    queries = (dot_plain(normed_in, w_query) + b_query.astype(jnp.float32)).astype(jnp.bfloat16)
    key_rows = dot_plain(normed_in, w_key).astype(jnp.bfloat16)
    value_rows = (dot_plain(normed_in, w_value) + b_value.astype(jnp.float32)).astype(jnp.bfloat16)
    long_mixed, long_total = attention_forward(
        queries[:split], key_rows[:split], value_rows[:split], long_lengths, LEN_L
    )
    short_mixed, short_total = attention_forward(
        queries[split:], key_rows[split:], value_rows[split:], short_lengths, LEN_S
    )
    attended = jnp.concatenate([long_mixed, short_mixed], axis=0).astype(jnp.bfloat16)
    attn_sum = lax.psum_scatter(dot_plain(attended, w_out), "tp", scatter_dimension=0, tiled=True)
    own_tokens = lax.dynamic_slice_in_dim(tokens, tp_rank * share, share, 0).astype(jnp.float32)
    resid = own_tokens + attn_sum + b_out.astype(jnp.float32)
    normed_mid = layer_norm(resid, gain_two, shift_two).astype(jnp.bfloat16)
    grad_out = cotangent.astype(jnp.float32)
    mid_rows = lax.all_gather(normed_mid, "tp", axis=0, tiled=True)
    pre_up = dot_plain(mid_rows, w_up) + b_up.astype(jnp.float32)
    activ = jax.nn.gelu(pre_up, approximate=False).astype(jnp.bfloat16)
    ffn_sum = lax.psum_scatter(
        dot_plain(activ, w_down).astype(jnp.bfloat16), "tp", scatter_dimension=0, tiled=True
    ).astype(jnp.float32)
    result = resid + ffn_sum + b_down.astype(jnp.float32)
    grad_rows = lax.all_gather(cotangent, "tp", axis=0, tiled=True)
    grad_w_down = dot_rows(activ, grad_rows)
    grad_activ = dot_back(grad_rows, w_down)
    _, gelu_back = jax.vjp(lambda inner: jax.nn.gelu(inner, approximate=False), pre_up)
    grad_pre = gelu_back(grad_activ)[0].astype(jnp.bfloat16)
    grad_w_up = dot_rows(mid_rows, grad_pre)
    grad_b_up = jnp.sum(grad_pre.astype(jnp.float32), axis=0)
    grad_mid = lax.psum_scatter(dot_back(grad_pre, w_up), "tp", scatter_dimension=0, tiled=True)
    _, norm_two_back = jax.vjp(layer_norm, resid, gain_two, shift_two)
    grad_resid_norm, grad_gain_two, grad_shift_two = norm_two_back(grad_mid)
    grad_resid = grad_out + grad_resid_norm
    grad_b_down = jnp.sum(grad_out, axis=0)
    grad_b_out = jnp.sum(grad_resid, axis=0)
    grad_branch = lax.all_gather(grad_resid.astype(jnp.bfloat16), "tp", axis=0, tiled=True)
    grad_w_out = dot_rows(attended, grad_branch)
    grad_attended = dot_back(grad_branch, w_out).astype(jnp.bfloat16)
    long_grads = attention_backward(
        queries[:split],
        key_rows[:split],
        value_rows[:split],
        grad_attended[:split],
        long_lengths,
        long_total,
        LEN_L,
    )
    short_grads = attention_backward(
        queries[split:],
        key_rows[split:],
        value_rows[split:],
        grad_attended[split:],
        short_lengths,
        short_total,
        LEN_S,
    )
    grad_queries = jnp.concatenate([long_grads[0], short_grads[0]], axis=0).astype(jnp.bfloat16)
    grad_keys = jnp.concatenate([long_grads[1], short_grads[1]], axis=0).astype(jnp.bfloat16)
    grad_values = jnp.concatenate([long_grads[2], short_grads[2]], axis=0).astype(jnp.bfloat16)
    grad_w_query = dot_rows(normed_in, grad_queries)
    grad_b_query = jnp.sum(grad_queries.astype(jnp.float32), axis=0)
    grad_w_key = dot_rows(normed_in, grad_keys)
    grad_w_value = dot_rows(normed_in, grad_values)
    grad_b_value = jnp.sum(grad_values.astype(jnp.float32), axis=0)
    grad_in = lax.psum_scatter(
        dot_back(grad_queries, w_query)
        + dot_back(grad_keys, w_key)
        + dot_back(grad_values, w_value),
        "tp",
        scatter_dimension=0,
        tiled=True,
    )
    _, norm_one_back = jax.vjp(layer_norm, own_tokens, gain_one, shift_one)
    grad_tokens_norm, grad_gain_one, grad_shift_one = norm_one_back(grad_in)
    grad_tokens = grad_resid + grad_tokens_norm
    summed = lax.psum(
        (
            grad_w_query,
            grad_b_query,
            grad_w_key,
            grad_w_value,
            grad_b_value,
            grad_w_out,
            grad_w_up,
            grad_b_up,
            grad_w_down,
        ),
        "dp",
    )
    shared = lax.psum(
        (grad_gain_one, grad_shift_one, grad_b_out, grad_gain_two, grad_shift_two, grad_b_down),
        ("dp", "tp"),
    )
    return (
        result.astype(jnp.bfloat16),
        grad_tokens,
        shared[0],
        shared[1],
        summed[0],
        summed[1],
        summed[2],
        summed[3],
        summed[4],
        summed[5],
        shared[2],
        shared[3],
        shared[4],
        summed[6],
        summed[7],
        summed[8],
        shared[5],
    )


def pick(*arrays):
    tokens, long_lengths, short_lengths, w_query, w_up = (arrays[i] for i in (0, 1, 2, 5, 14))
    fits = (
        lax.axis_size("tp") == 2
        and lax.axis_size("dp") == 16
        and long_lengths.shape[0] == 2
        and short_lengths.shape[0] == 8
        and tokens.shape == (2 * LEN_L + 8 * LEN_S, 768)
        and w_query.shape[1] == 8 * HEAD_DIM
        and w_up.shape[1] == 1536
    )
    return by_images(*arrays) if fits else local(*arrays)


def solution(mesh):
    placed = (
        P("dp", None),
        P("dp"),
        P("dp"),
        P(),
        P(),
        P(None, "tp"),
        P("tp"),
        P(None, "tp"),
        P(None, "tp"),
        P("tp"),
        P("tp", None),
        P(),
        P(),
        P(),
        P(None, "tp"),
        P("tp"),
        P("tp", None),
        P(),
        P(("dp", "tp"), None),
    )
    return jax.shard_map(
        pick,
        mesh=mesh,
        in_specs=placed,
        out_specs=(
            P(("dp", "tp"), None),
            P(("dp", "tp"), None),
            P(),
            P(),
            P(None, "tp"),
            P("tp"),
            P(None, "tp"),
            P(None, "tp"),
            P("tp"),
            P("tp", None),
            P(),
            P(),
            P(),
            P(None, "tp"),
            P("tp"),
            P("tp", None),
            P(),
        ),
        check_vma=False,
    )
```

```python
import functools
import math

import jax
import jax.numpy as jnp
from jax import lax
from jax.experimental import pallas as pl
from jax.experimental.pallas import tpu as pltpu
from jax.sharding import PartitionSpec as P

HEAD_DIM = 48
LEN_L = 1024
LEN_S = 256
F32 = jnp.float32
BF16 = jnp.bfloat16
LOG2E = math.log2(math.e)
SCALE = HEAD_DIM ** (-0.5)
VMEM_LIMIT = 58 << 20
HEAD_GROUP = 2


def contract(left, right, left_dim, right_dim):
    return lax.dot_general(
        left, right, (((left_dim,), (right_dim,)), ((), ())), preferred_element_type=F32
    )


def params():
    return pltpu.CompilerParams(vmem_limit_bytes=VMEM_LIMIT)


def cost(flops, bytes_accessed, transcendentals=0):
    return pl.CostEstimate(
        flops=int(flops), bytes_accessed=int(bytes_accessed), transcendentals=int(transcendentals)
    )


def whole(shape):
    zeros = (0,) * len(shape)
    return pl.BlockSpec(shape, lambda *_: zeros)


def norm_parts(values):
    center = values - jnp.mean(values, axis=-1, keepdims=True)
    inv = lax.rsqrt(jnp.mean(center * center, axis=-1, keepdims=True) + 1e-06)
    return center * inv, inv


def norm_back(hat, inv, grad_hat):
    mean_grad = jnp.mean(grad_hat, axis=-1, keepdims=True)
    mean_both = jnp.mean(grad_hat * hat, axis=-1, keepdims=True)
    return inv * (grad_hat - mean_grad - hat * mean_both)


def three_terms(value):
    high = value.astype(BF16).astype(F32)
    rest = value - high
    mid = rest.astype(BF16).astype(F32)
    return [high, mid, rest - mid]


def extra_rows(rows, count):
    at = lax.broadcasted_iota(jnp.int32, (16, count), 0)
    out = jnp.zeros((16, count), F32)
    for place, row in enumerate(rows):
        out = jnp.where(at == place, row, out)
    return out.astype(BF16)


def scaled_query(query):
    wide = query.astype(F32) * (SCALE * LOG2E)
    high = wide.astype(BF16)
    return [high, (wide - high.astype(F32)).astype(BF16)]


def pair_count(heads, rows):
    return heads * (LEN_L**2 + (rows - LEN_L) * LEN_S)


class Place:
    def __init__(self):
        me = lax.axis_index("dp")
        self.core, self.x, self.z = me % 2, (me // 2) % 2, me // 4
        self.rank = lax.axis_index("tp")

    def at(self, z=None, x=None, core=None):
        z = self.z if z is None else z
        x = self.x if x is None else x
        core = self.core if core is None else core
        return {"dp": (z * 2 + x) * 2 + core}

    def across_core(self):
        return self.at(core=1 - self.core)

    def across_x(self):
        return self.at(x=1 - self.x)

    def along_z(self, step):
        return self.at(z=(self.z + step) % 4)

    def partner(self):
        return {"tp": 1 - self.rank}

    def greet(self):
        barrier = pltpu.get_barrier_semaphore()
        others = [self.across_core(), self.across_x(), self.partner()]
        others += [self.along_z(step) for step in (1, 2, 3)]
        for other in others:
            pl.semaphore_signal(
                barrier, inc=1, device_id=other, device_id_type=pl.DeviceIdType.MESH
            )
        pl.semaphore_wait(barrier, len(others))


def send_to(source, target, send, recv, device):
    return pltpu.make_async_remote_copy(
        src_ref=source,
        dst_ref=target,
        send_sem=send,
        recv_sem=recv,
        device_id=device,
        device_id_type=pl.DeviceIdType.MESH,
    )


def part(ref, start, count):
    return ref.at[pl.ds(pl.multiple_of(start, 16), count)]


def add_rows(target, start, count, terms):
    tile = 48

    def body(i, _):
        at = pl.multiple_of(i * tile, 16)
        here = pl.ds(pl.multiple_of(start + at, 16), tile)
        total = target[here, :].astype(F32)
        for term in terms:
            total = total + term[pl.ds(at, tile), :].astype(F32)
        target[here, :] = total.astype(BF16)
        return 0

    lax.fori_loop(0, count // tile, body, 0)


class PlaneSum:
    def __init__(self, place, own, seen, out, refs):
        self.place, self.own, self.seen, self.out = place, own, seen, out
        (self.acc, self.seen_here, self.from_core, self.from_x, self.from_z,
         self.send, self.recv, self.local) = refs
        self.rows = own.shape[0]

    @staticmethod
    def buffers(rows, width):
        return [
            pltpu.VMEM((rows // 2, width), BF16),
            pltpu.VMEM((rows // 2, width), BF16),
            pltpu.VMEM((rows // 2, width), BF16),
            pltpu.VMEM((rows // 4, width), BF16),
            pltpu.VMEM((3, rows // 16, width), BF16),
            pltpu.SemaphoreType.DMA((10,)),
            pltpu.SemaphoreType.DMA((10,)),
            pltpu.SemaphoreType.DMA((3,)),
        ]

    def copy(self, source, target, place, device):
        return send_to(source, target, self.send.at[place], self.recv.at[place], device)

    def core_copy(self):
        half = self.rows // 2
        source = part(self.own, (1 - self.place.core) * half, half)
        return self.copy(source, self.from_core, 0, self.place.across_core())

    def local_copies(self):
        half = self.rows // 2
        source = part(self.own, self.place.core * half, half)
        copies = [pltpu.make_async_copy(source, self.acc, self.local.at[0])]
        if self.seen is not None:
            copies.append(pltpu.make_async_copy(self.seen, self.seen_here, self.local.at[1]))
        return copies

    def x_copy(self):
        count = self.rows // 4
        source = part(self.acc, (1 - self.place.x) * count, count)
        return self.copy(source, self.from_x, 1, self.place.across_x())

    def z_copies(self):
        count = self.rows // 16
        copies = []
        for step in (1, 2, 3):
            there = (self.place.z + step) % 4
            source = part(self.acc, self.place.x * 4 * count + there * count, count)
            target = self.from_z.at[step - 1]
            copies.append(self.copy(source, target, 1 + step, self.place.along_z(step)))
        return copies

    def piece(self):
        count = self.rows // 16
        inside = self.place.x * 4 * count + self.place.z * count
        return (
            part(self.acc, inside, count),
            part(self.out, self.place.core * 8 * count + inside, count),
        )

    def keep_copy(self):
        mine, there = self.piece()
        return pltpu.make_async_copy(mine, there, self.local.at[2])

    def back_z_copies(self):
        mine, there = self.piece()
        return [
            self.copy(mine, there, 4 + step, self.place.along_z(step)) for step in (1, 2, 3)
        ]

    def back_x_copy(self):
        count = self.rows // 4
        there = part(self.out, self.place.core * 2 * count + self.place.x * count, count)
        return self.copy(there, there, 8, self.place.across_x())

    def back_core_copy(self):
        count = self.rows // 2
        there = part(self.out, self.place.core * count, count)
        return self.copy(there, there, 9, self.place.across_core())

    def begin(self):
        self.core_copy().start()
        for copy in self.local_copies():
            copy.start()

    def along_x(self):
        self.core_copy().wait()
        for copy in self.local_copies():
            copy.wait()
        add_rows(self.acc, 0, self.rows // 2, [self.from_core, self.seen_here])
        self.x_copy().start()

    def along_z(self):
        self.x_copy().wait()
        count = self.rows // 4
        add_rows(self.acc, self.place.x * count, count, [self.from_x])
        for copy in self.z_copies():
            copy.start()

    def back_along_z(self):
        for copy in self.z_copies():
            copy.wait()
        count = self.rows // 16
        inside = self.place.x * 4 * count + self.place.z * count
        add_rows(self.acc, inside, count, [self.from_z.at[i] for i in range(3)])
        self.keep_copy().start()
        for copy in self.back_z_copies():
            copy.start()

    def back_along_x(self):
        self.keep_copy().wait()
        for copy in self.back_z_copies():
            copy.wait()
        self.back_x_copy().start()

    def back_to_core(self):
        self.back_x_copy().wait()
        self.back_core_copy().start()

    def end(self):
        self.back_core_copy().wait()


class PartnerTerm:
    def __init__(self, place, other, seen, refs):
        self.place, self.other, self.seen = place, other, seen
        self.from_core, self.send, self.recv = refs
        self.half = other.shape[0] // 2

    @staticmethod
    def buffers(rows, width):
        return [
            pltpu.VMEM((rows // 2, width), BF16),
            pltpu.SemaphoreType.DMA((2,)),
            pltpu.SemaphoreType.DMA((2,)),
        ]

    def core_copy(self):
        source = part(self.other, (1 - self.place.core) * self.half, self.half)
        return send_to(
            source, self.from_core, self.send.at[0], self.recv.at[0], self.place.across_core()
        )

    def partner_copy(self):
        return send_to(
            self.from_core, self.seen, self.send.at[1], self.recv.at[1], self.place.partner()
        )

    def begin(self):
        self.core_copy().start()

    def to_partner(self):
        self.core_copy().wait()
        mine = part(self.other, self.place.core * self.half, self.half)
        add_rows(self.from_core, 0, self.half, [mine])
        self.partner_copy().start()

    def end(self):
        self.partner_copy().wait()


class SmallSum:
    ROWS = 16

    def __init__(self, place, own, other, refs):
        self.place, self.own, self.other = place, own, other
        self.sums, self.got, self.send, self.recv = refs

    @staticmethod
    def buffers(width):
        rows = SmallSum.ROWS
        return [
            pltpu.VMEM((3, rows, width), F32),
            pltpu.VMEM((6, rows, width), F32),
            pltpu.SemaphoreType.DMA((6,)),
            pltpu.SemaphoreType.DMA((6,)),
        ]

    def copy(self, source, place, device):
        return send_to(source, self.got.at[place], self.send.at[place], self.recv.at[place], device)

    def partner_copy(self):
        return self.copy(self.other, 0, self.place.partner())

    def core_copy(self):
        return self.copy(self.sums.at[0], 1, self.place.across_core())

    def x_copy(self):
        return self.copy(self.sums.at[1], 2, self.place.across_x())

    def z_copies(self):
        return [
            self.copy(self.sums.at[2], 2 + step, self.place.along_z(step)) for step in (1, 2, 3)
        ]

    def begin(self):
        self.partner_copy().start()

    def over_cores(self):
        self.partner_copy().wait()
        self.sums[0] = self.own[...] + self.got[0]
        self.core_copy().start()

    def over_x(self):
        self.core_copy().wait()
        self.sums[1] = self.sums[0] + self.got[1]
        self.x_copy().start()

    def over_z(self):
        self.x_copy().wait()
        self.sums[2] = self.sums[1] + self.got[2]
        for copy in self.z_copies():
            copy.start()

    def end(self):
        for copy in self.z_copies():
            copy.wait()
        return self.sums[2] + self.got[3] + self.got[4] + self.got[5]


class Fetch:
    def __init__(self, place, own, got, refs, deep):
        self.place, self.own, self.got, self.deep = place, own, got, deep
        self.send, self.recv = refs
        self.half = own.shape[0] // 2
        self.quarter = self.half // 2
        self.count = self.quarter // 2 if deep else self.quarter
        self.core_at = place.core * self.half
        self.x_at = self.core_at + place.x * self.quarter
        odd = place.z % 2
        self.at = self.x_at + odd * self.count if deep else self.x_at
        self.z_at = self.x_at + (1 - odd) * self.count
        self.z_device = place.at(z=place.z + 1 - 2 * odd)

    @staticmethod
    def buffers():
        return [pltpu.SemaphoreType.DMA((5,)), pltpu.SemaphoreType.DMA((5,))]

    def copy(self, source, start, count, place, device):
        there = part(self.got, start, count)
        here = part(source, start, count)
        return send_to(here, there, self.send.at[place], self.recv.at[place], device)

    def partner_copy(self):
        return self.copy(self.own, self.at, self.count, 0, self.place.partner())

    def z_copy(self):
        return self.copy(self.got, self.at, self.count, 1, self.z_device)

    def x_copies(self):
        copies = [self.copy(self.got, self.at, self.count, 2, self.place.across_x())]
        if self.deep:
            copies.append(self.copy(self.got, self.z_at, self.count, 3, self.place.across_x()))
        return copies

    def core_copy(self):
        return self.copy(self.got, self.core_at, self.half, 4, self.place.across_core())

    def begin(self):
        self.partner_copy().start()

    def share(self):
        self.partner_copy().wait()
        if self.deep:
            self.z_copy().start()
        self.x_copies()[0].start()

    def more_x(self):
        self.z_copy().wait()
        self.x_copies()[1].start()

    def to_core(self):
        for copy in self.x_copies():
            copy.wait()
        self.core_copy().start()

    def end(self):
        self.core_copy().wait()


FRONT_BLOCK = 512


def front_kernel(
    mask_ref, gain_ref, shift_ref, bout_ref, gain2_ref, shift2_ref, bias_ref,
    tok_hbm, wq_hbm, wk_hbm, wv_hbm, wout_hbm, wup_hbm, wdown_hbm, cot_hbm,
    x_out, qkv_out, att_out, log_out, resid_out, mid_out,
    cat_hbm, wout_all_hbm, up2_hbm, down2_hbm, grads_hbm, bias2_hbm, tok_out,
    tok_ref, x_ref, qkv_ref, att_ref, cat_ref, wout_ref, bias2_ref, load_sem, out_sem, swap_send,
    swap_recv, *scratch, heads, block,
):
    step = pl.program_id(0)
    place = Place()
    half = heads * HEAD_DIM
    rows = tok_ref.shape[0]
    blocks = rows // FRONT_BLOCK
    pairs = heads // HEAD_GROUP
    base = [0, blocks, blocks + pairs, 2 * blocks + pairs, 2 * blocks + 2 * pairs]

    sems = [scratch[2 * i : 2 * i + 2] for i in range(6)]
    mine = [wq_hbm, wk_hbm, wv_hbm]
    projections = [
        Fetch(place, own, cat_ref.at[1, :, pl.ds(i * half, half)], sems[i], False)
        for i, own in enumerate(mine)
    ]
    fetch_out = Fetch(place, wout_hbm, wout_ref.at[pl.ds(half, half)], sems[3], False)
    fetch_up = Fetch(place, wup_hbm, up2_hbm, sems[4], True)
    fetch_down = Fetch(place, wdown_hbm, down2_hbm, sems[5], True)
    bias_copy = send_to(
        bias_ref, bias2_ref, swap_send.at[0], swap_recv.at[0], place.partner()
    )
    here = pl.ds(pl.multiple_of(place.rank * LEN_L, LEN_L), LEN_L)
    theirs = pl.ds(pl.multiple_of((1 - place.rank) * LEN_L, LEN_L), LEN_L)
    cot_copy = send_to(
        cot_hbm.at[theirs], grads_hbm.at[here], swap_send.at[1], swap_recv.at[1], place.partner()
    )

    def token_rows(i):
        start = pl.multiple_of(i * 2 * LEN_L + place.rank * LEN_L, LEN_L)
        return tok_hbm.at[pl.ds(start, LEN_L)]

    token_loads = [
        pltpu.make_async_copy(token_rows(i), tok_ref.at[pl.ds(i * LEN_L, LEN_L)], load_sem.at[i])
        for i in (0, 1)
    ]
    weight_loads = [
        pltpu.make_async_copy(
            own, cat_ref.at[0, :, pl.ds(i * half, half)], load_sem.at[2 + i]
        )
        for i, own in enumerate(mine)
    ]
    out_load = pltpu.make_async_copy(wout_hbm, wout_ref.at[pl.ds(0, half)], load_sem.at[5])
    kept_copy = pltpu.make_async_copy(cot_hbm.at[here], grads_hbm.at[here], out_sem.at[0])
    stores = [
        pltpu.make_async_copy(cat_ref, cat_hbm, out_sem.at[1]),
        pltpu.make_async_copy(wout_ref, wout_all_hbm, out_sem.at[2]),
        pltpu.make_async_copy(bias2_ref, bias2_hbm, out_sem.at[3]),
        pltpu.make_async_copy(tok_ref, tok_out, out_sem.at[4]),
    ]

    @pl.when(step == 0)
    def _():
        for copy in (*token_loads, *weight_loads, out_load):
            copy.start()
        place.greet()
        for one in projections:
            one.begin()
        bias_copy.start()
        fetch_out.begin()
        for copy in token_loads:
            copy.wait()
        for copy in weight_loads:
            copy.wait()

    def at_step(when):
        return pl.when(step == when)

    @at_step(base[1] - 1)
    def _():
        fetch_up.begin()
        fetch_down.begin()

    @at_step(base[1] + 1)
    def _():
        for one in (*projections, fetch_out):
            one.share()

    @at_step(base[2] - 1)
    def _():
        for one in (*projections, fetch_out):
            one.to_core()

    @at_step(base[2])
    def _():
        for one in (*projections, fetch_out):
            one.end()
        bias_copy.wait()
        out_load.wait()
        for copy in stores:
            copy.start()
        kept_copy.start()
        fetch_up.share()
        fetch_down.share()
        cot_copy.start()

    @at_step(base[3] + 2)
    def _():
        fetch_up.more_x()
        fetch_down.more_x()

    @at_step(base[4] + 2)
    def _():
        fetch_up.to_core()
        fetch_down.to_core()

    def project(which, i, bias):
        at = pl.ds(pl.multiple_of(i * FRONT_BLOCK, FRONT_BLOCK), FRONT_BLOCK)
        column = jnp.transpose(bias[:, : 3 * half])[:, :1]
        value = (contract(cat_ref[which], x_ref[at, :], 0, 1) + column).astype(BF16)
        qkv_ref[:, at] = value
        qkv_out[0] = value

    @pl.when(step < base[1])
    def _():
        at = pl.ds(pl.multiple_of(step * FRONT_BLOCK, FRONT_BLOCK), FRONT_BLOCK)
        hat, _ = norm_parts(tok_ref[at, :].astype(F32))
        normed = (hat * gain_ref[...] + shift_ref[...]).astype(BF16)
        x_ref[at, :] = normed
        x_out[...] = normed
        project(0, step, bias_ref[...])

    @pl.when(jnp.logical_and(step >= base[2], step < base[3]))
    def _():
        project(1, step - base[2], bias2_ref[...])

    own_part = jnp.logical_and(step >= base[1], step < base[2])
    other_part = jnp.logical_and(step >= base[3], step < base[4])

    @pl.when(jnp.logical_or(own_part, other_part))
    def _():
        second = (step >= base[3]).astype(jnp.int32)
        pair = step - base[1] - second * (base[3] - base[1])
        attend_pair(mask_ref, qkv_ref, att_ref, att_out, log_out, pair, second, heads, block)

    @pl.when(step >= base[4])
    def _():
        i = step - base[4]
        at = pl.ds(pl.multiple_of(i * FRONT_BLOCK, FRONT_BLOCK), FRONT_BLOCK)
        product = contract(att_ref[:, at], wout_ref[...], 0, 0)
        resid = tok_ref[at, :].astype(F32) + product + bout_ref[...]
        resid_out[...] = resid
        hat, _ = norm_parts(resid)
        mid_out[...] = (hat * gain2_ref[...] + shift2_ref[...]).astype(BF16)

    @pl.when(step == base[4] + blocks - 1)
    def _():
        for one in (fetch_up, fetch_down):
            one.end()
        cot_copy.wait()
        kept_copy.wait()
        for copy in stores:
            copy.wait()


def attend_pair(mask_ref, qkv_ref, att_ref, att_out, log_out, pair, second, heads, block):
    rows = qkv_ref.shape[1]
    half = heads * HEAD_DIM
    first = pair * HEAD_GROUP
    work = []
    for head in range(HEAD_GROUP):
        work += [(head, 0, LEN_L, at, block) for at in range(0, LEN_L, block)]
        work += [(head, start, LEN_S, 0, LEN_S) for start in range(LEN_L, rows, LEN_S)]

    def load(which, head, columns):
        start = pl.multiple_of(which * half + (first + head) * HEAD_DIM, HEAD_DIM)
        return qkv_ref[pl.ds(start, HEAD_DIM), columns]

    def scores(item):
        head, start, count, at, size = item
        every = slice(start, start + count)
        keys = load(1, head, every)
        key_rows = jnp.concatenate([keys, keys, extra_rows([mask_ref[:, every]], count)], 0)
        query = scaled_query(load(0, head, slice(start + at, start + at + size)))
        query_rows = jnp.concatenate([*query, jnp.ones((16, size), BF16)], 0)
        return contract(key_rows, query_rows, 0, 0)

    def finish(item, score):
        head, start, count, at, size = item
        here = slice(start + at, start + at + size)
        values = load(2, head, slice(start, start + count))
        value_rows = jnp.concatenate([values, jnp.ones((16, count), BF16)], 0)
        top = jnp.max(score, axis=0, keepdims=True)
        weights = jnp.exp2(score - top).astype(BF16)
        mixed = contract(value_rows, weights, 1, 0)
        total = mixed[HEAD_DIM : HEAD_DIM + 1]
        result = (mixed[:HEAD_DIM] * (1.0 / total)).astype(BF16)
        att_out[0, head, :, here] = result
        start = pl.multiple_of(second * half + (first + head) * HEAD_DIM, HEAD_DIM)
        att_ref[pl.ds(start, HEAD_DIM), here] = result
        log_out[0, head, :, here] = top + jnp.log2(total)

    score = scores(work[0])
    for place, item in enumerate(work):
        later = scores(work[place + 1]) if place + 1 < len(work) else None
        finish(item, score)
        score = later


def front(
    mask, gain, shift, b_out, gain2, shift2, bias, tokens, w_query, w_key, w_value, w_out, w_up,
    w_down, cotangent, heads, block=1024,
):
    width = tokens.shape[1]
    rows = tokens.shape[0] // 2
    half = heads * HEAD_DIM
    hidden = w_up.shape[1]
    blocks, pairs = rows // FRONT_BLOCK, heads // HEAD_GROUP
    base = [0, blocks, blocks + pairs, 2 * blocks + pairs, 2 * blocks + 2 * pairs]
    anywhere = pl.BlockSpec(memory_space=pl.ANY)

    def row_block(first):
        return lambda s: (jnp.clip(s - first, 0, blocks - 1), 0)

    def qkv_block(s):
        late = (s >= base[2]).astype(jnp.int32)
        return late, 0, jnp.clip(s - late * base[2], 0, blocks - 1)

    def head_block(s):
        late = (s >= base[3]).astype(jnp.int32)
        return late, jnp.clip(s - base[1] - late * (base[3] - base[1]), 0, pairs - 1), 0, 0

    by_row = lambda first: pl.BlockSpec((FRONT_BLOCK, width), row_block(first))
    bias_rows, bias_width = bias.shape
    pair_total = pair_count(2 * heads, rows)
    return pl.pallas_call(
        functools.partial(front_kernel, heads=heads, block=block),
        grid=(base[4] + blocks,),
        in_specs=[
            whole((1, rows)),
            *(whole((1, width)) for _ in range(5)),
            whole(bias.shape),
        ]
        + [anywhere] * 8,
        out_specs=[
            by_row(0),
            pl.BlockSpec((1, 3 * half, FRONT_BLOCK), qkv_block),
            pl.BlockSpec((1, HEAD_GROUP, HEAD_DIM, rows), head_block),
            pl.BlockSpec((1, HEAD_GROUP, 1, rows), head_block),
            by_row(base[4]),
            by_row(base[4]),
        ]
        + [anywhere] * 7,
        out_shape=[
            jax.ShapeDtypeStruct((rows, width), BF16),
            jax.ShapeDtypeStruct((2, 3 * half, rows), BF16),
            jax.ShapeDtypeStruct((2, heads, HEAD_DIM, rows), BF16),
            jax.ShapeDtypeStruct((2, heads, 1, rows), F32),
            jax.ShapeDtypeStruct((rows, width), F32),
            jax.ShapeDtypeStruct((rows, width), BF16),
            jax.ShapeDtypeStruct((2, width, 3 * half), BF16),
            jax.ShapeDtypeStruct((2 * half, width), BF16),
            jax.ShapeDtypeStruct((width, hidden), BF16),
            jax.ShapeDtypeStruct((hidden, width), BF16),
            jax.ShapeDtypeStruct((rows, width), BF16),
            jax.ShapeDtypeStruct((bias_rows, bias_width), F32),
            jax.ShapeDtypeStruct((rows, width), BF16),
        ],
        scratch_shapes=[
            pltpu.VMEM((rows, width), BF16),
            pltpu.VMEM((rows, width), BF16),
            pltpu.VMEM((3 * half, rows), BF16),
            pltpu.VMEM((2 * half, rows), BF16),
            pltpu.VMEM((2, width, 3 * half), BF16),
            pltpu.VMEM((2 * half, width), BF16),
            pltpu.VMEM((bias_rows, bias_width), F32),
            pltpu.SemaphoreType.DMA((6,)),
            pltpu.SemaphoreType.DMA((5,)),
            pltpu.SemaphoreType.DMA((2,)),
            pltpu.SemaphoreType.DMA((2,)),
        ]
        + [ref for _ in range(6) for ref in Fetch.buffers()],
        compiler_params=pltpu.CompilerParams(
            vmem_limit_bytes=VMEM_LIMIT, collective_id=1, has_side_effects=True
        ),
        cost_estimate=cost(
            pair_total * 2 * 512 + 14 * rows * width * half, 40 * rows * width, pair_total
        ),
        name="front",
    )(
        mask, gain, shift, b_out, gain2, shift2, bias, tokens, w_query, w_key, w_value, w_out,
        w_up, w_down, cotangent,
    )


ERFC_TERMS = (0.254829592, -0.284496736, 1.421413741, -1.453152027, 1.061405429)
ERFC_SLOPE = 0.3275911


def gelu_and_slope(value):
    bell = jnp.exp2(value * value * (-0.5 * LOG2E))
    base = 1.0 + jnp.abs(value) * (ERFC_SLOPE * math.sqrt(0.5))
    ratio = 1.0 / base
    poly = ERFC_TERMS[4] * 0.5
    for term in ERFC_TERMS[3::-1]:
        poly = poly * ratio + term * 0.5
    tail = poly * ratio * bell
    below = jnp.where(value < 0.0, tail, 1.0 - tail)
    return value * below, below + value * bell * (1.0 / math.sqrt(2.0 * math.pi))


def feed_kernel(
    mid_ref, grad_ref, up_ref, b_ref, down_ref, sum_ref, gmid_ref, dup_ref, ddown_ref, db_ref,
    act_ref, gpre_ref, *, chunk,
):
    @pl.when(pl.program_id(0) == 0)
    def _():
        sum_ref[...] = jnp.zeros_like(sum_ref)
        gmid_ref[...] = jnp.zeros_like(gmid_ref)

    rows = mid_ref.shape[0]
    up, down, bias = up_ref[...], down_ref[...], b_ref[...]

    def products(at):
        here = slice(at, at + chunk)
        return (
            contract(mid_ref[here], up, 1, 0) + bias,
            contract(grad_ref[here], down, 1, 1),
        )

    now = products(0)
    db = None
    for at in range(0, rows, chunk):
        here = slice(at, at + chunk)
        later = products(at + chunk) if at + chunk < rows else None
        value, slope = gelu_and_slope(now[0])
        act = value.astype(BF16)
        gpre = (slope * now[1]).astype(BF16)
        act_ref[here] = act
        gpre_ref[here] = gpre
        part = jnp.sum(gpre.astype(F32), axis=0, keepdims=True)
        db = part if db is None else db + part
        sum_ref[here] += contract(act, down, 1, 0)
        gmid_ref[here] += contract(gpre, up, 1, 1)
        now = later
    db_ref[...] = db
    ddown_ref[...] = contract(act_ref[...], grad_ref[...], 0, 0).astype(BF16)
    dup_ref[...] = contract(mid_ref[...], gpre_ref[...], 0, 0).astype(BF16)


def feed(mid, grads, w_up, b_up, w_down, block=512, chunk=512):
    rows, width = mid.shape
    hidden = w_up.shape[1]
    return pl.pallas_call(
        functools.partial(feed_kernel, chunk=chunk),
        grid=(hidden // block,),
        in_specs=[
            whole((rows, width)),
            whole((rows, width)),
            pl.BlockSpec((width, block), lambda j: (0, j)),
            pl.BlockSpec((1, block), lambda j: (0, j)),
            pl.BlockSpec((block, width), lambda j: (j, 0)),
        ],
        out_specs=[
            whole((rows, width)),
            whole((rows, width)),
            pl.BlockSpec((width, block), lambda j: (0, j)),
            pl.BlockSpec((block, width), lambda j: (j, 0)),
            pl.BlockSpec((1, block), lambda j: (0, j)),
        ],
        out_shape=[
            jax.ShapeDtypeStruct((rows, width), F32),
            jax.ShapeDtypeStruct((rows, width), F32),
            jax.ShapeDtypeStruct((width, hidden), BF16),
            jax.ShapeDtypeStruct((hidden, width), BF16),
            jax.ShapeDtypeStruct((1, hidden), F32),
        ],
        scratch_shapes=[pltpu.VMEM((rows, block), BF16), pltpu.VMEM((rows, block), BF16)],
        compiler_params=params(),
        cost_estimate=cost(12 * rows * width * hidden, 20 * rows * width, 2 * rows * hidden),
        name="feed",
    )(mid, grads, w_up, b_up, w_down)


def branch_kernel(
    resid_ref, sum1_ref, sum2_ref, gmid1_ref, gmid2_ref, grad_ref, gain_ref, bdown_ref, w_ref,
    att_ref, out_ref, gresid_ref, gatt_ref, dw_own_ref, dw_other_ref, small_ref, acc_ref,
):
    @pl.when(pl.program_id(0) == 0)
    def _():
        acc_ref[...] = jnp.zeros_like(acc_ref)
        small_ref[...] = jnp.zeros_like(small_ref)

    resid = resid_ref[...]
    grads = grad_ref[...].astype(F32)
    out_ref[...] = (resid + sum1_ref[...] + sum2_ref[...] + bdown_ref[...]).astype(BF16)
    gmid = gmid1_ref[...] + gmid2_ref[...]
    hat, inv = norm_parts(resid)
    gresid = grads + norm_back(hat, inv, gmid * gain_ref[...])
    gresid_ref[...] = gresid
    branch = gresid.astype(BF16)
    gatt_ref[...] = contract(w_ref[...], branch, 1, 1).astype(BF16)
    acc_ref[...] += contract(branch, att_ref[...], 0, 1)
    small_ref[0:1] += jnp.sum(gmid * hat, axis=0, keepdims=True)
    small_ref[1:2] += jnp.sum(gmid, axis=0, keepdims=True)
    small_ref[2:3] += jnp.sum(gresid, axis=0, keepdims=True)
    small_ref[3:4] += jnp.sum(grads, axis=0, keepdims=True)

    @pl.when(pl.program_id(0) == pl.num_programs(0) - 1)
    def _():
        half = dw_own_ref.shape[1]
        dw_own_ref[...] = acc_ref[:, :half].astype(BF16)
        dw_other_ref[...] = acc_ref[:, half:].astype(BF16)


def branch(resid, sums, gmids, grads, gain, b_down, w_out, attended, block):
    rows, width = resid.shape
    heads_width = attended.shape[0]
    by_row = pl.BlockSpec((block, width), lambda i: (i, 0))
    columns = pl.BlockSpec((heads_width, block), lambda i: (0, i))
    half = (width, heads_width // 2)
    return pl.pallas_call(
        branch_kernel,
        grid=(rows // block,),
        in_specs=[by_row] * 6
        + [whole((1, width)), whole((1, width)), whole((heads_width, width)), columns],
        out_specs=[by_row, by_row, columns, whole(half), whole(half), whole((8, width))],
        out_shape=[
            jax.ShapeDtypeStruct((rows, width), BF16),
            jax.ShapeDtypeStruct((rows, width), F32),
            jax.ShapeDtypeStruct((heads_width, rows), BF16),
            jax.ShapeDtypeStruct(half, BF16),
            jax.ShapeDtypeStruct(half, BF16),
            jax.ShapeDtypeStruct((8, width), F32),
        ],
        scratch_shapes=[pltpu.VMEM((width, heads_width), F32)],
        compiler_params=params(),
        cost_estimate=cost(4 * rows * width * heads_width, 32 * rows * width),
        name="branch",
    )(resid, *sums, *gmids, grads, gain, b_down, w_out, attended)


TAIL_BLOCK = 512
SUM_ACTIONS = ("begin", "along_x", "along_z", "back_along_z", "back_along_x", "back_to_core")
SUM_STEPS = (
    (0, 1, 3, 7, 9, 11),
    (0, 3, 5, 11, 13, 15),
    (0, 5, 9, 15, 17, 19),
    (0, 7, 13, 17, 20, 99),
    (0, 4, 6, 8, 10, 13),
    (17, 18, 20, 99, 99, 99),
)
LAST = 99


def tail_kernel(
    mask_ref, qkv_ref, att_ref, log_ref, gatt_ref, gain_ref, small2_ref, dbup1_ref, dbup2_ref,
    wout2_ref, x_hbm, w_hbm, tok_hbm, gresid_hbm, up_hbm, down_hbm, wout_hbm, seen_up,
    seen_down, out_hbm,
    gtok_ref, small_ref, got_hbm, gup_hbm, gdown_hbm, gout_hbm, gcat_hbm, got_out,
    d_ref, x_ref, w_ref, tok_ref, gresid_ref, dw_ref, dw2_ref, sent_ref, own_small, other_small,
    load_sem, row_sem, tok_send, tok_recv, *scratch, heads, block,
):
    step = pl.program_id(0)
    place = Place()
    first_rows = 2 * heads + 1
    width = x_ref.shape[1]
    half = heads * HEAD_DIM
    halves = width

    groups = []
    at = 0
    for count in [8] * 6 + [3, 3, 4]:
        groups.append(scratch[at : at + count])
        at += count
    columns = lambda ref, i: ref.at[:, pl.ds(i * halves, halves)]
    rows_of = lambda ref, i, count: ref.at[pl.ds(i * count, count)]
    sums = [
        PlaneSum(place, columns(up_hbm, i), columns(seen_up, i), columns(gup_hbm, i), groups[i])
        for i in (0, 1)
    ]
    down_rows = down_hbm.shape[0] // 2
    sums += [
        PlaneSum(
            place,
            rows_of(down_hbm, i, down_rows),
            rows_of(seen_down, i, down_rows // 2),
            rows_of(gdown_hbm, i, down_rows),
            groups[2 + i],
        )
        for i in (0, 1)
    ]
    sums.append(PlaneSum(place, wout_hbm, None, gout_hbm, groups[4]))
    sums.append(PlaneSum(place, dw_ref, None, gcat_hbm, groups[5]))
    cat_term = PartnerTerm(place, dw2_ref, groups[5][1], groups[6])
    out_term = PartnerTerm(place, wout2_ref, groups[4][1], groups[7])
    small = SmallSum(place, own_small, other_small, groups[8])
    theirs = pl.ds(pl.multiple_of((1 - place.rank) * LEN_L, LEN_L), LEN_L)
    out_copy = send_to(
        out_hbm.at[theirs], got_out, tok_send.at[2], tok_recv.at[2], place.partner()
    )

    loads = [
        pltpu.make_async_copy(x_hbm, x_ref, load_sem.at[0]),
        pltpu.make_async_copy(w_hbm, w_ref, load_sem.at[1]),
    ]

    def row_start(i):
        mine = i // 2
        return ((1 - mine) * (1 - place.rank) + mine * place.rank) * LEN_L + (i % 2) * TAIL_BLOCK

    def row_loads(i):
        start = pl.ds(pl.multiple_of(row_start(i), TAIL_BLOCK), TAIL_BLOCK)
        slot = i % 2
        return [
            pltpu.make_async_copy(tok_hbm.at[start], tok_ref.at[slot], row_sem.at[slot, 0]),
            pltpu.make_async_copy(gresid_hbm.at[start], gresid_ref.at[slot], row_sem.at[slot, 1]),
        ]

    def token_copy(i):
        there = pl.ds(i * TAIL_BLOCK, TAIL_BLOCK)
        return send_to(
            sent_ref.at[there], got_hbm.at[there], tok_send.at[i], tok_recv.at[i], place.partner()
        )

    def weight_gradient(source, target):
        for i in range(3):
            here = pl.ds(i * half, half)
            product = contract(x_ref[...], d_ref[source, here, :], 0, 1)
            target[:, here] = product.astype(BF16)

    def bias_rows(source, target):
        ones = jnp.ones((16, d_ref.shape[2]), BF16)
        for i, which in ((0, 0), (1, 2)):
            row = contract(ones, d_ref[source, pl.ds(which * half, half), :], 1, 1)
            target[8:9, pl.ds(i * half, half)] = row[:1]

    last_step = first_rows + 3
    events = {}
    for one, times in zip(sums, SUM_STEPS):
        for when, action in zip(times, SUM_ACTIONS):
            events.setdefault(when, []).append(getattr(one, action))
    late = events.pop(LAST, [])

    for when in sorted(events):

        @pl.when(step == when)
        def _(when=when):
            if when == 0:
                place.greet()
                out_term.begin()
            if when == 1:
                out_term.to_partner()
                out_copy.start()
            if when == 4:
                out_term.end()
            for action in events[when]:
                action()

    @pl.when(step == 2)
    def _():
        for copy in loads:
            copy.start()

    @pl.when(step == heads)
    def _():
        for copy in loads:
            copy.wait()
        weight_gradient(1, dw2_ref)
        cat_term.begin()

    @pl.when(step == heads + 1)
    def _():
        cat_term.to_partner()
        own_small[...] = jnp.zeros_like(own_small)
        other_small[...] = jnp.zeros_like(other_small)
        bias_rows(1, other_small)

    @pl.when(step < 2 * heads)
    def _():
        back_one_head(mask_ref, qkv_ref, att_ref, log_ref, gatt_ref, d_ref, step, heads, block)

    @pl.when(step == 2 * heads)
    def _():
        for copy in row_loads(0):
            copy.start()
        cat_term.end()
        weight_gradient(0, dw_ref)
        bias_rows(0, own_small)

    for i in range(4):

        @pl.when(step == first_rows + i)
        def _(i=i):
            for copy in row_loads(i):
                copy.wait()
            if i < 3:
                for copy in row_loads(i + 1):
                    copy.start()
            here = pl.ds(pl.multiple_of(row_start(i), TAIL_BLOCK), TAIL_BLOCK)
            gin = contract(d_ref[0, :, here], w_ref[0], 0, 1)
            gin += contract(d_ref[1, :, here], w_ref[1], 0, 1)
            hat, inv = norm_parts(tok_ref[i % 2].astype(F32))
            gtok = gresid_ref[i % 2] + norm_back(hat, inv, gin * gain_ref[...])
            own_small[0:1] += jnp.sum(gin * hat, axis=0, keepdims=True)
            own_small[1:2] += jnp.sum(gin, axis=0, keepdims=True)
            if i < 2:
                sent_ref[pl.ds(i * TAIL_BLOCK, TAIL_BLOCK), :] = gtok.astype(BF16)
                token_copy(i).start()
            else:
                gtok_ref[...] = gtok

    @pl.when(step == last_step)
    def _():
        own_small[2:6] = small2_ref[0:4]
        other_small[0:2] = own_small[0:2]
        other_small[2:6] = small2_ref[0:4]
        for i in (0, 1):
            own_small[6 + i : 7 + i] = dbup1_ref[:, pl.ds(i * width, width)]
            other_small[6 + i : 7 + i] = dbup2_ref[:, pl.ds(i * width, width)]
        small.begin()
        late_steps = iter(late)
        small.over_cores()
        small.over_x()
        small.over_z()
        for action in late_steps:
            action()
        small_ref[...] = small.end()
        out_copy.wait()
        for i in (0, 1):
            token_copy(i).wait()
        for one in sums:
            one.end()


def back_one_head(mask_ref, qkv_ref, att_ref, log_ref, gatt_ref, d_ref, step, heads, block):
    rows = qkv_ref.shape[4]
    half = heads * HEAD_DIM
    source = 1 - step // heads
    head_at = pl.multiple_of((step % heads) * HEAD_DIM, HEAD_DIM)

    def store(which, columns, value):
        d_ref[source, pl.ds(which * half + head_at, HEAD_DIM), columns] = value.astype(BF16)

    images = [(0, LEN_L, block)] + [(at, LEN_S, LEN_S) for at in range(LEN_L, rows, LEN_S)]
    for start, count, size in images:
        every = slice(start, start + count)
        keys = qkv_ref[0, 1, 0, :, every]
        values = qkv_ref[0, 2, 0, :, every]
        ones = jnp.ones((1, count), F32)
        key_rows = jnp.concatenate(
            [keys, keys, extra_rows([ones, ones, ones, mask_ref[:, every]], count)], 0
        )
        value_rows = jnp.concatenate([values, extra_rows([ones, ones, ones], count)], 0)
        grad_values = grad_keys = None
        for at in range(start, start + count, size):
            here = slice(at, at + size)
            query = qkv_ref[0, 0, 0, :, here]
            grads = gatt_ref[0, 0, :, here]
            inner = jnp.sum(
                grads.astype(F32) * att_ref[0, 0, :, here].astype(F32), axis=0, keepdims=True
            )
            terms = three_terms(-log_ref[0, 0, :, here]) + [jnp.ones((1, size), F32)]
            query_rows = jnp.concatenate([*scaled_query(query), extra_rows(terms, size)], 0)
            grad_rows = jnp.concatenate([grads, extra_rows(three_terms(-inner), size)], 0)
            score = contract(query_rows, key_rows, 0, 0)
            grad_probs = contract(grad_rows, value_rows, 0, 0)
            probs = jnp.exp2(score)
            grad_score = (probs * grad_probs).astype(BF16)
            part_values = contract(grads, probs.astype(BF16), 1, 0)
            part_keys = contract(query, grad_score, 1, 0)
            grad_values = part_values if grad_values is None else grad_values + part_values
            grad_keys = part_keys if grad_keys is None else grad_keys + part_keys
            store(0, here, contract(keys, grad_score, 1, 1) * SCALE)
        store(1, every, grad_keys * SCALE)
        store(2, every, grad_values)


def tail(
    mask, qkv, att, log_total, gatt, gain, small2, dbup1, dbup2, dwout2, normed, w_cat,
    tokens, gresid, dup, ddown, dwout, seen_up, seen_down, out_rows, block=256,
):
    _, _, heads, _, rows = qkv.shape
    _, width, out = w_cat.shape
    anywhere = pl.BlockSpec(memory_space=pl.ANY)
    last = 2 * heads - 1

    def head(h):
        h = jnp.minimum(h, last)
        return 1 - h // heads, h % heads

    all_three = pl.BlockSpec(
        (1, 3, 1, HEAD_DIM, rows), lambda h: (head(h)[0], 0, head(h)[1], 0, 0)
    )
    one = pl.BlockSpec((1, 1, HEAD_DIM, rows), lambda h: (*head(h), 0, 0))
    row = pl.BlockSpec((1, 1, 1, rows), lambda h: (*head(h), 0, 0))
    sum_shapes = [(width, width)] * 4 + [dwout.shape, (width, out)]
    scratch = [
        pltpu.VMEM((2, out, rows), BF16),
        pltpu.VMEM((rows, width), BF16),
        pltpu.VMEM((2, width, out), BF16),
        pltpu.VMEM((2, TAIL_BLOCK, width), BF16),
        pltpu.VMEM((2, TAIL_BLOCK, width), F32),
        pltpu.VMEM((width, out), BF16),
        pltpu.VMEM((width, out), BF16),
        pltpu.VMEM((rows // 2, width), BF16),
        pltpu.VMEM((SmallSum.ROWS, width), F32),
        pltpu.VMEM((SmallSum.ROWS, width), F32),
        pltpu.SemaphoreType.DMA((2,)),
        pltpu.SemaphoreType.DMA((2, 2)),
        pltpu.SemaphoreType.DMA((3,)),
        pltpu.SemaphoreType.DMA((3,)),
    ]
    for shape in sum_shapes:
        scratch += PlaneSum.buffers(*shape)
    scratch += PartnerTerm.buffers(width, out) + PartnerTerm.buffers(*dwout.shape)
    scratch += SmallSum.buffers(width)
    pairs = pair_count(2 * heads, rows)
    first_rows = 2 * heads + 1
    return pl.pallas_call(
        functools.partial(tail_kernel, heads=heads, block=block),
        grid=(first_rows + 4,),
        in_specs=[
            whole((1, rows)), all_three, one, row, one, whole((1, width)), whole((8, width)),
            whole((1, 2 * width)), whole((1, 2 * width)), whole(dwout.shape),
        ]
        + [anywhere] * 10,
        out_specs=[
            pl.BlockSpec(
                (TAIL_BLOCK, width), lambda h: (jnp.maximum(h - first_rows - 2, 0), 0)
            ),
            whole((SmallSum.ROWS, width)),
        ]
        + [anywhere] * 6,
        out_shape=[
            jax.ShapeDtypeStruct((rows // 2, width), F32),
            jax.ShapeDtypeStruct((SmallSum.ROWS, width), F32),
            jax.ShapeDtypeStruct((rows // 2, width), BF16),
            jax.ShapeDtypeStruct(dup.shape, BF16),
            jax.ShapeDtypeStruct(ddown.shape, BF16),
            jax.ShapeDtypeStruct(dwout.shape, BF16),
            jax.ShapeDtypeStruct((width, out), BF16),
            jax.ShapeDtypeStruct((rows // 2, width), BF16),
        ],
        scratch_shapes=scratch,
        compiler_params=pltpu.CompilerParams(
            vmem_limit_bytes=VMEM_LIMIT, collective_id=0, has_side_effects=True
        ),
        cost_estimate=cost(pairs * 5 * 512, 32 * heads * HEAD_DIM * rows, pairs),
        name="tail",
    )(
        mask, qkv, att, log_total, gatt, gain, small2, dbup1, dbup2, dwout2, normed, w_cat,
        tokens, gresid, dup, ddown, dwout, seen_up, seen_down, out_rows,
    )


def swap_tp(array):
    return lax.ppermute(array, "tp", [(0, 1), (1, 0)])


def swap_dp(array, bit):
    count = lax.axis_size("dp")
    return lax.ppermute(array, "dp", [(i, i ^ bit) for i in range(count)])


def dp_bit(bit):
    return (lax.axis_index("dp") & bit) != 0


def joined(mine, theirs, second):
    return jnp.where(second, jnp.concatenate([theirs, mine], 0), jnp.concatenate([mine, theirs], 0))


def half_of(array, second):
    size = array.shape[0] // 2
    return lax.dynamic_slice_in_dim(array, jnp.where(second, size, 0), size, 0)


def add_low(left, right):
    return (left.astype(F32) + right.astype(F32)).astype(BF16)


def over_cores(other, chunks=1):
    second = dp_bit(1)
    split = other.reshape(chunks, other.shape[0] // chunks, other.shape[1])
    half = split.shape[1] // 2
    take = lambda which: lax.dynamic_slice_in_dim(split, jnp.where(which, half, 0), half, 1)
    both = add_low(take(second), swap_dp(take(~second), 1))
    return both.reshape(-1, other.shape[1])


def by_images(
    tokens, long_lengths, short_lengths, ln1_gain, ln1_bias, w_query, b_query, w_key, w_value,
    b_value, w_out, b_out, ln2_gain, ln2_bias, w_up, b_up, w_down, b_down, cotangent,
):
    rank = lax.axis_index("tp")
    rank_arr = jnp.reshape(rank, (1,)).astype(jnp.int32)
    second = rank == 1
    rows = tokens.shape[0] // 2
    width = tokens.shape[1]
    half = w_query.shape[1]
    heads = half // HEAD_DIM
    long_len = lax.dynamic_slice_in_dim(long_lengths, rank, 1, 0)
    shorts = short_lengths.shape[0] // 2
    short_len = lax.dynamic_slice_in_dim(short_lengths, rank * shorts, shorts, 0)
    valid = jnp.concatenate(
        [
            jnp.arange(LEN_L) < long_len[0],
            (jnp.arange(LEN_S)[None, :] < short_len[:, None]).reshape(-1),
        ]
    )
    mask = jnp.where(valid, 0.0, -1e30).astype(F32).reshape(1, -1)
    row = lambda vector: vector.astype(F32).reshape(1, -1)
    biases = jnp.concatenate([b_query, jnp.zeros_like(b_query), b_value, b_up]).astype(F32)
    bias = jnp.broadcast_to(biases.reshape(1, -1), (8, biases.shape[0]))

    (normed, qkv, att, log_total, resid, mid, w_cat, w_out_all, w_up2, w_down2, grads, bias2,
     own_tokens) = front(
        mask, row(ln1_gain), row(ln1_bias), row(b_out), row(ln2_gain), row(ln2_bias), bias,
        tokens, w_query, w_key, w_value, w_out, w_up, w_down, cotangent, heads,
    )
    qkv = qkv.reshape(2, 3, heads, HEAD_DIM, rows)
    attended = att.reshape(2 * half, rows)
    up_bias = bias[:1, 3 * half :], bias2[:1, 3 * half :]
    sum2, gmid2, dup2, ddown2, dbup2 = feed(mid, grads, w_up2, up_bias[1], w_down2)
    mid, both_up, both_down = lax.optimization_barrier((mid, over_cores(dup2), over_cores(ddown2, 2)))
    seen_up, seen_down = swap_tp(both_up), swap_tp(both_down)
    sum1, gmid1, dup1, ddown1, dbup1 = feed(mid, grads, w_up, up_bias[0], w_down)
    out, gresid, gatt, dwout1, dwout2, small2 = branch(
        resid, (sum1, sum2), (gmid1, gmid2), grads, row(ln2_gain), row(b_down), w_out_all,
        attended, 512,
    )
    gtok, small, got_tok, grad_up, grad_down, grad_out_t, grad_cat, got_out = tail(
        mask, qkv, att, log_total, gatt.reshape(2, heads, HEAD_DIM, rows), row(ln1_gain), small2,
        dbup1, dbup2, dwout2, normed, w_cat, own_tokens, gresid, dup1, ddown1, dwout1,
        seen_up, seen_down, out,
    )
    result = joined(half_of(out, second), got_out, second)
    grad_tokens = joined(gtok, got_tok.astype(F32), second)
    grad_cat = grad_cat.astype(F32)
    return (
        result,
        grad_tokens,
        small[0],
        small[1],
        grad_cat[:, :half],
        small[8, :half],
        grad_cat[:, half : 2 * half],
        grad_cat[:, 2 * half :],
        small[8, half:],
        grad_out_t.T.astype(F32),
        small[4],
        small[2],
        small[3],
        grad_up.astype(F32),
        small[6:8].reshape(-1),
        grad_down.astype(F32),
        small[5],
    )


def layer_norm(values, gain, shift):
    center = values - jnp.mean(values, axis=-1, keepdims=True)
    spread = jnp.mean(center * center, axis=-1, keepdims=True)
    return center * lax.rsqrt(spread + 1e-06) * gain + shift


def dot_plain(left, right):
    return jnp.dot(left, right, preferred_element_type=jnp.float32)


def dot_rows(left, right):
    return lax.dot_general(
        left, right, (((0,), (0,)), ((), ())), preferred_element_type=jnp.float32
    )


def dot_back(left, right):
    return lax.dot_general(
        left, right, (((1,), (1,)), ((), ())), preferred_element_type=jnp.float32
    )


def group_shape(image_count, seq_len, head_count):
    per_step = math.gcd(image_count, max(1, 512 // seq_len))
    return (image_count // per_step, per_step, seq_len, head_count, HEAD_DIM)


def masked_scores(query_blk, key_blk, length_blk):
    seq_len = query_blk.shape[1]
    raw = jnp.einsum(
        "bqhd,bkhd->bhqk", query_blk, key_blk, preferred_element_type=jnp.float32
    ) * HEAD_DIM ** (-0.5)
    keep = jnp.arange(seq_len, dtype=jnp.int32)[None, :] < length_blk[:, None]
    return jnp.where(keep[:, None, None, :], raw, -1e30)


def attention_forward(queries, key_rows, value_rows, lengths, seq_len):
    image_count = lengths.shape[0]
    head_count = queries.shape[1] // HEAD_DIM
    block_shape = group_shape(image_count, seq_len, head_count)

    def one_step(block):
        query_blk, key_blk, value_blk, length_blk = block
        scores = masked_scores(query_blk, key_blk, length_blk)
        row_top = jnp.max(scores, axis=-1, keepdims=True)
        exp_terms = jnp.exp(scores - row_top)
        row_total = jnp.sum(exp_terms, axis=-1, keepdims=True)
        weights = (exp_terms / row_total).astype(jnp.bfloat16)
        mixed = jnp.einsum(
            "bhqk,bkhd->bqhd", weights, value_blk, preferred_element_type=jnp.float32
        )
        return (mixed, (row_top + jnp.log(row_total))[..., 0])

    mixed, log_total = lax.map(
        one_step,
        (
            queries.reshape(block_shape),
            key_rows.reshape(block_shape),
            value_rows.reshape(block_shape),
            lengths.reshape(block_shape[:2]),
        ),
    )
    return (mixed.reshape(image_count * seq_len, head_count * HEAD_DIM), log_total)


def attention_backward(queries, key_rows, value_rows, grads, lengths, log_total, seq_len):
    image_count = lengths.shape[0]
    head_count = queries.shape[1] // HEAD_DIM
    block_shape = group_shape(image_count, seq_len, head_count)
    scale = HEAD_DIM ** (-0.5)

    def one_step(block):
        query_blk, key_blk, value_blk, grad_blk, length_blk, total_blk = block
        scores = masked_scores(query_blk, key_blk, length_blk)
        probs = jnp.exp(scores - total_blk[..., None])
        grad_values = jnp.einsum(
            "bhqk,bqhd->bkhd",
            probs.astype(jnp.bfloat16),
            grad_blk,
            preferred_element_type=jnp.float32,
        )
        grad_probs = jnp.einsum(
            "bqhd,bkhd->bhqk", grad_blk, value_blk, preferred_element_type=jnp.float32
        )
        inner = jnp.sum(probs * grad_probs, axis=-1, keepdims=True)
        grad_scores = (probs * (grad_probs - inner)).astype(jnp.bfloat16)
        grad_queries = (
            jnp.einsum("bhqk,bkhd->bqhd", grad_scores, key_blk, preferred_element_type=jnp.float32)
            * scale
        )
        grad_keys = (
            jnp.einsum(
                "bhqk,bqhd->bkhd", grad_scores, query_blk, preferred_element_type=jnp.float32
            )
            * scale
        )
        return (grad_queries, grad_keys, grad_values)

    results = lax.map(
        one_step,
        (
            queries.reshape(block_shape),
            key_rows.reshape(block_shape),
            value_rows.reshape(block_shape),
            grads.reshape(block_shape),
            lengths.reshape(block_shape[:2]),
            log_total,
        ),
    )
    flat = (image_count * seq_len, head_count * HEAD_DIM)
    return tuple((item.reshape(flat) for item in results))


def local(
    tokens,
    long_lengths,
    short_lengths,
    ln1_gain,
    ln1_bias,
    w_query,
    b_query,
    w_key,
    w_value,
    b_value,
    w_out,
    b_out,
    ln2_gain,
    ln2_bias,
    w_up,
    b_up,
    w_down,
    b_down,
    cotangent,
):
    tp_count = lax.axis_size("tp")
    tp_rank = lax.axis_index("tp")
    row_count = tokens.shape[0]
    share = row_count // tp_count
    split = long_lengths.shape[0] * LEN_L
    gain_one = ln1_gain.astype(jnp.float32)
    shift_one = ln1_bias.astype(jnp.float32)
    gain_two = ln2_gain.astype(jnp.float32)
    shift_two = ln2_bias.astype(jnp.float32)
    normed_in = layer_norm(tokens.astype(jnp.float32), gain_one, shift_one).astype(jnp.bfloat16)
    queries = (dot_plain(normed_in, w_query) + b_query.astype(jnp.float32)).astype(jnp.bfloat16)
    key_rows = dot_plain(normed_in, w_key).astype(jnp.bfloat16)
    value_rows = (dot_plain(normed_in, w_value) + b_value.astype(jnp.float32)).astype(jnp.bfloat16)
    long_mixed, long_total = attention_forward(
        queries[:split], key_rows[:split], value_rows[:split], long_lengths, LEN_L
    )
    short_mixed, short_total = attention_forward(
        queries[split:], key_rows[split:], value_rows[split:], short_lengths, LEN_S
    )
    attended = jnp.concatenate([long_mixed, short_mixed], axis=0).astype(jnp.bfloat16)
    attn_sum = lax.psum_scatter(dot_plain(attended, w_out), "tp", scatter_dimension=0, tiled=True)
    own_tokens = lax.dynamic_slice_in_dim(tokens, tp_rank * share, share, 0).astype(jnp.float32)
    resid = own_tokens + attn_sum + b_out.astype(jnp.float32)
    normed_mid = layer_norm(resid, gain_two, shift_two).astype(jnp.bfloat16)
    grad_out = cotangent.astype(jnp.float32)
    mid_rows = lax.all_gather(normed_mid, "tp", axis=0, tiled=True)
    pre_up = dot_plain(mid_rows, w_up) + b_up.astype(jnp.float32)
    activ = jax.nn.gelu(pre_up, approximate=False).astype(jnp.bfloat16)
    ffn_sum = lax.psum_scatter(
        dot_plain(activ, w_down).astype(jnp.bfloat16), "tp", scatter_dimension=0, tiled=True
    ).astype(jnp.float32)
    result = resid + ffn_sum + b_down.astype(jnp.float32)
    grad_rows = lax.all_gather(cotangent, "tp", axis=0, tiled=True)
    grad_w_down = dot_rows(activ, grad_rows)
    grad_activ = dot_back(grad_rows, w_down)
    _, gelu_back = jax.vjp(lambda inner: jax.nn.gelu(inner, approximate=False), pre_up)
    grad_pre = gelu_back(grad_activ)[0].astype(jnp.bfloat16)
    grad_w_up = dot_rows(mid_rows, grad_pre)
    grad_b_up = jnp.sum(grad_pre.astype(jnp.float32), axis=0)
    grad_mid = lax.psum_scatter(dot_back(grad_pre, w_up), "tp", scatter_dimension=0, tiled=True)
    _, norm_two_back = jax.vjp(layer_norm, resid, gain_two, shift_two)
    grad_resid_norm, grad_gain_two, grad_shift_two = norm_two_back(grad_mid)
    grad_resid = grad_out + grad_resid_norm
    grad_b_down = jnp.sum(grad_out, axis=0)
    grad_b_out = jnp.sum(grad_resid, axis=0)
    grad_branch = lax.all_gather(grad_resid.astype(jnp.bfloat16), "tp", axis=0, tiled=True)
    grad_w_out = dot_rows(attended, grad_branch)
    grad_attended = dot_back(grad_branch, w_out).astype(jnp.bfloat16)
    long_grads = attention_backward(
        queries[:split],
        key_rows[:split],
        value_rows[:split],
        grad_attended[:split],
        long_lengths,
        long_total,
        LEN_L,
    )
    short_grads = attention_backward(
        queries[split:],
        key_rows[split:],
        value_rows[split:],
        grad_attended[split:],
        short_lengths,
        short_total,
        LEN_S,
    )
    grad_queries = jnp.concatenate([long_grads[0], short_grads[0]], axis=0).astype(jnp.bfloat16)
    grad_keys = jnp.concatenate([long_grads[1], short_grads[1]], axis=0).astype(jnp.bfloat16)
    grad_values = jnp.concatenate([long_grads[2], short_grads[2]], axis=0).astype(jnp.bfloat16)
    grad_w_query = dot_rows(normed_in, grad_queries)
    grad_b_query = jnp.sum(grad_queries.astype(jnp.float32), axis=0)
    grad_w_key = dot_rows(normed_in, grad_keys)
    grad_w_value = dot_rows(normed_in, grad_values)
    grad_b_value = jnp.sum(grad_values.astype(jnp.float32), axis=0)
    grad_in = lax.psum_scatter(
        dot_back(grad_queries, w_query)
        + dot_back(grad_keys, w_key)
        + dot_back(grad_values, w_value),
        "tp",
        scatter_dimension=0,
        tiled=True,
    )
    _, norm_one_back = jax.vjp(layer_norm, own_tokens, gain_one, shift_one)
    grad_tokens_norm, grad_gain_one, grad_shift_one = norm_one_back(grad_in)
    grad_tokens = grad_resid + grad_tokens_norm
    summed = lax.psum(
        (
            grad_w_query,
            grad_b_query,
            grad_w_key,
            grad_w_value,
            grad_b_value,
            grad_w_out,
            grad_w_up,
            grad_b_up,
            grad_w_down,
        ),
        "dp",
    )
    shared = lax.psum(
        (grad_gain_one, grad_shift_one, grad_b_out, grad_gain_two, grad_shift_two, grad_b_down),
        ("dp", "tp"),
    )
    return (
        result.astype(jnp.bfloat16),
        grad_tokens,
        shared[0],
        shared[1],
        summed[0],
        summed[1],
        summed[2],
        summed[3],
        summed[4],
        summed[5],
        shared[2],
        shared[3],
        shared[4],
        summed[6],
        summed[7],
        summed[8],
        shared[5],
    )


def pick(*arrays):
    tokens, long_lengths, short_lengths, w_query, w_up = (arrays[i] for i in (0, 1, 2, 5, 14))
    fits = (
        lax.axis_size("tp") == 2
        and lax.axis_size("dp") == 16
        and long_lengths.shape[0] == 2
        and short_lengths.shape[0] == 8
        and tokens.shape == (2 * LEN_L + 8 * LEN_S, 768)
        and w_query.shape[1] == 8 * HEAD_DIM
        and w_up.shape[1] == 1536
    )
    return by_images(*arrays) if fits else local(*arrays)


def solution(mesh):
    placed = (
        P("dp", None),
        P("dp"),
        P("dp"),
        P(),
        P(),
        P(None, "tp"),
        P("tp"),
        P(None, "tp"),
        P(None, "tp"),
        P("tp"),
        P("tp", None),
        P(),
        P(),
        P(),
        P(None, "tp"),
        P("tp"),
        P("tp", None),
        P(),
        P(("dp", "tp"), None),
    )
    return jax.shard_map(
        pick,
        mesh=mesh,
        in_specs=placed,
        out_specs=(
            P(("dp", "tp"), None),
            P(("dp", "tp"), None),
            P(),
            P(),
            P(None, "tp"),
            P("tp"),
            P(None, "tp"),
            P(None, "tp"),
            P("tp"),
            P("tp", None),
            P(),
            P(),
            P(),
            P(None, "tp"),
            P("tp"),
            P("tp", None),
            P(),
        ),
        check_vma=False,
    )
```

```python
import functools
import math

import jax
import jax.numpy as jnp
from jax import lax
from jax.experimental import pallas as pl
from jax.experimental.pallas import tpu as pltpu
from jax.sharding import PartitionSpec as P

HEAD_DIM = 48
LEN_L = 1024
LEN_S = 256
F32 = jnp.float32
BF16 = jnp.bfloat16
LOG2E = math.log2(math.e)
SCALE = HEAD_DIM ** (-0.5)
VMEM_LIMIT = 58 << 20
HEAD_GROUP = 2


def contract(left, right, left_dim, right_dim):
    return lax.dot_general(
        left, right, (((left_dim,), (right_dim,)), ((), ())), preferred_element_type=F32
    )


def params():
    return pltpu.CompilerParams(vmem_limit_bytes=VMEM_LIMIT)


def cost(flops, bytes_accessed, transcendentals=0):
    return pl.CostEstimate(
        flops=int(flops), bytes_accessed=int(bytes_accessed), transcendentals=int(transcendentals)
    )


def whole(shape):
    zeros = (0,) * len(shape)
    return pl.BlockSpec(shape, lambda *_: zeros)


def norm_parts(values):
    center = values - jnp.mean(values, axis=-1, keepdims=True)
    inv = lax.rsqrt(jnp.mean(center * center, axis=-1, keepdims=True) + 1e-06)
    return center * inv, inv


def norm_back(hat, inv, grad_hat):
    mean_grad = jnp.mean(grad_hat, axis=-1, keepdims=True)
    mean_both = jnp.mean(grad_hat * hat, axis=-1, keepdims=True)
    return inv * (grad_hat - mean_grad - hat * mean_both)


def three_terms(value):
    high = value.astype(BF16).astype(F32)
    rest = value - high
    mid = rest.astype(BF16).astype(F32)
    return [high, mid, rest - mid]


def extra_rows(rows, count):
    at = lax.broadcasted_iota(jnp.int32, (16, count), 0)
    out = jnp.zeros((16, count), F32)
    for place, row in enumerate(rows):
        out = jnp.where(at == place, row, out)
    return out.astype(BF16)


def scaled_query(query):
    wide = query.astype(F32) * (SCALE * LOG2E)
    high = wide.astype(BF16)
    return [high, (wide - high.astype(F32)).astype(BF16)]


def pair_count(heads, rows):
    return heads * (LEN_L**2 + (rows - LEN_L) * LEN_S)


class Place:
    def __init__(self):
        me = lax.axis_index("dp")
        self.core, self.x, self.z = me % 2, (me // 2) % 2, me // 4
        self.rank = lax.axis_index("tp")

    def at(self, z=None, x=None, core=None):
        z = self.z if z is None else z
        x = self.x if x is None else x
        core = self.core if core is None else core
        return {"dp": (z * 2 + x) * 2 + core}

    def across_core(self):
        return self.at(core=1 - self.core)

    def across_x(self):
        return self.at(x=1 - self.x)

    def along_z(self, step):
        return self.at(z=(self.z + step) % 4)

    def partner(self):
        return {"tp": 1 - self.rank}

    def greet(self):
        barrier = pltpu.get_barrier_semaphore()
        others = [self.across_core(), self.across_x(), self.partner()]
        others += [self.along_z(step) for step in (1, 2, 3)]
        for other in others:
            pl.semaphore_signal(
                barrier, inc=1, device_id=other, device_id_type=pl.DeviceIdType.MESH
            )
        pl.semaphore_wait(barrier, len(others))


def send_to(source, target, send, recv, device):
    return pltpu.make_async_remote_copy(
        src_ref=source,
        dst_ref=target,
        send_sem=send,
        recv_sem=recv,
        device_id=device,
        device_id_type=pl.DeviceIdType.MESH,
    )


def part(ref, start, count):
    return ref.at[pl.ds(pl.multiple_of(start, 16), count)]


def add_rows(target, start, count, terms):
    tile = 48

    def body(i, _):
        at = pl.multiple_of(i * tile, 16)
        here = pl.ds(pl.multiple_of(start + at, 16), tile)
        total = target[here, :].astype(F32)
        for term in terms:
            total = total + term[pl.ds(at, tile), :].astype(F32)
        target[here, :] = total.astype(BF16)
        return 0

    lax.fori_loop(0, count // tile, body, 0)


class PlaneSum:
    def __init__(self, place, own, seen, out, refs):
        self.place, self.own, self.seen, self.out = place, own, seen, out
        (self.acc, self.seen_here, self.from_core, self.from_x, self.from_z, self.whole,
         self.send, self.recv, self.local) = refs
        self.rows = own.shape[0]

    @staticmethod
    def buffers(rows, width):
        return [
            pltpu.VMEM((rows // 2, width), BF16),
            pltpu.VMEM((rows // 2, width), BF16),
            pltpu.VMEM((rows // 2, width), BF16),
            pltpu.VMEM((rows // 4, width), BF16),
            pltpu.VMEM((3, rows // 16, width), BF16),
            pltpu.VMEM((rows // 2, width), BF16),
            pltpu.SemaphoreType.DMA((10,)),
            pltpu.SemaphoreType.DMA((10,)),
            pltpu.SemaphoreType.DMA((4,)),
        ]

    def copy(self, source, target, place, device):
        return send_to(source, target, self.send.at[place], self.recv.at[place], device)

    def core_copy(self):
        half = self.rows // 2
        source = part(self.own, (1 - self.place.core) * half, half)
        return self.copy(source, self.from_core, 0, self.place.across_core())

    def local_copies(self):
        half = self.rows // 2
        source = part(self.own, self.place.core * half, half)
        copies = [pltpu.make_async_copy(source, self.acc, self.local.at[0])]
        if self.seen is not None:
            copies.append(pltpu.make_async_copy(self.seen, self.seen_here, self.local.at[1]))
        return copies

    def x_copy(self):
        count = self.rows // 4
        source = part(self.acc, (1 - self.place.x) * count, count)
        return self.copy(source, self.from_x, 1, self.place.across_x())

    def z_copies(self):
        count = self.rows // 16
        copies = []
        for step in (1, 2, 3):
            there = (self.place.z + step) % 4
            source = part(self.acc, self.place.x * 4 * count + there * count, count)
            target = self.from_z.at[step - 1]
            copies.append(self.copy(source, target, 1 + step, self.place.along_z(step)))
        return copies

    def piece(self):
        count = self.rows // 16
        inside = self.place.x * 4 * count + self.place.z * count
        return part(self.acc, inside, count), part(self.whole, inside, count)

    def keep_copy(self):
        mine, there = self.piece()
        return pltpu.make_async_copy(mine, there, self.local.at[2])

    def back_z_copies(self):
        mine, there = self.piece()
        return [
            self.copy(mine, there, 4 + step, self.place.along_z(step)) for step in (1, 2, 3)
        ]

    def back_x_copy(self):
        count = self.rows // 4
        there = part(self.whole, self.place.x * count, count)
        return self.copy(there, there, 8, self.place.across_x())

    def back_core_copy(self):
        count = self.rows // 2
        there = part(self.out, self.place.core * count, count)
        return self.copy(self.whole, there, 9, self.place.across_core())

    def store_copy(self):
        count = self.rows // 2
        there = part(self.out, self.place.core * count, count)
        return pltpu.make_async_copy(self.whole, there, self.local.at[3])

    def begin(self):
        self.core_copy().start()
        for copy in self.local_copies():
            copy.start()

    def along_x(self):
        self.core_copy().wait()
        for copy in self.local_copies():
            copy.wait()
        add_rows(self.acc, 0, self.rows // 2, [self.from_core, self.seen_here])
        self.x_copy().start()

    def along_z(self):
        self.x_copy().wait()
        count = self.rows // 4
        add_rows(self.acc, self.place.x * count, count, [self.from_x])
        for copy in self.z_copies():
            copy.start()

    def back_along_z(self):
        for copy in self.z_copies():
            copy.wait()
        count = self.rows // 16
        inside = self.place.x * 4 * count + self.place.z * count
        add_rows(self.acc, inside, count, [self.from_z.at[i] for i in range(3)])
        self.keep_copy().start()
        for copy in self.back_z_copies():
            copy.start()

    def back_along_x(self):
        self.keep_copy().wait()
        for copy in self.back_z_copies():
            copy.wait()
        self.back_x_copy().start()

    def back_to_core(self):
        self.back_x_copy().wait()
        self.back_core_copy().start()
        self.store_copy().start()

    def end(self):
        self.back_core_copy().wait()
        self.store_copy().wait()


class PartnerTerm:
    def __init__(self, place, other, seen, refs):
        self.place, self.other, self.seen = place, other, seen
        self.from_core, self.send, self.recv = refs
        self.half = other.shape[0] // 2

    @staticmethod
    def buffers(rows, width):
        return [
            pltpu.VMEM((rows // 2, width), BF16),
            pltpu.SemaphoreType.DMA((2,)),
            pltpu.SemaphoreType.DMA((2,)),
        ]

    def core_copy(self):
        source = part(self.other, (1 - self.place.core) * self.half, self.half)
        return send_to(
            source, self.from_core, self.send.at[0], self.recv.at[0], self.place.across_core()
        )

    def partner_copy(self):
        return send_to(
            self.from_core, self.seen, self.send.at[1], self.recv.at[1], self.place.partner()
        )

    def begin(self):
        self.core_copy().start()

    def to_partner(self):
        self.core_copy().wait()
        mine = part(self.other, self.place.core * self.half, self.half)
        add_rows(self.from_core, 0, self.half, [mine])
        self.partner_copy().start()

    def end(self):
        self.partner_copy().wait()


class SmallSum:
    ROWS = 16

    def __init__(self, place, own, other, refs):
        self.place, self.own, self.other = place, own, other
        self.sums, self.got, self.send, self.recv = refs

    @staticmethod
    def buffers(width):
        rows = SmallSum.ROWS
        return [
            pltpu.VMEM((3, rows, width), F32),
            pltpu.VMEM((6, rows, width), F32),
            pltpu.SemaphoreType.DMA((6,)),
            pltpu.SemaphoreType.DMA((6,)),
        ]

    def copy(self, source, place, device):
        return send_to(source, self.got.at[place], self.send.at[place], self.recv.at[place], device)

    def partner_copy(self):
        return self.copy(self.other, 0, self.place.partner())

    def core_copy(self):
        return self.copy(self.sums.at[0], 1, self.place.across_core())

    def x_copy(self):
        return self.copy(self.sums.at[1], 2, self.place.across_x())

    def z_copies(self):
        return [
            self.copy(self.sums.at[2], 2 + step, self.place.along_z(step)) for step in (1, 2, 3)
        ]

    def begin(self):
        self.partner_copy().start()

    def over_cores(self):
        self.partner_copy().wait()
        self.sums[0] = self.own[...] + self.got[0]
        self.core_copy().start()

    def over_x(self):
        self.core_copy().wait()
        self.sums[1] = self.sums[0] + self.got[1]
        self.x_copy().start()

    def over_z(self):
        self.x_copy().wait()
        self.sums[2] = self.sums[1] + self.got[2]
        for copy in self.z_copies():
            copy.start()

    def end(self):
        for copy in self.z_copies():
            copy.wait()
        return self.sums[2] + self.got[3] + self.got[4] + self.got[5]


class Fetch:
    def __init__(self, place, own, got, refs, deep):
        self.place, self.own, self.got, self.deep = place, own, got, deep
        self.send, self.recv = refs
        self.half = own.shape[0] // 2
        self.quarter = self.half // 2
        self.count = self.quarter // 2 if deep else self.quarter
        self.core_at = place.core * self.half
        self.x_at = self.core_at + place.x * self.quarter
        odd = place.z % 2
        self.at = self.x_at + odd * self.count if deep else self.x_at
        self.z_at = self.x_at + (1 - odd) * self.count
        self.z_device = place.at(z=place.z + 1 - 2 * odd)

    @staticmethod
    def buffers():
        return [pltpu.SemaphoreType.DMA((5,)), pltpu.SemaphoreType.DMA((5,))]

    def copy(self, source, start, count, place, device):
        there = part(self.got, start, count)
        here = part(source, start, count)
        return send_to(here, there, self.send.at[place], self.recv.at[place], device)

    def partner_copy(self):
        return self.copy(self.own, self.at, self.count, 0, self.place.partner())

    def z_copy(self):
        return self.copy(self.got, self.at, self.count, 1, self.z_device)

    def x_copies(self):
        copies = [self.copy(self.got, self.at, self.count, 2, self.place.across_x())]
        if self.deep:
            copies.append(self.copy(self.got, self.z_at, self.count, 3, self.place.across_x()))
        return copies

    def core_copy(self):
        return self.copy(self.got, self.core_at, self.half, 4, self.place.across_core())

    def begin(self):
        self.partner_copy().start()

    def share(self):
        self.partner_copy().wait()
        if self.deep:
            self.z_copy().start()
        self.x_copies()[0].start()

    def more_x(self):
        self.z_copy().wait()
        self.x_copies()[1].start()

    def to_core(self):
        for copy in self.x_copies():
            copy.wait()
        self.core_copy().start()

    def end(self):
        self.core_copy().wait()


FRONT_BLOCK = 512


def front_kernel(
    mask_ref, gain_ref, shift_ref, bout_ref, gain2_ref, shift2_ref, bias_ref,
    tok_hbm, wq_hbm, wk_hbm, wv_hbm, wout_hbm, wup_hbm, wdown_hbm, cot_hbm,
    x_out, qkv_out, att_out, log_out, resid_out, mid_out,
    cat_hbm, wout_all_hbm, up2_hbm, down2_hbm, grads_hbm, bias2_hbm, tok_out,
    tok_ref, x_ref, qkv_ref, att_ref, cat_ref, wout_ref, bias2_ref, up2_ref, down2_ref, grads_ref,
    load_sem, out_sem, swap_send, swap_recv, *scratch, heads, block,
):
    step = pl.program_id(0)
    place = Place()
    half = heads * HEAD_DIM
    rows = tok_ref.shape[0]
    blocks = rows // FRONT_BLOCK
    pairs = heads // HEAD_GROUP
    base = [0, blocks, blocks + pairs, 2 * blocks + pairs, 2 * blocks + 2 * pairs]

    sems = [scratch[2 * i : 2 * i + 2] for i in range(6)]
    mine = [wq_hbm, wk_hbm, wv_hbm]
    projections = [
        Fetch(place, own, cat_ref.at[1, :, pl.ds(i * half, half)], sems[i], False)
        for i, own in enumerate(mine)
    ]
    fetch_out = Fetch(place, wout_hbm, wout_ref.at[pl.ds(half, half)], sems[3], False)
    fetch_up = Fetch(place, wup_hbm, up2_ref, sems[4], True)
    fetch_down = Fetch(place, wdown_hbm, down2_ref, sems[5], True)
    bias_copy = send_to(
        bias_ref, bias2_ref, swap_send.at[0], swap_recv.at[0], place.partner()
    )
    here = pl.ds(pl.multiple_of(place.rank * LEN_L, LEN_L), LEN_L)
    theirs = pl.ds(pl.multiple_of((1 - place.rank) * LEN_L, LEN_L), LEN_L)
    cot_copy = send_to(
        cot_hbm.at[theirs], grads_ref.at[here], swap_send.at[1], swap_recv.at[1], place.partner()
    )

    def token_rows(i):
        start = pl.multiple_of(i * 2 * LEN_L + place.rank * LEN_L, LEN_L)
        return tok_hbm.at[pl.ds(start, LEN_L)]

    token_loads = [
        pltpu.make_async_copy(token_rows(i), tok_ref.at[pl.ds(i * LEN_L, LEN_L)], load_sem.at[i])
        for i in (0, 1)
    ]
    weight_loads = [
        pltpu.make_async_copy(
            own, cat_ref.at[0, :, pl.ds(i * half, half)], load_sem.at[2 + i]
        )
        for i, own in enumerate(mine)
    ]
    out_load = pltpu.make_async_copy(wout_hbm, wout_ref.at[pl.ds(0, half)], load_sem.at[5])
    kept_copy = pltpu.make_async_copy(cot_hbm.at[here], grads_ref.at[here], out_sem.at[0])
    stores = [
        pltpu.make_async_copy(cat_ref, cat_hbm, out_sem.at[1]),
        pltpu.make_async_copy(wout_ref, wout_all_hbm, out_sem.at[2]),
        pltpu.make_async_copy(bias2_ref, bias2_hbm, out_sem.at[3]),
        pltpu.make_async_copy(tok_ref, tok_out, out_sem.at[4]),
    ]
    last_stores = [
        pltpu.make_async_copy(grads_ref, grads_hbm, out_sem.at[5]),
        pltpu.make_async_copy(up2_ref, up2_hbm, out_sem.at[6]),
        pltpu.make_async_copy(down2_ref, down2_hbm, out_sem.at[7]),
    ]

    @pl.when(step == 0)
    def _():
        for copy in (*token_loads, *weight_loads, out_load):
            copy.start()
        place.greet()
        for one in projections:
            one.begin()
        bias_copy.start()
        fetch_out.begin()
        for copy in token_loads:
            copy.wait()
        for copy in weight_loads:
            copy.wait()

    def at_step(when):
        return pl.when(step == when)

    @at_step(base[1] - 1)
    def _():
        fetch_up.begin()
        fetch_down.begin()

    @at_step(base[1] + 1)
    def _():
        for one in (*projections, fetch_out):
            one.share()

    @at_step(base[2] - 1)
    def _():
        for one in (*projections, fetch_out):
            one.to_core()

    @at_step(base[2])
    def _():
        for one in (*projections, fetch_out):
            one.end()
        bias_copy.wait()
        out_load.wait()
        for copy in stores:
            copy.start()
        kept_copy.start()
        fetch_up.share()
        fetch_down.share()
        cot_copy.start()

    @at_step(base[3] + 2)
    def _():
        fetch_up.more_x()
        fetch_down.more_x()

    @at_step(base[4] + 2)
    def _():
        fetch_up.to_core()
        fetch_down.to_core()

    def project(which, i, bias):
        at = pl.ds(pl.multiple_of(i * FRONT_BLOCK, FRONT_BLOCK), FRONT_BLOCK)
        column = jnp.transpose(bias[:, : 3 * half])[:, :1]
        value = (contract(cat_ref[which], x_ref[at, :], 0, 1) + column).astype(BF16)
        qkv_ref[:, at] = value
        qkv_out[0] = value

    @pl.when(step < base[1])
    def _():
        at = pl.ds(pl.multiple_of(step * FRONT_BLOCK, FRONT_BLOCK), FRONT_BLOCK)
        hat, _ = norm_parts(tok_ref[at, :].astype(F32))
        normed = (hat * gain_ref[...] + shift_ref[...]).astype(BF16)
        x_ref[at, :] = normed
        x_out[...] = normed
        project(0, step, bias_ref[...])

    @pl.when(jnp.logical_and(step >= base[2], step < base[3]))
    def _():
        project(1, step - base[2], bias2_ref[...])

    own_part = jnp.logical_and(step >= base[1], step < base[2])
    other_part = jnp.logical_and(step >= base[3], step < base[4])

    @pl.when(jnp.logical_or(own_part, other_part))
    def _():
        second = (step >= base[3]).astype(jnp.int32)
        pair = step - base[1] - second * (base[3] - base[1])
        attend_pair(mask_ref, qkv_ref, att_ref, att_out, log_out, pair, second, heads, block)

    @pl.when(step >= base[4])
    def _():
        i = step - base[4]
        at = pl.ds(pl.multiple_of(i * FRONT_BLOCK, FRONT_BLOCK), FRONT_BLOCK)
        product = contract(att_ref[:, at], wout_ref[...], 0, 0)
        resid = tok_ref[at, :].astype(F32) + product + bout_ref[...]
        resid_out[...] = resid
        hat, _ = norm_parts(resid)
        mid_out[...] = (hat * gain2_ref[...] + shift2_ref[...]).astype(BF16)

    @pl.when(step == base[4] + blocks - 1)
    def _():
        for one in (fetch_up, fetch_down):
            one.end()
        for copy in last_stores[1:]:
            copy.start()
        cot_copy.wait()
        kept_copy.wait()
        last_stores[0].start()
        for copy in (*stores, *last_stores):
            copy.wait()


def attend_pair(mask_ref, qkv_ref, att_ref, att_out, log_out, pair, second, heads, block):
    rows = qkv_ref.shape[1]
    half = heads * HEAD_DIM
    first = pair * HEAD_GROUP
    work = []
    for head in range(HEAD_GROUP):
        work += [(head, 0, LEN_L, at, block) for at in range(0, LEN_L, block)]
        work += [(head, start, LEN_S, 0, LEN_S) for start in range(LEN_L, rows, LEN_S)]

    def load(which, head, columns):
        start = pl.multiple_of(which * half + (first + head) * HEAD_DIM, HEAD_DIM)
        return qkv_ref[pl.ds(start, HEAD_DIM), columns]

    def scores(item):
        head, start, count, at, size = item
        every = slice(start, start + count)
        keys = load(1, head, every)
        key_rows = jnp.concatenate([keys, keys, extra_rows([mask_ref[:, every]], count)], 0)
        query = scaled_query(load(0, head, slice(start + at, start + at + size)))
        query_rows = jnp.concatenate([*query, jnp.ones((16, size), BF16)], 0)
        return contract(key_rows, query_rows, 0, 0)

    def finish(item, score):
        head, start, count, at, size = item
        here = slice(start + at, start + at + size)
        values = load(2, head, slice(start, start + count))
        value_rows = jnp.concatenate([values, jnp.ones((16, count), BF16)], 0)
        top = jnp.max(score, axis=0, keepdims=True)
        weights = jnp.exp2(score - top).astype(BF16)
        mixed = contract(value_rows, weights, 1, 0)
        total = mixed[HEAD_DIM : HEAD_DIM + 1]
        result = (mixed[:HEAD_DIM] * (1.0 / total)).astype(BF16)
        att_out[0, head, :, here] = result
        start = pl.multiple_of(second * half + (first + head) * HEAD_DIM, HEAD_DIM)
        att_ref[pl.ds(start, HEAD_DIM), here] = result
        log_out[0, head, :, here] = top + jnp.log2(total)

    score = scores(work[0])
    for place, item in enumerate(work):
        later = scores(work[place + 1]) if place + 1 < len(work) else None
        finish(item, score)
        score = later


def front(
    mask, gain, shift, b_out, gain2, shift2, bias, tokens, w_query, w_key, w_value, w_out, w_up,
    w_down, cotangent, heads, block=1024,
):
    width = tokens.shape[1]
    rows = tokens.shape[0] // 2
    half = heads * HEAD_DIM
    hidden = w_up.shape[1]
    blocks, pairs = rows // FRONT_BLOCK, heads // HEAD_GROUP
    base = [0, blocks, blocks + pairs, 2 * blocks + pairs, 2 * blocks + 2 * pairs]
    anywhere = pl.BlockSpec(memory_space=pl.ANY)

    def row_block(first):
        return lambda s: (jnp.clip(s - first, 0, blocks - 1), 0)

    def qkv_block(s):
        late = (s >= base[2]).astype(jnp.int32)
        return late, 0, jnp.clip(s - late * base[2], 0, blocks - 1)

    def head_block(s):
        late = (s >= base[3]).astype(jnp.int32)
        return late, jnp.clip(s - base[1] - late * (base[3] - base[1]), 0, pairs - 1), 0, 0

    by_row = lambda first: pl.BlockSpec((FRONT_BLOCK, width), row_block(first))
    bias_rows, bias_width = bias.shape
    pair_total = pair_count(2 * heads, rows)
    return pl.pallas_call(
        functools.partial(front_kernel, heads=heads, block=block),
        grid=(base[4] + blocks,),
        in_specs=[
            whole((1, rows)),
            *(whole((1, width)) for _ in range(5)),
            whole(bias.shape),
        ]
        + [anywhere] * 8,
        out_specs=[
            by_row(0),
            pl.BlockSpec((1, 3 * half, FRONT_BLOCK), qkv_block),
            pl.BlockSpec((1, HEAD_GROUP, HEAD_DIM, rows), head_block),
            pl.BlockSpec((1, HEAD_GROUP, 1, rows), head_block),
            by_row(base[4]),
            by_row(base[4]),
        ]
        + [anywhere] * 7,
        out_shape=[
            jax.ShapeDtypeStruct((rows, width), BF16),
            jax.ShapeDtypeStruct((2, 3 * half, rows), BF16),
            jax.ShapeDtypeStruct((2, heads, HEAD_DIM, rows), BF16),
            jax.ShapeDtypeStruct((2, heads, 1, rows), F32),
            jax.ShapeDtypeStruct((rows, width), F32),
            jax.ShapeDtypeStruct((rows, width), BF16),
            jax.ShapeDtypeStruct((2, width, 3 * half), BF16),
            jax.ShapeDtypeStruct((2 * half, width), BF16),
            jax.ShapeDtypeStruct((width, hidden), BF16),
            jax.ShapeDtypeStruct((hidden, width), BF16),
            jax.ShapeDtypeStruct((rows, width), BF16),
            jax.ShapeDtypeStruct((bias_rows, bias_width), F32),
            jax.ShapeDtypeStruct((rows, width), BF16),
        ],
        scratch_shapes=[
            pltpu.VMEM((rows, width), BF16),
            pltpu.VMEM((rows, width), BF16),
            pltpu.VMEM((3 * half, rows), BF16),
            pltpu.VMEM((2 * half, rows), BF16),
            pltpu.VMEM((2, width, 3 * half), BF16),
            pltpu.VMEM((2 * half, width), BF16),
            pltpu.VMEM((bias_rows, bias_width), F32),
            pltpu.VMEM((width, hidden), BF16),
            pltpu.VMEM((hidden, width), BF16),
            pltpu.VMEM((rows, width), BF16),
            pltpu.SemaphoreType.DMA((6,)),
            pltpu.SemaphoreType.DMA((8,)),
            pltpu.SemaphoreType.DMA((2,)),
            pltpu.SemaphoreType.DMA((2,)),
        ]
        + [ref for _ in range(6) for ref in Fetch.buffers()],
        compiler_params=pltpu.CompilerParams(
            vmem_limit_bytes=VMEM_LIMIT, collective_id=1, has_side_effects=True
        ),
        cost_estimate=cost(
            pair_total * 2 * 512 + 14 * rows * width * half, 40 * rows * width, pair_total
        ),
        name="front",
    )(
        mask, gain, shift, b_out, gain2, shift2, bias, tokens, w_query, w_key, w_value, w_out,
        w_up, w_down, cotangent,
    )


ERFC_TERMS = (0.254829592, -0.284496736, 1.421413741, -1.453152027, 1.061405429)
ERFC_SLOPE = 0.3275911


def gelu_and_slope(value):
    bell = jnp.exp2(value * value * (-0.5 * LOG2E))
    base = 1.0 + jnp.abs(value) * (ERFC_SLOPE * math.sqrt(0.5))
    ratio = 1.0 / base
    poly = ERFC_TERMS[4] * 0.5
    for term in ERFC_TERMS[3::-1]:
        poly = poly * ratio + term * 0.5
    tail = poly * ratio * bell
    below = jnp.where(value < 0.0, tail, 1.0 - tail)
    return value * below, below + value * bell * (1.0 / math.sqrt(2.0 * math.pi))


def feed_kernel(
    mid_ref, grad_ref, up_ref, b_ref, down_ref, sum_ref, gmid_ref, dup_ref, ddown_ref, db_ref,
    act_ref, gpre_ref, *, chunk,
):
    @pl.when(pl.program_id(0) == 0)
    def _():
        sum_ref[...] = jnp.zeros_like(sum_ref)
        gmid_ref[...] = jnp.zeros_like(gmid_ref)

    rows = mid_ref.shape[0]
    up, down, bias = up_ref[...], down_ref[...], b_ref[...]

    def products(at):
        here = slice(at, at + chunk)
        return (
            contract(mid_ref[here], up, 1, 0) + bias,
            contract(grad_ref[here], down, 1, 1),
        )

    now = products(0)
    db = None
    for at in range(0, rows, chunk):
        here = slice(at, at + chunk)
        later = products(at + chunk) if at + chunk < rows else None
        value, slope = gelu_and_slope(now[0])
        act = value.astype(BF16)
        gpre = (slope * now[1]).astype(BF16)
        act_ref[here] = act
        gpre_ref[here] = gpre
        part = jnp.sum(gpre.astype(F32), axis=0, keepdims=True)
        db = part if db is None else db + part
        sum_ref[here] += contract(act, down, 1, 0)
        gmid_ref[here] += contract(gpre, up, 1, 1)
        now = later
    db_ref[...] = db
    ddown_ref[...] = contract(act_ref[...], grad_ref[...], 0, 0).astype(BF16)
    dup_ref[...] = contract(mid_ref[...], gpre_ref[...], 0, 0).astype(BF16)


def feed(mid, grads, w_up, b_up, w_down, block=512, chunk=512):
    rows, width = mid.shape
    hidden = w_up.shape[1]
    return pl.pallas_call(
        functools.partial(feed_kernel, chunk=chunk),
        grid=(hidden // block,),
        in_specs=[
            whole((rows, width)),
            whole((rows, width)),
            pl.BlockSpec((width, block), lambda j: (0, j)),
            pl.BlockSpec((1, block), lambda j: (0, j)),
            pl.BlockSpec((block, width), lambda j: (j, 0)),
        ],
        out_specs=[
            whole((rows, width)),
            whole((rows, width)),
            pl.BlockSpec((width, block), lambda j: (0, j)),
            pl.BlockSpec((block, width), lambda j: (j, 0)),
            pl.BlockSpec((1, block), lambda j: (0, j)),
        ],
        out_shape=[
            jax.ShapeDtypeStruct((rows, width), F32),
            jax.ShapeDtypeStruct((rows, width), F32),
            jax.ShapeDtypeStruct((width, hidden), BF16),
            jax.ShapeDtypeStruct((hidden, width), BF16),
            jax.ShapeDtypeStruct((1, hidden), F32),
        ],
        scratch_shapes=[pltpu.VMEM((rows, block), BF16), pltpu.VMEM((rows, block), BF16)],
        compiler_params=params(),
        cost_estimate=cost(12 * rows * width * hidden, 20 * rows * width, 2 * rows * hidden),
        name="feed",
    )(mid, grads, w_up, b_up, w_down)


def branch_kernel(
    resid_ref, sum1_ref, sum2_ref, gmid1_ref, gmid2_ref, grad_ref, gain_ref, bdown_ref, w_ref,
    att_ref, out_ref, gresid_ref, gatt_ref, dw_own_ref, dw_other_ref, small_ref, acc_ref,
):
    @pl.when(pl.program_id(0) == 0)
    def _():
        acc_ref[...] = jnp.zeros_like(acc_ref)
        small_ref[...] = jnp.zeros_like(small_ref)

    resid = resid_ref[...]
    grads = grad_ref[...].astype(F32)
    out_ref[...] = (resid + sum1_ref[...] + sum2_ref[...] + bdown_ref[...]).astype(BF16)
    gmid = gmid1_ref[...] + gmid2_ref[...]
    hat, inv = norm_parts(resid)
    gresid = grads + norm_back(hat, inv, gmid * gain_ref[...])
    gresid_ref[...] = gresid
    branch = gresid.astype(BF16)
    gatt_ref[...] = contract(w_ref[...], branch, 1, 1).astype(BF16)
    acc_ref[...] += contract(branch, att_ref[...], 0, 1)
    small_ref[0:1] += jnp.sum(gmid * hat, axis=0, keepdims=True)
    small_ref[1:2] += jnp.sum(gmid, axis=0, keepdims=True)
    small_ref[2:3] += jnp.sum(gresid, axis=0, keepdims=True)
    small_ref[3:4] += jnp.sum(grads, axis=0, keepdims=True)

    @pl.when(pl.program_id(0) == pl.num_programs(0) - 1)
    def _():
        half = dw_own_ref.shape[1]
        dw_own_ref[...] = acc_ref[:, :half].astype(BF16)
        dw_other_ref[...] = acc_ref[:, half:].astype(BF16)


def branch(resid, sums, gmids, grads, gain, b_down, w_out, attended, block):
    rows, width = resid.shape
    heads_width = attended.shape[0]
    by_row = pl.BlockSpec((block, width), lambda i: (i, 0))
    columns = pl.BlockSpec((heads_width, block), lambda i: (0, i))
    half = (width, heads_width // 2)
    return pl.pallas_call(
        branch_kernel,
        grid=(rows // block,),
        in_specs=[by_row] * 6
        + [whole((1, width)), whole((1, width)), whole((heads_width, width)), columns],
        out_specs=[by_row, by_row, columns, whole(half), whole(half), whole((8, width))],
        out_shape=[
            jax.ShapeDtypeStruct((rows, width), BF16),
            jax.ShapeDtypeStruct((rows, width), F32),
            jax.ShapeDtypeStruct((heads_width, rows), BF16),
            jax.ShapeDtypeStruct(half, BF16),
            jax.ShapeDtypeStruct(half, BF16),
            jax.ShapeDtypeStruct((8, width), F32),
        ],
        scratch_shapes=[pltpu.VMEM((width, heads_width), F32)],
        compiler_params=params(),
        cost_estimate=cost(4 * rows * width * heads_width, 32 * rows * width),
        name="branch",
    )(resid, *sums, *gmids, grads, gain, b_down, w_out, attended)


TAIL_BLOCK = 512
SUM_ACTIONS = ("begin", "along_x", "along_z", "back_along_z", "back_along_x", "back_to_core")
SUM_STEPS = (
    (0, 1, 4, 12, 14, 16),
    (0, 3, 6, 14, 16, 18),
    (0, 5, 8, 16, 18, 20),
    (0, 7, 10, 18, 20),
    (0, 9, 12, 15, 17, 19),
    (None, 17, 19),
    (None, 17, 20),
    (None, 17),
)
LAST_ACTIONS = (
    (7, "along_z"), 0, (5, "back_along_z"), 1, (6, "back_along_z"), (3, "back_to_core"), 2,
    (7, "back_along_z"), (5, "back_along_x"), (6, "back_along_x"), (7, "back_along_x"),
    (5, "back_to_core"), (6, "back_to_core"), (7, "back_to_core"),
)


def tail_kernel(
    mask_ref, qkv_ref, att_ref, log_ref, gatt_ref, gain_ref, small2_ref, dbup1_ref, dbup2_ref,
    wout2_ref, x_hbm, w_hbm, tok_hbm, gresid_hbm, up_hbm, down_hbm, wout_hbm, seen_up,
    seen_down, out_hbm,
    gtok_ref, small_ref, got_hbm, gup_hbm, gdown_hbm, gout_hbm, gcat_hbm, got_out,
    d_ref, x_ref, w_ref, tok_ref, gresid_ref, dw_ref, dw2_ref, seen_cat, sent_ref, own_small,
    other_small, load_sem, row_sem, tok_send, tok_recv, *scratch, heads, block,
):
    step = pl.program_id(0)
    place = Place()
    first_rows = 2 * heads + 1
    last_step = first_rows + 3
    width = x_ref.shape[1]
    half = heads * HEAD_DIM
    halves = width

    groups = []
    at = 0
    for count in [9] * 8 + [3, 3, 4]:
        groups.append(scratch[at : at + count])
        at += count
    columns = lambda ref, i: ref.at[:, pl.ds(i * halves, halves)]
    rows_of = lambda ref, i, count: ref.at[pl.ds(i * count, count)]
    sums = [
        PlaneSum(place, columns(up_hbm, i), columns(seen_up, i), columns(gup_hbm, i), groups[i])
        for i in (0, 1)
    ]
    down_rows = down_hbm.shape[0] // 2
    sums += [
        PlaneSum(
            place,
            rows_of(down_hbm, i, down_rows),
            rows_of(seen_down, i, down_rows // 2),
            rows_of(gdown_hbm, i, down_rows),
            groups[2 + i],
        )
        for i in (0, 1)
    ]
    sums.append(PlaneSum(place, wout_hbm, None, gout_hbm, groups[4]))
    third = lambda ref, i: ref.at[:, pl.ds(i * half, half)]
    cat_sums = [
        PlaneSum(
            place, third(dw_ref, i), None, third(gcat_hbm, i),
            (groups[5 + i][0], third(seen_cat, i), *groups[5 + i][2:]),
        )
        for i in range(3)
    ]
    cat_term = PartnerTerm(place, dw2_ref, seen_cat, groups[8])
    out_term = PartnerTerm(place, wout2_ref, groups[4][1], groups[9])
    small = SmallSum(place, own_small, other_small, groups[10])
    theirs = pl.ds(pl.multiple_of((1 - place.rank) * LEN_L, LEN_L), LEN_L)
    out_load = pltpu.make_async_copy(out_hbm.at[theirs], sent_ref, load_sem.at[2])
    out_copy = send_to(sent_ref, got_out, tok_send.at[2], tok_recv.at[2], place.partner())

    loads = [
        pltpu.make_async_copy(x_hbm, x_ref, load_sem.at[0]),
        pltpu.make_async_copy(w_hbm, w_ref, load_sem.at[1]),
    ]

    def row_start(i):
        mine = i // 2
        return ((1 - mine) * (1 - place.rank) + mine * place.rank) * LEN_L + (i % 2) * TAIL_BLOCK

    def row_loads(i):
        start = pl.ds(pl.multiple_of(row_start(i), TAIL_BLOCK), TAIL_BLOCK)
        slot = i % 2
        return [
            pltpu.make_async_copy(tok_hbm.at[start], tok_ref.at[slot], row_sem.at[slot, 0]),
            pltpu.make_async_copy(gresid_hbm.at[start], gresid_ref.at[slot], row_sem.at[slot, 1]),
        ]

    def token_copy(i):
        there = pl.ds(i * TAIL_BLOCK, TAIL_BLOCK)
        return send_to(
            sent_ref.at[there], got_hbm.at[there], tok_send.at[i], tok_recv.at[i], place.partner()
        )

    def weight_gradient(source, target, i):
        here = pl.ds(i * half, half)
        product = contract(x_ref[...], d_ref[source, here, :], 0, 1)
        target[:, here] = product.astype(BF16)

    def bias_rows(source, target):
        ones = jnp.ones((16, d_ref.shape[2]), BF16)
        for i, which in ((0, 0), (1, 2)):
            row = contract(ones, d_ref[source, pl.ds(which * half, half), :], 1, 1)
            target[8:9, pl.ds(i * half, half)] = row[:1]

    events = {}
    sums += cat_sums
    for one, times in zip(sums, SUM_STEPS):
        for when, action in zip(times, SUM_ACTIONS):
            if when is None:
                continue
            events.setdefault(when, []).append(getattr(one, action))

    for when in sorted(events):

        @pl.when(step == when)
        def _(when=when):
            if when == 0:
                out_load.start()
                place.greet()
                out_term.begin()
            if when == 1:
                out_term.to_partner()
                out_load.wait()
                out_copy.start()
            if when == 4:
                out_term.end()
            for action in events[when]:
                action()

    @pl.when(step == 2)
    def _():
        for copy in loads:
            copy.start()

    @pl.when(step == heads)
    def _():
        for copy in loads:
            copy.wait()
        for i in range(3):
            weight_gradient(1, dw2_ref, i)
        cat_term.begin()

    @pl.when(step == heads + 1)
    def _():
        cat_term.to_partner()
        own_small[...] = jnp.zeros_like(own_small)
        other_small[...] = jnp.zeros_like(other_small)
        bias_rows(1, other_small)

    @pl.when(step < 2 * heads)
    def _():
        back_one_head(mask_ref, qkv_ref, att_ref, log_ref, gatt_ref, d_ref, step, heads, block)

    @pl.when(step == 2 * heads)
    def _():
        for copy in row_loads(0):
            copy.start()
        cat_term.end()
        out_copy.wait()
        for i in range(3):
            weight_gradient(0, dw_ref, i)
            cat_sums[i].begin()
        bias_rows(0, own_small)


    for i in range(4):

        @pl.when(step == first_rows + i)
        def _(i=i):
            for copy in row_loads(i):
                copy.wait()
            if i < 3:
                for copy in row_loads(i + 1):
                    copy.start()
            here = pl.ds(pl.multiple_of(row_start(i), TAIL_BLOCK), TAIL_BLOCK)
            gin = contract(d_ref[0, :, here], w_ref[0], 0, 1)
            gin += contract(d_ref[1, :, here], w_ref[1], 0, 1)
            hat, inv = norm_parts(tok_ref[i % 2].astype(F32))
            gtok = gresid_ref[i % 2] + norm_back(hat, inv, gin * gain_ref[...])
            own_small[0:1] += jnp.sum(gin * hat, axis=0, keepdims=True)
            own_small[1:2] += jnp.sum(gin, axis=0, keepdims=True)
            if i < 2:
                sent_ref[pl.ds(i * TAIL_BLOCK, TAIL_BLOCK), :] = gtok.astype(BF16)
                token_copy(i).start()
            else:
                gtok_ref[...] = gtok

    @pl.when(step == last_step)
    def _():
        own_small[2:6] = small2_ref[0:4]
        other_small[0:2] = own_small[0:2]
        other_small[2:6] = small2_ref[0:4]
        for i in (0, 1):
            own_small[6 + i : 7 + i] = dbup1_ref[:, pl.ds(i * width, width)]
            other_small[6 + i : 7 + i] = dbup2_ref[:, pl.ds(i * width, width)]
        small.begin()
        small_actions = (small.over_cores, small.over_x, small.over_z)
        for item in LAST_ACTIONS:
            if isinstance(item, int):
                small_actions[item]()
            else:
                getattr(sums[item[0]], item[1])()
        small_ref[...] = small.end()
        for i in (0, 1):
            token_copy(i).wait()
        for one in sums:
            one.end()


def back_one_head(mask_ref, qkv_ref, att_ref, log_ref, gatt_ref, d_ref, step, heads, block):
    rows = qkv_ref.shape[4]
    half = heads * HEAD_DIM
    source = 1 - step // heads
    head_at = pl.multiple_of((step % heads) * HEAD_DIM, HEAD_DIM)

    def store(which, columns, value):
        d_ref[source, pl.ds(which * half + head_at, HEAD_DIM), columns] = value.astype(BF16)

    images = [(0, LEN_L, block)] + [(at, LEN_S, LEN_S) for at in range(LEN_L, rows, LEN_S)]
    for start, count, size in images:
        every = slice(start, start + count)
        keys = qkv_ref[0, 1, 0, :, every]
        values = qkv_ref[0, 2, 0, :, every]
        ones = jnp.ones((1, count), F32)
        key_rows = jnp.concatenate(
            [keys, keys, extra_rows([ones, ones, ones, mask_ref[:, every]], count)], 0
        )
        value_rows = jnp.concatenate([values, extra_rows([ones, ones, ones], count)], 0)
        grad_values = grad_keys = None
        for at in range(start, start + count, size):
            here = slice(at, at + size)
            query = qkv_ref[0, 0, 0, :, here]
            grads = gatt_ref[0, 0, :, here]
            inner = jnp.sum(
                grads.astype(F32) * att_ref[0, 0, :, here].astype(F32), axis=0, keepdims=True
            )
            terms = three_terms(-log_ref[0, 0, :, here]) + [jnp.ones((1, size), F32)]
            query_rows = jnp.concatenate([*scaled_query(query), extra_rows(terms, size)], 0)
            grad_rows = jnp.concatenate([grads, extra_rows(three_terms(-inner), size)], 0)
            score = contract(query_rows, key_rows, 0, 0)
            grad_probs = contract(grad_rows, value_rows, 0, 0)
            probs = jnp.exp2(score)
            grad_score = (probs * grad_probs).astype(BF16)
            part_values = contract(grads, probs.astype(BF16), 1, 0)
            part_keys = contract(query, grad_score, 1, 0)
            grad_values = part_values if grad_values is None else grad_values + part_values
            grad_keys = part_keys if grad_keys is None else grad_keys + part_keys
            store(0, here, contract(keys, grad_score, 1, 1) * SCALE)
        store(1, every, grad_keys * SCALE)
        store(2, every, grad_values)


def tail(
    mask, qkv, att, log_total, gatt, gain, small2, dbup1, dbup2, dwout2, normed, w_cat,
    tokens, gresid, dup, ddown, dwout, seen_up, seen_down, out_rows, block=256,
):
    _, _, heads, _, rows = qkv.shape
    _, width, out = w_cat.shape
    anywhere = pl.BlockSpec(memory_space=pl.ANY)
    last = 2 * heads - 1

    def head(h):
        h = jnp.minimum(h, last)
        return 1 - h // heads, h % heads

    all_three = pl.BlockSpec(
        (1, 3, 1, HEAD_DIM, rows), lambda h: (head(h)[0], 0, head(h)[1], 0, 0)
    )
    one = pl.BlockSpec((1, 1, HEAD_DIM, rows), lambda h: (*head(h), 0, 0))
    row = pl.BlockSpec((1, 1, 1, rows), lambda h: (*head(h), 0, 0))
    sum_shapes = [(width, width)] * 4 + [dwout.shape] + [(width, out // 3)] * 3
    scratch = [
        pltpu.VMEM((2, out, rows), BF16),
        pltpu.VMEM((rows, width), BF16),
        pltpu.VMEM((2, width, out), BF16),
        pltpu.VMEM((2, TAIL_BLOCK, width), BF16),
        pltpu.VMEM((2, TAIL_BLOCK, width), F32),
        pltpu.VMEM((width, out), BF16),
        pltpu.VMEM((width, out), BF16),
        pltpu.VMEM((width // 2, out), BF16),
        pltpu.VMEM((rows // 2, width), BF16),
        pltpu.VMEM((SmallSum.ROWS, width), F32),
        pltpu.VMEM((SmallSum.ROWS, width), F32),
        pltpu.SemaphoreType.DMA((3,)),
        pltpu.SemaphoreType.DMA((2, 2)),
        pltpu.SemaphoreType.DMA((3,)),
        pltpu.SemaphoreType.DMA((3,)),
    ]
    for shape in sum_shapes:
        scratch += PlaneSum.buffers(*shape)
    scratch += PartnerTerm.buffers(width, out) + PartnerTerm.buffers(*dwout.shape)
    scratch += SmallSum.buffers(width)
    pairs = pair_count(2 * heads, rows)
    first_rows = 2 * heads + 1
    return pl.pallas_call(
        functools.partial(tail_kernel, heads=heads, block=block),
        grid=(first_rows + 4,),
        in_specs=[
            whole((1, rows)), all_three, one, row, one, whole((1, width)), whole((8, width)),
            whole((1, 2 * width)), whole((1, 2 * width)), whole(dwout.shape),
        ]
        + [anywhere] * 10,
        out_specs=[
            pl.BlockSpec(
                (TAIL_BLOCK, width), lambda h: (jnp.maximum(h - first_rows - 2, 0), 0)
            ),
            whole((SmallSum.ROWS, width)),
        ]
        + [anywhere] * 6,
        out_shape=[
            jax.ShapeDtypeStruct((rows // 2, width), F32),
            jax.ShapeDtypeStruct((SmallSum.ROWS, width), F32),
            jax.ShapeDtypeStruct((rows // 2, width), BF16),
            jax.ShapeDtypeStruct(dup.shape, BF16),
            jax.ShapeDtypeStruct(ddown.shape, BF16),
            jax.ShapeDtypeStruct(dwout.shape, BF16),
            jax.ShapeDtypeStruct((width, out), BF16),
            jax.ShapeDtypeStruct((rows // 2, width), BF16),
        ],
        scratch_shapes=scratch,
        compiler_params=pltpu.CompilerParams(
            vmem_limit_bytes=VMEM_LIMIT, collective_id=0, has_side_effects=True
        ),
        cost_estimate=cost(pairs * 5 * 512, 32 * heads * HEAD_DIM * rows, pairs),
        name="tail",
    )(
        mask, qkv, att, log_total, gatt, gain, small2, dbup1, dbup2, dwout2, normed, w_cat,
        tokens, gresid, dup, ddown, dwout, seen_up, seen_down, out_rows,
    )


def swap_tp(array):
    return lax.ppermute(array, "tp", [(0, 1), (1, 0)])


def swap_dp(array, bit):
    count = lax.axis_size("dp")
    return lax.ppermute(array, "dp", [(i, i ^ bit) for i in range(count)])


def dp_bit(bit):
    return (lax.axis_index("dp") & bit) != 0


def joined(mine, theirs, second):
    return jnp.where(second, jnp.concatenate([theirs, mine], 0), jnp.concatenate([mine, theirs], 0))


def half_of(array, second):
    size = array.shape[0] // 2
    return lax.dynamic_slice_in_dim(array, jnp.where(second, size, 0), size, 0)


def add_low(left, right):
    return (left.astype(F32) + right.astype(F32)).astype(BF16)


def over_cores(other, chunks=1):
    second = dp_bit(1)
    split = other.reshape(chunks, other.shape[0] // chunks, other.shape[1])
    half = split.shape[1] // 2
    take = lambda which: lax.dynamic_slice_in_dim(split, jnp.where(which, half, 0), half, 1)
    both = add_low(take(second), swap_dp(take(~second), 1))
    return both.reshape(-1, other.shape[1])


def by_images(
    tokens, long_lengths, short_lengths, ln1_gain, ln1_bias, w_query, b_query, w_key, w_value,
    b_value, w_out, b_out, ln2_gain, ln2_bias, w_up, b_up, w_down, b_down, cotangent,
):
    rank = lax.axis_index("tp")
    rank_arr = jnp.reshape(rank, (1,)).astype(jnp.int32)
    second = rank == 1
    rows = tokens.shape[0] // 2
    width = tokens.shape[1]
    half = w_query.shape[1]
    heads = half // HEAD_DIM
    long_len = lax.dynamic_slice_in_dim(long_lengths, rank, 1, 0)
    shorts = short_lengths.shape[0] // 2
    short_len = lax.dynamic_slice_in_dim(short_lengths, rank * shorts, shorts, 0)
    valid = jnp.concatenate(
        [
            jnp.arange(LEN_L) < long_len[0],
            (jnp.arange(LEN_S)[None, :] < short_len[:, None]).reshape(-1),
        ]
    )
    mask = jnp.where(valid, 0.0, -1e30).astype(F32).reshape(1, -1)
    row = lambda vector: vector.astype(F32).reshape(1, -1)
    biases = jnp.concatenate([b_query, jnp.zeros_like(b_query), b_value, b_up]).astype(F32)
    bias = jnp.broadcast_to(biases.reshape(1, -1), (8, biases.shape[0]))

    (normed, qkv, att, log_total, resid, mid, w_cat, w_out_all, w_up2, w_down2, grads, bias2,
     own_tokens) = front(
        mask, row(ln1_gain), row(ln1_bias), row(b_out), row(ln2_gain), row(ln2_bias), bias,
        tokens, w_query, w_key, w_value, w_out, w_up, w_down, cotangent, heads,
    )
    qkv = qkv.reshape(2, 3, heads, HEAD_DIM, rows)
    attended = att.reshape(2 * half, rows)
    up_bias = bias[:1, 3 * half :], bias2[:1, 3 * half :]
    sum2, gmid2, dup2, ddown2, dbup2 = feed(mid, grads, w_up2, up_bias[1], w_down2)
    mid, both_up, both_down = lax.optimization_barrier((mid, over_cores(dup2), over_cores(ddown2, 2)))
    seen_up, seen_down = swap_tp(both_up), swap_tp(both_down)
    sum1, gmid1, dup1, ddown1, dbup1 = feed(mid, grads, w_up, up_bias[0], w_down)
    out, gresid, gatt, dwout1, dwout2, small2 = branch(
        resid, (sum1, sum2), (gmid1, gmid2), grads, row(ln2_gain), row(b_down), w_out_all,
        attended, 512,
    )
    gtok, small, got_tok, grad_up, grad_down, grad_out_t, grad_cat, got_out = tail(
        mask, qkv, att, log_total, gatt.reshape(2, heads, HEAD_DIM, rows), row(ln1_gain), small2,
        dbup1, dbup2, dwout2, normed, w_cat, own_tokens, gresid, dup1, ddown1, dwout1,
        seen_up, seen_down, out,
    )
    result = joined(half_of(out, second), got_out, second)
    grad_tokens = joined(gtok, got_tok.astype(F32), second)
    grad_cat = grad_cat.astype(F32)
    return (
        result,
        grad_tokens,
        small[0],
        small[1],
        grad_cat[:, :half],
        small[8, :half],
        grad_cat[:, half : 2 * half],
        grad_cat[:, 2 * half :],
        small[8, half:],
        grad_out_t.T.astype(F32),
        small[4],
        small[2],
        small[3],
        grad_up.astype(F32),
        small[6:8].reshape(-1),
        grad_down.astype(F32),
        small[5],
    )


def layer_norm(values, gain, shift):
    center = values - jnp.mean(values, axis=-1, keepdims=True)
    spread = jnp.mean(center * center, axis=-1, keepdims=True)
    return center * lax.rsqrt(spread + 1e-06) * gain + shift


def dot_plain(left, right):
    return jnp.dot(left, right, preferred_element_type=jnp.float32)


def dot_rows(left, right):
    return lax.dot_general(
        left, right, (((0,), (0,)), ((), ())), preferred_element_type=jnp.float32
    )


def dot_back(left, right):
    return lax.dot_general(
        left, right, (((1,), (1,)), ((), ())), preferred_element_type=jnp.float32
    )


def group_shape(image_count, seq_len, head_count):
    per_step = math.gcd(image_count, max(1, 512 // seq_len))
    return (image_count // per_step, per_step, seq_len, head_count, HEAD_DIM)


def masked_scores(query_blk, key_blk, length_blk):
    seq_len = query_blk.shape[1]
    raw = jnp.einsum(
        "bqhd,bkhd->bhqk", query_blk, key_blk, preferred_element_type=jnp.float32
    ) * HEAD_DIM ** (-0.5)
    keep = jnp.arange(seq_len, dtype=jnp.int32)[None, :] < length_blk[:, None]
    return jnp.where(keep[:, None, None, :], raw, -1e30)


def attention_forward(queries, key_rows, value_rows, lengths, seq_len):
    image_count = lengths.shape[0]
    head_count = queries.shape[1] // HEAD_DIM
    block_shape = group_shape(image_count, seq_len, head_count)

    def one_step(block):
        query_blk, key_blk, value_blk, length_blk = block
        scores = masked_scores(query_blk, key_blk, length_blk)
        row_top = jnp.max(scores, axis=-1, keepdims=True)
        exp_terms = jnp.exp(scores - row_top)
        row_total = jnp.sum(exp_terms, axis=-1, keepdims=True)
        weights = (exp_terms / row_total).astype(jnp.bfloat16)
        mixed = jnp.einsum(
            "bhqk,bkhd->bqhd", weights, value_blk, preferred_element_type=jnp.float32
        )
        return (mixed, (row_top + jnp.log(row_total))[..., 0])

    mixed, log_total = lax.map(
        one_step,
        (
            queries.reshape(block_shape),
            key_rows.reshape(block_shape),
            value_rows.reshape(block_shape),
            lengths.reshape(block_shape[:2]),
        ),
    )
    return (mixed.reshape(image_count * seq_len, head_count * HEAD_DIM), log_total)


def attention_backward(queries, key_rows, value_rows, grads, lengths, log_total, seq_len):
    image_count = lengths.shape[0]
    head_count = queries.shape[1] // HEAD_DIM
    block_shape = group_shape(image_count, seq_len, head_count)
    scale = HEAD_DIM ** (-0.5)

    def one_step(block):
        query_blk, key_blk, value_blk, grad_blk, length_blk, total_blk = block
        scores = masked_scores(query_blk, key_blk, length_blk)
        probs = jnp.exp(scores - total_blk[..., None])
        grad_values = jnp.einsum(
            "bhqk,bqhd->bkhd",
            probs.astype(jnp.bfloat16),
            grad_blk,
            preferred_element_type=jnp.float32,
        )
        grad_probs = jnp.einsum(
            "bqhd,bkhd->bhqk", grad_blk, value_blk, preferred_element_type=jnp.float32
        )
        inner = jnp.sum(probs * grad_probs, axis=-1, keepdims=True)
        grad_scores = (probs * (grad_probs - inner)).astype(jnp.bfloat16)
        grad_queries = (
            jnp.einsum("bhqk,bkhd->bqhd", grad_scores, key_blk, preferred_element_type=jnp.float32)
            * scale
        )
        grad_keys = (
            jnp.einsum(
                "bhqk,bqhd->bkhd", grad_scores, query_blk, preferred_element_type=jnp.float32
            )
            * scale
        )
        return (grad_queries, grad_keys, grad_values)

    results = lax.map(
        one_step,
        (
            queries.reshape(block_shape),
            key_rows.reshape(block_shape),
            value_rows.reshape(block_shape),
            grads.reshape(block_shape),
            lengths.reshape(block_shape[:2]),
            log_total,
        ),
    )
    flat = (image_count * seq_len, head_count * HEAD_DIM)
    return tuple((item.reshape(flat) for item in results))


def local(
    tokens,
    long_lengths,
    short_lengths,
    ln1_gain,
    ln1_bias,
    w_query,
    b_query,
    w_key,
    w_value,
    b_value,
    w_out,
    b_out,
    ln2_gain,
    ln2_bias,
    w_up,
    b_up,
    w_down,
    b_down,
    cotangent,
):
    tp_count = lax.axis_size("tp")
    tp_rank = lax.axis_index("tp")
    row_count = tokens.shape[0]
    share = row_count // tp_count
    split = long_lengths.shape[0] * LEN_L
    gain_one = ln1_gain.astype(jnp.float32)
    shift_one = ln1_bias.astype(jnp.float32)
    gain_two = ln2_gain.astype(jnp.float32)
    shift_two = ln2_bias.astype(jnp.float32)
    normed_in = layer_norm(tokens.astype(jnp.float32), gain_one, shift_one).astype(jnp.bfloat16)
    queries = (dot_plain(normed_in, w_query) + b_query.astype(jnp.float32)).astype(jnp.bfloat16)
    key_rows = dot_plain(normed_in, w_key).astype(jnp.bfloat16)
    value_rows = (dot_plain(normed_in, w_value) + b_value.astype(jnp.float32)).astype(jnp.bfloat16)
    long_mixed, long_total = attention_forward(
        queries[:split], key_rows[:split], value_rows[:split], long_lengths, LEN_L
    )
    short_mixed, short_total = attention_forward(
        queries[split:], key_rows[split:], value_rows[split:], short_lengths, LEN_S
    )
    attended = jnp.concatenate([long_mixed, short_mixed], axis=0).astype(jnp.bfloat16)
    attn_sum = lax.psum_scatter(dot_plain(attended, w_out), "tp", scatter_dimension=0, tiled=True)
    own_tokens = lax.dynamic_slice_in_dim(tokens, tp_rank * share, share, 0).astype(jnp.float32)
    resid = own_tokens + attn_sum + b_out.astype(jnp.float32)
    normed_mid = layer_norm(resid, gain_two, shift_two).astype(jnp.bfloat16)
    grad_out = cotangent.astype(jnp.float32)
    mid_rows = lax.all_gather(normed_mid, "tp", axis=0, tiled=True)
    pre_up = dot_plain(mid_rows, w_up) + b_up.astype(jnp.float32)
    activ = jax.nn.gelu(pre_up, approximate=False).astype(jnp.bfloat16)
    ffn_sum = lax.psum_scatter(
        dot_plain(activ, w_down).astype(jnp.bfloat16), "tp", scatter_dimension=0, tiled=True
    ).astype(jnp.float32)
    result = resid + ffn_sum + b_down.astype(jnp.float32)
    grad_rows = lax.all_gather(cotangent, "tp", axis=0, tiled=True)
    grad_w_down = dot_rows(activ, grad_rows)
    grad_activ = dot_back(grad_rows, w_down)
    _, gelu_back = jax.vjp(lambda inner: jax.nn.gelu(inner, approximate=False), pre_up)
    grad_pre = gelu_back(grad_activ)[0].astype(jnp.bfloat16)
    grad_w_up = dot_rows(mid_rows, grad_pre)
    grad_b_up = jnp.sum(grad_pre.astype(jnp.float32), axis=0)
    grad_mid = lax.psum_scatter(dot_back(grad_pre, w_up), "tp", scatter_dimension=0, tiled=True)
    _, norm_two_back = jax.vjp(layer_norm, resid, gain_two, shift_two)
    grad_resid_norm, grad_gain_two, grad_shift_two = norm_two_back(grad_mid)
    grad_resid = grad_out + grad_resid_norm
    grad_b_down = jnp.sum(grad_out, axis=0)
    grad_b_out = jnp.sum(grad_resid, axis=0)
    grad_branch = lax.all_gather(grad_resid.astype(jnp.bfloat16), "tp", axis=0, tiled=True)
    grad_w_out = dot_rows(attended, grad_branch)
    grad_attended = dot_back(grad_branch, w_out).astype(jnp.bfloat16)
    long_grads = attention_backward(
        queries[:split],
        key_rows[:split],
        value_rows[:split],
        grad_attended[:split],
        long_lengths,
        long_total,
        LEN_L,
    )
    short_grads = attention_backward(
        queries[split:],
        key_rows[split:],
        value_rows[split:],
        grad_attended[split:],
        short_lengths,
        short_total,
        LEN_S,
    )
    grad_queries = jnp.concatenate([long_grads[0], short_grads[0]], axis=0).astype(jnp.bfloat16)
    grad_keys = jnp.concatenate([long_grads[1], short_grads[1]], axis=0).astype(jnp.bfloat16)
    grad_values = jnp.concatenate([long_grads[2], short_grads[2]], axis=0).astype(jnp.bfloat16)
    grad_w_query = dot_rows(normed_in, grad_queries)
    grad_b_query = jnp.sum(grad_queries.astype(jnp.float32), axis=0)
    grad_w_key = dot_rows(normed_in, grad_keys)
    grad_w_value = dot_rows(normed_in, grad_values)
    grad_b_value = jnp.sum(grad_values.astype(jnp.float32), axis=0)
    grad_in = lax.psum_scatter(
        dot_back(grad_queries, w_query)
        + dot_back(grad_keys, w_key)
        + dot_back(grad_values, w_value),
        "tp",
        scatter_dimension=0,
        tiled=True,
    )
    _, norm_one_back = jax.vjp(layer_norm, own_tokens, gain_one, shift_one)
    grad_tokens_norm, grad_gain_one, grad_shift_one = norm_one_back(grad_in)
    grad_tokens = grad_resid + grad_tokens_norm
    summed = lax.psum(
        (
            grad_w_query,
            grad_b_query,
            grad_w_key,
            grad_w_value,
            grad_b_value,
            grad_w_out,
            grad_w_up,
            grad_b_up,
            grad_w_down,
        ),
        "dp",
    )
    shared = lax.psum(
        (grad_gain_one, grad_shift_one, grad_b_out, grad_gain_two, grad_shift_two, grad_b_down),
        ("dp", "tp"),
    )
    return (
        result.astype(jnp.bfloat16),
        grad_tokens,
        shared[0],
        shared[1],
        summed[0],
        summed[1],
        summed[2],
        summed[3],
        summed[4],
        summed[5],
        shared[2],
        shared[3],
        shared[4],
        summed[6],
        summed[7],
        summed[8],
        shared[5],
    )


def pick(*arrays):
    tokens, long_lengths, short_lengths, w_query, w_up = (arrays[i] for i in (0, 1, 2, 5, 14))
    fits = (
        lax.axis_size("tp") == 2
        and lax.axis_size("dp") == 16
        and long_lengths.shape[0] == 2
        and short_lengths.shape[0] == 8
        and tokens.shape == (2 * LEN_L + 8 * LEN_S, 768)
        and w_query.shape[1] == 8 * HEAD_DIM
        and w_up.shape[1] == 1536
    )
    return by_images(*arrays) if fits else local(*arrays)


def solution(mesh):
    placed = (
        P("dp", None),
        P("dp"),
        P("dp"),
        P(),
        P(),
        P(None, "tp"),
        P("tp"),
        P(None, "tp"),
        P(None, "tp"),
        P("tp"),
        P("tp", None),
        P(),
        P(),
        P(),
        P(None, "tp"),
        P("tp"),
        P("tp", None),
        P(),
        P(("dp", "tp"), None),
    )
    return jax.shard_map(
        pick,
        mesh=mesh,
        in_specs=placed,
        out_specs=(
            P(("dp", "tp"), None),
            P(("dp", "tp"), None),
            P(),
            P(),
            P(None, "tp"),
            P("tp"),
            P(None, "tp"),
            P(None, "tp"),
            P("tp"),
            P("tp", None),
            P(),
            P(),
            P(),
            P(None, "tp"),
            P("tp"),
            P("tp", None),
            P(),
        ),
        check_vma=False,
    )
```

```python
import functools
import math

import jax
import jax.numpy as jnp
from jax import lax
from jax.experimental import pallas as pl
from jax.experimental.pallas import tpu as pltpu
from jax.sharding import PartitionSpec as P

HEAD_DIM = 48
LEN_L = 1024
LEN_S = 256
F32 = jnp.float32
BF16 = jnp.bfloat16
LOG2E = math.log2(math.e)
SCALE = HEAD_DIM ** (-0.5)
VMEM_LIMIT = 60 << 20
HEAD_GROUP = 2


def contract(left, right, left_dim, right_dim):
    return lax.dot_general(
        left, right, (((left_dim,), (right_dim,)), ((), ())), preferred_element_type=F32
    )


def params():
    return pltpu.CompilerParams(vmem_limit_bytes=VMEM_LIMIT)


def cost(flops, bytes_accessed, transcendentals=0):
    return pl.CostEstimate(
        flops=int(flops), bytes_accessed=int(bytes_accessed), transcendentals=int(transcendentals)
    )


def whole(shape):
    zeros = (0,) * len(shape)
    return pl.BlockSpec(shape, lambda *_: zeros)


def norm_parts(values):
    center = values - jnp.mean(values, axis=-1, keepdims=True)
    inv = lax.rsqrt(jnp.mean(center * center, axis=-1, keepdims=True) + 1e-06)
    return center * inv, inv


def norm_back(hat, inv, grad_hat):
    mean_grad = jnp.mean(grad_hat, axis=-1, keepdims=True)
    mean_both = jnp.mean(grad_hat * hat, axis=-1, keepdims=True)
    return inv * (grad_hat - mean_grad - hat * mean_both)


def three_terms(value):
    high = value.astype(BF16).astype(F32)
    rest = value - high
    mid = rest.astype(BF16).astype(F32)
    return [high, mid, rest - mid]


def extra_rows(rows, count):
    at = lax.broadcasted_iota(jnp.int32, (16, count), 0)
    out = jnp.zeros((16, count), F32)
    for place, row in enumerate(rows):
        out = jnp.where(at == place, row, out)
    return out.astype(BF16)


def scaled_query(query):
    wide = query.astype(F32) * (SCALE * LOG2E)
    high = wide.astype(BF16)
    return [high, (wide - high.astype(F32)).astype(BF16)]


def pair_count(heads, rows):
    return heads * (LEN_L**2 + (rows - LEN_L) * LEN_S)


class Place:
    def __init__(self):
        me = lax.axis_index("dp")
        self.core, self.x, self.z = me % 2, (me // 2) % 2, me // 4
        self.rank = lax.axis_index("tp")

    def at(self, z=None, x=None, core=None):
        z = self.z if z is None else z
        x = self.x if x is None else x
        core = self.core if core is None else core
        return {"dp": (z * 2 + x) * 2 + core}

    def across_core(self):
        return self.at(core=1 - self.core)

    def across_x(self):
        return self.at(x=1 - self.x)

    def along_z(self, step):
        return self.at(z=(self.z + step) % 4)

    def partner(self):
        return {"tp": 1 - self.rank}

    def greet(self):
        barrier = pltpu.get_barrier_semaphore()
        others = [self.across_core(), self.across_x(), self.partner()]
        others += [self.along_z(step) for step in (1, 2, 3)]
        for other in others:
            pl.semaphore_signal(
                barrier, inc=1, device_id=other, device_id_type=pl.DeviceIdType.MESH
            )
        pl.semaphore_wait(barrier, len(others))


def send_to(source, target, send, recv, device):
    return pltpu.make_async_remote_copy(
        src_ref=source,
        dst_ref=target,
        send_sem=send,
        recv_sem=recv,
        device_id=device,
        device_id_type=pl.DeviceIdType.MESH,
    )


def part(ref, start, count):
    return ref.at[pl.ds(pl.multiple_of(start, 16), count)]


def add_rows(target, start, count, terms):
    tile = 48 if count % 48 == 0 else 32

    def body(i, _):
        at = pl.multiple_of(i * tile, 16)
        here = pl.ds(pl.multiple_of(start + at, 16), tile)
        total = target[here, :].astype(F32)
        for term in terms:
            total = total + term[pl.ds(at, tile), :].astype(F32)
        target[here, :] = total.astype(BF16)
        return 0

    lax.fori_loop(0, count // tile, body, 0)


class PlaneSum:
    def __init__(self, place, own, seen, out, refs):
        self.place, self.own, self.seen, self.out = place, own, seen, out
        (self.acc, self.seen_here, self.from_core, self.from_x, self.from_z, self.whole,
         self.send, self.recv, self.local) = refs
        self.rows = own.shape[0]

    @staticmethod
    def buffers(rows, width):
        return [
            pltpu.VMEM((rows // 2, width), BF16),
            pltpu.VMEM((rows // 2, width), BF16),
            pltpu.VMEM((rows // 2, width), BF16),
            pltpu.VMEM((rows // 4, width), BF16),
            pltpu.VMEM((3, rows // 16, width), BF16),
            pltpu.VMEM((rows // 2, width), BF16),
            pltpu.SemaphoreType.DMA((10,)),
            pltpu.SemaphoreType.DMA((10,)),
            pltpu.SemaphoreType.DMA((4,)),
        ]

    def copy(self, source, target, place, device):
        return send_to(source, target, self.send.at[place], self.recv.at[place], device)

    def core_copy(self):
        half = self.rows // 2
        source = part(self.own, (1 - self.place.core) * half, half)
        return self.copy(source, self.from_core, 0, self.place.across_core())

    def local_copies(self):
        half = self.rows // 2
        source = part(self.own, self.place.core * half, half)
        copies = [pltpu.make_async_copy(source, self.acc, self.local.at[0])]
        if self.seen is not None:
            copies.append(pltpu.make_async_copy(self.seen, self.seen_here, self.local.at[1]))
        return copies

    def x_copy(self):
        count = self.rows // 4
        source = part(self.acc, (1 - self.place.x) * count, count)
        return self.copy(source, self.from_x, 1, self.place.across_x())

    def z_copies(self):
        count = self.rows // 16
        copies = []
        for step in (1, 2, 3):
            there = (self.place.z + step) % 4
            source = part(self.acc, self.place.x * 4 * count + there * count, count)
            target = self.from_z.at[step - 1]
            copies.append(self.copy(source, target, 1 + step, self.place.along_z(step)))
        return copies

    def piece(self):
        count = self.rows // 16
        inside = self.place.x * 4 * count + self.place.z * count
        return part(self.acc, inside, count), part(self.whole, inside, count)

    def keep_copy(self):
        mine, there = self.piece()
        return pltpu.make_async_copy(mine, there, self.local.at[2])

    def back_z_copies(self):
        mine, there = self.piece()
        return [
            self.copy(mine, there, 4 + step, self.place.along_z(step)) for step in (1, 2, 3)
        ]

    def back_x_copy(self):
        count = self.rows // 4
        there = part(self.whole, self.place.x * count, count)
        return self.copy(there, there, 8, self.place.across_x())

    def back_core_copy(self):
        count = self.rows // 2
        there = part(self.out, self.place.core * count, count)
        return self.copy(self.whole, there, 9, self.place.across_core())

    def store_copy(self):
        count = self.rows // 2
        there = part(self.out, self.place.core * count, count)
        return pltpu.make_async_copy(self.whole, there, self.local.at[3])

    def begin(self):
        self.core_copy().start()
        for copy in self.local_copies():
            copy.start()

    def along_x(self):
        self.core_copy().wait()
        for copy in self.local_copies():
            copy.wait()
        add_rows(self.acc, 0, self.rows // 2, [self.from_core, self.seen_here])
        self.x_copy().start()

    def along_z(self):
        self.x_copy().wait()
        count = self.rows // 4
        add_rows(self.acc, self.place.x * count, count, [self.from_x])
        for copy in self.z_copies():
            copy.start()

    def back_along_z(self):
        for copy in self.z_copies():
            copy.wait()
        count = self.rows // 16
        inside = self.place.x * 4 * count + self.place.z * count
        add_rows(self.acc, inside, count, [self.from_z.at[i] for i in range(3)])
        self.keep_copy().start()
        for copy in self.back_z_copies():
            copy.start()

    def back_along_x(self):
        self.keep_copy().wait()
        for copy in self.back_z_copies():
            copy.wait()
        self.back_x_copy().start()

    def back_to_core(self):
        self.back_x_copy().wait()
        self.back_core_copy().start()
        self.store_copy().start()

    def end(self):
        self.back_core_copy().wait()
        self.store_copy().wait()


class PartnerTerm:
    def __init__(self, place, other, seen, refs):
        self.place, self.other, self.seen = place, other, seen
        self.from_core, self.send, self.recv = refs
        self.half = other.shape[0] // 2

    @staticmethod
    def buffers(rows, width):
        return [
            pltpu.VMEM((rows // 2, width), BF16),
            pltpu.SemaphoreType.DMA((2,)),
            pltpu.SemaphoreType.DMA((2,)),
        ]

    def core_copy(self):
        source = part(self.other, (1 - self.place.core) * self.half, self.half)
        return send_to(
            source, self.from_core, self.send.at[0], self.recv.at[0], self.place.across_core()
        )

    def partner_copy(self):
        return send_to(
            self.from_core, self.seen, self.send.at[1], self.recv.at[1], self.place.partner()
        )

    def begin(self):
        self.core_copy().start()

    def to_partner(self):
        self.core_copy().wait()
        mine = part(self.other, self.place.core * self.half, self.half)
        add_rows(self.from_core, 0, self.half, [mine])
        self.partner_copy().start()

    def end(self):
        self.partner_copy().wait()


class SmallSum:
    ROWS = 16

    def __init__(self, place, own, other, refs):
        self.place, self.own, self.other = place, own, other
        self.sums, self.got, self.send, self.recv = refs

    @staticmethod
    def buffers(width):
        rows = SmallSum.ROWS
        return [
            pltpu.VMEM((3, rows, width), F32),
            pltpu.VMEM((6, rows, width), F32),
            pltpu.SemaphoreType.DMA((6,)),
            pltpu.SemaphoreType.DMA((6,)),
        ]

    def copy(self, source, place, device):
        return send_to(source, self.got.at[place], self.send.at[place], self.recv.at[place], device)

    def partner_copy(self):
        return self.copy(self.other, 0, self.place.partner())

    def core_copy(self):
        return self.copy(self.sums.at[0], 1, self.place.across_core())

    def x_copy(self):
        return self.copy(self.sums.at[1], 2, self.place.across_x())

    def z_copies(self):
        return [
            self.copy(self.sums.at[2], 2 + step, self.place.along_z(step)) for step in (1, 2, 3)
        ]

    def begin(self):
        self.partner_copy().start()

    def over_cores(self):
        self.partner_copy().wait()
        self.sums[0] = self.own[...] + self.got[0]
        self.core_copy().start()

    def over_x(self):
        self.core_copy().wait()
        self.sums[1] = self.sums[0] + self.got[1]
        self.x_copy().start()

    def over_z(self):
        self.x_copy().wait()
        self.sums[2] = self.sums[1] + self.got[2]
        for copy in self.z_copies():
            copy.start()

    def end(self):
        for copy in self.z_copies():
            copy.wait()
        return self.sums[2] + self.got[3] + self.got[4] + self.got[5]


class Fetch:
    def __init__(self, place, own, got, refs, deep):
        self.place, self.own, self.got, self.deep = place, own, got, deep
        self.send, self.recv = refs
        self.half = own.shape[0] // 2
        self.quarter = self.half // 2
        self.count = self.quarter // 2 if deep else self.quarter
        self.core_at = place.core * self.half
        self.x_at = self.core_at + place.x * self.quarter
        odd = place.z % 2
        self.at = self.x_at + odd * self.count if deep else self.x_at
        self.z_at = self.x_at + (1 - odd) * self.count
        self.z_device = place.at(z=place.z + 1 - 2 * odd)

    @staticmethod
    def buffers():
        return [pltpu.SemaphoreType.DMA((5,)), pltpu.SemaphoreType.DMA((5,))]

    def copy(self, source, start, count, place, device):
        there = part(self.got, start, count)
        here = part(source, start, count)
        return send_to(here, there, self.send.at[place], self.recv.at[place], device)

    def partner_copy(self):
        return self.copy(self.own, self.at, self.count, 0, self.place.partner())

    def z_copy(self):
        return self.copy(self.got, self.at, self.count, 1, self.z_device)

    def x_copies(self):
        copies = [self.copy(self.got, self.at, self.count, 2, self.place.across_x())]
        if self.deep:
            copies.append(self.copy(self.got, self.z_at, self.count, 3, self.place.across_x()))
        return copies

    def core_copy(self):
        return self.copy(self.got, self.core_at, self.half, 4, self.place.across_core())

    def begin(self):
        self.partner_copy().start()

    def share(self):
        self.partner_copy().wait()
        if self.deep:
            self.z_copy().start()
        self.x_copies()[0].start()

    def more_x(self):
        self.z_copy().wait()
        self.x_copies()[1].start()

    def to_core(self):
        for copy in self.x_copies():
            copy.wait()
        self.core_copy().start()

    def end(self):
        self.core_copy().wait()


FRONT_BLOCK = 512


def front_kernel(
    mask_ref, gain_ref, shift_ref, bout_ref, gain2_ref, shift2_ref, bias_ref,
    tok_hbm, wq_hbm, wk_hbm, wv_hbm, wout_hbm, wup_hbm, wdown_hbm, cot_hbm,
    x_out, qkv_out, att_out, log_out, resid_out, mid_out,
    cat_hbm, wout_all_hbm, up2_hbm, down2_hbm, grads_hbm, bias2_hbm, tok_out,
    tok_ref, x_ref, qkv_ref, att_ref, cat_ref, wout_ref, bias2_ref, up2_ref, down2_ref, grads_ref,
    load_sem, out_sem, swap_send, swap_recv, *scratch, heads, block,
):
    step = pl.program_id(0)
    place = Place()
    half = heads * HEAD_DIM
    rows = tok_ref.shape[0]
    blocks = rows // FRONT_BLOCK
    pairs = heads // HEAD_GROUP
    base = [0, blocks, blocks + pairs, 2 * blocks + pairs, 2 * blocks + 2 * pairs]

    sems = [scratch[2 * i : 2 * i + 2] for i in range(6)]
    mine = [wq_hbm, wk_hbm, wv_hbm]
    projections = [
        Fetch(place, own, cat_ref.at[1, :, pl.ds(i * half, half)], sems[i], False)
        for i, own in enumerate(mine)
    ]
    fetch_out = Fetch(place, wout_hbm, wout_ref.at[pl.ds(half, half)], sems[3], False)
    fetch_up = Fetch(place, wup_hbm, up2_ref, sems[4], True)
    fetch_down = Fetch(place, wdown_hbm, down2_ref, sems[5], True)
    bias_copy = send_to(
        bias_ref, bias2_ref, swap_send.at[0], swap_recv.at[0], place.partner()
    )
    here = pl.ds(pl.multiple_of(place.rank * LEN_L, LEN_L), LEN_L)
    theirs = pl.ds(pl.multiple_of((1 - place.rank) * LEN_L, LEN_L), LEN_L)
    cot_copy = send_to(
        cot_hbm.at[theirs], grads_ref.at[here], swap_send.at[1], swap_recv.at[1], place.partner()
    )

    def token_rows(i):
        start = pl.multiple_of(i * 2 * LEN_L + place.rank * LEN_L, LEN_L)
        return tok_hbm.at[pl.ds(start, LEN_L)]

    token_loads = [
        pltpu.make_async_copy(token_rows(i), tok_ref.at[pl.ds(i * LEN_L, LEN_L)], load_sem.at[i])
        for i in (0, 1)
    ]
    weight_loads = [
        pltpu.make_async_copy(
            own, cat_ref.at[0, :, pl.ds(i * half, half)], load_sem.at[2 + i]
        )
        for i, own in enumerate(mine)
    ]
    out_load = pltpu.make_async_copy(wout_hbm, wout_ref.at[pl.ds(0, half)], load_sem.at[5])
    kept_copy = pltpu.make_async_copy(cot_hbm.at[here], grads_ref.at[here], out_sem.at[0])
    stores = [
        pltpu.make_async_copy(cat_ref, cat_hbm, out_sem.at[1]),
        pltpu.make_async_copy(wout_ref, wout_all_hbm, out_sem.at[2]),
        pltpu.make_async_copy(bias2_ref, bias2_hbm, out_sem.at[3]),
        pltpu.make_async_copy(tok_ref, tok_out, out_sem.at[4]),
    ]
    last_stores = [
        pltpu.make_async_copy(grads_ref, grads_hbm, out_sem.at[5]),
        pltpu.make_async_copy(up2_ref, up2_hbm, out_sem.at[6]),
        pltpu.make_async_copy(down2_ref, down2_hbm, out_sem.at[7]),
    ]

    @pl.when(step == 0)
    def _():
        for copy in (*token_loads, *weight_loads, out_load):
            copy.start()
        place.greet()
        for one in projections:
            one.begin()
        bias_copy.start()
        fetch_out.begin()
        for copy in token_loads:
            copy.wait()
        for copy in weight_loads:
            copy.wait()

    def at_step(when):
        return pl.when(step == when)

    @at_step(base[1] - 1)
    def _():
        fetch_up.begin()
        fetch_down.begin()

    @at_step(base[1] + 1)
    def _():
        for one in (*projections, fetch_out):
            one.share()

    @at_step(base[2] - 1)
    def _():
        for one in (*projections, fetch_out):
            one.to_core()

    @at_step(base[2])
    def _():
        for one in (*projections, fetch_out):
            one.end()
        bias_copy.wait()
        out_load.wait()
        for copy in stores:
            copy.start()
        kept_copy.start()
        fetch_up.share()
        fetch_down.share()
        cot_copy.start()

    @at_step(base[3] + 2)
    def _():
        fetch_up.more_x()
        fetch_down.more_x()

    @at_step(base[4] + 2)
    def _():
        fetch_up.to_core()
        fetch_down.to_core()

    def project(which, i, bias):
        at = pl.ds(pl.multiple_of(i * FRONT_BLOCK, FRONT_BLOCK), FRONT_BLOCK)
        column = jnp.transpose(bias[:, : 3 * half])[:, :1]
        value = (contract(cat_ref[which], x_ref[at, :], 0, 1) + column).astype(BF16)
        qkv_ref[:, at] = value
        qkv_out[0] = value

    @pl.when(step < base[1])
    def _():
        at = pl.ds(pl.multiple_of(step * FRONT_BLOCK, FRONT_BLOCK), FRONT_BLOCK)
        hat, _ = norm_parts(tok_ref[at, :].astype(F32))
        normed = (hat * gain_ref[...] + shift_ref[...]).astype(BF16)
        x_ref[at, :] = normed
        x_out[...] = normed
        project(0, step, bias_ref[...])

    @pl.when(jnp.logical_and(step >= base[2], step < base[3]))
    def _():
        project(1, step - base[2], bias2_ref[...])

    own_part = jnp.logical_and(step >= base[1], step < base[2])
    other_part = jnp.logical_and(step >= base[3], step < base[4])

    @pl.when(jnp.logical_or(own_part, other_part))
    def _():
        second = (step >= base[3]).astype(jnp.int32)
        pair = step - base[1] - second * (base[3] - base[1])
        attend_pair(mask_ref, qkv_ref, att_ref, att_out, log_out, pair, second, heads, block)

    @pl.when(step >= base[4])
    def _():
        i = step - base[4]
        at = pl.ds(pl.multiple_of(i * FRONT_BLOCK, FRONT_BLOCK), FRONT_BLOCK)
        product = contract(att_ref[:, at], wout_ref[...], 0, 0)
        resid = tok_ref[at, :].astype(F32) + product + bout_ref[...]
        resid_out[...] = resid
        hat, _ = norm_parts(resid)
        mid_out[...] = (hat * gain2_ref[...] + shift2_ref[...]).astype(BF16)

    @pl.when(step == base[4] + blocks - 1)
    def _():
        for one in (fetch_up, fetch_down):
            one.end()
        for copy in last_stores[1:]:
            copy.start()
        cot_copy.wait()
        kept_copy.wait()
        last_stores[0].start()
        for copy in (*stores, *last_stores):
            copy.wait()


def attend_pair(mask_ref, qkv_ref, att_ref, att_out, log_out, pair, second, heads, block):
    rows = qkv_ref.shape[1]
    half = heads * HEAD_DIM
    first = pair * HEAD_GROUP
    work = []
    for head in range(HEAD_GROUP):
        work += [(head, 0, LEN_L, at, block) for at in range(0, LEN_L, block)]
        work += [(head, start, LEN_S, 0, LEN_S) for start in range(LEN_L, rows, LEN_S)]

    def load(which, head, columns):
        start = pl.multiple_of(which * half + (first + head) * HEAD_DIM, HEAD_DIM)
        return qkv_ref[pl.ds(start, HEAD_DIM), columns]

    def scores(item):
        head, start, count, at, size = item
        every = slice(start, start + count)
        keys = load(1, head, every)
        key_rows = jnp.concatenate([keys, keys, extra_rows([mask_ref[:, every]], count)], 0)
        query = scaled_query(load(0, head, slice(start + at, start + at + size)))
        query_rows = jnp.concatenate([*query, jnp.ones((16, size), BF16)], 0)
        return contract(key_rows, query_rows, 0, 0)

    def finish(item, score):
        head, start, count, at, size = item
        here = slice(start + at, start + at + size)
        values = load(2, head, slice(start, start + count))
        value_rows = jnp.concatenate([values, jnp.ones((16, count), BF16)], 0)
        top = jnp.max(score, axis=0, keepdims=True)
        weights = jnp.exp2(score - top).astype(BF16)
        mixed = contract(value_rows, weights, 1, 0)
        total = mixed[HEAD_DIM : HEAD_DIM + 1]
        result = (mixed[:HEAD_DIM] * (1.0 / total)).astype(BF16)
        att_out[0, head, :, here] = result
        start = pl.multiple_of(second * half + (first + head) * HEAD_DIM, HEAD_DIM)
        att_ref[pl.ds(start, HEAD_DIM), here] = result
        log_out[0, head, :, here] = top + jnp.log2(total)

    score = scores(work[0])
    for place, item in enumerate(work):
        later = scores(work[place + 1]) if place + 1 < len(work) else None
        finish(item, score)
        score = later


def front(
    mask, gain, shift, b_out, gain2, shift2, bias, tokens, w_query, w_key, w_value, w_out, w_up,
    w_down, cotangent, heads, block=1024,
):
    width = tokens.shape[1]
    rows = tokens.shape[0] // 2
    half = heads * HEAD_DIM
    hidden = w_up.shape[1]
    blocks, pairs = rows // FRONT_BLOCK, heads // HEAD_GROUP
    base = [0, blocks, blocks + pairs, 2 * blocks + pairs, 2 * blocks + 2 * pairs]
    anywhere = pl.BlockSpec(memory_space=pl.ANY)

    def row_block(first):
        return lambda s: (jnp.clip(s - first, 0, blocks - 1), 0)

    def qkv_block(s):
        late = (s >= base[2]).astype(jnp.int32)
        return late, 0, jnp.clip(s - late * base[2], 0, blocks - 1)

    def head_block(s):
        late = (s >= base[3]).astype(jnp.int32)
        return late, jnp.clip(s - base[1] - late * (base[3] - base[1]), 0, pairs - 1), 0, 0

    by_row = lambda first: pl.BlockSpec((FRONT_BLOCK, width), row_block(first))
    bias_rows, bias_width = bias.shape
    pair_total = pair_count(2 * heads, rows)
    return pl.pallas_call(
        functools.partial(front_kernel, heads=heads, block=block),
        grid=(base[4] + blocks,),
        in_specs=[
            whole((1, rows)),
            *(whole((1, width)) for _ in range(5)),
            whole(bias.shape),
        ]
        + [anywhere] * 8,
        out_specs=[
            by_row(0),
            pl.BlockSpec((1, 3 * half, FRONT_BLOCK), qkv_block),
            pl.BlockSpec((1, HEAD_GROUP, HEAD_DIM, rows), head_block),
            pl.BlockSpec((1, HEAD_GROUP, 1, rows), head_block),
            by_row(base[4]),
            by_row(base[4]),
        ]
        + [anywhere] * 7,
        out_shape=[
            jax.ShapeDtypeStruct((rows, width), BF16),
            jax.ShapeDtypeStruct((2, 3 * half, rows), BF16),
            jax.ShapeDtypeStruct((2, heads, HEAD_DIM, rows), BF16),
            jax.ShapeDtypeStruct((2, heads, 1, rows), F32),
            jax.ShapeDtypeStruct((rows, width), F32),
            jax.ShapeDtypeStruct((rows, width), BF16),
            jax.ShapeDtypeStruct((2, width, 3 * half), BF16),
            jax.ShapeDtypeStruct((2 * half, width), BF16),
            jax.ShapeDtypeStruct((width, hidden), BF16),
            jax.ShapeDtypeStruct((hidden, width), BF16),
            jax.ShapeDtypeStruct((rows, width), BF16),
            jax.ShapeDtypeStruct((bias_rows, bias_width), F32),
            jax.ShapeDtypeStruct((rows, width), BF16),
        ],
        scratch_shapes=[
            pltpu.VMEM((rows, width), BF16),
            pltpu.VMEM((rows, width), BF16),
            pltpu.VMEM((3 * half, rows), BF16),
            pltpu.VMEM((2 * half, rows), BF16),
            pltpu.VMEM((2, width, 3 * half), BF16),
            pltpu.VMEM((2 * half, width), BF16),
            pltpu.VMEM((bias_rows, bias_width), F32),
            pltpu.VMEM((width, hidden), BF16),
            pltpu.VMEM((hidden, width), BF16),
            pltpu.VMEM((rows, width), BF16),
            pltpu.SemaphoreType.DMA((6,)),
            pltpu.SemaphoreType.DMA((8,)),
            pltpu.SemaphoreType.DMA((2,)),
            pltpu.SemaphoreType.DMA((2,)),
        ]
        + [ref for _ in range(6) for ref in Fetch.buffers()],
        compiler_params=pltpu.CompilerParams(
            vmem_limit_bytes=VMEM_LIMIT, collective_id=1, has_side_effects=True
        ),
        cost_estimate=cost(
            pair_total * 2 * 512 + 14 * rows * width * half, 40 * rows * width, pair_total
        ),
        name="front",
    )(
        mask, gain, shift, b_out, gain2, shift2, bias, tokens, w_query, w_key, w_value, w_out,
        w_up, w_down, cotangent,
    )


ERFC_TERMS = (0.254829592, -0.284496736, 1.421413741, -1.453152027, 1.061405429)
ERFC_SLOPE = 0.3275911


def gelu_and_slope(value):
    bell = jnp.exp2(value * value * (-0.5 * LOG2E))
    base = 1.0 + jnp.abs(value) * (ERFC_SLOPE * math.sqrt(0.5))
    ratio = 1.0 / base
    poly = ERFC_TERMS[4] * 0.5
    for term in ERFC_TERMS[3::-1]:
        poly = poly * ratio + term * 0.5
    tail = poly * ratio * bell
    below = jnp.where(value < 0.0, tail, 1.0 - tail)
    return value * below, below + value * bell * (1.0 / math.sqrt(2.0 * math.pi))


HIDDEN_BLOCK = 512
MID_BLOCK = 512
MID_CHUNK = 512


def mid_kernel(
    mid_ref, grad_ref, bias_ref, resid_ref, gain_ref, bdown_ref, w_ref, att_ref,
    up2_hbm, up_hbm, down2_hbm, down_hbm,
    out_ref, gresid_ref, gatt_ref, dw_own_ref, dw_other_ref, small_ref, db_ref,
    dup_hbm, ddown_hbm, seen_up, seen_down,
    sum_ref, gmid_ref, act_ref, gpre_ref, up_ref, down_ref, dup_ref, ddown_ref, acc_ref,
    load_sem, store_sem, *scratch, blocks,
):
    step = pl.program_id(0)
    place = Place()
    rows, width = mid_ref.shape
    cut = lambda ref, i: ref.at[:, pl.ds(i * HIDDEN_BLOCK, HIDDEN_BLOCK)]
    take = lambda ref, i, count: ref.at[pl.ds(i * count, count)]
    terms = []
    for i in range(blocks):
        refs = [scratch[6 * i : 6 * i + 3], scratch[6 * i + 3 : 6 * i + 6]]
        terms.append(
            (
                PartnerTerm(place, dup_ref.at[i], cut(seen_up, i), refs[0]),
                PartnerTerm(
                    place, ddown_ref.at[i], take(seen_down, i, HIDDEN_BLOCK // 2), refs[1]
                ),
            )
        )

    def loads(at):
        up, down = (up2_hbm, down2_hbm) if at < blocks else (up_hbm, down_hbm)
        i, slot = at % blocks, at % 2
        return [
            pltpu.make_async_copy(cut(up, i), up_ref.at[slot], load_sem.at[slot, 0]),
            pltpu.make_async_copy(
                take(down, i, HIDDEN_BLOCK), down_ref.at[slot], load_sem.at[slot, 1]
            ),
        ]

    def stores(i):
        return [
            pltpu.make_async_copy(dup_ref.at[i], cut(dup_hbm, i), store_sem.at[i, 0]),
            pltpu.make_async_copy(
                ddown_ref.at[i], take(ddown_hbm, i, HIDDEN_BLOCK), store_sem.at[i, 1]
            ),
        ]

    for at in range(2 * blocks + 1):

        @pl.when(step == at)
        def _(at=at):
            if at == 0:
                for copy in loads(0):
                    copy.start()
                place.greet()
                sum_ref[...] = jnp.zeros_like(sum_ref)
                gmid_ref[...] = jnp.zeros_like(gmid_ref)
            if at < 2 * blocks:
                for copy in loads(at):
                    copy.wait()
            if at + 1 < 2 * blocks:
                for copy in loads(at + 1):
                    copy.start()
            if 2 <= at < blocks + 2:
                for one in terms[at - 2]:
                    one.to_partner()
            if 1 <= at < blocks + 1:
                for one in terms[at - 1]:
                    one.begin()
            if at > blocks:
                for copy in stores(at - blocks - 1):
                    copy.start()
            if at == 2 * blocks:
                acc_ref[...] = jnp.zeros_like(acc_ref)
                small_ref[...] = jnp.zeros_like(small_ref)

    @pl.when(step < 2 * blocks)
    def _():
        up, down, bias = up_ref[step % 2], down_ref[step % 2], bias_ref[0]

        def products(at):
            here = slice(at, at + MID_CHUNK)
            return (
                contract(mid_ref[here], up, 1, 0) + bias,
                contract(grad_ref[here], down, 1, 1),
            )

        now = products(0)
        db = None
        for at in range(0, rows, MID_CHUNK):
            here = slice(at, at + MID_CHUNK)
            later = products(at + MID_CHUNK) if at + MID_CHUNK < rows else None
            value, slope = gelu_and_slope(now[0])
            act = value.astype(BF16)
            gpre = (slope * now[1]).astype(BF16)
            act_ref[here] = act
            gpre_ref[here] = gpre
            term = jnp.sum(gpre.astype(F32), axis=0, keepdims=True)
            db = term if db is None else db + term
            sum_ref[here] += contract(act, down, 1, 0)
            gmid_ref[here] += contract(gpre, up, 1, 1)
            now = later
        db_ref[0] = db
        slot = lax.rem(step, blocks)
        ddown_ref[slot] = contract(act_ref[...], grad_ref[...], 0, 0).astype(BF16)
        dup_ref[slot] = contract(mid_ref[...], gpre_ref[...], 0, 0).astype(BF16)

    @pl.when(step >= 2 * blocks)
    def _():
        start = (step - 2 * blocks) * MID_BLOCK
        here = pl.ds(pl.multiple_of(start, MID_BLOCK), MID_BLOCK)
        resid = resid_ref[...]
        grads = grad_ref[here, :].astype(F32)
        out_ref[...] = (resid + sum_ref[here, :] + bdown_ref[...]).astype(BF16)
        gmid = gmid_ref[here, :]
        hat, inv = norm_parts(resid)
        gresid = grads + norm_back(hat, inv, gmid * gain_ref[...])
        gresid_ref[...] = gresid
        branch = gresid.astype(BF16)
        gatt_ref[...] = contract(w_ref[...], branch, 1, 1).astype(BF16)
        acc_ref[...] += contract(branch, att_ref[...], 0, 1)
        small_ref[0:1] += jnp.sum(gmid * hat, axis=0, keepdims=True)
        small_ref[1:2] += jnp.sum(gmid, axis=0, keepdims=True)
        small_ref[2:3] += jnp.sum(gresid, axis=0, keepdims=True)
        small_ref[3:4] += jnp.sum(grads, axis=0, keepdims=True)

    @pl.when(step == pl.num_programs(0) - 1)
    def _():
        half = dw_own_ref.shape[1]
        dw_own_ref[...] = acc_ref[:, :half].astype(BF16)
        dw_other_ref[...] = acc_ref[:, half:].astype(BF16)
        for i in range(blocks):
            for copy in stores(i):
                copy.wait()
            for one in terms[i]:
                one.end()


def mid_part(mid, grads, biases, resid, gain, b_down, w_out, attended, up2, up, down2, down):
    rows, width = mid.shape
    hidden = up.shape[1]
    blocks = hidden // HIDDEN_BLOCK
    first = 2 * blocks
    heads_width = attended.shape[0]
    anywhere = pl.BlockSpec(memory_space=pl.ANY)
    once = lambda shape: pl.BlockSpec(
        shape, lambda *_: (0,) * len(shape), pipeline_mode=pl.Buffered(1)
    )
    row_step = lambda s: jnp.maximum(s - first, 0)
    by_row = pl.BlockSpec((MID_BLOCK, width), lambda s: (row_step(s), 0))
    columns = pl.BlockSpec((heads_width, MID_BLOCK), lambda s: (0, row_step(s)))
    by_hidden = pl.BlockSpec((1, 1, HIDDEN_BLOCK), lambda s: (jnp.minimum(s, first - 1), 0, 0))
    half = (width, heads_width // 2)
    scratch = [
        pltpu.VMEM((rows, width), F32),
        pltpu.VMEM((rows, width), F32),
        pltpu.VMEM((rows, HIDDEN_BLOCK), BF16),
        pltpu.VMEM((rows, HIDDEN_BLOCK), BF16),
        pltpu.VMEM((2, width, HIDDEN_BLOCK), BF16),
        pltpu.VMEM((2, HIDDEN_BLOCK, width), BF16),
        pltpu.VMEM((blocks, width, HIDDEN_BLOCK), BF16),
        pltpu.VMEM((blocks, HIDDEN_BLOCK, width), BF16),
        pltpu.VMEM((width, heads_width), F32),
        pltpu.SemaphoreType.DMA((2, 2)),
        pltpu.SemaphoreType.DMA((blocks, 2)),
    ]
    for _ in range(blocks):
        scratch += PartnerTerm.buffers(width, HIDDEN_BLOCK)
        scratch += PartnerTerm.buffers(HIDDEN_BLOCK, width)
    return pl.pallas_call(
        functools.partial(mid_kernel, blocks=blocks),
        grid=(first + rows // MID_BLOCK,),
        in_specs=[
            once((rows, width)), once((rows, width)), by_hidden, by_row, whole((1, width)),
            whole((1, width)), once((heads_width, width)), columns,
        ]
        + [anywhere] * 4,
        out_specs=[
            by_row, by_row, columns, whole(half), whole(half), whole((8, width)), by_hidden,
        ]
        + [anywhere] * 4,
        out_shape=[
            jax.ShapeDtypeStruct((rows, width), BF16),
            jax.ShapeDtypeStruct((rows, width), F32),
            jax.ShapeDtypeStruct((heads_width, rows), BF16),
            jax.ShapeDtypeStruct(half, BF16),
            jax.ShapeDtypeStruct(half, BF16),
            jax.ShapeDtypeStruct((8, width), F32),
            jax.ShapeDtypeStruct((first, 1, HIDDEN_BLOCK), F32),
            jax.ShapeDtypeStruct((width, hidden), BF16),
            jax.ShapeDtypeStruct((hidden, width), BF16),
            jax.ShapeDtypeStruct((width // 2, hidden), BF16),
            jax.ShapeDtypeStruct((hidden // 2, width), BF16),
        ],
        scratch_shapes=scratch,
        compiler_params=pltpu.CompilerParams(
            vmem_limit_bytes=VMEM_LIMIT, collective_id=2, has_side_effects=True
        ),
        cost_estimate=cost(
            24 * rows * width * hidden + 4 * rows * width * heads_width, 60 * rows * width,
            4 * rows * hidden,
        ),
        name="mid",
    )(mid, grads, biases, resid, gain, b_down, w_out, attended, up2, up, down2, down)


TAIL_BLOCK = 512
SUM_ACTIONS = ("begin", "along_x", "along_z", "back_along_z", "back_along_x", "back_to_core")
SUM_STEPS = (
    (0, 1, 4, 11, 14, 16),
    (0, 3, 6, 13, 15, 17),
    (0, 5, 8, 14, 16, 18),
    (0, 6, 9, 15, 17, 19),
    (0, 8, 10, 17, 19, 20),
    (0, 10, 12, 16, 18, 20),
    (None, 17, 19),
    (None, 17, 20),
    (None, 17),
)
LAST_ACTIONS = (
    (8, "along_z"), 0, (6, "back_along_z"), 1, (7, "back_along_z"), 2,
    (8, "back_along_z"), (6, "back_along_x"), (7, "back_along_x"), (8, "back_along_x"),
    (6, "back_to_core"), (7, "back_to_core"), (8, "back_to_core"),
)


def tail_kernel(
    mask_ref, qkv_ref, att_ref, log_ref, gatt_ref, gain_ref, small2_ref, dbup1_ref, dbup2_ref,
    wout2_ref, x_hbm, w_hbm, tok_hbm, gresid_hbm, up_hbm, down_hbm, wout_hbm, seen_up,
    seen_down, out_hbm,
    gtok_ref, small_ref, got_hbm, gup_hbm, gdown_hbm, gout_hbm, gcat_hbm, got_out,
    d_ref, x_ref, w_ref, tok_ref, gresid_ref, dw_ref, dw2_ref, seen_cat, sent_ref, own_small,
    other_small, load_sem, row_sem, tok_send, tok_recv, *scratch, heads, block,
):
    step = pl.program_id(0)
    place = Place()
    first_rows = 2 * heads + 1
    last_step = first_rows + 3
    width = x_ref.shape[1]
    half = heads * HEAD_DIM
    halves = width

    groups = []
    at = 0
    for count in [9] * 9 + [3, 3, 4]:
        groups.append(scratch[at : at + count])
        at += count
    columns = lambda ref, i: ref.at[:, pl.ds(i * halves, halves)]
    rows_of = lambda ref, i, count: ref.at[pl.ds(i * count, count)]
    sums = [
        PlaneSum(place, columns(up_hbm, i), columns(seen_up, i), columns(gup_hbm, i), groups[i])
        for i in (0, 1)
    ]
    down_rows = HIDDEN_BLOCK
    sums += [
        PlaneSum(
            place,
            rows_of(down_hbm, i, down_rows),
            rows_of(seen_down, i, down_rows // 2),
            rows_of(gdown_hbm, i, down_rows),
            groups[2 + i],
        )
        for i in range(3)
    ]
    sums.append(PlaneSum(place, wout_hbm, None, gout_hbm, groups[5]))
    third = lambda ref, i: ref.at[:, pl.ds(i * half, half)]
    cat_sums = [
        PlaneSum(
            place, third(dw_ref, i), None, third(gcat_hbm, i),
            (groups[6 + i][0], third(seen_cat, i), *groups[6 + i][2:]),
        )
        for i in range(3)
    ]
    cat_term = PartnerTerm(place, dw2_ref, seen_cat, groups[9])
    out_term = PartnerTerm(place, wout2_ref, groups[5][1], groups[10])
    small = SmallSum(place, own_small, other_small, groups[11])
    theirs = pl.ds(pl.multiple_of((1 - place.rank) * LEN_L, LEN_L), LEN_L)
    out_load = pltpu.make_async_copy(out_hbm.at[theirs], sent_ref, load_sem.at[2])
    out_copy = send_to(sent_ref, got_out, tok_send.at[2], tok_recv.at[2], place.partner())

    loads = [
        pltpu.make_async_copy(x_hbm, x_ref, load_sem.at[0]),
        pltpu.make_async_copy(w_hbm, w_ref, load_sem.at[1]),
    ]

    def row_start(i):
        mine = i // 2
        return ((1 - mine) * (1 - place.rank) + mine * place.rank) * LEN_L + (i % 2) * TAIL_BLOCK

    def row_loads(i):
        start = pl.ds(pl.multiple_of(row_start(i), TAIL_BLOCK), TAIL_BLOCK)
        slot = i % 2
        return [
            pltpu.make_async_copy(tok_hbm.at[start], tok_ref.at[slot], row_sem.at[slot, 0]),
            pltpu.make_async_copy(gresid_hbm.at[start], gresid_ref.at[slot], row_sem.at[slot, 1]),
        ]

    def token_copy(i):
        there = pl.ds(i * TAIL_BLOCK, TAIL_BLOCK)
        return send_to(
            sent_ref.at[there], got_hbm.at[there], tok_send.at[i], tok_recv.at[i], place.partner()
        )

    def weight_gradient(source, target, i):
        here = pl.ds(i * half, half)
        product = contract(x_ref[...], d_ref[source, here, :], 0, 1)
        target[:, here] = product.astype(BF16)

    def bias_rows(source, target):
        ones = jnp.ones((16, d_ref.shape[2]), BF16)
        for i, which in ((0, 0), (1, 2)):
            row = contract(ones, d_ref[source, pl.ds(which * half, half), :], 1, 1)
            target[8:9, pl.ds(i * half, half)] = row[:1]

    events = {}
    sums += cat_sums
    for one, times in zip(sums, SUM_STEPS):
        for when, action in zip(times, SUM_ACTIONS):
            if when is None:
                continue
            events.setdefault(when, []).append(getattr(one, action))

    for when in sorted(events):

        @pl.when(step == when)
        def _(when=when):
            if when == 0:
                out_load.start()
                place.greet()
                out_term.begin()
            if when == 1:
                out_term.to_partner()
                out_load.wait()
                out_copy.start()
            if when == 4:
                out_term.end()
            for action in events[when]:
                action()

    @pl.when(step == 2)
    def _():
        for copy in loads:
            copy.start()

    @pl.when(step == heads)
    def _():
        for copy in loads:
            copy.wait()
        for i in range(3):
            weight_gradient(1, dw2_ref, i)
        cat_term.begin()

    @pl.when(step == heads + 1)
    def _():
        cat_term.to_partner()
        own_small[...] = jnp.zeros_like(own_small)
        other_small[...] = jnp.zeros_like(other_small)
        bias_rows(1, other_small)

    @pl.when(step < 2 * heads)
    def _():
        back_one_head(mask_ref, qkv_ref, att_ref, log_ref, gatt_ref, d_ref, step, heads, block)

    @pl.when(step == 2 * heads)
    def _():
        for copy in row_loads(0):
            copy.start()
        cat_term.end()
        out_copy.wait()
        for i in range(3):
            weight_gradient(0, dw_ref, i)
            cat_sums[i].begin()
        bias_rows(0, own_small)


    for i in range(4):

        @pl.when(step == first_rows + i)
        def _(i=i):
            for copy in row_loads(i):
                copy.wait()
            if i < 3:
                for copy in row_loads(i + 1):
                    copy.start()
            here = pl.ds(pl.multiple_of(row_start(i), TAIL_BLOCK), TAIL_BLOCK)
            gin = contract(d_ref[0, :, here], w_ref[0], 0, 1)
            gin += contract(d_ref[1, :, here], w_ref[1], 0, 1)
            hat, inv = norm_parts(tok_ref[i % 2].astype(F32))
            gtok = gresid_ref[i % 2] + norm_back(hat, inv, gin * gain_ref[...])
            own_small[0:1] += jnp.sum(gin * hat, axis=0, keepdims=True)
            own_small[1:2] += jnp.sum(gin, axis=0, keepdims=True)
            if i < 2:
                sent_ref[pl.ds(i * TAIL_BLOCK, TAIL_BLOCK), :] = gtok.astype(BF16)
                token_copy(i).start()
            else:
                gtok_ref[...] = gtok

    @pl.when(step == last_step)
    def _():
        own_small[2:6] = small2_ref[0:4]
        other_small[0:2] = own_small[0:2]
        other_small[2:6] = small2_ref[0:4]
        for i in (0, 1):
            own_small[6 + i : 7 + i] = dbup1_ref[:, pl.ds(i * width, width)]
            other_small[6 + i : 7 + i] = dbup2_ref[:, pl.ds(i * width, width)]
        small.begin()
        small_actions = (small.over_cores, small.over_x, small.over_z)
        for item in LAST_ACTIONS:
            if isinstance(item, int):
                small_actions[item]()
            else:
                getattr(sums[item[0]], item[1])()
        small_ref[...] = small.end()
        for i in (0, 1):
            token_copy(i).wait()
        for one in sums:
            one.end()


def back_one_head(mask_ref, qkv_ref, att_ref, log_ref, gatt_ref, d_ref, step, heads, block):
    rows = qkv_ref.shape[4]
    half = heads * HEAD_DIM
    source = 1 - step // heads
    head_at = pl.multiple_of((step % heads) * HEAD_DIM, HEAD_DIM)

    def store(which, columns, value):
        d_ref[source, pl.ds(which * half + head_at, HEAD_DIM), columns] = value.astype(BF16)

    work = []
    images = [(0, LEN_L, block)] + [(at, LEN_S, LEN_S) for at in range(LEN_L, rows, LEN_S)]
    for start, count, size in images:
        work += [(start, count, at, size) for at in range(start, start + count, size)]
    kept = {}

    def operands(start, count):
        if start not in kept:
            every = slice(start, start + count)
            keys = qkv_ref[0, 1, 0, :, every]
            values = qkv_ref[0, 2, 0, :, every]
            ones = jnp.ones((1, count), F32)
            key_rows = jnp.concatenate(
                [keys, keys, extra_rows([ones, ones, ones, mask_ref[:, every]], count)], 0
            )
            value_rows = jnp.concatenate([values, extra_rows([ones, ones, ones], count)], 0)
            kept[start] = keys, key_rows, value_rows
        return kept[start]

    def products(item):
        start, count, at, size = item
        here = slice(at, at + size)
        _, key_rows, value_rows = operands(start, count)
        query = qkv_ref[0, 0, 0, :, here]
        grads = gatt_ref[0, 0, :, here]
        inner = jnp.sum(
            grads.astype(F32) * att_ref[0, 0, :, here].astype(F32), axis=0, keepdims=True
        )
        terms = three_terms(-log_ref[0, 0, :, here]) + [jnp.ones((1, size), F32)]
        query_rows = jnp.concatenate([*scaled_query(query), extra_rows(terms, size)], 0)
        grad_rows = jnp.concatenate([grads, extra_rows(three_terms(-inner), size)], 0)
        return contract(query_rows, key_rows, 0, 0), contract(grad_rows, value_rows, 0, 0)

    sums = {}
    now = products(work[0])
    for place, item in enumerate(work):
        later = products(work[place + 1]) if place + 1 < len(work) else None
        start, count, at, size = item
        here = slice(at, at + size)
        keys = operands(start, count)[0]
        query = qkv_ref[0, 0, 0, :, here]
        grads = gatt_ref[0, 0, :, here]
        score, grad_probs = now
        probs = jnp.exp2(score)
        grad_score = (probs * grad_probs).astype(BF16)
        part_values = contract(grads, probs.astype(BF16), 1, 0)
        part_keys = contract(query, grad_score, 1, 0)
        store(0, here, contract(keys, grad_score, 1, 1) * SCALE)
        if start in sums:
            part_keys, part_values = sums[start][0] + part_keys, sums[start][1] + part_values
        sums[start] = part_keys, part_values
        if at + size == start + count:
            every = slice(start, start + count)
            store(1, every, part_keys * SCALE)
            store(2, every, part_values)
        now = later


def tail(
    mask, qkv, att, log_total, gatt, gain, small2, dbup1, dbup2, dwout2, normed, w_cat,
    tokens, gresid, dup, ddown, dwout, seen_up, seen_down, out_rows, block=256,
):
    _, _, heads, _, rows = qkv.shape
    _, width, out = w_cat.shape
    anywhere = pl.BlockSpec(memory_space=pl.ANY)
    last = 2 * heads - 1

    def head(h):
        h = jnp.minimum(h, last)
        return 1 - h // heads, h % heads

    all_three = pl.BlockSpec(
        (1, 3, 1, HEAD_DIM, rows), lambda h: (head(h)[0], 0, head(h)[1], 0, 0)
    )
    one = pl.BlockSpec((1, 1, HEAD_DIM, rows), lambda h: (*head(h), 0, 0))
    row = pl.BlockSpec((1, 1, 1, rows), lambda h: (*head(h), 0, 0))
    sum_shapes = [(width, width)] * 2 + [(HIDDEN_BLOCK, width)] * 3 + [dwout.shape] + [(width, out // 3)] * 3
    scratch = [
        pltpu.VMEM((2, out, rows), BF16),
        pltpu.VMEM((rows, width), BF16),
        pltpu.VMEM((2, width, out), BF16),
        pltpu.VMEM((2, TAIL_BLOCK, width), BF16),
        pltpu.VMEM((2, TAIL_BLOCK, width), F32),
        pltpu.VMEM((width, out), BF16),
        pltpu.VMEM((width, out), BF16),
        pltpu.VMEM((width // 2, out), BF16),
        pltpu.VMEM((rows // 2, width), BF16),
        pltpu.VMEM((SmallSum.ROWS, width), F32),
        pltpu.VMEM((SmallSum.ROWS, width), F32),
        pltpu.SemaphoreType.DMA((3,)),
        pltpu.SemaphoreType.DMA((2, 2)),
        pltpu.SemaphoreType.DMA((3,)),
        pltpu.SemaphoreType.DMA((3,)),
    ]
    for shape in sum_shapes:
        scratch += PlaneSum.buffers(*shape)
    scratch += PartnerTerm.buffers(width, out) + PartnerTerm.buffers(*dwout.shape)
    scratch += SmallSum.buffers(width)
    pairs = pair_count(2 * heads, rows)
    first_rows = 2 * heads + 1
    return pl.pallas_call(
        functools.partial(tail_kernel, heads=heads, block=block),
        grid=(first_rows + 4,),
        in_specs=[
            whole((1, rows)), all_three, one, row, one, whole((1, width)), whole((8, width)),
            whole((1, 2 * width)), whole((1, 2 * width)), whole(dwout.shape),
        ]
        + [anywhere] * 10,
        out_specs=[
            pl.BlockSpec(
                (TAIL_BLOCK, width), lambda h: (jnp.maximum(h - first_rows - 2, 0), 0)
            ),
            whole((SmallSum.ROWS, width)),
        ]
        + [anywhere] * 6,
        out_shape=[
            jax.ShapeDtypeStruct((rows // 2, width), F32),
            jax.ShapeDtypeStruct((SmallSum.ROWS, width), F32),
            jax.ShapeDtypeStruct((rows // 2, width), BF16),
            jax.ShapeDtypeStruct(dup.shape, BF16),
            jax.ShapeDtypeStruct(ddown.shape, BF16),
            jax.ShapeDtypeStruct(dwout.shape, BF16),
            jax.ShapeDtypeStruct((width, out), BF16),
            jax.ShapeDtypeStruct((rows // 2, width), BF16),
        ],
        scratch_shapes=scratch,
        compiler_params=pltpu.CompilerParams(
            vmem_limit_bytes=VMEM_LIMIT, collective_id=0, has_side_effects=True
        ),
        cost_estimate=cost(pairs * 5 * 512, 32 * heads * HEAD_DIM * rows, pairs),
        name="tail",
    )(
        mask, qkv, att, log_total, gatt, gain, small2, dbup1, dbup2, dwout2, normed, w_cat,
        tokens, gresid, dup, ddown, dwout, seen_up, seen_down, out_rows,
    )


def joined(mine, theirs, second):
    return jnp.where(second, jnp.concatenate([theirs, mine], 0), jnp.concatenate([mine, theirs], 0))


def half_of(array, second):
    size = array.shape[0] // 2
    return lax.dynamic_slice_in_dim(array, jnp.where(second, size, 0), size, 0)


def by_images(
    tokens, long_lengths, short_lengths, ln1_gain, ln1_bias, w_query, b_query, w_key, w_value,
    b_value, w_out, b_out, ln2_gain, ln2_bias, w_up, b_up, w_down, b_down, cotangent,
):
    rank = lax.axis_index("tp")
    rank_arr = jnp.reshape(rank, (1,)).astype(jnp.int32)
    second = rank == 1
    rows = tokens.shape[0] // 2
    width = tokens.shape[1]
    half = w_query.shape[1]
    heads = half // HEAD_DIM
    long_len = lax.dynamic_slice_in_dim(long_lengths, rank, 1, 0)
    shorts = short_lengths.shape[0] // 2
    short_len = lax.dynamic_slice_in_dim(short_lengths, rank * shorts, shorts, 0)
    valid = jnp.concatenate(
        [
            jnp.arange(LEN_L) < long_len[0],
            (jnp.arange(LEN_S)[None, :] < short_len[:, None]).reshape(-1),
        ]
    )
    mask = jnp.where(valid, 0.0, -1e30).astype(F32).reshape(1, -1)
    row = lambda vector: vector.astype(F32).reshape(1, -1)
    biases = jnp.concatenate([b_query, jnp.zeros_like(b_query), b_value, b_up]).astype(F32)
    bias = jnp.broadcast_to(biases.reshape(1, -1), (8, biases.shape[0]))

    (normed, qkv, att, log_total, resid, mid, w_cat, w_out_all, w_up2, w_down2, grads, bias2,
     own_tokens) = front(
        mask, row(ln1_gain), row(ln1_bias), row(b_out), row(ln2_gain), row(ln2_bias), bias,
        tokens, w_query, w_key, w_value, w_out, w_up, w_down, cotangent, heads,
    )
    qkv = qkv.reshape(2, 3, heads, HEAD_DIM, rows)
    attended = att.reshape(2 * half, rows)
    up_bias = jnp.concatenate([bias2[:1, 3 * half :], bias[:1, 3 * half :]], 1)
    (out, gresid, gatt, dwout1, dwout2, small2, db_up, dup1, ddown1, seen_up, seen_down) = mid_part(
        mid, grads, up_bias.reshape(-1, 1, HIDDEN_BLOCK), resid, row(ln2_gain), row(b_down),
        w_out_all, attended, w_up2, w_up, w_down2, w_down,
    )
    dbup2, dbup1 = db_up.reshape(2, 1, -1)
    gtok, small, got_tok, grad_up, grad_down, grad_out_t, grad_cat, got_out = tail(
        mask, qkv, att, log_total, gatt.reshape(2, heads, HEAD_DIM, rows), row(ln1_gain), small2,
        dbup1, dbup2, dwout2, normed, w_cat, own_tokens, gresid, dup1, ddown1, dwout1,
        seen_up, seen_down, out,
    )
    result = joined(half_of(out, second), got_out, second)
    grad_tokens = joined(gtok, got_tok.astype(F32), second)
    grad_cat = grad_cat.astype(F32)
    return (
        result,
        grad_tokens,
        small[0],
        small[1],
        grad_cat[:, :half],
        small[8, :half],
        grad_cat[:, half : 2 * half],
        grad_cat[:, 2 * half :],
        small[8, half:],
        grad_out_t.T.astype(F32),
        small[4],
        small[2],
        small[3],
        grad_up.astype(F32),
        small[6:8].reshape(-1),
        grad_down.astype(F32),
        small[5],
    )


def layer_norm(values, gain, shift):
    center = values - jnp.mean(values, axis=-1, keepdims=True)
    spread = jnp.mean(center * center, axis=-1, keepdims=True)
    return center * lax.rsqrt(spread + 1e-06) * gain + shift


def dot_plain(left, right):
    return jnp.dot(left, right, preferred_element_type=jnp.float32)


def dot_rows(left, right):
    return lax.dot_general(
        left, right, (((0,), (0,)), ((), ())), preferred_element_type=jnp.float32
    )


def dot_back(left, right):
    return lax.dot_general(
        left, right, (((1,), (1,)), ((), ())), preferred_element_type=jnp.float32
    )


def group_shape(image_count, seq_len, head_count):
    per_step = math.gcd(image_count, max(1, 512 // seq_len))
    return (image_count // per_step, per_step, seq_len, head_count, HEAD_DIM)


def masked_scores(query_blk, key_blk, length_blk):
    seq_len = query_blk.shape[1]
    raw = jnp.einsum(
        "bqhd,bkhd->bhqk", query_blk, key_blk, preferred_element_type=jnp.float32
    ) * HEAD_DIM ** (-0.5)
    keep = jnp.arange(seq_len, dtype=jnp.int32)[None, :] < length_blk[:, None]
    return jnp.where(keep[:, None, None, :], raw, -1e30)


def attention_forward(queries, key_rows, value_rows, lengths, seq_len):
    image_count = lengths.shape[0]
    head_count = queries.shape[1] // HEAD_DIM
    block_shape = group_shape(image_count, seq_len, head_count)

    def one_step(block):
        query_blk, key_blk, value_blk, length_blk = block
        scores = masked_scores(query_blk, key_blk, length_blk)
        row_top = jnp.max(scores, axis=-1, keepdims=True)
        exp_terms = jnp.exp(scores - row_top)
        row_total = jnp.sum(exp_terms, axis=-1, keepdims=True)
        weights = (exp_terms / row_total).astype(jnp.bfloat16)
        mixed = jnp.einsum(
            "bhqk,bkhd->bqhd", weights, value_blk, preferred_element_type=jnp.float32
        )
        return (mixed, (row_top + jnp.log(row_total))[..., 0])

    mixed, log_total = lax.map(
        one_step,
        (
            queries.reshape(block_shape),
            key_rows.reshape(block_shape),
            value_rows.reshape(block_shape),
            lengths.reshape(block_shape[:2]),
        ),
    )
    return (mixed.reshape(image_count * seq_len, head_count * HEAD_DIM), log_total)


def attention_backward(queries, key_rows, value_rows, grads, lengths, log_total, seq_len):
    image_count = lengths.shape[0]
    head_count = queries.shape[1] // HEAD_DIM
    block_shape = group_shape(image_count, seq_len, head_count)
    scale = HEAD_DIM ** (-0.5)

    def one_step(block):
        query_blk, key_blk, value_blk, grad_blk, length_blk, total_blk = block
        scores = masked_scores(query_blk, key_blk, length_blk)
        probs = jnp.exp(scores - total_blk[..., None])
        grad_values = jnp.einsum(
            "bhqk,bqhd->bkhd",
            probs.astype(jnp.bfloat16),
            grad_blk,
            preferred_element_type=jnp.float32,
        )
        grad_probs = jnp.einsum(
            "bqhd,bkhd->bhqk", grad_blk, value_blk, preferred_element_type=jnp.float32
        )
        inner = jnp.sum(probs * grad_probs, axis=-1, keepdims=True)
        grad_scores = (probs * (grad_probs - inner)).astype(jnp.bfloat16)
        grad_queries = (
            jnp.einsum("bhqk,bkhd->bqhd", grad_scores, key_blk, preferred_element_type=jnp.float32)
            * scale
        )
        grad_keys = (
            jnp.einsum(
                "bhqk,bqhd->bkhd", grad_scores, query_blk, preferred_element_type=jnp.float32
            )
            * scale
        )
        return (grad_queries, grad_keys, grad_values)

    results = lax.map(
        one_step,
        (
            queries.reshape(block_shape),
            key_rows.reshape(block_shape),
            value_rows.reshape(block_shape),
            grads.reshape(block_shape),
            lengths.reshape(block_shape[:2]),
            log_total,
        ),
    )
    flat = (image_count * seq_len, head_count * HEAD_DIM)
    return tuple((item.reshape(flat) for item in results))


def local(
    tokens,
    long_lengths,
    short_lengths,
    ln1_gain,
    ln1_bias,
    w_query,
    b_query,
    w_key,
    w_value,
    b_value,
    w_out,
    b_out,
    ln2_gain,
    ln2_bias,
    w_up,
    b_up,
    w_down,
    b_down,
    cotangent,
):
    tp_count = lax.axis_size("tp")
    tp_rank = lax.axis_index("tp")
    row_count = tokens.shape[0]
    share = row_count // tp_count
    split = long_lengths.shape[0] * LEN_L
    gain_one = ln1_gain.astype(jnp.float32)
    shift_one = ln1_bias.astype(jnp.float32)
    gain_two = ln2_gain.astype(jnp.float32)
    shift_two = ln2_bias.astype(jnp.float32)
    normed_in = layer_norm(tokens.astype(jnp.float32), gain_one, shift_one).astype(jnp.bfloat16)
    queries = (dot_plain(normed_in, w_query) + b_query.astype(jnp.float32)).astype(jnp.bfloat16)
    key_rows = dot_plain(normed_in, w_key).astype(jnp.bfloat16)
    value_rows = (dot_plain(normed_in, w_value) + b_value.astype(jnp.float32)).astype(jnp.bfloat16)
    long_mixed, long_total = attention_forward(
        queries[:split], key_rows[:split], value_rows[:split], long_lengths, LEN_L
    )
    short_mixed, short_total = attention_forward(
        queries[split:], key_rows[split:], value_rows[split:], short_lengths, LEN_S
    )
    attended = jnp.concatenate([long_mixed, short_mixed], axis=0).astype(jnp.bfloat16)
    attn_sum = lax.psum_scatter(dot_plain(attended, w_out), "tp", scatter_dimension=0, tiled=True)
    own_tokens = lax.dynamic_slice_in_dim(tokens, tp_rank * share, share, 0).astype(jnp.float32)
    resid = own_tokens + attn_sum + b_out.astype(jnp.float32)
    normed_mid = layer_norm(resid, gain_two, shift_two).astype(jnp.bfloat16)
    grad_out = cotangent.astype(jnp.float32)
    mid_rows = lax.all_gather(normed_mid, "tp", axis=0, tiled=True)
    pre_up = dot_plain(mid_rows, w_up) + b_up.astype(jnp.float32)
    activ = jax.nn.gelu(pre_up, approximate=False).astype(jnp.bfloat16)
    ffn_sum = lax.psum_scatter(
        dot_plain(activ, w_down).astype(jnp.bfloat16), "tp", scatter_dimension=0, tiled=True
    ).astype(jnp.float32)
    result = resid + ffn_sum + b_down.astype(jnp.float32)
    grad_rows = lax.all_gather(cotangent, "tp", axis=0, tiled=True)
    grad_w_down = dot_rows(activ, grad_rows)
    grad_activ = dot_back(grad_rows, w_down)
    _, gelu_back = jax.vjp(lambda inner: jax.nn.gelu(inner, approximate=False), pre_up)
    grad_pre = gelu_back(grad_activ)[0].astype(jnp.bfloat16)
    grad_w_up = dot_rows(mid_rows, grad_pre)
    grad_b_up = jnp.sum(grad_pre.astype(jnp.float32), axis=0)
    grad_mid = lax.psum_scatter(dot_back(grad_pre, w_up), "tp", scatter_dimension=0, tiled=True)
    _, norm_two_back = jax.vjp(layer_norm, resid, gain_two, shift_two)
    grad_resid_norm, grad_gain_two, grad_shift_two = norm_two_back(grad_mid)
    grad_resid = grad_out + grad_resid_norm
    grad_b_down = jnp.sum(grad_out, axis=0)
    grad_b_out = jnp.sum(grad_resid, axis=0)
    grad_branch = lax.all_gather(grad_resid.astype(jnp.bfloat16), "tp", axis=0, tiled=True)
    grad_w_out = dot_rows(attended, grad_branch)
    grad_attended = dot_back(grad_branch, w_out).astype(jnp.bfloat16)
    long_grads = attention_backward(
        queries[:split],
        key_rows[:split],
        value_rows[:split],
        grad_attended[:split],
        long_lengths,
        long_total,
        LEN_L,
    )
    short_grads = attention_backward(
        queries[split:],
        key_rows[split:],
        value_rows[split:],
        grad_attended[split:],
        short_lengths,
        short_total,
        LEN_S,
    )
    grad_queries = jnp.concatenate([long_grads[0], short_grads[0]], axis=0).astype(jnp.bfloat16)
    grad_keys = jnp.concatenate([long_grads[1], short_grads[1]], axis=0).astype(jnp.bfloat16)
    grad_values = jnp.concatenate([long_grads[2], short_grads[2]], axis=0).astype(jnp.bfloat16)
    grad_w_query = dot_rows(normed_in, grad_queries)
    grad_b_query = jnp.sum(grad_queries.astype(jnp.float32), axis=0)
    grad_w_key = dot_rows(normed_in, grad_keys)
    grad_w_value = dot_rows(normed_in, grad_values)
    grad_b_value = jnp.sum(grad_values.astype(jnp.float32), axis=0)
    grad_in = lax.psum_scatter(
        dot_back(grad_queries, w_query)
        + dot_back(grad_keys, w_key)
        + dot_back(grad_values, w_value),
        "tp",
        scatter_dimension=0,
        tiled=True,
    )
    _, norm_one_back = jax.vjp(layer_norm, own_tokens, gain_one, shift_one)
    grad_tokens_norm, grad_gain_one, grad_shift_one = norm_one_back(grad_in)
    grad_tokens = grad_resid + grad_tokens_norm
    summed = lax.psum(
        (
            grad_w_query,
            grad_b_query,
            grad_w_key,
            grad_w_value,
            grad_b_value,
            grad_w_out,
            grad_w_up,
            grad_b_up,
            grad_w_down,
        ),
        "dp",
    )
    shared = lax.psum(
        (grad_gain_one, grad_shift_one, grad_b_out, grad_gain_two, grad_shift_two, grad_b_down),
        ("dp", "tp"),
    )
    return (
        result.astype(jnp.bfloat16),
        grad_tokens,
        shared[0],
        shared[1],
        summed[0],
        summed[1],
        summed[2],
        summed[3],
        summed[4],
        summed[5],
        shared[2],
        shared[3],
        shared[4],
        summed[6],
        summed[7],
        summed[8],
        shared[5],
    )


def pick(*arrays):
    tokens, long_lengths, short_lengths, w_query, w_up = (arrays[i] for i in (0, 1, 2, 5, 14))
    fits = (
        lax.axis_size("tp") == 2
        and lax.axis_size("dp") == 16
        and long_lengths.shape[0] == 2
        and short_lengths.shape[0] == 8
        and tokens.shape == (2 * LEN_L + 8 * LEN_S, 768)
        and w_query.shape[1] == 8 * HEAD_DIM
        and w_up.shape[1] == 1536
    )
    return by_images(*arrays) if fits else local(*arrays)


def solution(mesh):
    placed = (
        P("dp", None),
        P("dp"),
        P("dp"),
        P(),
        P(),
        P(None, "tp"),
        P("tp"),
        P(None, "tp"),
        P(None, "tp"),
        P("tp"),
        P("tp", None),
        P(),
        P(),
        P(),
        P(None, "tp"),
        P("tp"),
        P("tp", None),
        P(),
        P(("dp", "tp"), None),
    )
    return jax.shard_map(
        pick,
        mesh=mesh,
        in_specs=placed,
        out_specs=(
            P(("dp", "tp"), None),
            P(("dp", "tp"), None),
            P(),
            P(),
            P(None, "tp"),
            P("tp"),
            P(None, "tp"),
            P(None, "tp"),
            P("tp"),
            P("tp", None),
            P(),
            P(),
            P(),
            P(None, "tp"),
            P("tp"),
            P("tp", None),
            P(),
        ),
        check_vma=False,
    )
```

```python
import functools
import math

import jax
import jax.numpy as jnp
from jax import lax
from jax.experimental import pallas as pl
from jax.experimental.pallas import tpu as pltpu
from jax.sharding import PartitionSpec as P

HEAD_DIM = 48
LEN_L = 1024
LEN_S = 256
F32 = jnp.float32
BF16 = jnp.bfloat16
LOG2E = math.log2(math.e)
SCALE = HEAD_DIM ** (-0.5)
VMEM_LIMIT = 60 << 20
HEAD_GROUP = 2


def contract(left, right, left_dim, right_dim):
    return lax.dot_general(
        left, right, (((left_dim,), (right_dim,)), ((), ())), preferred_element_type=F32
    )


def params():
    return pltpu.CompilerParams(vmem_limit_bytes=VMEM_LIMIT)


def cost(flops, bytes_accessed, transcendentals=0):
    return pl.CostEstimate(
        flops=int(flops), bytes_accessed=int(bytes_accessed), transcendentals=int(transcendentals)
    )


def whole(shape):
    zeros = (0,) * len(shape)
    return pl.BlockSpec(shape, lambda *_: zeros)


def norm_parts(values):
    center = values - jnp.mean(values, axis=-1, keepdims=True)
    inv = lax.rsqrt(jnp.mean(center * center, axis=-1, keepdims=True) + 1e-06)
    return center * inv, inv


def norm_back(hat, inv, grad_hat):
    mean_grad = jnp.mean(grad_hat, axis=-1, keepdims=True)
    mean_both = jnp.mean(grad_hat * hat, axis=-1, keepdims=True)
    return inv * (grad_hat - mean_grad - hat * mean_both)


def three_terms(value):
    high = value.astype(BF16).astype(F32)
    rest = value - high
    mid = rest.astype(BF16).astype(F32)
    return [high, mid, rest - mid]


def extra_rows(rows, count):
    at = lax.broadcasted_iota(jnp.int32, (16, count), 0)
    out = jnp.zeros((16, count), F32)
    for place, row in enumerate(rows):
        out = jnp.where(at == place, row, out)
    return out.astype(BF16)


def scaled_query(query):
    wide = query.astype(F32) * (SCALE * LOG2E)
    high = wide.astype(BF16)
    return [high, (wide - high.astype(F32)).astype(BF16)]


def pair_count(heads, rows):
    return heads * (LEN_L**2 + (rows - LEN_L) * LEN_S)


class Place:
    def __init__(self):
        me = lax.axis_index("dp")
        self.core, self.x, self.z = me % 2, (me // 2) % 2, me // 4
        self.rank = lax.axis_index("tp")

    def at(self, z=None, x=None, core=None):
        z = self.z if z is None else z
        x = self.x if x is None else x
        core = self.core if core is None else core
        return {"dp": (z * 2 + x) * 2 + core}

    def across_core(self):
        return self.at(core=1 - self.core)

    def across_x(self):
        return self.at(x=1 - self.x)

    def along_z(self, step):
        return self.at(z=(self.z + step) % 4)

    def partner(self):
        return {"tp": 1 - self.rank}

    def greet(self):
        barrier = pltpu.get_barrier_semaphore()
        others = [self.across_core(), self.across_x(), self.partner()]
        others += [self.along_z(step) for step in (1, 2, 3)]
        for other in others:
            pl.semaphore_signal(
                barrier, inc=1, device_id=other, device_id_type=pl.DeviceIdType.MESH
            )
        pl.semaphore_wait(barrier, len(others))


def send_to(source, target, send, recv, device):
    return pltpu.make_async_remote_copy(
        src_ref=source,
        dst_ref=target,
        send_sem=send,
        recv_sem=recv,
        device_id=device,
        device_id_type=pl.DeviceIdType.MESH,
    )


def part(ref, start, count):
    return ref.at[pl.ds(pl.multiple_of(start, 16), count)]


def add_rows(target, start, count, terms):
    tile = 48 if count % 48 == 0 else 32

    def body(i, _):
        at = pl.multiple_of(i * tile, 16)
        here = pl.ds(pl.multiple_of(start + at, 16), tile)
        total = target[here, :].astype(F32)
        for term in terms:
            total = total + term[pl.ds(at, tile), :].astype(F32)
        target[here, :] = total.astype(BF16)
        return 0

    lax.fori_loop(0, count // tile, body, 0)


class PlaneSum:
    def __init__(self, place, own, seen, out, refs):
        self.place, self.own, self.seen, self.out = place, own, seen, out
        (self.acc, self.seen_here, self.from_core, self.from_x, self.from_z, self.whole,
         self.send, self.recv, self.local) = refs
        self.rows = own.shape[0]

    @staticmethod
    def buffers(rows, width):
        return [
            pltpu.VMEM((rows // 2, width), BF16),
            pltpu.VMEM((rows // 2, width), BF16),
            pltpu.VMEM((rows // 2, width), BF16),
            pltpu.VMEM((rows // 4, width), BF16),
            pltpu.VMEM((3, rows // 16, width), BF16),
            pltpu.VMEM((rows // 2, width), BF16),
            pltpu.SemaphoreType.DMA((10,)),
            pltpu.SemaphoreType.DMA((10,)),
            pltpu.SemaphoreType.DMA((4,)),
        ]

    def copy(self, source, target, place, device):
        return send_to(source, target, self.send.at[place], self.recv.at[place], device)

    def core_copy(self):
        half = self.rows // 2
        source = part(self.own, (1 - self.place.core) * half, half)
        return self.copy(source, self.from_core, 0, self.place.across_core())

    def local_copies(self):
        half = self.rows // 2
        source = part(self.own, self.place.core * half, half)
        copies = [pltpu.make_async_copy(source, self.acc, self.local.at[0])]
        if self.seen is not None:
            copies.append(pltpu.make_async_copy(self.seen, self.seen_here, self.local.at[1]))
        return copies

    def x_copy(self):
        count = self.rows // 4
        source = part(self.acc, (1 - self.place.x) * count, count)
        return self.copy(source, self.from_x, 1, self.place.across_x())

    def z_copies(self):
        count = self.rows // 16
        copies = []
        for step in (1, 2, 3):
            there = (self.place.z + step) % 4
            source = part(self.acc, self.place.x * 4 * count + there * count, count)
            target = self.from_z.at[step - 1]
            copies.append(self.copy(source, target, 1 + step, self.place.along_z(step)))
        return copies

    def piece(self):
        count = self.rows // 16
        inside = self.place.x * 4 * count + self.place.z * count
        return part(self.acc, inside, count), part(self.whole, inside, count)

    def keep_copy(self):
        mine, there = self.piece()
        return pltpu.make_async_copy(mine, there, self.local.at[2])

    def back_z_copies(self):
        mine, there = self.piece()
        return [
            self.copy(mine, there, 4 + step, self.place.along_z(step)) for step in (1, 2, 3)
        ]

    def back_x_copy(self):
        count = self.rows // 4
        there = part(self.whole, self.place.x * count, count)
        return self.copy(there, there, 8, self.place.across_x())

    def back_core_copy(self):
        count = self.rows // 2
        there = part(self.out, self.place.core * count, count)
        return self.copy(self.whole, there, 9, self.place.across_core())

    def store_copy(self):
        count = self.rows // 2
        there = part(self.out, self.place.core * count, count)
        return pltpu.make_async_copy(self.whole, there, self.local.at[3])

    def begin_own(self):
        self.core_copy().start()
        self.local_copies()[0].start()

    def begin_seen(self):
        for copy in self.local_copies()[1:]:
            copy.start()

    def begin(self):
        self.begin_own()
        self.begin_seen()

    def along_x(self):
        self.core_copy().wait()
        for copy in self.local_copies():
            copy.wait()
        add_rows(self.acc, 0, self.rows // 2, [self.from_core, self.seen_here])
        self.x_copy().start()

    def along_z(self):
        self.x_copy().wait()
        count = self.rows // 4
        add_rows(self.acc, self.place.x * count, count, [self.from_x])
        for copy in self.z_copies():
            copy.start()

    def back_along_z(self):
        for copy in self.z_copies():
            copy.wait()
        count = self.rows // 16
        inside = self.place.x * 4 * count + self.place.z * count
        add_rows(self.acc, inside, count, [self.from_z.at[i] for i in range(3)])
        self.keep_copy().start()
        for copy in self.back_z_copies():
            copy.start()

    def back_along_x(self):
        self.keep_copy().wait()
        for copy in self.back_z_copies():
            copy.wait()
        self.back_x_copy().start()

    def back_to_core(self):
        self.back_x_copy().wait()
        self.back_core_copy().start()
        self.store_copy().start()

    def end(self):
        self.back_core_copy().wait()
        self.store_copy().wait()


class PartnerTerm:
    def __init__(self, place, other, seen, refs):
        self.place, self.other, self.seen = place, other, seen
        self.from_core, self.send, self.recv = refs
        self.half = other.shape[0] // 2

    @staticmethod
    def buffers(rows, width):
        return [
            pltpu.VMEM((rows // 2, width), BF16),
            pltpu.SemaphoreType.DMA((2,)),
            pltpu.SemaphoreType.DMA((2,)),
        ]

    def core_copy(self):
        source = part(self.other, (1 - self.place.core) * self.half, self.half)
        return send_to(
            source, self.from_core, self.send.at[0], self.recv.at[0], self.place.across_core()
        )

    def partner_copy(self):
        return send_to(
            self.from_core, self.seen, self.send.at[1], self.recv.at[1], self.place.partner()
        )

    def begin(self):
        self.core_copy().start()

    def to_partner(self):
        self.core_copy().wait()
        mine = part(self.other, self.place.core * self.half, self.half)
        add_rows(self.from_core, 0, self.half, [mine])
        self.partner_copy().start()

    def end(self):
        self.partner_copy().wait()


class SmallSum:
    ROWS = 16

    def __init__(self, place, pair, refs):
        self.place, self.pair = place, pair
        self.sums, self.got, self.got_own, self.send, self.recv = refs

    @staticmethod
    def buffers(width):
        rows = SmallSum.ROWS
        return [
            pltpu.VMEM((3, 2, rows, width), F32),
            pltpu.VMEM((5, 2, rows, width), F32),
            pltpu.VMEM((rows, width), F32),
            pltpu.SemaphoreType.DMA((6,)),
            pltpu.SemaphoreType.DMA((6,)),
        ]

    def copy(self, source, place, device):
        return send_to(source, self.got.at[place], self.send.at[place], self.recv.at[place], device)

    def core_copy(self):
        return self.copy(self.pair, 0, self.place.across_core())

    def x_copy(self):
        return self.copy(self.sums.at[0], 1, self.place.across_x())

    def z_copies(self):
        return [
            self.copy(self.sums.at[1], 1 + step, self.place.along_z(step)) for step in (1, 2, 3)
        ]

    def partner_copy(self):
        return send_to(
            self.sums.at[2, 1], self.got_own, self.send.at[5], self.recv.at[5],
            self.place.partner(),
        )

    def begin(self):
        self.core_copy().start()

    def over_x(self):
        self.core_copy().wait()
        self.sums[0] = self.pair[...] + self.got[0]
        self.x_copy().start()

    def over_z(self):
        self.x_copy().wait()
        self.sums[1] = self.sums[0] + self.got[1]
        for copy in self.z_copies():
            copy.start()

    def over_tp(self):
        for copy in self.z_copies():
            copy.wait()
        self.sums[2] = self.sums[1] + self.got[2] + self.got[3] + self.got[4]
        self.partner_copy().start()

    def end(self):
        self.partner_copy().wait()
        return self.sums[2, 0] + self.got_own[...]


class Fetch:
    def __init__(self, place, own, got, refs, deep):
        self.place, self.own, self.got, self.deep = place, own, got, deep
        self.send, self.recv = refs
        self.half = own.shape[0] // 2
        self.quarter = self.half // 2
        self.count = self.quarter // 2 if deep else self.quarter
        self.core_at = place.core * self.half
        self.x_at = self.core_at + place.x * self.quarter
        odd = place.z % 2
        self.at = self.x_at + odd * self.count if deep else self.x_at
        self.z_at = self.x_at + (1 - odd) * self.count
        self.z_device = place.at(z=place.z + 1 - 2 * odd)

    @staticmethod
    def buffers():
        return [pltpu.SemaphoreType.DMA((5,)), pltpu.SemaphoreType.DMA((5,))]

    def copy(self, source, start, count, place, device):
        there = part(self.got, start, count)
        here = part(source, start, count)
        return send_to(here, there, self.send.at[place], self.recv.at[place], device)

    def partner_copy(self):
        return self.copy(self.own, self.at, self.count, 0, self.place.partner())

    def z_copy(self):
        return self.copy(self.got, self.at, self.count, 1, self.z_device)

    def x_copies(self):
        copies = [self.copy(self.got, self.at, self.count, 2, self.place.across_x())]
        if self.deep:
            copies.append(self.copy(self.got, self.z_at, self.count, 3, self.place.across_x()))
        return copies

    def core_copy(self):
        return self.copy(self.got, self.core_at, self.half, 4, self.place.across_core())

    def begin(self):
        self.partner_copy().start()

    def share(self):
        self.partner_copy().wait()
        if self.deep:
            self.z_copy().start()
        self.x_copies()[0].start()

    def more_x(self):
        self.z_copy().wait()
        self.x_copies()[1].start()

    def to_core(self):
        for copy in self.x_copies():
            copy.wait()
        self.core_copy().start()

    def end(self):
        self.core_copy().wait()


FRONT_BLOCK = 512


def front_kernel(
    mask_ref, vec_ref, bias_ref, tok_hbm, wq_hbm, wk_hbm, wv_hbm, wout_hbm, wup_hbm, wdown_hbm, cot_hbm,
    x_out, qkv_out, att_out, log_out, resid_out, mid_out,
    cat_hbm, wout_all_hbm, up2_hbm, down2_hbm, grads_hbm, bias2_hbm, tok_out,
    tok_ref, x_ref, qkv_ref, att_ref, cat_ref, wout_ref, bias2_ref, up2_ref, down2_ref, grads_ref,
    load_sem, out_sem, swap_send, swap_recv, *scratch, heads, block,
):
    step = pl.program_id(0)
    place = Place()
    gain_ref, shift_ref, bout_ref, gain2_ref, shift2_ref = (
        vec_ref.at[pl.ds(i, 1)] for i in range(5)
    )
    half = heads * HEAD_DIM
    rows = tok_ref.shape[0]
    blocks = rows // FRONT_BLOCK
    pairs = heads // HEAD_GROUP
    base = [0, blocks, blocks + pairs, 2 * blocks + pairs, 2 * blocks + 2 * pairs]

    sems = [scratch[2 * i : 2 * i + 2] for i in range(6)]
    mine = [wq_hbm, wk_hbm, wv_hbm]
    projections = [
        Fetch(place, own, cat_ref.at[1, :, pl.ds(i * half, half)], sems[i], False)
        for i, own in enumerate(mine)
    ]
    fetch_out = Fetch(place, wout_hbm, wout_ref.at[pl.ds(half, half)], sems[3], False)
    fetch_up = Fetch(place, wup_hbm, up2_ref, sems[4], True)
    fetch_down = Fetch(place, wdown_hbm, down2_ref, sems[5], True)
    bias_copy = send_to(
        bias_ref, bias2_ref, swap_send.at[0], swap_recv.at[0], place.partner()
    )
    here = pl.ds(pl.multiple_of(place.rank * LEN_L, LEN_L), LEN_L)
    theirs = pl.ds(pl.multiple_of((1 - place.rank) * LEN_L, LEN_L), LEN_L)
    cot_copy = send_to(
        cot_hbm.at[theirs], grads_ref.at[here], swap_send.at[1], swap_recv.at[1], place.partner()
    )

    def token_rows(i):
        start = pl.multiple_of(i * 2 * LEN_L + place.rank * LEN_L, LEN_L)
        return tok_hbm.at[pl.ds(start, LEN_L)]

    token_loads = [
        pltpu.make_async_copy(token_rows(i), tok_ref.at[pl.ds(i * LEN_L, LEN_L)], load_sem.at[i])
        for i in (0, 1)
    ]
    weight_loads = [
        pltpu.make_async_copy(
            own, cat_ref.at[0, :, pl.ds(i * half, half)], load_sem.at[2 + i]
        )
        for i, own in enumerate(mine)
    ]
    out_load = pltpu.make_async_copy(wout_hbm, wout_ref.at[pl.ds(0, half)], load_sem.at[5])
    kept_copy = pltpu.make_async_copy(cot_hbm.at[here], grads_ref.at[here], out_sem.at[0])
    stores = [
        pltpu.make_async_copy(cat_ref, cat_hbm, out_sem.at[1]),
        pltpu.make_async_copy(wout_ref, wout_all_hbm, out_sem.at[2]),
        pltpu.make_async_copy(bias2_ref, bias2_hbm, out_sem.at[3]),
        pltpu.make_async_copy(tok_ref, tok_out, out_sem.at[4]),
    ]
    last_stores = [
        pltpu.make_async_copy(grads_ref, grads_hbm, out_sem.at[5]),
        pltpu.make_async_copy(up2_ref, up2_hbm, out_sem.at[6]),
        pltpu.make_async_copy(down2_ref, down2_hbm, out_sem.at[7]),
    ]

    @pl.when(step == 0)
    def _():
        for copy in (*token_loads, *weight_loads, out_load):
            copy.start()
        place.greet()
        for one in projections:
            one.begin()
        bias_copy.start()
        fetch_out.begin()
        for copy in token_loads:
            copy.wait()
        for copy in weight_loads:
            copy.wait()

    def at_step(when):
        return pl.when(step == when)

    @at_step(base[1] - 1)
    def _():
        fetch_up.begin()
        fetch_down.begin()

    @at_step(base[1] + 1)
    def _():
        for one in (*projections, fetch_out):
            one.share()

    @at_step(base[2] - 1)
    def _():
        for one in (*projections, fetch_out):
            one.to_core()

    @at_step(base[2])
    def _():
        for one in (*projections, fetch_out):
            one.end()
        bias_copy.wait()
        out_load.wait()
        for copy in stores:
            copy.start()
        kept_copy.start()
        fetch_up.share()
        fetch_down.share()
        cot_copy.start()

    @at_step(base[3] + 2)
    def _():
        fetch_up.more_x()
        fetch_down.more_x()

    @at_step(base[4] + 2)
    def _():
        fetch_up.to_core()
        fetch_down.to_core()

    def project(which, i, bias):
        at = pl.ds(pl.multiple_of(i * FRONT_BLOCK, FRONT_BLOCK), FRONT_BLOCK)
        column = jnp.transpose(bias[:, : 3 * half])[:, :1]
        value = (contract(cat_ref[which], x_ref[at, :], 0, 1) + column).astype(BF16)
        qkv_ref[:, at] = value
        qkv_out[0] = value

    @pl.when(step < base[1])
    def _():
        at = pl.ds(pl.multiple_of(step * FRONT_BLOCK, FRONT_BLOCK), FRONT_BLOCK)
        hat, _ = norm_parts(tok_ref[at, :].astype(F32))
        normed = (hat * gain_ref[...] + shift_ref[...]).astype(BF16)
        x_ref[at, :] = normed
        x_out[...] = normed
        project(0, step, bias_ref[...])

    @pl.when(jnp.logical_and(step >= base[2], step < base[3]))
    def _():
        project(1, step - base[2], bias2_ref[...])

    own_part = jnp.logical_and(step >= base[1], step < base[2])
    other_part = jnp.logical_and(step >= base[3], step < base[4])

    @pl.when(jnp.logical_or(own_part, other_part))
    def _():
        second = (step >= base[3]).astype(jnp.int32)
        pair = step - base[1] - second * (base[3] - base[1])
        attend_pair(mask_ref, qkv_ref, att_ref, att_out, log_out, pair, second, heads, block)

    @pl.when(step >= base[4])
    def _():
        i = step - base[4]
        at = pl.ds(pl.multiple_of(i * FRONT_BLOCK, FRONT_BLOCK), FRONT_BLOCK)
        product = contract(att_ref[:, at], wout_ref[...], 0, 0)
        resid = tok_ref[at, :].astype(F32) + product + bout_ref[...]
        resid_out[...] = resid
        hat, _ = norm_parts(resid)
        mid_out[...] = (hat * gain2_ref[...] + shift2_ref[...]).astype(BF16)

    @pl.when(step == base[4] + blocks - 1)
    def _():
        for one in (fetch_up, fetch_down):
            one.end()
        for copy in last_stores[1:]:
            copy.start()
        cot_copy.wait()
        kept_copy.wait()
        last_stores[0].start()
        for copy in (*stores, *last_stores):
            copy.wait()


def attend_pair(mask_ref, qkv_ref, att_ref, att_out, log_out, pair, second, heads, block):
    rows = qkv_ref.shape[1]
    half = heads * HEAD_DIM
    first = pair * HEAD_GROUP
    work = []
    for head in range(HEAD_GROUP):
        work += [(head, 0, LEN_L, at, block) for at in range(0, LEN_L, block)]
        work += [(head, start, LEN_S, 0, LEN_S) for start in range(LEN_L, rows, LEN_S)]

    def load(which, head, columns):
        start = pl.multiple_of(which * half + (first + head) * HEAD_DIM, HEAD_DIM)
        return qkv_ref[pl.ds(start, HEAD_DIM), columns]

    def scores(item):
        head, start, count, at, size = item
        every = slice(start, start + count)
        keys = load(1, head, every)
        key_rows = jnp.concatenate([keys, keys, extra_rows([mask_ref[:, every]], count)], 0)
        query = scaled_query(load(0, head, slice(start + at, start + at + size)))
        query_rows = jnp.concatenate([*query, jnp.ones((16, size), BF16)], 0)
        return contract(key_rows, query_rows, 0, 0)

    def finish(item, score):
        head, start, count, at, size = item
        here = slice(start + at, start + at + size)
        values = load(2, head, slice(start, start + count))
        value_rows = jnp.concatenate([values, jnp.ones((16, count), BF16)], 0)
        top = jnp.max(score, axis=0, keepdims=True)
        weights = jnp.exp2(score - top).astype(BF16)
        mixed = contract(value_rows, weights, 1, 0)
        total = mixed[HEAD_DIM : HEAD_DIM + 1]
        result = (mixed[:HEAD_DIM] * (1.0 / total)).astype(BF16)
        att_out[0, head, :, here] = result
        start = pl.multiple_of(second * half + (first + head) * HEAD_DIM, HEAD_DIM)
        att_ref[pl.ds(start, HEAD_DIM), here] = result
        log_out[0, head, :, here] = top + jnp.log2(total)

    score = scores(work[0])
    for place, item in enumerate(work):
        later = scores(work[place + 1]) if place + 1 < len(work) else None
        finish(item, score)
        score = later


def front(
    mask, vectors, bias, tokens, w_query, w_key, w_value, w_out, w_up, w_down, cotangent, heads,
    block=1024,
):
    width = tokens.shape[1]
    rows = tokens.shape[0] // 2
    half = heads * HEAD_DIM
    hidden = w_up.shape[1]
    blocks, pairs = rows // FRONT_BLOCK, heads // HEAD_GROUP
    base = [0, blocks, blocks + pairs, 2 * blocks + pairs, 2 * blocks + 2 * pairs]
    anywhere = pl.BlockSpec(memory_space=pl.ANY)

    def row_block(first):
        return lambda s: (jnp.clip(s - first, 0, blocks - 1), 0)

    def qkv_block(s):
        late = (s >= base[2]).astype(jnp.int32)
        return late, 0, jnp.clip(s - late * base[2], 0, blocks - 1)

    def head_block(s):
        late = (s >= base[3]).astype(jnp.int32)
        return late, jnp.clip(s - base[1] - late * (base[3] - base[1]), 0, pairs - 1), 0, 0

    by_row = lambda first: pl.BlockSpec((FRONT_BLOCK, width), row_block(first))
    bias_rows, bias_width = bias.shape
    pair_total = pair_count(2 * heads, rows)
    return pl.pallas_call(
        functools.partial(front_kernel, heads=heads, block=block),
        grid=(base[4] + blocks,),
        in_specs=[
            whole((1, rows)),
            whole((8, width)),
            whole(bias.shape),
        ]
        + [anywhere] * 8,
        out_specs=[
            by_row(0),
            pl.BlockSpec((1, 3 * half, FRONT_BLOCK), qkv_block),
            pl.BlockSpec((1, HEAD_GROUP, HEAD_DIM, rows), head_block),
            pl.BlockSpec((1, HEAD_GROUP, 1, rows), head_block),
            by_row(base[4]),
            by_row(base[4]),
        ]
        + [anywhere] * 7,
        out_shape=[
            jax.ShapeDtypeStruct((rows, width), BF16),
            jax.ShapeDtypeStruct((2, 3 * half, rows), BF16),
            jax.ShapeDtypeStruct((2, heads, HEAD_DIM, rows), BF16),
            jax.ShapeDtypeStruct((2, heads, 1, rows), F32),
            jax.ShapeDtypeStruct((rows, width), F32),
            jax.ShapeDtypeStruct((rows, width), BF16),
            jax.ShapeDtypeStruct((2, width, 3 * half), BF16),
            jax.ShapeDtypeStruct((2 * half, width), BF16),
            jax.ShapeDtypeStruct((width, hidden), BF16),
            jax.ShapeDtypeStruct((hidden, width), BF16),
            jax.ShapeDtypeStruct((rows, width), BF16),
            jax.ShapeDtypeStruct((bias_rows, bias_width), F32),
            jax.ShapeDtypeStruct((rows, width), BF16),
        ],
        scratch_shapes=[
            pltpu.VMEM((rows, width), BF16),
            pltpu.VMEM((rows, width), BF16),
            pltpu.VMEM((3 * half, rows), BF16),
            pltpu.VMEM((2 * half, rows), BF16),
            pltpu.VMEM((2, width, 3 * half), BF16),
            pltpu.VMEM((2 * half, width), BF16),
            pltpu.VMEM((bias_rows, bias_width), F32),
            pltpu.VMEM((width, hidden), BF16),
            pltpu.VMEM((hidden, width), BF16),
            pltpu.VMEM((rows, width), BF16),
            pltpu.SemaphoreType.DMA((6,)),
            pltpu.SemaphoreType.DMA((8,)),
            pltpu.SemaphoreType.DMA((2,)),
            pltpu.SemaphoreType.DMA((2,)),
        ]
        + [ref for _ in range(6) for ref in Fetch.buffers()],
        compiler_params=pltpu.CompilerParams(
            vmem_limit_bytes=VMEM_LIMIT, collective_id=1, has_side_effects=True
        ),
        cost_estimate=cost(
            pair_total * 2 * 512 + 14 * rows * width * half, 40 * rows * width, pair_total
        ),
        name="front",
    )(
        mask, vectors, bias, tokens, w_query, w_key, w_value, w_out, w_up, w_down, cotangent,
    )


ERFC_TERMS = (0.254829592, -0.284496736, 1.421413741, -1.453152027, 1.061405429)
ERFC_SLOPE = 0.3275911


def gelu_and_slope(value):
    bell = jnp.exp2(value * value * (-0.5 * LOG2E))
    base = 1.0 + jnp.abs(value) * (ERFC_SLOPE * math.sqrt(0.5))
    ratio = 1.0 / base
    poly = ERFC_TERMS[4] * 0.5
    for term in ERFC_TERMS[3::-1]:
        poly = poly * ratio + term * 0.5
    tail = poly * ratio * bell
    below = jnp.where(value < 0.0, tail, 1.0 - tail)
    return value * below, below + value * bell * (1.0 / math.sqrt(2.0 * math.pi))


HIDDEN_BLOCK = 512
MID_BLOCK = 512
HIDDEN_ORDER = ((1, 0), (0, 0), (1, 1), (1, 2), (0, 1), (0, 2))
SLOTS = 4
MID_CHUNK = 512


def mid_kernel(
    mid_ref, grad_ref, bias_ref, resid_ref, vec_ref, w_ref, att_ref,
    up2_hbm, up_hbm, down2_hbm, down_hbm,
    out_ref, gresid_ref, gatt_ref, dw_own_ref, dw_other_ref, small_ref, db_ref,
    dup_hbm, ddown_hbm, seen_up, seen_down, gup_hbm, gdown_hbm,
    sum_ref, gmid_ref, act_ref, gpre_ref, up_ref, down_ref, dup_ref, ddown_ref, acc_ref,
    load_sem, store_sem, *scratch, blocks,
):
    step = pl.program_id(0)
    place = Place()
    rows, width = mid_ref.shape
    cut = lambda ref, i: ref.at[:, pl.ds(i * HIDDEN_BLOCK, HIDDEN_BLOCK)]
    take = lambda ref, i, count: ref.at[pl.ds(i * count, count)]
    terms = []
    for i in range(blocks):
        refs = [scratch[6 * i : 6 * i + 3], scratch[6 * i + 3 : 6 * i + 6]]
        slot = HIDDEN_ORDER.index((1, i)) % SLOTS
        terms.append(
            (
                PartnerTerm(place, dup_ref.at[slot], cut(seen_up, i), refs[0]),
                PartnerTerm(
                    place, ddown_ref.at[slot], take(seen_down, i, HIDDEN_BLOCK // 2), refs[1]
                ),
            )
        )

    first_sums = [
        PlaneSum(
            place, dup_ref.at[1], cut(seen_up, 0), gup_hbm, scratch[6 * blocks : 6 * blocks + 9]
        ),
        PlaneSum(
            place, ddown_ref.at[1], take(seen_down, 0, HIDDEN_BLOCK // 2), gdown_hbm,
            scratch[6 * blocks + 9 :],
        ),
    ]

    def loads(at):
        side, i = HIDDEN_ORDER[at]
        up, down = (up2_hbm, down2_hbm) if side else (up_hbm, down_hbm)
        slot = at % 2
        return [
            pltpu.make_async_copy(cut(up, i), up_ref.at[slot], load_sem.at[slot, 0]),
            pltpu.make_async_copy(
                take(down, i, HIDDEN_BLOCK), down_ref.at[slot], load_sem.at[slot, 1]
            ),
        ]

    def stores(i):
        slot = HIDDEN_ORDER.index((0, i)) % SLOTS
        return [
            pltpu.make_async_copy(dup_ref.at[slot], cut(dup_hbm, i), store_sem.at[i, 0]),
            pltpu.make_async_copy(
                ddown_ref.at[slot], take(ddown_hbm, i, HIDDEN_BLOCK), store_sem.at[i, 1]
            ),
        ]

    to_core = {3: terms[1], 4: terms[2]}
    to_partner = {1: terms[0], 4: terms[1], 5: terms[2]}

    for at in range(2 * blocks + 1):

        @pl.when(step == at)
        def _(at=at):
            if at == 0:
                for copy in loads(0):
                    copy.start()
                place.greet()
                sum_ref[...] = jnp.zeros_like(sum_ref)
                gmid_ref[...] = jnp.zeros_like(gmid_ref)
            if at < 2 * blocks:
                for copy in loads(at):
                    copy.wait()
            if at + 1 < 2 * blocks:
                for copy in loads(at + 1):
                    copy.start()
            for one in to_partner.get(at, ()):
                one.to_partner()
            for one in to_core.get(at, ()):
                one.begin()
            if at >= 1 and HIDDEN_ORDER[at - 1] in ((0, 1), (0, 2)):
                for copy in stores(HIDDEN_ORDER[at - 1][1]):
                    copy.start()
            if at == 2:
                for one in first_sums:
                    one.begin_own()
            if at == 3:
                for one in terms[0]:
                    one.end()
                for one in first_sums:
                    one.begin_seen()
                for one in first_sums:
                    one.along_x()
            if at == 4:
                for one in first_sums:
                    one.along_z()
            if at == 5:
                for one in first_sums:
                    one.back_along_z()
            if at == 6:
                for one in first_sums:
                    one.back_along_x()
            if at == 2 * blocks:
                acc_ref[...] = jnp.zeros_like(acc_ref)
                small_ref[...] = jnp.zeros_like(small_ref)

    @pl.when(step < 2 * blocks)
    def _():
        up, down, bias = up_ref[step % 2], down_ref[step % 2], bias_ref[0]

        def products(at):
            here = slice(at, at + MID_CHUNK)
            return (
                contract(mid_ref[here], up, 1, 0) + bias,
                contract(grad_ref[here], down, 1, 1),
            )

        now = products(0)
        db = None
        for at in range(0, rows, MID_CHUNK):
            here = slice(at, at + MID_CHUNK)
            later = products(at + MID_CHUNK) if at + MID_CHUNK < rows else None
            value, slope = gelu_and_slope(now[0])
            act = value.astype(BF16)
            gpre = (slope * now[1]).astype(BF16)
            act_ref[here] = act
            gpre_ref[here] = gpre
            term = jnp.sum(gpre.astype(F32), axis=0, keepdims=True)
            db = term if db is None else db + term
            sum_ref[here] += contract(act, down, 1, 0)
            gmid_ref[here] += contract(gpre, up, 1, 1)
            now = later
        db_ref[0] = db
        slot = lax.rem(step, SLOTS)
        ddown_ref[slot] = contract(act_ref[...], grad_ref[...], 0, 0).astype(BF16)
        dup_ref[slot] = contract(mid_ref[...], gpre_ref[...], 0, 0).astype(BF16)

    @pl.when(step == 0)
    def _():
        for one in terms[0]:
            one.begin()

    @pl.when(step >= 2 * blocks)
    def _():
        start = (step - 2 * blocks) * MID_BLOCK
        here = pl.ds(pl.multiple_of(start, MID_BLOCK), MID_BLOCK)
        resid = resid_ref[...]
        grads = grad_ref[here, :].astype(F32)
        out_ref[...] = (resid + sum_ref[here, :] + vec_ref[5:6]).astype(BF16)
        gmid = gmid_ref[here, :]
        hat, inv = norm_parts(resid)
        gresid = grads + norm_back(hat, inv, gmid * vec_ref[3:4])
        gresid_ref[...] = gresid
        branch = gresid.astype(BF16)
        gatt_ref[...] = contract(w_ref[...], branch, 1, 1).astype(BF16)
        acc_ref[...] += contract(branch, att_ref[...], 0, 1)
        small_ref[0:1] += jnp.sum(gmid * hat, axis=0, keepdims=True)
        small_ref[1:2] += jnp.sum(gmid, axis=0, keepdims=True)
        small_ref[2:3] += jnp.sum(gresid, axis=0, keepdims=True)
        small_ref[3:4] += jnp.sum(grads, axis=0, keepdims=True)

    @pl.when(step == pl.num_programs(0) - 1)
    def _():
        for one in first_sums:
            one.back_to_core()
        half = dw_own_ref.shape[1]
        dw_own_ref[...] = acc_ref[:, :half].astype(BF16)
        dw_other_ref[...] = acc_ref[:, half:].astype(BF16)
        for i in range(1, blocks):
            for copy in stores(i):
                copy.wait()
            for one in terms[i]:
                one.end()
        for one in first_sums:
            one.end()


def mid_part(mid, grads, biases, resid, vectors, w_out, attended, up2, up, down2, down):
    rows, width = mid.shape
    hidden = up.shape[1]
    blocks = hidden // HIDDEN_BLOCK
    first = 2 * blocks
    heads_width = attended.shape[0]
    anywhere = pl.BlockSpec(memory_space=pl.ANY)
    once = lambda shape: pl.BlockSpec(
        shape, lambda *_: (0,) * len(shape), pipeline_mode=pl.Buffered(1)
    )
    row_step = lambda s: jnp.maximum(s - first, 0)
    by_row = pl.BlockSpec((MID_BLOCK, width), lambda s: (row_step(s), 0))
    columns = pl.BlockSpec((heads_width, MID_BLOCK), lambda s: (0, row_step(s)))
    by_hidden = pl.BlockSpec((1, 1, HIDDEN_BLOCK), lambda s: (jnp.minimum(s, first - 1), 0, 0))
    half = (width, heads_width // 2)
    scratch = [
        pltpu.VMEM((rows, width), F32),
        pltpu.VMEM((rows, width), F32),
        pltpu.VMEM((rows, HIDDEN_BLOCK), BF16),
        pltpu.VMEM((rows, HIDDEN_BLOCK), BF16),
        pltpu.VMEM((2, width, HIDDEN_BLOCK), BF16),
        pltpu.VMEM((2, HIDDEN_BLOCK, width), BF16),
        pltpu.VMEM((SLOTS, width, HIDDEN_BLOCK), BF16),
        pltpu.VMEM((SLOTS, HIDDEN_BLOCK, width), BF16),
        pltpu.VMEM((width, heads_width), F32),
        pltpu.SemaphoreType.DMA((2, 2)),
        pltpu.SemaphoreType.DMA((blocks, 2)),
    ]
    for _ in range(blocks):
        scratch += PartnerTerm.buffers(width, HIDDEN_BLOCK)
        scratch += PartnerTerm.buffers(HIDDEN_BLOCK, width)
    scratch += PlaneSum.buffers(width, HIDDEN_BLOCK) + PlaneSum.buffers(HIDDEN_BLOCK, width)
    return pl.pallas_call(
        functools.partial(mid_kernel, blocks=blocks),
        grid=(first + rows // MID_BLOCK,),
        in_specs=[
            once((rows, width)), once((rows, width)), by_hidden, by_row, whole((8, width)),
            once((heads_width, width)), columns,
        ]
        + [anywhere] * 4,
        out_specs=[
            by_row, by_row, columns, whole(half), whole(half), whole((8, width)), by_hidden,
        ]
        + [anywhere] * 6,
        out_shape=[
            jax.ShapeDtypeStruct((rows, width), BF16),
            jax.ShapeDtypeStruct((rows, width), F32),
            jax.ShapeDtypeStruct((heads_width, rows), BF16),
            jax.ShapeDtypeStruct(half, BF16),
            jax.ShapeDtypeStruct(half, BF16),
            jax.ShapeDtypeStruct((8, width), F32),
            jax.ShapeDtypeStruct((first, 1, HIDDEN_BLOCK), F32),
            jax.ShapeDtypeStruct((width, hidden), BF16),
            jax.ShapeDtypeStruct((hidden, width), BF16),
            jax.ShapeDtypeStruct((width // 2, hidden), BF16),
            jax.ShapeDtypeStruct((hidden // 2, width), BF16),
            jax.ShapeDtypeStruct((width, HIDDEN_BLOCK), BF16),
            jax.ShapeDtypeStruct((HIDDEN_BLOCK, width), BF16),
        ],
        scratch_shapes=scratch,
        compiler_params=pltpu.CompilerParams(
            vmem_limit_bytes=VMEM_LIMIT, collective_id=2, has_side_effects=True
        ),
        cost_estimate=cost(
            24 * rows * width * hidden + 4 * rows * width * heads_width, 60 * rows * width,
            4 * rows * hidden,
        ),
        name="mid",
    )(mid, grads, biases, resid, vectors, w_out, attended, up2, up, down2, down)


TAIL_BLOCK = 512
SUM_ACTIONS = ("begin", "along_x", "along_z", "back_along_z", "back_along_x", "back_to_core")
SUM_STEPS = (
    (0, 1, 3, 6, 9, 11),
    (0, 2, 5, 8, 11, 13),
    (0, 4, 6, 10, 13, 15),
    (0, 5, 8, 12, 14, 16),
    (0, 8, 10, 13, 15, 17),
    (None, 17, 19),
    (None, 17, 20),
    (None, 17),
)
LAST_ACTIONS = (
    (7, "along_z"), 0, (5, "back_along_z"), 1, (6, "back_along_z"), 2,
    (7, "back_along_z"), (5, "back_along_x"), (6, "back_along_x"), (7, "back_along_x"),
    (5, "back_to_core"), (6, "back_to_core"), (7, "back_to_core"),
)


def tail_kernel(
    mask_ref, qkv_ref, att_ref, log_ref, gatt_ref, vec_ref, small2_ref, dbup1_ref, dbup2_ref,
    wout2_ref, x_hbm, w_hbm, tok_hbm, gresid_hbm, up_hbm, down_hbm, wout_hbm, seen_up,
    seen_down, out_hbm,
    gtok_ref, small_ref, got_hbm, gup_hbm, gdown_hbm, gout_hbm, gcat_hbm, got_out,
    d_ref, x_ref, w_ref, tok_ref, gresid_ref, dw_ref, dw2_ref, seen_cat, sent_ref, pair_ref,
    load_sem, row_sem, tok_send, tok_recv, *scratch, heads, block,
):
    step = pl.program_id(0)
    place = Place()
    first_rows = 2 * heads + 1
    last_step = first_rows + 3
    width = x_ref.shape[1]
    half = heads * HEAD_DIM

    groups = []
    at = 0
    for count in [9] * 5 + [0] + [9] * 3 + [3, 3, 5]:
        groups.append(scratch[at : at + count])
        at += count
    columns = lambda ref, i: ref.at[:, pl.ds(i * HIDDEN_BLOCK, HIDDEN_BLOCK)]
    rows_of = lambda ref, i, count: ref.at[pl.ds(i * count, count)]
    sums = [
        PlaneSum(place, columns(up_hbm, i), columns(seen_up, i), columns(gup_hbm, i - 1), groups[i])
        for i in (1, 2)
    ]
    sums += [
        PlaneSum(
            place,
            rows_of(down_hbm, i, HIDDEN_BLOCK),
            rows_of(seen_down, i, HIDDEN_BLOCK // 2),
            rows_of(gdown_hbm, i - 1, HIDDEN_BLOCK),
            groups[2 + i],
        )
        for i in (1, 2)
    ]
    sums.append(PlaneSum(place, wout_hbm, None, gout_hbm, groups[0]))
    third = lambda ref, i: ref.at[:, pl.ds(i * half, half)]
    cat_sums = [
        PlaneSum(
            place, third(dw_ref, i), None, third(gcat_hbm, i),
            (groups[6 + i][0], third(seen_cat, i), *groups[6 + i][2:]),
        )
        for i in range(3)
    ]
    cat_term = PartnerTerm(place, dw2_ref, seen_cat, groups[9])
    out_term = PartnerTerm(place, wout2_ref, groups[0][1], groups[10])
    own_small, other_small = pair_ref.at[0], pair_ref.at[1]
    small = SmallSum(place, pair_ref, groups[11])
    theirs = pl.ds(pl.multiple_of((1 - place.rank) * LEN_L, LEN_L), LEN_L)
    out_load = pltpu.make_async_copy(out_hbm.at[theirs], sent_ref, load_sem.at[2])
    piece = LEN_L // 4
    out_copies = [
        send_to(
            sent_ref.at[pl.ds(i * piece, piece)], got_out.at[pl.ds(i * piece, piece)],
            tok_send.at[2 + i], tok_recv.at[2 + i], place.partner(),
        )
        for i in range(4)
    ]

    loads = [
        pltpu.make_async_copy(x_hbm, x_ref, load_sem.at[0]),
        pltpu.make_async_copy(w_hbm, w_ref, load_sem.at[1]),
    ]

    def row_start(i):
        mine = i // 2
        return ((1 - mine) * (1 - place.rank) + mine * place.rank) * LEN_L + (i % 2) * TAIL_BLOCK

    def row_loads(i):
        start = pl.ds(pl.multiple_of(row_start(i), TAIL_BLOCK), TAIL_BLOCK)
        slot = i % 2
        return [
            pltpu.make_async_copy(tok_hbm.at[start], tok_ref.at[slot], row_sem.at[slot, 0]),
            pltpu.make_async_copy(gresid_hbm.at[start], gresid_ref.at[slot], row_sem.at[slot, 1]),
        ]

    def token_copy(i):
        there = pl.ds(i * TAIL_BLOCK, TAIL_BLOCK)
        return send_to(
            sent_ref.at[there], got_hbm.at[there], tok_send.at[i], tok_recv.at[i], place.partner()
        )

    def weight_gradient(source, target, i):
        here = pl.ds(i * half, half)
        product = contract(x_ref[...], d_ref[source, here, :], 0, 1)
        target[:, here] = product.astype(BF16)

    def bias_rows(source, target):
        ones = jnp.ones((16, d_ref.shape[2]), BF16)
        for i, which in ((0, 0), (1, 2)):
            row = contract(ones, d_ref[source, pl.ds(which * half, half), :], 1, 1)
            target[8:9, pl.ds(i * half, half)] = row[:1]

    events = {}
    sums += cat_sums
    for one, times in zip(sums, SUM_STEPS):
        for when, action in zip(times, SUM_ACTIONS):
            if when is None:
                continue
            events.setdefault(when, []).append(getattr(one, action))

    for when in sorted(events):

        @pl.when(step == when)
        def _(when=when):
            if when == 0:
                out_load.start()
                place.greet()
                out_term.begin()
            if when == 1:
                out_term.to_partner()
                out_load.wait()
                out_copies[0].start()
                out_copies[1].start()
            if when == 3:
                out_copies[2].start()
            if when == 13:
                out_copies[3].start()
            if when == 8:
                out_term.end()
            for action in events[when]:
                action()

    @pl.when(step == 2)
    def _():
        for copy in loads:
            copy.start()

    @pl.when(step == heads)
    def _():
        for copy in loads:
            copy.wait()
        for i in range(3):
            weight_gradient(1, dw2_ref, i)
        cat_term.begin()

    @pl.when(step == heads + 1)
    def _():
        cat_term.to_partner()
        own_small[...] = jnp.zeros_like(own_small)
        other_small[...] = jnp.zeros_like(other_small)
        bias_rows(1, other_small)

    @pl.when(step < 2 * heads)
    def _():
        back_one_head(mask_ref, qkv_ref, att_ref, log_ref, gatt_ref, d_ref, step, heads, block)

    @pl.when(step == 2 * heads)
    def _():
        for copy in row_loads(0):
            copy.start()
        cat_term.end()
        for i in range(3):
            weight_gradient(0, dw_ref, i)
            cat_sums[i].begin()
        bias_rows(0, own_small)


    for i in range(4):

        @pl.when(step == first_rows + i)
        def _(i=i):
            for copy in row_loads(i):
                copy.wait()
            if i == 0:
                for copy in out_copies:
                    copy.wait()
            if i < 3:
                for copy in row_loads(i + 1):
                    copy.start()
            here = pl.ds(pl.multiple_of(row_start(i), TAIL_BLOCK), TAIL_BLOCK)
            gin = contract(d_ref[0, :, here], w_ref[0], 0, 1)
            gin += contract(d_ref[1, :, here], w_ref[1], 0, 1)
            hat, inv = norm_parts(tok_ref[i % 2].astype(F32))
            gtok = gresid_ref[i % 2] + norm_back(hat, inv, gin * vec_ref[0:1])
            own_small[0:1] += jnp.sum(gin * hat, axis=0, keepdims=True)
            own_small[1:2] += jnp.sum(gin, axis=0, keepdims=True)
            if i < 2:
                sent_ref[pl.ds(i * TAIL_BLOCK, TAIL_BLOCK), :] = gtok.astype(BF16)
                token_copy(i).start()
            else:
                gtok_ref[...] = gtok

    @pl.when(step == last_step)
    def _():
        own_small[2:6] = small2_ref[0:4]
        other_small[0:2] = own_small[0:2]
        other_small[2:6] = small2_ref[0:4]
        for i in (0, 1):
            own_small[6 + i : 7 + i] = dbup1_ref[:, pl.ds(i * width, width)]
            other_small[6 + i : 7 + i] = dbup2_ref[:, pl.ds(i * width, width)]
        small.begin()
        small_actions = (small.over_x, small.over_z, small.over_tp)
        for item in LAST_ACTIONS:
            if isinstance(item, int):
                small_actions[item]()
            else:
                getattr(sums[item[0]], item[1])()
        small_ref[...] = small.end()
        for i in (0, 1):
            token_copy(i).wait()
        for one in sums:
            one.end()


def back_one_head(mask_ref, qkv_ref, att_ref, log_ref, gatt_ref, d_ref, step, heads, block):
    rows = qkv_ref.shape[4]
    half = heads * HEAD_DIM
    source = 1 - step // heads
    head_at = pl.multiple_of((step % heads) * HEAD_DIM, HEAD_DIM)

    def store(which, columns, value):
        d_ref[source, pl.ds(which * half + head_at, HEAD_DIM), columns] = value.astype(BF16)

    work = []
    images = [(0, LEN_L, block)] + [(at, LEN_S, LEN_S) for at in range(LEN_L, rows, LEN_S)]
    for start, count, size in images:
        work += [(start, count, at, size) for at in range(start, start + count, size)]
    kept = {}

    def operands(start, count):
        if start not in kept:
            every = slice(start, start + count)
            keys = qkv_ref[0, 1, 0, :, every]
            values = qkv_ref[0, 2, 0, :, every]
            ones = jnp.ones((1, count), F32)
            key_rows = jnp.concatenate(
                [keys, keys, extra_rows([ones, ones, ones, mask_ref[:, every]], count)], 0
            )
            value_rows = jnp.concatenate([values, extra_rows([ones, ones, ones], count)], 0)
            kept[start] = keys, key_rows, value_rows
        return kept[start]

    def products(item):
        start, count, at, size = item
        here = slice(at, at + size)
        _, key_rows, value_rows = operands(start, count)
        query = qkv_ref[0, 0, 0, :, here]
        grads = gatt_ref[0, 0, :, here]
        inner = jnp.sum(
            grads.astype(F32) * att_ref[0, 0, :, here].astype(F32), axis=0, keepdims=True
        )
        terms = three_terms(-log_ref[0, 0, :, here]) + [jnp.ones((1, size), F32)]
        query_rows = jnp.concatenate([*scaled_query(query), extra_rows(terms, size)], 0)
        grad_rows = jnp.concatenate([grads, extra_rows(three_terms(-inner), size)], 0)
        return contract(query_rows, key_rows, 0, 0), contract(grad_rows, value_rows, 0, 0)

    sums = {}
    now = products(work[0])
    for place, item in enumerate(work):
        later = products(work[place + 1]) if place + 1 < len(work) else None
        start, count, at, size = item
        here = slice(at, at + size)
        keys = operands(start, count)[0]
        query = qkv_ref[0, 0, 0, :, here]
        grads = gatt_ref[0, 0, :, here]
        score, grad_probs = now
        probs = jnp.exp2(score)
        grad_score = (probs * grad_probs).astype(BF16)
        part_values = contract(grads, probs.astype(BF16), 1, 0)
        part_keys = contract(query, grad_score, 1, 0)
        store(0, here, contract(keys, grad_score, 1, 1) * SCALE)
        if start in sums:
            part_keys, part_values = sums[start][0] + part_keys, sums[start][1] + part_values
        sums[start] = part_keys, part_values
        if at + size == start + count:
            every = slice(start, start + count)
            store(1, every, part_keys * SCALE)
            store(2, every, part_values)
        now = later


def tail(
    mask, qkv, att, log_total, gatt, vectors, small2, dbup1, dbup2, dwout2, normed, w_cat,
    tokens, gresid, dup, ddown, dwout, seen_up, seen_down, out_rows, block=256,
):
    _, _, heads, _, rows = qkv.shape
    _, width, out = w_cat.shape
    anywhere = pl.BlockSpec(memory_space=pl.ANY)
    last = 2 * heads - 1

    def head(h):
        h = jnp.minimum(h, last)
        return 1 - h // heads, h % heads

    all_three = pl.BlockSpec(
        (1, 3, 1, HEAD_DIM, rows), lambda h: (head(h)[0], 0, head(h)[1], 0, 0)
    )
    one = pl.BlockSpec((1, 1, HEAD_DIM, rows), lambda h: (*head(h), 0, 0))
    row = pl.BlockSpec((1, 1, 1, rows), lambda h: (*head(h), 0, 0))
    sum_shapes = [dwout.shape] + [(width, HIDDEN_BLOCK)] * 2 + [(HIDDEN_BLOCK, width)] * 2 + [(width, out // 3)] * 3
    scratch = [
        pltpu.VMEM((2, out, rows), BF16),
        pltpu.VMEM((rows, width), BF16),
        pltpu.VMEM((2, width, out), BF16),
        pltpu.VMEM((2, TAIL_BLOCK, width), BF16),
        pltpu.VMEM((2, TAIL_BLOCK, width), F32),
        pltpu.VMEM((width, out), BF16),
        pltpu.VMEM((width, out), BF16),
        pltpu.VMEM((width // 2, out), BF16),
        pltpu.VMEM((rows // 2, width), BF16),
        pltpu.VMEM((2, SmallSum.ROWS, width), F32),
        pltpu.SemaphoreType.DMA((3,)),
        pltpu.SemaphoreType.DMA((2, 2)),
        pltpu.SemaphoreType.DMA((6,)),
        pltpu.SemaphoreType.DMA((6,)),
    ]
    for shape in sum_shapes:
        scratch += PlaneSum.buffers(*shape)
    scratch += PartnerTerm.buffers(width, out) + PartnerTerm.buffers(*dwout.shape)
    scratch += SmallSum.buffers(width)
    pairs = pair_count(2 * heads, rows)
    first_rows = 2 * heads + 1
    return pl.pallas_call(
        functools.partial(tail_kernel, heads=heads, block=block),
        grid=(first_rows + 4,),
        in_specs=[
            whole((1, rows)), all_three, one, row, one, whole((8, width)), whole((8, width)),
            whole((1, 2 * width)), whole((1, 2 * width)), whole(dwout.shape),
        ]
        + [anywhere] * 10,
        out_specs=[
            pl.BlockSpec(
                (TAIL_BLOCK, width), lambda h: (jnp.maximum(h - first_rows - 2, 0), 0)
            ),
            whole((SmallSum.ROWS, width)),
        ]
        + [anywhere] * 6,
        out_shape=[
            jax.ShapeDtypeStruct((rows // 2, width), F32),
            jax.ShapeDtypeStruct((SmallSum.ROWS, width), F32),
            jax.ShapeDtypeStruct((rows // 2, width), BF16),
            jax.ShapeDtypeStruct((width, dup.shape[1] - HIDDEN_BLOCK), BF16),
            jax.ShapeDtypeStruct((ddown.shape[0] - HIDDEN_BLOCK, width), BF16),
            jax.ShapeDtypeStruct(dwout.shape, BF16),
            jax.ShapeDtypeStruct((width, out), BF16),
            jax.ShapeDtypeStruct((rows // 2, width), BF16),
        ],
        scratch_shapes=scratch,
        compiler_params=pltpu.CompilerParams(
            vmem_limit_bytes=VMEM_LIMIT, collective_id=0, has_side_effects=True
        ),
        cost_estimate=cost(pairs * 5 * 512, 32 * heads * HEAD_DIM * rows, pairs),
        name="tail",
    )(
        mask, qkv, att, log_total, gatt, vectors, small2, dbup1, dbup2, dwout2, normed, w_cat,
        tokens, gresid, dup, ddown, dwout, seen_up, seen_down, out_rows,
    )


def joined(mine, theirs, second):
    return jnp.where(second, jnp.concatenate([theirs, mine], 0), jnp.concatenate([mine, theirs], 0))


def half_of(array, second):
    size = array.shape[0] // 2
    return lax.dynamic_slice_in_dim(array, jnp.where(second, size, 0), size, 0)


def by_images(
    tokens, long_lengths, short_lengths, ln1_gain, ln1_bias, w_query, b_query, w_key, w_value,
    b_value, w_out, b_out, ln2_gain, ln2_bias, w_up, b_up, w_down, b_down, cotangent,
):
    rank = lax.axis_index("tp")
    rank_arr = jnp.reshape(rank, (1,)).astype(jnp.int32)
    second = rank == 1
    rows = tokens.shape[0] // 2
    width = tokens.shape[1]
    half = w_query.shape[1]
    heads = half // HEAD_DIM
    long_len = lax.dynamic_slice_in_dim(long_lengths, rank, 1, 0)
    shorts = short_lengths.shape[0] // 2
    short_len = lax.dynamic_slice_in_dim(short_lengths, rank * shorts, shorts, 0)
    valid = jnp.concatenate(
        [
            jnp.arange(LEN_L) < long_len[0],
            (jnp.arange(LEN_S)[None, :] < short_len[:, None]).reshape(-1),
        ]
    )
    mask = jnp.where(valid, 0.0, -1e30).astype(F32).reshape(1, -1)
    vectors = jnp.stack(
        [ln1_gain, ln1_bias, b_out, ln2_gain, ln2_bias, b_down, b_down, b_down]
    ).astype(F32)
    biases = jnp.concatenate([b_query, jnp.zeros_like(b_query), b_value, b_up]).astype(F32)
    bias = jnp.broadcast_to(biases.reshape(1, -1), (8, biases.shape[0]))

    (normed, qkv, att, log_total, resid, mid, w_cat, w_out_all, w_up2, w_down2, grads, bias2,
     own_tokens) = front(
        mask, vectors, bias, tokens, w_query, w_key, w_value, w_out, w_up, w_down, cotangent, heads,
    )
    qkv = qkv.reshape(2, 3, heads, HEAD_DIM, rows)
    attended = att.reshape(2 * half, rows)
    up_bias = [
        rows_of.reshape(-1, 1, HIDDEN_BLOCK)
        for rows_of in (bias[0, 3 * half :], bias2[0, 3 * half :])
    ]
    up_bias = jnp.stack([up_bias[side][i] for side, i in HIDDEN_ORDER])
    (out, gresid, gatt, dwout1, dwout2, small2, db_up, dup1, ddown1, seen_up, seen_down,
     first_up, first_down) = mid_part(
        mid, grads, up_bias, resid, vectors, w_out_all,
        attended, w_up2, w_up, w_down2, w_down,
    )
    dbup1, dbup2 = (
        jnp.concatenate([db_up[at] for at, (own, _) in enumerate(HIDDEN_ORDER) if own == side], 1)
        for side in (0, 1)
    )
    gtok, small, got_tok, grad_up, grad_down, grad_out_t, grad_cat, got_out = tail(
        mask, qkv, att, log_total, gatt.reshape(2, heads, HEAD_DIM, rows), vectors, small2,
        dbup1, dbup2, dwout2, normed, w_cat, own_tokens, gresid, dup1, ddown1, dwout1,
        seen_up, seen_down, out,
    )
    result = joined(half_of(out, second), got_out, second)
    grad_tokens = joined(gtok, got_tok.astype(F32), second)
    grad_cat = grad_cat.astype(F32)
    return (
        result,
        grad_tokens,
        small[0],
        small[1],
        grad_cat[:, :half],
        small[8, :half],
        grad_cat[:, half : 2 * half],
        grad_cat[:, 2 * half :],
        small[8, half:],
        grad_out_t.T.astype(F32),
        small[4],
        small[2],
        small[3],
        jnp.concatenate([first_up, grad_up], 1).astype(F32),
        small[6:8].reshape(-1),
        jnp.concatenate([first_down, grad_down], 0).astype(F32),
        small[5],
    )


def layer_norm(values, gain, shift):
    center = values - jnp.mean(values, axis=-1, keepdims=True)
    spread = jnp.mean(center * center, axis=-1, keepdims=True)
    return center * lax.rsqrt(spread + 1e-06) * gain + shift


def dot_plain(left, right):
    return jnp.dot(left, right, preferred_element_type=jnp.float32)


def dot_rows(left, right):
    return lax.dot_general(
        left, right, (((0,), (0,)), ((), ())), preferred_element_type=jnp.float32
    )


def dot_back(left, right):
    return lax.dot_general(
        left, right, (((1,), (1,)), ((), ())), preferred_element_type=jnp.float32
    )


def group_shape(image_count, seq_len, head_count):
    per_step = math.gcd(image_count, max(1, 512 // seq_len))
    return (image_count // per_step, per_step, seq_len, head_count, HEAD_DIM)


def masked_scores(query_blk, key_blk, length_blk):
    seq_len = query_blk.shape[1]
    raw = jnp.einsum(
        "bqhd,bkhd->bhqk", query_blk, key_blk, preferred_element_type=jnp.float32
    ) * HEAD_DIM ** (-0.5)
    keep = jnp.arange(seq_len, dtype=jnp.int32)[None, :] < length_blk[:, None]
    return jnp.where(keep[:, None, None, :], raw, -1e30)


def attention_forward(queries, key_rows, value_rows, lengths, seq_len):
    image_count = lengths.shape[0]
    head_count = queries.shape[1] // HEAD_DIM
    block_shape = group_shape(image_count, seq_len, head_count)

    def one_step(block):
        query_blk, key_blk, value_blk, length_blk = block
        scores = masked_scores(query_blk, key_blk, length_blk)
        row_top = jnp.max(scores, axis=-1, keepdims=True)
        exp_terms = jnp.exp(scores - row_top)
        row_total = jnp.sum(exp_terms, axis=-1, keepdims=True)
        weights = (exp_terms / row_total).astype(jnp.bfloat16)
        mixed = jnp.einsum(
            "bhqk,bkhd->bqhd", weights, value_blk, preferred_element_type=jnp.float32
        )
        return (mixed, (row_top + jnp.log(row_total))[..., 0])

    mixed, log_total = lax.map(
        one_step,
        (
            queries.reshape(block_shape),
            key_rows.reshape(block_shape),
            value_rows.reshape(block_shape),
            lengths.reshape(block_shape[:2]),
        ),
    )
    return (mixed.reshape(image_count * seq_len, head_count * HEAD_DIM), log_total)


def attention_backward(queries, key_rows, value_rows, grads, lengths, log_total, seq_len):
    image_count = lengths.shape[0]
    head_count = queries.shape[1] // HEAD_DIM
    block_shape = group_shape(image_count, seq_len, head_count)
    scale = HEAD_DIM ** (-0.5)

    def one_step(block):
        query_blk, key_blk, value_blk, grad_blk, length_blk, total_blk = block
        scores = masked_scores(query_blk, key_blk, length_blk)
        probs = jnp.exp(scores - total_blk[..., None])
        grad_values = jnp.einsum(
            "bhqk,bqhd->bkhd",
            probs.astype(jnp.bfloat16),
            grad_blk,
            preferred_element_type=jnp.float32,
        )
        grad_probs = jnp.einsum(
            "bqhd,bkhd->bhqk", grad_blk, value_blk, preferred_element_type=jnp.float32
        )
        inner = jnp.sum(probs * grad_probs, axis=-1, keepdims=True)
        grad_scores = (probs * (grad_probs - inner)).astype(jnp.bfloat16)
        grad_queries = (
            jnp.einsum("bhqk,bkhd->bqhd", grad_scores, key_blk, preferred_element_type=jnp.float32)
            * scale
        )
        grad_keys = (
            jnp.einsum(
                "bhqk,bqhd->bkhd", grad_scores, query_blk, preferred_element_type=jnp.float32
            )
            * scale
        )
        return (grad_queries, grad_keys, grad_values)

    results = lax.map(
        one_step,
        (
            queries.reshape(block_shape),
            key_rows.reshape(block_shape),
            value_rows.reshape(block_shape),
            grads.reshape(block_shape),
            lengths.reshape(block_shape[:2]),
            log_total,
        ),
    )
    flat = (image_count * seq_len, head_count * HEAD_DIM)
    return tuple((item.reshape(flat) for item in results))


def local(
    tokens,
    long_lengths,
    short_lengths,
    ln1_gain,
    ln1_bias,
    w_query,
    b_query,
    w_key,
    w_value,
    b_value,
    w_out,
    b_out,
    ln2_gain,
    ln2_bias,
    w_up,
    b_up,
    w_down,
    b_down,
    cotangent,
):
    tp_count = lax.axis_size("tp")
    tp_rank = lax.axis_index("tp")
    row_count = tokens.shape[0]
    share = row_count // tp_count
    split = long_lengths.shape[0] * LEN_L
    gain_one = ln1_gain.astype(jnp.float32)
    shift_one = ln1_bias.astype(jnp.float32)
    gain_two = ln2_gain.astype(jnp.float32)
    shift_two = ln2_bias.astype(jnp.float32)
    normed_in = layer_norm(tokens.astype(jnp.float32), gain_one, shift_one).astype(jnp.bfloat16)
    queries = (dot_plain(normed_in, w_query) + b_query.astype(jnp.float32)).astype(jnp.bfloat16)
    key_rows = dot_plain(normed_in, w_key).astype(jnp.bfloat16)
    value_rows = (dot_plain(normed_in, w_value) + b_value.astype(jnp.float32)).astype(jnp.bfloat16)
    long_mixed, long_total = attention_forward(
        queries[:split], key_rows[:split], value_rows[:split], long_lengths, LEN_L
    )
    short_mixed, short_total = attention_forward(
        queries[split:], key_rows[split:], value_rows[split:], short_lengths, LEN_S
    )
    attended = jnp.concatenate([long_mixed, short_mixed], axis=0).astype(jnp.bfloat16)
    attn_sum = lax.psum_scatter(dot_plain(attended, w_out), "tp", scatter_dimension=0, tiled=True)
    own_tokens = lax.dynamic_slice_in_dim(tokens, tp_rank * share, share, 0).astype(jnp.float32)
    resid = own_tokens + attn_sum + b_out.astype(jnp.float32)
    normed_mid = layer_norm(resid, gain_two, shift_two).astype(jnp.bfloat16)
    grad_out = cotangent.astype(jnp.float32)
    mid_rows = lax.all_gather(normed_mid, "tp", axis=0, tiled=True)
    pre_up = dot_plain(mid_rows, w_up) + b_up.astype(jnp.float32)
    activ = jax.nn.gelu(pre_up, approximate=False).astype(jnp.bfloat16)
    ffn_sum = lax.psum_scatter(
        dot_plain(activ, w_down).astype(jnp.bfloat16), "tp", scatter_dimension=0, tiled=True
    ).astype(jnp.float32)
    result = resid + ffn_sum + b_down.astype(jnp.float32)
    grad_rows = lax.all_gather(cotangent, "tp", axis=0, tiled=True)
    grad_w_down = dot_rows(activ, grad_rows)
    grad_activ = dot_back(grad_rows, w_down)
    _, gelu_back = jax.vjp(lambda inner: jax.nn.gelu(inner, approximate=False), pre_up)
    grad_pre = gelu_back(grad_activ)[0].astype(jnp.bfloat16)
    grad_w_up = dot_rows(mid_rows, grad_pre)
    grad_b_up = jnp.sum(grad_pre.astype(jnp.float32), axis=0)
    grad_mid = lax.psum_scatter(dot_back(grad_pre, w_up), "tp", scatter_dimension=0, tiled=True)
    _, norm_two_back = jax.vjp(layer_norm, resid, gain_two, shift_two)
    grad_resid_norm, grad_gain_two, grad_shift_two = norm_two_back(grad_mid)
    grad_resid = grad_out + grad_resid_norm
    grad_b_down = jnp.sum(grad_out, axis=0)
    grad_b_out = jnp.sum(grad_resid, axis=0)
    grad_branch = lax.all_gather(grad_resid.astype(jnp.bfloat16), "tp", axis=0, tiled=True)
    grad_w_out = dot_rows(attended, grad_branch)
    grad_attended = dot_back(grad_branch, w_out).astype(jnp.bfloat16)
    long_grads = attention_backward(
        queries[:split],
        key_rows[:split],
        value_rows[:split],
        grad_attended[:split],
        long_lengths,
        long_total,
        LEN_L,
    )
    short_grads = attention_backward(
        queries[split:],
        key_rows[split:],
        value_rows[split:],
        grad_attended[split:],
        short_lengths,
        short_total,
        LEN_S,
    )
    grad_queries = jnp.concatenate([long_grads[0], short_grads[0]], axis=0).astype(jnp.bfloat16)
    grad_keys = jnp.concatenate([long_grads[1], short_grads[1]], axis=0).astype(jnp.bfloat16)
    grad_values = jnp.concatenate([long_grads[2], short_grads[2]], axis=0).astype(jnp.bfloat16)
    grad_w_query = dot_rows(normed_in, grad_queries)
    grad_b_query = jnp.sum(grad_queries.astype(jnp.float32), axis=0)
    grad_w_key = dot_rows(normed_in, grad_keys)
    grad_w_value = dot_rows(normed_in, grad_values)
    grad_b_value = jnp.sum(grad_values.astype(jnp.float32), axis=0)
    grad_in = lax.psum_scatter(
        dot_back(grad_queries, w_query)
        + dot_back(grad_keys, w_key)
        + dot_back(grad_values, w_value),
        "tp",
        scatter_dimension=0,
        tiled=True,
    )
    _, norm_one_back = jax.vjp(layer_norm, own_tokens, gain_one, shift_one)
    grad_tokens_norm, grad_gain_one, grad_shift_one = norm_one_back(grad_in)
    grad_tokens = grad_resid + grad_tokens_norm
    summed = lax.psum(
        (
            grad_w_query,
            grad_b_query,
            grad_w_key,
            grad_w_value,
            grad_b_value,
            grad_w_out,
            grad_w_up,
            grad_b_up,
            grad_w_down,
        ),
        "dp",
    )
    shared = lax.psum(
        (grad_gain_one, grad_shift_one, grad_b_out, grad_gain_two, grad_shift_two, grad_b_down),
        ("dp", "tp"),
    )
    return (
        result.astype(jnp.bfloat16),
        grad_tokens,
        shared[0],
        shared[1],
        summed[0],
        summed[1],
        summed[2],
        summed[3],
        summed[4],
        summed[5],
        shared[2],
        shared[3],
        shared[4],
        summed[6],
        summed[7],
        summed[8],
        shared[5],
    )


def pick(*arrays):
    tokens, long_lengths, short_lengths, w_query, w_up = (arrays[i] for i in (0, 1, 2, 5, 14))
    fits = (
        lax.axis_size("tp") == 2
        and lax.axis_size("dp") == 16
        and long_lengths.shape[0] == 2
        and short_lengths.shape[0] == 8
        and tokens.shape == (2 * LEN_L + 8 * LEN_S, 768)
        and w_query.shape[1] == 8 * HEAD_DIM
        and w_up.shape[1] == 1536
    )
    return by_images(*arrays) if fits else local(*arrays)


def solution(mesh):
    placed = (
        P("dp", None),
        P("dp"),
        P("dp"),
        P(),
        P(),
        P(None, "tp"),
        P("tp"),
        P(None, "tp"),
        P(None, "tp"),
        P("tp"),
        P("tp", None),
        P(),
        P(),
        P(),
        P(None, "tp"),
        P("tp"),
        P("tp", None),
        P(),
        P(("dp", "tp"), None),
    )
    return jax.shard_map(
        pick,
        mesh=mesh,
        in_specs=placed,
        out_specs=(
            P(("dp", "tp"), None),
            P(("dp", "tp"), None),
            P(),
            P(),
            P(None, "tp"),
            P("tp"),
            P(None, "tp"),
            P(None, "tp"),
            P("tp"),
            P("tp", None),
            P(),
            P(),
            P(),
            P(None, "tp"),
            P("tp"),
            P("tp", None),
            P(),
        ),
        check_vma=False,
    )
```

```python
import functools
import math

import jax
import jax.numpy as jnp
from jax import lax
from jax.experimental import pallas as pl
from jax.experimental.pallas import tpu as pltpu
from jax.sharding import PartitionSpec as P

HEAD_DIM = 48
LEN_L = 1024
LEN_S = 256
F32 = jnp.float32
BF16 = jnp.bfloat16
LOG2E = math.log2(math.e)
SCALE = HEAD_DIM ** (-0.5)
VMEM_LIMIT = 60 << 20
HEAD_GROUP = 2


def contract(left, right, left_dim, right_dim):
    return lax.dot_general(
        left, right, (((left_dim,), (right_dim,)), ((), ())), preferred_element_type=F32
    )


def params():
    return pltpu.CompilerParams(vmem_limit_bytes=VMEM_LIMIT)


def cost(flops, bytes_accessed, transcendentals=0):
    return pl.CostEstimate(
        flops=int(flops), bytes_accessed=int(bytes_accessed), transcendentals=int(transcendentals)
    )


def whole(shape):
    zeros = (0,) * len(shape)
    return pl.BlockSpec(shape, lambda *_: zeros)


def norm_parts(values):
    center = values - jnp.mean(values, axis=-1, keepdims=True)
    inv = lax.rsqrt(jnp.mean(center * center, axis=-1, keepdims=True) + 1e-06)
    return center * inv, inv


def norm_back(hat, inv, grad_hat):
    mean_grad = jnp.mean(grad_hat, axis=-1, keepdims=True)
    mean_both = jnp.mean(grad_hat * hat, axis=-1, keepdims=True)
    return inv * (grad_hat - mean_grad - hat * mean_both)


def three_terms(value):
    high = value.astype(BF16).astype(F32)
    rest = value - high
    mid = rest.astype(BF16).astype(F32)
    return [high, mid, rest - mid]


def extra_rows(rows, count):
    at = lax.broadcasted_iota(jnp.int32, (16, count), 0)
    out = jnp.zeros((16, count), F32)
    for place, row in enumerate(rows):
        out = jnp.where(at == place, row, out)
    return out.astype(BF16)


def scaled_query(query):
    wide = query.astype(F32) * (SCALE * LOG2E)
    high = wide.astype(BF16)
    return [high, (wide - high.astype(F32)).astype(BF16)]


def pair_count(heads, rows):
    return heads * (LEN_L**2 + (rows - LEN_L) * LEN_S)


class Place:
    def __init__(self):
        me = lax.axis_index("dp")
        self.core, self.x, self.z = me % 2, (me // 2) % 2, me // 4
        self.rank = lax.axis_index("tp")

    def at(self, z=None, x=None, core=None):
        z = self.z if z is None else z
        x = self.x if x is None else x
        core = self.core if core is None else core
        return {"dp": (z * 2 + x) * 2 + core}

    def across_core(self):
        return self.at(core=1 - self.core)

    def across_x(self):
        return self.at(x=1 - self.x)

    def along_z(self, step):
        return self.at(z=(self.z + step) % 4)

    def partner(self):
        return {"tp": 1 - self.rank}

    def greet(self):
        barrier = pltpu.get_barrier_semaphore()
        others = [self.across_core(), self.across_x(), self.partner()]
        others += [self.along_z(step) for step in (1, 2, 3)]
        for other in others:
            pl.semaphore_signal(
                barrier, inc=1, device_id=other, device_id_type=pl.DeviceIdType.MESH
            )
        pl.semaphore_wait(barrier, len(others))


def send_to(source, target, send, recv, device):
    return pltpu.make_async_remote_copy(
        src_ref=source,
        dst_ref=target,
        send_sem=send,
        recv_sem=recv,
        device_id=device,
        device_id_type=pl.DeviceIdType.MESH,
    )


def part(ref, start, count):
    return ref.at[pl.ds(pl.multiple_of(start, 16), count)]


def add_rows(target, start, count, terms):
    tile = 48 if count % 48 == 0 else 32

    def body(i, _):
        at = pl.multiple_of(i * tile, 16)
        here = pl.ds(pl.multiple_of(start + at, 16), tile)
        total = target[here, :].astype(F32)
        for term in terms:
            total = total + term[pl.ds(at, tile), :].astype(F32)
        target[here, :] = total.astype(BF16)
        return 0

    lax.fori_loop(0, count // tile, body, 0)


class PlaneSum:
    def __init__(self, place, own, seen, out, refs):
        self.place, self.own, self.seen, self.out = place, own, seen, out
        (self.acc, self.seen_here, self.from_core, self.from_x, self.from_z, self.whole,
         self.send, self.recv, self.local) = refs
        self.rows = own.shape[0]

    @staticmethod
    def buffers(rows, width):
        return [
            pltpu.VMEM((rows // 2, width), BF16),
            pltpu.VMEM((rows // 2, width), BF16),
            pltpu.VMEM((rows // 2, width), BF16),
            pltpu.VMEM((rows // 4, width), BF16),
            pltpu.VMEM((3, rows // 16, width), BF16),
            pltpu.VMEM((rows // 2, width), BF16),
            pltpu.SemaphoreType.DMA((10,)),
            pltpu.SemaphoreType.DMA((10,)),
            pltpu.SemaphoreType.DMA((4,)),
        ]

    def copy(self, source, target, place, device):
        return send_to(source, target, self.send.at[place], self.recv.at[place], device)

    def core_copy(self):
        half = self.rows // 2
        source = part(self.own, (1 - self.place.core) * half, half)
        return self.copy(source, self.from_core, 0, self.place.across_core())

    def local_copies(self):
        half = self.rows // 2
        source = part(self.own, self.place.core * half, half)
        copies = [pltpu.make_async_copy(source, self.acc, self.local.at[0])]
        if self.seen is not None:
            copies.append(pltpu.make_async_copy(self.seen, self.seen_here, self.local.at[1]))
        return copies

    def x_copy(self):
        count = self.rows // 4
        source = part(self.acc, (1 - self.place.x) * count, count)
        return self.copy(source, self.from_x, 1, self.place.across_x())

    def z_copies(self):
        count = self.rows // 16
        copies = []
        for step in (1, 2, 3):
            there = (self.place.z + step) % 4
            source = part(self.acc, self.place.x * 4 * count + there * count, count)
            target = self.from_z.at[step - 1]
            copies.append(self.copy(source, target, 1 + step, self.place.along_z(step)))
        return copies

    def piece(self):
        count = self.rows // 16
        inside = self.place.x * 4 * count + self.place.z * count
        return part(self.acc, inside, count), part(self.whole, inside, count)

    def keep_copy(self):
        mine, there = self.piece()
        return pltpu.make_async_copy(mine, there, self.local.at[2])

    def back_z_copies(self):
        mine, there = self.piece()
        return [
            self.copy(mine, there, 4 + step, self.place.along_z(step)) for step in (1, 2, 3)
        ]

    def back_x_copy(self):
        count = self.rows // 4
        there = part(self.whole, self.place.x * count, count)
        return self.copy(there, there, 8, self.place.across_x())

    def back_core_copy(self):
        count = self.rows // 2
        there = part(self.out, self.place.core * count, count)
        return self.copy(self.whole, there, 9, self.place.across_core())

    def store_copy(self):
        count = self.rows // 2
        there = part(self.out, self.place.core * count, count)
        return pltpu.make_async_copy(self.whole, there, self.local.at[3])

    def begin_own(self):
        self.core_copy().start()
        self.local_copies()[0].start()

    def begin_seen(self):
        for copy in self.local_copies()[1:]:
            copy.start()

    def begin(self):
        self.begin_own()
        self.begin_seen()

    def along_x(self):
        self.core_copy().wait()
        for copy in self.local_copies():
            copy.wait()
        add_rows(self.acc, 0, self.rows // 2, [self.from_core, self.seen_here])
        self.x_copy().start()

    def along_z(self):
        self.x_copy().wait()
        count = self.rows // 4
        add_rows(self.acc, self.place.x * count, count, [self.from_x])
        for copy in self.z_copies():
            copy.start()

    def back_along_z(self):
        for copy in self.z_copies():
            copy.wait()
        count = self.rows // 16
        inside = self.place.x * 4 * count + self.place.z * count
        add_rows(self.acc, inside, count, [self.from_z.at[i] for i in range(3)])
        self.keep_copy().start()
        for copy in self.back_z_copies():
            copy.start()

    def back_along_x(self):
        self.keep_copy().wait()
        for copy in self.back_z_copies():
            copy.wait()
        self.back_x_copy().start()

    def back_to_core(self):
        self.back_x_copy().wait()
        self.back_core_copy().start()
        self.store_copy().start()

    def end(self):
        self.back_core_copy().wait()
        self.store_copy().wait()


class PartnerTerm:
    def __init__(self, place, other, seen, refs):
        self.place, self.other, self.seen = place, other, seen
        self.from_core, self.send, self.recv = refs
        self.half = other.shape[0] // 2

    @staticmethod
    def buffers(rows, width):
        return [
            pltpu.VMEM((rows // 2, width), BF16),
            pltpu.SemaphoreType.DMA((2,)),
            pltpu.SemaphoreType.DMA((2,)),
        ]

    def core_copy(self):
        source = part(self.other, (1 - self.place.core) * self.half, self.half)
        return send_to(
            source, self.from_core, self.send.at[0], self.recv.at[0], self.place.across_core()
        )

    def partner_copy(self):
        return send_to(
            self.from_core, self.seen, self.send.at[1], self.recv.at[1], self.place.partner()
        )

    def begin(self):
        self.core_copy().start()

    def to_partner(self):
        self.core_copy().wait()
        mine = part(self.other, self.place.core * self.half, self.half)
        add_rows(self.from_core, 0, self.half, [mine])
        self.partner_copy().start()

    def end(self):
        self.partner_copy().wait()


class SmallSum:
    ROWS = 16

    def __init__(self, place, pair, refs):
        self.place, self.pair = place, pair
        self.sums, self.got, self.got_own, self.send, self.recv = refs

    @staticmethod
    def buffers(width):
        rows = SmallSum.ROWS
        return [
            pltpu.VMEM((3, 2, rows, width), F32),
            pltpu.VMEM((5, 2, rows, width), F32),
            pltpu.VMEM((rows, width), F32),
            pltpu.SemaphoreType.DMA((6,)),
            pltpu.SemaphoreType.DMA((6,)),
        ]

    def copy(self, source, place, device):
        return send_to(source, self.got.at[place], self.send.at[place], self.recv.at[place], device)

    def core_copy(self):
        return self.copy(self.pair, 0, self.place.across_core())

    def x_copy(self):
        return self.copy(self.sums.at[0], 1, self.place.across_x())

    def z_copies(self):
        return [
            self.copy(self.sums.at[1], 1 + step, self.place.along_z(step)) for step in (1, 2, 3)
        ]

    def partner_copy(self):
        return send_to(
            self.sums.at[2, 1], self.got_own, self.send.at[5], self.recv.at[5],
            self.place.partner(),
        )

    def begin(self):
        self.core_copy().start()

    def over_x(self):
        self.core_copy().wait()
        self.sums[0] = self.pair[...] + self.got[0]
        self.x_copy().start()

    def over_z(self):
        self.x_copy().wait()
        self.sums[1] = self.sums[0] + self.got[1]
        for copy in self.z_copies():
            copy.start()

    def over_tp(self):
        for copy in self.z_copies():
            copy.wait()
        self.sums[2] = self.sums[1] + self.got[2] + self.got[3] + self.got[4]
        self.partner_copy().start()

    def end(self):
        self.partner_copy().wait()
        return self.sums[2, 0] + self.got_own[...]


class Fetch:
    def __init__(self, place, own, got, refs, deep):
        self.place, self.own, self.got, self.deep = place, own, got, deep
        self.send, self.recv = refs
        self.half = own.shape[0] // 2
        self.quarter = self.half // 2
        self.count = self.quarter // 2 if deep else self.quarter
        self.core_at = place.core * self.half
        self.x_at = self.core_at + place.x * self.quarter
        odd = place.z % 2
        self.at = self.x_at + odd * self.count if deep else self.x_at
        self.z_at = self.x_at + (1 - odd) * self.count
        self.z_device = place.at(z=place.z + 1 - 2 * odd)

    @staticmethod
    def buffers():
        return [pltpu.SemaphoreType.DMA((5,)), pltpu.SemaphoreType.DMA((5,))]

    def copy(self, source, start, count, place, device):
        there = part(self.got, start, count)
        here = part(source, start, count)
        return send_to(here, there, self.send.at[place], self.recv.at[place], device)

    def partner_copy(self):
        return self.copy(self.own, self.at, self.count, 0, self.place.partner())

    def z_copy(self):
        return self.copy(self.got, self.at, self.count, 1, self.z_device)

    def x_copies(self):
        copies = [self.copy(self.got, self.at, self.count, 2, self.place.across_x())]
        if self.deep:
            copies.append(self.copy(self.got, self.z_at, self.count, 3, self.place.across_x()))
        return copies

    def core_copy(self):
        return self.copy(self.got, self.core_at, self.half, 4, self.place.across_core())

    def begin(self):
        self.partner_copy().start()

    def share(self):
        self.partner_copy().wait()
        if self.deep:
            self.z_copy().start()
        self.x_copies()[0].start()

    def more_x(self):
        self.z_copy().wait()
        self.x_copies()[1].start()

    def to_core(self):
        for copy in self.x_copies():
            copy.wait()
        self.core_copy().start()

    def end(self):
        self.core_copy().wait()


FRONT_BLOCK = 512


def front_kernel(
    mask_ref, vec_ref, bias_ref, tok_hbm, wq_hbm, wk_hbm, wv_hbm, wout_hbm, wup_hbm, wdown_hbm, cot_hbm,
    x_out, qkv_out, att_out, log_out, resid_out, mid_out,
    cat_hbm, wout_all_hbm, up2_hbm, down2_hbm, grads_hbm, bias2_hbm, tok_out,
    tok_ref, x_ref, qkv_ref, att_ref, cat_ref, wout_ref, bias2_ref, up2_ref, down2_ref, grads_ref,
    load_sem, out_sem, swap_send, swap_recv, *scratch, heads, block,
):
    step = pl.program_id(0)
    place = Place()
    gain_ref, shift_ref, bout_ref, gain2_ref, shift2_ref = (
        vec_ref.at[pl.ds(i, 1)] for i in range(5)
    )
    half = heads * HEAD_DIM
    rows = tok_ref.shape[0]
    blocks = rows // FRONT_BLOCK
    pairs = heads // HEAD_GROUP
    base = [0, blocks, blocks + pairs, 2 * blocks + pairs, 2 * blocks + 2 * pairs]

    sems = [scratch[2 * i : 2 * i + 2] for i in range(6)]
    mine = [wq_hbm, wk_hbm, wv_hbm]
    projections = [
        Fetch(place, own, cat_ref.at[1, :, pl.ds(i * half, half)], sems[i], True)
        for i, own in enumerate(mine)
    ]
    fetch_out = Fetch(place, wout_hbm, wout_ref.at[pl.ds(half, half)], sems[3], True)
    fetch_up = Fetch(place, wup_hbm, up2_ref, sems[4], True)
    fetch_down = Fetch(place, wdown_hbm, down2_ref, sems[5], True)
    bias_copy = send_to(
        bias_ref, bias2_ref, swap_send.at[0], swap_recv.at[0], place.partner()
    )
    here = pl.ds(pl.multiple_of(place.rank * LEN_L, LEN_L), LEN_L)
    theirs = pl.ds(pl.multiple_of((1 - place.rank) * LEN_L, LEN_L), LEN_L)
    cot_copy = send_to(
        cot_hbm.at[theirs], grads_ref.at[here], swap_send.at[1], swap_recv.at[1], place.partner()
    )

    def token_rows(i):
        start = pl.multiple_of(i * 2 * LEN_L + place.rank * LEN_L, LEN_L)
        return tok_hbm.at[pl.ds(start, LEN_L)]

    token_loads = [
        pltpu.make_async_copy(token_rows(i), tok_ref.at[pl.ds(i * LEN_L, LEN_L)], load_sem.at[i])
        for i in (0, 1)
    ]
    weight_loads = [
        pltpu.make_async_copy(
            own, cat_ref.at[0, :, pl.ds(i * half, half)], load_sem.at[2 + i]
        )
        for i, own in enumerate(mine)
    ]
    out_load = pltpu.make_async_copy(wout_hbm, wout_ref.at[pl.ds(0, half)], load_sem.at[5])
    kept_copy = pltpu.make_async_copy(cot_hbm.at[here], grads_ref.at[here], out_sem.at[0])
    stores = [
        pltpu.make_async_copy(cat_ref, cat_hbm, out_sem.at[1]),
        pltpu.make_async_copy(wout_ref, wout_all_hbm, out_sem.at[2]),
        pltpu.make_async_copy(bias2_ref, bias2_hbm, out_sem.at[3]),
        pltpu.make_async_copy(tok_ref, tok_out, out_sem.at[4]),
    ]
    last_stores = [
        pltpu.make_async_copy(grads_ref, grads_hbm, out_sem.at[5]),
        pltpu.make_async_copy(up2_ref, up2_hbm, out_sem.at[6]),
        pltpu.make_async_copy(down2_ref, down2_hbm, out_sem.at[7]),
    ]

    @pl.when(step == 0)
    def _():
        for copy in (*token_loads, *weight_loads, out_load):
            copy.start()
        place.greet()
        for one in projections:
            one.begin()
        bias_copy.start()
        fetch_out.begin()
        for copy in token_loads:
            copy.wait()
        for copy in weight_loads:
            copy.wait()

    def at_step(when):
        return pl.when(step == when)

    @at_step(base[1] - 2)
    def _():
        fetch_up.begin()
        fetch_down.begin()

    @at_step(base[1])
    def _():
        for one in (*projections, fetch_out):
            one.share()

    @at_step(base[1] + 1)
    def _():
        for one in (*projections, fetch_out):
            one.more_x()

    @at_step(base[2] - 1)
    def _():
        for one in (*projections, fetch_out):
            one.to_core()
        kept_copy.start()
        fetch_up.share()
        fetch_down.share()
        cot_copy.start()

    @at_step(base[2])
    def _():
        for one in (*projections, fetch_out):
            one.end()
        bias_copy.wait()
        out_load.wait()
        for copy in stores:
            copy.start()

    @at_step(base[3] + 1)
    def _():
        fetch_up.more_x()
        fetch_down.more_x()

    @at_step(base[4] + 1)
    def _():
        fetch_up.to_core()
        fetch_down.to_core()

    @at_step(base[4] + blocks - 1)
    def _():
        for one in (fetch_up, fetch_down):
            one.end()
        kept_copy.wait()
        cot_copy.wait()
        for copy in last_stores:
            copy.start()

    def project(which, i, bias):
        at = pl.ds(pl.multiple_of(i * FRONT_BLOCK, FRONT_BLOCK), FRONT_BLOCK)
        column = jnp.transpose(bias[:, : 3 * half])[:, :1]
        value = (contract(cat_ref[which], x_ref[at, :], 0, 1) + column).astype(BF16)
        qkv_ref[:, at] = value
        qkv_out[0] = value

    @pl.when(step < base[1])
    def _():
        at = pl.ds(pl.multiple_of(step * FRONT_BLOCK, FRONT_BLOCK), FRONT_BLOCK)
        hat, _ = norm_parts(tok_ref[at, :].astype(F32))
        normed = (hat * gain_ref[...] + shift_ref[...]).astype(BF16)
        x_ref[at, :] = normed
        x_out[...] = normed
        project(0, step, bias_ref[...])

    @pl.when(jnp.logical_and(step >= base[2], step < base[3]))
    def _():
        project(1, step - base[2], bias2_ref[...])

    own_part = jnp.logical_and(step >= base[1], step < base[2])
    other_part = jnp.logical_and(step >= base[3], step < base[4])

    @pl.when(jnp.logical_or(own_part, other_part))
    def _():
        second = (step >= base[3]).astype(jnp.int32)
        pair = step - base[1] - second * (base[3] - base[1])
        attend_pair(mask_ref, qkv_ref, att_ref, att_out, log_out, pair, second, heads, block)

    @pl.when(step >= base[4])
    def _():
        i = step - base[4]
        at = pl.ds(pl.multiple_of(i * FRONT_BLOCK, FRONT_BLOCK), FRONT_BLOCK)
        product = contract(att_ref[:, at], wout_ref[...], 0, 0)
        resid = tok_ref[at, :].astype(F32) + product + bout_ref[...]
        resid_out[...] = resid
        hat, _ = norm_parts(resid)
        mid_out[...] = (hat * gain2_ref[...] + shift2_ref[...]).astype(BF16)

    @pl.when(step == base[4] + blocks - 1)
    def _():
        for copy in (*stores, *last_stores):
            copy.wait()


def attend_pair(mask_ref, qkv_ref, att_ref, att_out, log_out, pair, second, heads, block):
    rows = qkv_ref.shape[1]
    half = heads * HEAD_DIM
    first = pair * HEAD_GROUP
    work = []
    for head in range(HEAD_GROUP):
        work += [(head, 0, LEN_L, at, block) for at in range(0, LEN_L, block)]
        work += [(head, start, LEN_S, 0, LEN_S) for start in range(LEN_L, rows, LEN_S)]

    def load(which, head, columns):
        start = pl.multiple_of(which * half + (first + head) * HEAD_DIM, HEAD_DIM)
        return qkv_ref[pl.ds(start, HEAD_DIM), columns]

    def scores(item):
        head, start, count, at, size = item
        every = slice(start, start + count)
        keys = load(1, head, every)
        key_rows = jnp.concatenate([keys, keys, extra_rows([mask_ref[:, every]], count)], 0)
        query = scaled_query(load(0, head, slice(start + at, start + at + size)))
        query_rows = jnp.concatenate([*query, jnp.ones((16, size), BF16)], 0)
        return contract(key_rows, query_rows, 0, 0)

    def finish(item, score):
        head, start, count, at, size = item
        here = slice(start + at, start + at + size)
        values = load(2, head, slice(start, start + count))
        value_rows = jnp.concatenate([values, jnp.ones((16, count), BF16)], 0)
        top = jnp.max(score, axis=0, keepdims=True)
        weights = jnp.exp2(score - top).astype(BF16)
        mixed = contract(value_rows, weights, 1, 0)
        total = mixed[HEAD_DIM : HEAD_DIM + 1]
        result = (mixed[:HEAD_DIM] * (1.0 / total)).astype(BF16)
        att_out[0, head, :, here] = result
        start = pl.multiple_of(second * half + (first + head) * HEAD_DIM, HEAD_DIM)
        att_ref[pl.ds(start, HEAD_DIM), here] = result
        log_out[0, head, :, here] = top + jnp.log2(total)

    score = scores(work[0])
    for place, item in enumerate(work):
        later = scores(work[place + 1]) if place + 1 < len(work) else None
        finish(item, score)
        score = later


def front(
    mask, vectors, bias, tokens, w_query, w_key, w_value, w_out, w_up, w_down, cotangent, heads,
    block=1024,
):
    width = tokens.shape[1]
    rows = tokens.shape[0] // 2
    half = heads * HEAD_DIM
    hidden = w_up.shape[1]
    blocks, pairs = rows // FRONT_BLOCK, heads // HEAD_GROUP
    base = [0, blocks, blocks + pairs, 2 * blocks + pairs, 2 * blocks + 2 * pairs]
    anywhere = pl.BlockSpec(memory_space=pl.ANY)

    def row_block(first):
        return lambda s: (jnp.clip(s - first, 0, blocks - 1), 0)

    def qkv_block(s):
        late = (s >= base[2]).astype(jnp.int32)
        return late, 0, jnp.clip(s - late * base[2], 0, blocks - 1)

    def head_block(s):
        late = (s >= base[3]).astype(jnp.int32)
        return late, jnp.clip(s - base[1] - late * (base[3] - base[1]), 0, pairs - 1), 0, 0

    by_row = lambda first: pl.BlockSpec((FRONT_BLOCK, width), row_block(first))
    bias_rows, bias_width = bias.shape
    pair_total = pair_count(2 * heads, rows)
    return pl.pallas_call(
        functools.partial(front_kernel, heads=heads, block=block),
        grid=(base[4] + blocks,),
        in_specs=[
            whole((1, rows)),
            whole((8, width)),
            whole(bias.shape),
        ]
        + [anywhere] * 8,
        out_specs=[
            by_row(0),
            pl.BlockSpec((1, 3 * half, FRONT_BLOCK), qkv_block),
            pl.BlockSpec((1, HEAD_GROUP, HEAD_DIM, rows), head_block),
            pl.BlockSpec((1, HEAD_GROUP, 1, rows), head_block),
            by_row(base[4]),
            by_row(base[4]),
        ]
        + [anywhere] * 7,
        out_shape=[
            jax.ShapeDtypeStruct((rows, width), BF16),
            jax.ShapeDtypeStruct((2, 3 * half, rows), BF16),
            jax.ShapeDtypeStruct((2, heads, HEAD_DIM, rows), BF16),
            jax.ShapeDtypeStruct((2, heads, 1, rows), F32),
            jax.ShapeDtypeStruct((rows, width), F32),
            jax.ShapeDtypeStruct((rows, width), BF16),
            jax.ShapeDtypeStruct((2, width, 3 * half), BF16),
            jax.ShapeDtypeStruct((2 * half, width), BF16),
            jax.ShapeDtypeStruct((width, hidden), BF16),
            jax.ShapeDtypeStruct((hidden, width), BF16),
            jax.ShapeDtypeStruct((rows, width), BF16),
            jax.ShapeDtypeStruct((bias_rows, bias_width), F32),
            jax.ShapeDtypeStruct((rows, width), BF16),
        ],
        scratch_shapes=[
            pltpu.VMEM((rows, width), BF16),
            pltpu.VMEM((rows, width), BF16),
            pltpu.VMEM((3 * half, rows), BF16),
            pltpu.VMEM((2 * half, rows), BF16),
            pltpu.VMEM((2, width, 3 * half), BF16),
            pltpu.VMEM((2 * half, width), BF16),
            pltpu.VMEM((bias_rows, bias_width), F32),
            pltpu.VMEM((width, hidden), BF16),
            pltpu.VMEM((hidden, width), BF16),
            pltpu.VMEM((rows, width), BF16),
            pltpu.SemaphoreType.DMA((6,)),
            pltpu.SemaphoreType.DMA((8,)),
            pltpu.SemaphoreType.DMA((2,)),
            pltpu.SemaphoreType.DMA((2,)),
        ]
        + [ref for _ in range(6) for ref in Fetch.buffers()],
        compiler_params=pltpu.CompilerParams(
            vmem_limit_bytes=VMEM_LIMIT, collective_id=1, has_side_effects=True
        ),
        cost_estimate=cost(
            pair_total * 2 * 512 + 14 * rows * width * half, 40 * rows * width, pair_total
        ),
        name="front",
    )(
        mask, vectors, bias, tokens, w_query, w_key, w_value, w_out, w_up, w_down, cotangent,
    )


ERFC_TERMS = (0.254829592, -0.284496736, 1.421413741, -1.453152027, 1.061405429)
ERFC_SLOPE = 0.3275911


def gelu_and_slope(value):
    bell = jnp.exp2(value * value * (-0.5 * LOG2E))
    base = 1.0 + jnp.abs(value) * (ERFC_SLOPE * math.sqrt(0.5))
    ratio = 1.0 / base
    poly = ERFC_TERMS[4] * 0.5
    for term in ERFC_TERMS[3::-1]:
        poly = poly * ratio + term * 0.5
    tail = poly * ratio * bell
    below = jnp.where(value < 0.0, tail, 1.0 - tail)
    return value * below, below + value * bell * (1.0 / math.sqrt(2.0 * math.pi))


HIDDEN_BLOCK = 512
MID_BLOCK = 512
HIDDEN_ORDER = ((1, 0), (0, 0), (1, 1), (1, 2), (0, 1), (0, 2))
SLOTS = 4
MID_CHUNK = 512


def mid_kernel(
    mid_ref, grad_ref, bias_ref, resid_ref, vec_ref, w_ref, att_ref,
    up2_hbm, up_hbm, down2_hbm, down_hbm,
    out_ref, gresid_ref, gatt_ref, dw_own_ref, dw_other_ref, small_ref, db_ref,
    dup_hbm, ddown_hbm, seen_up, seen_down, gup_hbm, gdown_hbm,
    sum_ref, gmid_ref, act_ref, gpre_ref, up_ref, down_ref, dup_ref, ddown_ref, acc_ref,
    load_sem, store_sem, *scratch, blocks,
):
    step = pl.program_id(0)
    place = Place()
    rows, width = mid_ref.shape
    cut = lambda ref, i: ref.at[:, pl.ds(i * HIDDEN_BLOCK, HIDDEN_BLOCK)]
    take = lambda ref, i, count: ref.at[pl.ds(i * count, count)]
    terms = []
    for i in range(blocks):
        refs = [scratch[6 * i : 6 * i + 3], scratch[6 * i + 3 : 6 * i + 6]]
        slot = HIDDEN_ORDER.index((1, i)) % SLOTS
        terms.append(
            (
                PartnerTerm(place, dup_ref.at[slot], cut(seen_up, i), refs[0]),
                PartnerTerm(
                    place, ddown_ref.at[slot], take(seen_down, i, HIDDEN_BLOCK // 2), refs[1]
                ),
            )
        )

    first_sums = [
        PlaneSum(
            place, dup_ref.at[1], cut(seen_up, 0), gup_hbm, scratch[6 * blocks : 6 * blocks + 9]
        ),
        PlaneSum(
            place, ddown_ref.at[1], take(seen_down, 0, HIDDEN_BLOCK // 2), gdown_hbm,
            scratch[6 * blocks + 9 :],
        ),
    ]

    def loads(at):
        side, i = HIDDEN_ORDER[at]
        up, down = (up2_hbm, down2_hbm) if side else (up_hbm, down_hbm)
        slot = at % 2
        return [
            pltpu.make_async_copy(cut(up, i), up_ref.at[slot], load_sem.at[slot, 0]),
            pltpu.make_async_copy(
                take(down, i, HIDDEN_BLOCK), down_ref.at[slot], load_sem.at[slot, 1]
            ),
        ]

    def stores(i):
        slot = HIDDEN_ORDER.index((0, i)) % SLOTS
        return [
            pltpu.make_async_copy(dup_ref.at[slot], cut(dup_hbm, i), store_sem.at[i, 0]),
            pltpu.make_async_copy(
                ddown_ref.at[slot], take(ddown_hbm, i, HIDDEN_BLOCK), store_sem.at[i, 1]
            ),
        ]

    to_core = {3: terms[1], 4: terms[2]}
    to_partner = {1: terms[0], 4: terms[1], 5: terms[2]}

    for at in range(2 * blocks + 1):

        @pl.when(step == at)
        def _(at=at):
            if at == 0:
                for copy in loads(0):
                    copy.start()
                place.greet()
                sum_ref[...] = jnp.zeros_like(sum_ref)
                gmid_ref[...] = jnp.zeros_like(gmid_ref)
            if at < 2 * blocks:
                for copy in loads(at):
                    copy.wait()
            if at + 1 < 2 * blocks:
                for copy in loads(at + 1):
                    copy.start()
            for one in to_partner.get(at, ()):
                one.to_partner()
            for one in to_core.get(at, ()):
                one.begin()
            if at >= 1 and HIDDEN_ORDER[at - 1] in ((0, 1), (0, 2)):
                for copy in stores(HIDDEN_ORDER[at - 1][1]):
                    copy.start()
            if at == 2:
                for one in first_sums:
                    one.begin_own()
            if at == 3:
                for one in terms[0]:
                    one.end()
                for one in first_sums:
                    one.begin_seen()
                for one in first_sums:
                    one.along_x()
            if at == 4:
                for one in first_sums:
                    one.along_z()
            if at == 5:
                for one in first_sums:
                    one.back_along_z()
            if at == 6:
                for one in first_sums:
                    one.back_along_x()
            if at == 2 * blocks:
                acc_ref[...] = jnp.zeros_like(acc_ref)
                small_ref[...] = jnp.zeros_like(small_ref)

    @pl.when(step < 2 * blocks)
    def _():
        up, down, bias = up_ref[step % 2], down_ref[step % 2], bias_ref[0]

        def products(at):
            here = slice(at, at + MID_CHUNK)
            return (
                contract(mid_ref[here], up, 1, 0) + bias,
                contract(grad_ref[here], down, 1, 1),
            )

        now = products(0)
        db = None
        for at in range(0, rows, MID_CHUNK):
            here = slice(at, at + MID_CHUNK)
            later = products(at + MID_CHUNK) if at + MID_CHUNK < rows else None
            value, slope = gelu_and_slope(now[0])
            act = value.astype(BF16)
            gpre = (slope * now[1]).astype(BF16)
            act_ref[here] = act
            gpre_ref[here] = gpre
            term = jnp.sum(gpre.astype(F32), axis=0, keepdims=True)
            db = term if db is None else db + term
            sum_ref[here] += contract(act, down, 1, 0)
            gmid_ref[here] += contract(gpre, up, 1, 1)
            now = later
        db_ref[0] = db
        slot = lax.rem(step, SLOTS)
        ddown_ref[slot] = contract(act_ref[...], grad_ref[...], 0, 0).astype(BF16)
        dup_ref[slot] = contract(mid_ref[...], gpre_ref[...], 0, 0).astype(BF16)

    @pl.when(step == 0)
    def _():
        for one in terms[0]:
            one.begin()

    @pl.when(step >= 2 * blocks)
    def _():
        start = (step - 2 * blocks) * MID_BLOCK
        here = pl.ds(pl.multiple_of(start, MID_BLOCK), MID_BLOCK)
        resid = resid_ref[...]
        grads = grad_ref[here, :].astype(F32)
        out_ref[...] = (resid + sum_ref[here, :] + vec_ref[5:6]).astype(BF16)
        gmid = gmid_ref[here, :]
        hat, inv = norm_parts(resid)
        gresid = grads + norm_back(hat, inv, gmid * vec_ref[3:4])
        gresid_ref[...] = gresid
        branch = gresid.astype(BF16)
        gatt_ref[...] = contract(w_ref[...], branch, 1, 1).astype(BF16)
        acc_ref[...] += contract(branch, att_ref[...], 0, 1)
        small_ref[0:1] += jnp.sum(gmid * hat, axis=0, keepdims=True)
        small_ref[1:2] += jnp.sum(gmid, axis=0, keepdims=True)
        small_ref[2:3] += jnp.sum(gresid, axis=0, keepdims=True)
        small_ref[3:4] += jnp.sum(grads, axis=0, keepdims=True)

    @pl.when(step == pl.num_programs(0) - 1)
    def _():
        for one in first_sums:
            one.back_to_core()
        half = dw_own_ref.shape[1]
        dw_own_ref[...] = acc_ref[:, :half].astype(BF16)
        dw_other_ref[...] = acc_ref[:, half:].astype(BF16)
        for i in range(1, blocks):
            for copy in stores(i):
                copy.wait()
            for one in terms[i]:
                one.end()
        for one in first_sums:
            one.end()


def mid_part(mid, grads, biases, resid, vectors, w_out, attended, up2, up, down2, down):
    rows, width = mid.shape
    hidden = up.shape[1]
    blocks = hidden // HIDDEN_BLOCK
    first = 2 * blocks
    heads_width = attended.shape[0]
    anywhere = pl.BlockSpec(memory_space=pl.ANY)
    once = lambda shape: pl.BlockSpec(
        shape, lambda *_: (0,) * len(shape), pipeline_mode=pl.Buffered(1)
    )
    row_step = lambda s: jnp.maximum(s - first, 0)
    by_row = pl.BlockSpec((MID_BLOCK, width), lambda s: (row_step(s), 0))
    columns = pl.BlockSpec((heads_width, MID_BLOCK), lambda s: (0, row_step(s)))
    by_hidden = pl.BlockSpec((1, 1, HIDDEN_BLOCK), lambda s: (jnp.minimum(s, first - 1), 0, 0))
    half = (width, heads_width // 2)
    scratch = [
        pltpu.VMEM((rows, width), F32),
        pltpu.VMEM((rows, width), F32),
        pltpu.VMEM((rows, HIDDEN_BLOCK), BF16),
        pltpu.VMEM((rows, HIDDEN_BLOCK), BF16),
        pltpu.VMEM((2, width, HIDDEN_BLOCK), BF16),
        pltpu.VMEM((2, HIDDEN_BLOCK, width), BF16),
        pltpu.VMEM((SLOTS, width, HIDDEN_BLOCK), BF16),
        pltpu.VMEM((SLOTS, HIDDEN_BLOCK, width), BF16),
        pltpu.VMEM((width, heads_width), F32),
        pltpu.SemaphoreType.DMA((2, 2)),
        pltpu.SemaphoreType.DMA((blocks, 2)),
    ]
    for _ in range(blocks):
        scratch += PartnerTerm.buffers(width, HIDDEN_BLOCK)
        scratch += PartnerTerm.buffers(HIDDEN_BLOCK, width)
    scratch += PlaneSum.buffers(width, HIDDEN_BLOCK) + PlaneSum.buffers(HIDDEN_BLOCK, width)
    return pl.pallas_call(
        functools.partial(mid_kernel, blocks=blocks),
        grid=(first + rows // MID_BLOCK,),
        in_specs=[
            once((rows, width)), once((rows, width)), by_hidden, by_row, whole((8, width)),
            once((heads_width, width)), columns,
        ]
        + [anywhere] * 4,
        out_specs=[
            by_row, by_row, columns, whole(half), whole(half), whole((8, width)), by_hidden,
        ]
        + [anywhere] * 6,
        out_shape=[
            jax.ShapeDtypeStruct((rows, width), BF16),
            jax.ShapeDtypeStruct((rows, width), F32),
            jax.ShapeDtypeStruct((heads_width, rows), BF16),
            jax.ShapeDtypeStruct(half, BF16),
            jax.ShapeDtypeStruct(half, BF16),
            jax.ShapeDtypeStruct((8, width), F32),
            jax.ShapeDtypeStruct((first, 1, HIDDEN_BLOCK), F32),
            jax.ShapeDtypeStruct((width, hidden), BF16),
            jax.ShapeDtypeStruct((hidden, width), BF16),
            jax.ShapeDtypeStruct((width // 2, hidden), BF16),
            jax.ShapeDtypeStruct((hidden // 2, width), BF16),
            jax.ShapeDtypeStruct((width, HIDDEN_BLOCK), BF16),
            jax.ShapeDtypeStruct((HIDDEN_BLOCK, width), BF16),
        ],
        scratch_shapes=scratch,
        compiler_params=pltpu.CompilerParams(
            vmem_limit_bytes=VMEM_LIMIT, collective_id=2, has_side_effects=True
        ),
        cost_estimate=cost(
            24 * rows * width * hidden + 4 * rows * width * heads_width, 60 * rows * width,
            4 * rows * hidden,
        ),
        name="mid",
    )(mid, grads, biases, resid, vectors, w_out, attended, up2, up, down2, down)


TAIL_BLOCK = 512
SUM_ACTIONS = ("begin", "along_x", "along_z", "back_along_z", "back_along_x", "back_to_core")
SUM_STEPS = (
    (0, 1, 3, 6, 9, 11),
    (0, 2, 5, 8, 11, 13),
    (0, 4, 6, 10, 13, 15),
    (0, 5, 8, 12, 14, 16),
    (0, 8, 10, 13, 15, 17),
    (None, 17, 18, 20),
    (None, 17, 19),
    (None, 17, 20),
)
LAST_ACTIONS = (
    0, (6, "back_along_z"), (5, "back_along_x"), 1, (7, "back_along_z"), (6, "back_along_x"),
    (5, "back_to_core"), 2, (7, "back_along_x"), (6, "back_to_core"), (7, "back_to_core"),
)


def tail_kernel(
    mask_ref, qkv_ref, att_ref, log_ref, gatt_ref, vec_ref, small2_ref, dbup1_ref, dbup2_ref,
    wout2_ref, x_hbm, w_hbm, tok_hbm, gresid_hbm, up_hbm, down_hbm, wout_hbm, seen_up,
    seen_down, out_hbm,
    gtok_ref, small_ref, got_hbm, gup_hbm, gdown_hbm, gout_hbm, gcat_hbm, got_out,
    d_ref, x_ref, w_ref, tok_ref, gresid_ref, dw_ref, dw2_ref, seen_cat, sent_ref, pair_ref,
    load_sem, row_sem, tok_send, tok_recv, *scratch, heads, block,
):
    step = pl.program_id(0)
    place = Place()
    first_rows = 2 * heads + 1
    last_step = first_rows + 3
    width = x_ref.shape[1]
    half = heads * HEAD_DIM

    groups = []
    at = 0
    for count in [9] * 5 + [0] + [9] * 3 + [3, 3, 5]:
        groups.append(scratch[at : at + count])
        at += count
    columns = lambda ref, i: ref.at[:, pl.ds(i * HIDDEN_BLOCK, HIDDEN_BLOCK)]
    rows_of = lambda ref, i, count: ref.at[pl.ds(i * count, count)]
    sums = [
        PlaneSum(place, columns(up_hbm, i), columns(seen_up, i), columns(gup_hbm, i - 1), groups[i])
        for i in (1, 2)
    ]
    sums += [
        PlaneSum(
            place,
            rows_of(down_hbm, i, HIDDEN_BLOCK),
            rows_of(seen_down, i, HIDDEN_BLOCK // 2),
            rows_of(gdown_hbm, i - 1, HIDDEN_BLOCK),
            groups[2 + i],
        )
        for i in (1, 2)
    ]
    sums.append(PlaneSum(place, wout_hbm, None, gout_hbm, groups[0]))
    third = lambda ref, i: ref.at[:, pl.ds(i * half, half)]
    cat_sums = [
        PlaneSum(
            place, third(dw_ref, i), None, third(gcat_hbm, i),
            (groups[6 + i][0], third(seen_cat, i), *groups[6 + i][2:]),
        )
        for i in range(3)
    ]
    cat_term = PartnerTerm(place, dw2_ref, seen_cat, groups[9])
    out_term = PartnerTerm(place, wout2_ref, groups[0][1], groups[10])
    own_small, other_small = pair_ref.at[0], pair_ref.at[1]
    small = SmallSum(place, pair_ref, groups[11])
    theirs = pl.ds(pl.multiple_of((1 - place.rank) * LEN_L, LEN_L), LEN_L)
    out_load = pltpu.make_async_copy(out_hbm.at[theirs], sent_ref, load_sem.at[2])
    piece = LEN_L // 4
    out_copies = [
        send_to(
            sent_ref.at[pl.ds(i * piece, piece)], got_out.at[pl.ds(i * piece, piece)],
            tok_send.at[2 + i], tok_recv.at[2 + i], place.partner(),
        )
        for i in range(4)
    ]

    loads = [
        pltpu.make_async_copy(x_hbm, x_ref, load_sem.at[0]),
        pltpu.make_async_copy(w_hbm, w_ref, load_sem.at[1]),
    ]

    def row_start(i):
        mine = i // 2
        return ((1 - mine) * (1 - place.rank) + mine * place.rank) * LEN_L + (i % 2) * TAIL_BLOCK

    def row_loads(i):
        start = pl.ds(pl.multiple_of(row_start(i), TAIL_BLOCK), TAIL_BLOCK)
        slot = i % 2
        return [
            pltpu.make_async_copy(tok_hbm.at[start], tok_ref.at[slot], row_sem.at[slot, 0]),
            pltpu.make_async_copy(gresid_hbm.at[start], gresid_ref.at[slot], row_sem.at[slot, 1]),
        ]

    def token_copy(i):
        there = pl.ds(i * TAIL_BLOCK, TAIL_BLOCK)
        return send_to(
            sent_ref.at[there], got_hbm.at[there], tok_send.at[i], tok_recv.at[i], place.partner()
        )

    def weight_gradient(source, target, i):
        here = pl.ds(i * half, half)
        product = contract(x_ref[...], d_ref[source, here, :], 0, 1)
        target[:, here] = product.astype(BF16)

    def bias_rows(source, target):
        ones = jnp.ones((16, d_ref.shape[2]), BF16)
        for i, which in ((0, 0), (1, 2)):
            row = contract(ones, d_ref[source, pl.ds(which * half, half), :], 1, 1)
            target[8:9, pl.ds(i * half, half)] = row[:1]

    events = {}
    sums += cat_sums
    for one, times in zip(sums, SUM_STEPS):
        for when, action in zip(times, SUM_ACTIONS):
            if when is None:
                continue
            events.setdefault(when, []).append(getattr(one, action))

    for when in sorted(events):

        @pl.when(step == when)
        def _(when=when):
            if when == 0:
                out_load.start()
                place.greet()
                out_term.begin()
            if when == 1:
                out_term.to_partner()
                out_load.wait()
                out_copies[0].start()
                out_copies[1].start()
            if when == 3:
                out_copies[2].start()
            if when == 13:
                out_copies[3].start()
            if when == 8:
                out_term.end()
            for action in events[when]:
                action()

    @pl.when(step == 2)
    def _():
        for copy in loads:
            copy.start()

    @pl.when(step == heads)
    def _():
        for copy in loads:
            copy.wait()
        for i in range(3):
            weight_gradient(1, dw2_ref, i)
        cat_term.begin()

    @pl.when(step == heads + 1)
    def _():
        cat_term.to_partner()
        own_small[...] = jnp.zeros_like(own_small)
        other_small[...] = jnp.zeros_like(other_small)
        bias_rows(1, other_small)

    @pl.when(step < 2 * heads)
    def _():
        back_one_head(mask_ref, qkv_ref, att_ref, log_ref, gatt_ref, d_ref, step, heads, block)

    @pl.when(step == 2 * heads)
    def _():
        for copy in row_loads(0):
            copy.start()
        cat_term.end()
        for i in range(3):
            weight_gradient(0, dw_ref, i)
            cat_sums[i].begin()
        bias_rows(0, own_small)


    for i in range(4):

        @pl.when(step == first_rows + i)
        def _(i=i):
            for copy in row_loads(i):
                copy.wait()
            if i == 0:
                for copy in out_copies:
                    copy.wait()
            if i < 3:
                for copy in row_loads(i + 1):
                    copy.start()
            here = pl.ds(pl.multiple_of(row_start(i), TAIL_BLOCK), TAIL_BLOCK)
            gin = contract(d_ref[0, :, here], w_ref[0], 0, 1)
            gin += contract(d_ref[1, :, here], w_ref[1], 0, 1)
            hat, inv = norm_parts(tok_ref[i % 2].astype(F32))
            gtok = gresid_ref[i % 2] + norm_back(hat, inv, gin * vec_ref[0:1])
            own_small[0:1] += jnp.sum(gin * hat, axis=0, keepdims=True)
            own_small[1:2] += jnp.sum(gin, axis=0, keepdims=True)
            if i < 2:
                sent_ref[pl.ds(i * TAIL_BLOCK, TAIL_BLOCK), :] = gtok.astype(BF16)
                token_copy(i).start()
            else:
                gtok_ref[...] = gtok

    @pl.when(step == last_step)
    def _():
        own_small[2:6] = small2_ref[0:4]
        other_small[0:2] = own_small[0:2]
        other_small[2:6] = small2_ref[0:4]
        for i in (0, 1):
            own_small[6 + i : 7 + i] = dbup1_ref[:, pl.ds(i * width, width)]
            other_small[6 + i : 7 + i] = dbup2_ref[:, pl.ds(i * width, width)]
        small.begin()
        small_actions = (small.over_x, small.over_z, small.over_tp)
        for item in LAST_ACTIONS:
            if isinstance(item, int):
                small_actions[item]()
            else:
                getattr(sums[item[0]], item[1])()
        small_ref[...] = small.end()
        for i in (0, 1):
            token_copy(i).wait()
        for one in sums:
            one.end()


def back_one_head(mask_ref, qkv_ref, att_ref, log_ref, gatt_ref, d_ref, step, heads, block):
    rows = qkv_ref.shape[4]
    half = heads * HEAD_DIM
    source = 1 - step // heads
    head_at = pl.multiple_of((step % heads) * HEAD_DIM, HEAD_DIM)

    def store(which, columns, value):
        d_ref[source, pl.ds(which * half + head_at, HEAD_DIM), columns] = value.astype(BF16)

    work = []
    images = [(0, LEN_L, block)] + [(at, LEN_S, LEN_S) for at in range(LEN_L, rows, LEN_S)]
    for start, count, size in images:
        work += [(start, count, at, size) for at in range(start, start + count, size)]
    kept = {}

    def operands(start, count):
        if start not in kept:
            every = slice(start, start + count)
            keys = qkv_ref[0, 1, 0, :, every]
            values = qkv_ref[0, 2, 0, :, every]
            ones = jnp.ones((1, count), F32)
            key_rows = jnp.concatenate(
                [keys, keys, extra_rows([ones, ones, ones, mask_ref[:, every]], count)], 0
            )
            value_rows = jnp.concatenate([values, extra_rows([ones, ones, ones], count)], 0)
            kept[start] = keys, key_rows, value_rows
        return kept[start]

    def products(item):
        start, count, at, size = item
        here = slice(at, at + size)
        _, key_rows, value_rows = operands(start, count)
        query = qkv_ref[0, 0, 0, :, here]
        grads = gatt_ref[0, 0, :, here]
        inner = jnp.sum(
            grads.astype(F32) * att_ref[0, 0, :, here].astype(F32), axis=0, keepdims=True
        )
        terms = three_terms(-log_ref[0, 0, :, here]) + [jnp.ones((1, size), F32)]
        query_rows = jnp.concatenate([*scaled_query(query), extra_rows(terms, size)], 0)
        grad_rows = jnp.concatenate([grads, extra_rows(three_terms(-inner), size)], 0)
        return contract(query_rows, key_rows, 0, 0), contract(grad_rows, value_rows, 0, 0)

    sums = {}
    now = products(work[0])
    for place, item in enumerate(work):
        later = products(work[place + 1]) if place + 1 < len(work) else None
        start, count, at, size = item
        here = slice(at, at + size)
        keys = operands(start, count)[0]
        query = qkv_ref[0, 0, 0, :, here]
        grads = gatt_ref[0, 0, :, here]
        score, grad_probs = now
        probs = jnp.exp2(score)
        grad_score = (probs * grad_probs).astype(BF16)
        part_values = contract(grads, probs.astype(BF16), 1, 0)
        part_keys = contract(query, grad_score, 1, 0)
        store(0, here, contract(keys, grad_score, 1, 1) * SCALE)
        if start in sums:
            part_keys, part_values = sums[start][0] + part_keys, sums[start][1] + part_values
        sums[start] = part_keys, part_values
        if at + size == start + count:
            every = slice(start, start + count)
            store(1, every, part_keys * SCALE)
            store(2, every, part_values)
        now = later


def tail(
    mask, qkv, att, log_total, gatt, vectors, small2, dbup1, dbup2, dwout2, normed, w_cat,
    tokens, gresid, dup, ddown, dwout, seen_up, seen_down, out_rows, block=256,
):
    _, _, heads, _, rows = qkv.shape
    _, width, out = w_cat.shape
    anywhere = pl.BlockSpec(memory_space=pl.ANY)
    last = 2 * heads - 1

    def head(h):
        h = jnp.minimum(h, last)
        return 1 - h // heads, h % heads

    all_three = pl.BlockSpec(
        (1, 3, 1, HEAD_DIM, rows), lambda h: (head(h)[0], 0, head(h)[1], 0, 0)
    )
    one = pl.BlockSpec((1, 1, HEAD_DIM, rows), lambda h: (*head(h), 0, 0))
    row = pl.BlockSpec((1, 1, 1, rows), lambda h: (*head(h), 0, 0))
    sum_shapes = [dwout.shape] + [(width, HIDDEN_BLOCK)] * 2 + [(HIDDEN_BLOCK, width)] * 2 + [(width, out // 3)] * 3
    scratch = [
        pltpu.VMEM((2, out, rows), BF16),
        pltpu.VMEM((rows, width), BF16),
        pltpu.VMEM((2, width, out), BF16),
        pltpu.VMEM((2, TAIL_BLOCK, width), BF16),
        pltpu.VMEM((2, TAIL_BLOCK, width), F32),
        pltpu.VMEM((width, out), BF16),
        pltpu.VMEM((width, out), BF16),
        pltpu.VMEM((width // 2, out), BF16),
        pltpu.VMEM((rows // 2, width), BF16),
        pltpu.VMEM((2, SmallSum.ROWS, width), F32),
        pltpu.SemaphoreType.DMA((3,)),
        pltpu.SemaphoreType.DMA((2, 2)),
        pltpu.SemaphoreType.DMA((6,)),
        pltpu.SemaphoreType.DMA((6,)),
    ]
    for shape in sum_shapes:
        scratch += PlaneSum.buffers(*shape)
    scratch += PartnerTerm.buffers(width, out) + PartnerTerm.buffers(*dwout.shape)
    scratch += SmallSum.buffers(width)
    pairs = pair_count(2 * heads, rows)
    first_rows = 2 * heads + 1
    return pl.pallas_call(
        functools.partial(tail_kernel, heads=heads, block=block),
        grid=(first_rows + 4,),
        in_specs=[
            whole((1, rows)), all_three, one, row, one, whole((8, width)), whole((8, width)),
            whole((1, 2 * width)), whole((1, 2 * width)), whole(dwout.shape),
        ]
        + [anywhere] * 10,
        out_specs=[
            pl.BlockSpec(
                (TAIL_BLOCK, width), lambda h: (jnp.maximum(h - first_rows - 2, 0), 0)
            ),
            whole((SmallSum.ROWS, width)),
        ]
        + [anywhere] * 6,
        out_shape=[
            jax.ShapeDtypeStruct((rows // 2, width), F32),
            jax.ShapeDtypeStruct((SmallSum.ROWS, width), F32),
            jax.ShapeDtypeStruct((rows // 2, width), BF16),
            jax.ShapeDtypeStruct((width, dup.shape[1] - HIDDEN_BLOCK), BF16),
            jax.ShapeDtypeStruct((ddown.shape[0] - HIDDEN_BLOCK, width), BF16),
            jax.ShapeDtypeStruct(dwout.shape, BF16),
            jax.ShapeDtypeStruct((width, out), BF16),
            jax.ShapeDtypeStruct((rows // 2, width), BF16),
        ],
        scratch_shapes=scratch,
        compiler_params=pltpu.CompilerParams(
            vmem_limit_bytes=VMEM_LIMIT, collective_id=0, has_side_effects=True
        ),
        cost_estimate=cost(pairs * 5 * 512, 32 * heads * HEAD_DIM * rows, pairs),
        name="tail",
    )(
        mask, qkv, att, log_total, gatt, vectors, small2, dbup1, dbup2, dwout2, normed, w_cat,
        tokens, gresid, dup, ddown, dwout, seen_up, seen_down, out_rows,
    )


def joined(mine, theirs, second):
    return jnp.where(second, jnp.concatenate([theirs, mine], 0), jnp.concatenate([mine, theirs], 0))


def half_of(array, second):
    size = array.shape[0] // 2
    return lax.dynamic_slice_in_dim(array, jnp.where(second, size, 0), size, 0)


def by_images(
    tokens, long_lengths, short_lengths, ln1_gain, ln1_bias, w_query, b_query, w_key, w_value,
    b_value, w_out, b_out, ln2_gain, ln2_bias, w_up, b_up, w_down, b_down, cotangent,
):
    rank = lax.axis_index("tp")
    rank_arr = jnp.reshape(rank, (1,)).astype(jnp.int32)
    second = rank == 1
    rows = tokens.shape[0] // 2
    width = tokens.shape[1]
    half = w_query.shape[1]
    heads = half // HEAD_DIM
    long_len = lax.dynamic_slice_in_dim(long_lengths, rank, 1, 0)
    shorts = short_lengths.shape[0] // 2
    short_len = lax.dynamic_slice_in_dim(short_lengths, rank * shorts, shorts, 0)
    valid = jnp.concatenate(
        [
            jnp.arange(LEN_L) < long_len[0],
            (jnp.arange(LEN_S)[None, :] < short_len[:, None]).reshape(-1),
        ]
    )
    mask = jnp.where(valid, 0.0, -1e30).astype(F32).reshape(1, -1)
    vectors = jnp.stack(
        [ln1_gain, ln1_bias, b_out, ln2_gain, ln2_bias, b_down, b_down, b_down]
    ).astype(F32)
    biases = jnp.concatenate([b_query, jnp.zeros_like(b_query), b_value, b_up]).astype(F32)
    bias = jnp.broadcast_to(biases.reshape(1, -1), (8, biases.shape[0]))

    (normed, qkv, att, log_total, resid, mid, w_cat, w_out_all, w_up2, w_down2, grads, bias2,
     own_tokens) = front(
        mask, vectors, bias, tokens, w_query, w_key, w_value, w_out, w_up, w_down, cotangent, heads,
    )
    qkv = qkv.reshape(2, 3, heads, HEAD_DIM, rows)
    attended = att.reshape(2 * half, rows)
    up_bias = [
        rows_of.reshape(-1, 1, HIDDEN_BLOCK)
        for rows_of in (bias[0, 3 * half :], bias2[0, 3 * half :])
    ]
    up_bias = jnp.stack([up_bias[side][i] for side, i in HIDDEN_ORDER])
    (out, gresid, gatt, dwout1, dwout2, small2, db_up, dup1, ddown1, seen_up, seen_down,
     first_up, first_down) = mid_part(
        mid, grads, up_bias, resid, vectors, w_out_all,
        attended, w_up2, w_up, w_down2, w_down,
    )
    dbup1, dbup2 = (
        jnp.concatenate([db_up[at] for at, (own, _) in enumerate(HIDDEN_ORDER) if own == side], 1)
        for side in (0, 1)
    )
    gtok, small, got_tok, grad_up, grad_down, grad_out_t, grad_cat, got_out = tail(
        mask, qkv, att, log_total, gatt.reshape(2, heads, HEAD_DIM, rows), vectors, small2,
        dbup1, dbup2, dwout2, normed, w_cat, own_tokens, gresid, dup1, ddown1, dwout1,
        seen_up, seen_down, out,
    )
    result = joined(half_of(out, second), got_out, second)
    grad_tokens = joined(gtok, got_tok.astype(F32), second)
    grad_cat = grad_cat.astype(F32)
    return (
        result,
        grad_tokens,
        small[0],
        small[1],
        grad_cat[:, :half],
        small[8, :half],
        grad_cat[:, half : 2 * half],
        grad_cat[:, 2 * half :],
        small[8, half:],
        grad_out_t.T.astype(F32),
        small[4],
        small[2],
        small[3],
        jnp.concatenate([first_up, grad_up], 1).astype(F32),
        small[6:8].reshape(-1),
        jnp.concatenate([first_down, grad_down], 0).astype(F32),
        small[5],
    )


def layer_norm(values, gain, shift):
    center = values - jnp.mean(values, axis=-1, keepdims=True)
    spread = jnp.mean(center * center, axis=-1, keepdims=True)
    return center * lax.rsqrt(spread + 1e-06) * gain + shift


def dot_plain(left, right):
    return jnp.dot(left, right, preferred_element_type=jnp.float32)


def dot_rows(left, right):
    return lax.dot_general(
        left, right, (((0,), (0,)), ((), ())), preferred_element_type=jnp.float32
    )


def dot_back(left, right):
    return lax.dot_general(
        left, right, (((1,), (1,)), ((), ())), preferred_element_type=jnp.float32
    )


def group_shape(image_count, seq_len, head_count):
    per_step = math.gcd(image_count, max(1, 512 // seq_len))
    return (image_count // per_step, per_step, seq_len, head_count, HEAD_DIM)


def masked_scores(query_blk, key_blk, length_blk):
    seq_len = query_blk.shape[1]
    raw = jnp.einsum(
        "bqhd,bkhd->bhqk", query_blk, key_blk, preferred_element_type=jnp.float32
    ) * HEAD_DIM ** (-0.5)
    keep = jnp.arange(seq_len, dtype=jnp.int32)[None, :] < length_blk[:, None]
    return jnp.where(keep[:, None, None, :], raw, -1e30)


def attention_forward(queries, key_rows, value_rows, lengths, seq_len):
    image_count = lengths.shape[0]
    head_count = queries.shape[1] // HEAD_DIM
    block_shape = group_shape(image_count, seq_len, head_count)

    def one_step(block):
        query_blk, key_blk, value_blk, length_blk = block
        scores = masked_scores(query_blk, key_blk, length_blk)
        row_top = jnp.max(scores, axis=-1, keepdims=True)
        exp_terms = jnp.exp(scores - row_top)
        row_total = jnp.sum(exp_terms, axis=-1, keepdims=True)
        weights = (exp_terms / row_total).astype(jnp.bfloat16)
        mixed = jnp.einsum(
            "bhqk,bkhd->bqhd", weights, value_blk, preferred_element_type=jnp.float32
        )
        return (mixed, (row_top + jnp.log(row_total))[..., 0])

    mixed, log_total = lax.map(
        one_step,
        (
            queries.reshape(block_shape),
            key_rows.reshape(block_shape),
            value_rows.reshape(block_shape),
            lengths.reshape(block_shape[:2]),
        ),
    )
    return (mixed.reshape(image_count * seq_len, head_count * HEAD_DIM), log_total)


def attention_backward(queries, key_rows, value_rows, grads, lengths, log_total, seq_len):
    image_count = lengths.shape[0]
    head_count = queries.shape[1] // HEAD_DIM
    block_shape = group_shape(image_count, seq_len, head_count)
    scale = HEAD_DIM ** (-0.5)

    def one_step(block):
        query_blk, key_blk, value_blk, grad_blk, length_blk, total_blk = block
        scores = masked_scores(query_blk, key_blk, length_blk)
        probs = jnp.exp(scores - total_blk[..., None])
        grad_values = jnp.einsum(
            "bhqk,bqhd->bkhd",
            probs.astype(jnp.bfloat16),
            grad_blk,
            preferred_element_type=jnp.float32,
        )
        grad_probs = jnp.einsum(
            "bqhd,bkhd->bhqk", grad_blk, value_blk, preferred_element_type=jnp.float32
        )
        inner = jnp.sum(probs * grad_probs, axis=-1, keepdims=True)
        grad_scores = (probs * (grad_probs - inner)).astype(jnp.bfloat16)
        grad_queries = (
            jnp.einsum("bhqk,bkhd->bqhd", grad_scores, key_blk, preferred_element_type=jnp.float32)
            * scale
        )
        grad_keys = (
            jnp.einsum(
                "bhqk,bqhd->bkhd", grad_scores, query_blk, preferred_element_type=jnp.float32
            )
            * scale
        )
        return (grad_queries, grad_keys, grad_values)

    results = lax.map(
        one_step,
        (
            queries.reshape(block_shape),
            key_rows.reshape(block_shape),
            value_rows.reshape(block_shape),
            grads.reshape(block_shape),
            lengths.reshape(block_shape[:2]),
            log_total,
        ),
    )
    flat = (image_count * seq_len, head_count * HEAD_DIM)
    return tuple((item.reshape(flat) for item in results))


def local(
    tokens,
    long_lengths,
    short_lengths,
    ln1_gain,
    ln1_bias,
    w_query,
    b_query,
    w_key,
    w_value,
    b_value,
    w_out,
    b_out,
    ln2_gain,
    ln2_bias,
    w_up,
    b_up,
    w_down,
    b_down,
    cotangent,
):
    tp_count = lax.axis_size("tp")
    tp_rank = lax.axis_index("tp")
    row_count = tokens.shape[0]
    share = row_count // tp_count
    split = long_lengths.shape[0] * LEN_L
    gain_one = ln1_gain.astype(jnp.float32)
    shift_one = ln1_bias.astype(jnp.float32)
    gain_two = ln2_gain.astype(jnp.float32)
    shift_two = ln2_bias.astype(jnp.float32)
    normed_in = layer_norm(tokens.astype(jnp.float32), gain_one, shift_one).astype(jnp.bfloat16)
    queries = (dot_plain(normed_in, w_query) + b_query.astype(jnp.float32)).astype(jnp.bfloat16)
    key_rows = dot_plain(normed_in, w_key).astype(jnp.bfloat16)
    value_rows = (dot_plain(normed_in, w_value) + b_value.astype(jnp.float32)).astype(jnp.bfloat16)
    long_mixed, long_total = attention_forward(
        queries[:split], key_rows[:split], value_rows[:split], long_lengths, LEN_L
    )
    short_mixed, short_total = attention_forward(
        queries[split:], key_rows[split:], value_rows[split:], short_lengths, LEN_S
    )
    attended = jnp.concatenate([long_mixed, short_mixed], axis=0).astype(jnp.bfloat16)
    attn_sum = lax.psum_scatter(dot_plain(attended, w_out), "tp", scatter_dimension=0, tiled=True)
    own_tokens = lax.dynamic_slice_in_dim(tokens, tp_rank * share, share, 0).astype(jnp.float32)
    resid = own_tokens + attn_sum + b_out.astype(jnp.float32)
    normed_mid = layer_norm(resid, gain_two, shift_two).astype(jnp.bfloat16)
    grad_out = cotangent.astype(jnp.float32)
    mid_rows = lax.all_gather(normed_mid, "tp", axis=0, tiled=True)
    pre_up = dot_plain(mid_rows, w_up) + b_up.astype(jnp.float32)
    activ = jax.nn.gelu(pre_up, approximate=False).astype(jnp.bfloat16)
    ffn_sum = lax.psum_scatter(
        dot_plain(activ, w_down).astype(jnp.bfloat16), "tp", scatter_dimension=0, tiled=True
    ).astype(jnp.float32)
    result = resid + ffn_sum + b_down.astype(jnp.float32)
    grad_rows = lax.all_gather(cotangent, "tp", axis=0, tiled=True)
    grad_w_down = dot_rows(activ, grad_rows)
    grad_activ = dot_back(grad_rows, w_down)
    _, gelu_back = jax.vjp(lambda inner: jax.nn.gelu(inner, approximate=False), pre_up)
    grad_pre = gelu_back(grad_activ)[0].astype(jnp.bfloat16)
    grad_w_up = dot_rows(mid_rows, grad_pre)
    grad_b_up = jnp.sum(grad_pre.astype(jnp.float32), axis=0)
    grad_mid = lax.psum_scatter(dot_back(grad_pre, w_up), "tp", scatter_dimension=0, tiled=True)
    _, norm_two_back = jax.vjp(layer_norm, resid, gain_two, shift_two)
    grad_resid_norm, grad_gain_two, grad_shift_two = norm_two_back(grad_mid)
    grad_resid = grad_out + grad_resid_norm
    grad_b_down = jnp.sum(grad_out, axis=0)
    grad_b_out = jnp.sum(grad_resid, axis=0)
    grad_branch = lax.all_gather(grad_resid.astype(jnp.bfloat16), "tp", axis=0, tiled=True)
    grad_w_out = dot_rows(attended, grad_branch)
    grad_attended = dot_back(grad_branch, w_out).astype(jnp.bfloat16)
    long_grads = attention_backward(
        queries[:split],
        key_rows[:split],
        value_rows[:split],
        grad_attended[:split],
        long_lengths,
        long_total,
        LEN_L,
    )
    short_grads = attention_backward(
        queries[split:],
        key_rows[split:],
        value_rows[split:],
        grad_attended[split:],
        short_lengths,
        short_total,
        LEN_S,
    )
    grad_queries = jnp.concatenate([long_grads[0], short_grads[0]], axis=0).astype(jnp.bfloat16)
    grad_keys = jnp.concatenate([long_grads[1], short_grads[1]], axis=0).astype(jnp.bfloat16)
    grad_values = jnp.concatenate([long_grads[2], short_grads[2]], axis=0).astype(jnp.bfloat16)
    grad_w_query = dot_rows(normed_in, grad_queries)
    grad_b_query = jnp.sum(grad_queries.astype(jnp.float32), axis=0)
    grad_w_key = dot_rows(normed_in, grad_keys)
    grad_w_value = dot_rows(normed_in, grad_values)
    grad_b_value = jnp.sum(grad_values.astype(jnp.float32), axis=0)
    grad_in = lax.psum_scatter(
        dot_back(grad_queries, w_query)
        + dot_back(grad_keys, w_key)
        + dot_back(grad_values, w_value),
        "tp",
        scatter_dimension=0,
        tiled=True,
    )
    _, norm_one_back = jax.vjp(layer_norm, own_tokens, gain_one, shift_one)
    grad_tokens_norm, grad_gain_one, grad_shift_one = norm_one_back(grad_in)
    grad_tokens = grad_resid + grad_tokens_norm
    summed = lax.psum(
        (
            grad_w_query,
            grad_b_query,
            grad_w_key,
            grad_w_value,
            grad_b_value,
            grad_w_out,
            grad_w_up,
            grad_b_up,
            grad_w_down,
        ),
        "dp",
    )
    shared = lax.psum(
        (grad_gain_one, grad_shift_one, grad_b_out, grad_gain_two, grad_shift_two, grad_b_down),
        ("dp", "tp"),
    )
    return (
        result.astype(jnp.bfloat16),
        grad_tokens,
        shared[0],
        shared[1],
        summed[0],
        summed[1],
        summed[2],
        summed[3],
        summed[4],
        summed[5],
        shared[2],
        shared[3],
        shared[4],
        summed[6],
        summed[7],
        summed[8],
        shared[5],
    )


def pick(*arrays):
    tokens, long_lengths, short_lengths, w_query, w_up = (arrays[i] for i in (0, 1, 2, 5, 14))
    fits = (
        lax.axis_size("tp") == 2
        and lax.axis_size("dp") == 16
        and long_lengths.shape[0] == 2
        and short_lengths.shape[0] == 8
        and tokens.shape == (2 * LEN_L + 8 * LEN_S, 768)
        and w_query.shape[1] == 8 * HEAD_DIM
        and w_up.shape[1] == 1536
    )
    return by_images(*arrays) if fits else local(*arrays)


def solution(mesh):
    placed = (
        P("dp", None),
        P("dp"),
        P("dp"),
        P(),
        P(),
        P(None, "tp"),
        P("tp"),
        P(None, "tp"),
        P(None, "tp"),
        P("tp"),
        P("tp", None),
        P(),
        P(),
        P(),
        P(None, "tp"),
        P("tp"),
        P("tp", None),
        P(),
        P(("dp", "tp"), None),
    )
    return jax.shard_map(
        pick,
        mesh=mesh,
        in_specs=placed,
        out_specs=(
            P(("dp", "tp"), None),
            P(("dp", "tp"), None),
            P(),
            P(),
            P(None, "tp"),
            P("tp"),
            P(None, "tp"),
            P(None, "tp"),
            P("tp"),
            P("tp", None),
            P(),
            P(),
            P(),
            P(None, "tp"),
            P("tp"),
            P("tp", None),
            P(),
        ),
        check_vma=False,
    )
```

```python
import functools
import math

import jax
import jax.numpy as jnp
from jax import lax
from jax.experimental import pallas as pl
from jax.experimental.pallas import tpu as pltpu
from jax.sharding import PartitionSpec as P

HEAD_DIM = 48
LEN_L = 1024
LEN_S = 256
F32 = jnp.float32
BF16 = jnp.bfloat16
LOG2E = math.log2(math.e)
SCALE = HEAD_DIM ** (-0.5)
VMEM_LIMIT = 60 << 20
HEAD_GROUP = 2


def contract(left, right, left_dim, right_dim):
    return lax.dot_general(
        left, right, (((left_dim,), (right_dim,)), ((), ())), preferred_element_type=F32
    )


def params():
    return pltpu.CompilerParams(vmem_limit_bytes=VMEM_LIMIT)


def cost(flops, bytes_accessed, transcendentals=0):
    return pl.CostEstimate(
        flops=int(flops), bytes_accessed=int(bytes_accessed), transcendentals=int(transcendentals)
    )


def row(ref):
    return ref[...].astype(F32).reshape(1, ref.shape[0])


def whole(shape):
    zeros = (0,) * len(shape)
    return pl.BlockSpec(shape, lambda *_: zeros)


def norm_parts(values):
    center = values - jnp.mean(values, axis=-1, keepdims=True)
    inv = lax.rsqrt(jnp.mean(center * center, axis=-1, keepdims=True) + 1e-06)
    return center * inv, inv


def norm_back(hat, inv, grad_hat):
    mean_grad = jnp.mean(grad_hat, axis=-1, keepdims=True)
    mean_both = jnp.mean(grad_hat * hat, axis=-1, keepdims=True)
    return inv * (grad_hat - mean_grad - hat * mean_both)


def three_terms(value):
    high = value.astype(BF16).astype(F32)
    rest = value - high
    mid = rest.astype(BF16).astype(F32)
    return [high, mid, rest - mid]


def extra_rows(rows, count):
    at = lax.broadcasted_iota(jnp.int32, (16, count), 0)
    out = jnp.zeros((16, count), F32)
    for place, row in enumerate(rows):
        out = jnp.where(at == place, row, out)
    return out.astype(BF16)


def scaled_query(query):
    wide = query.astype(F32) * (SCALE * LOG2E)
    high = wide.astype(BF16)
    return [high, (wide - high.astype(F32)).astype(BF16)]


def pair_count(heads, rows):
    return heads * (LEN_L**2 + (rows - LEN_L) * LEN_S)


class Place:
    def __init__(self):
        me = lax.axis_index("dp")
        self.core, self.x, self.z = me % 2, (me // 2) % 2, me // 4
        self.rank = lax.axis_index("tp")

    def at(self, z=None, x=None, core=None):
        z = self.z if z is None else z
        x = self.x if x is None else x
        core = self.core if core is None else core
        return {"dp": (z * 2 + x) * 2 + core}

    def across_core(self):
        return self.at(core=1 - self.core)

    def across_x(self):
        return self.at(x=1 - self.x)

    def along_z(self, step):
        return self.at(z=(self.z + step) % 4)

    def partner(self):
        return {"tp": 1 - self.rank}

    def greet(self):
        barrier = pltpu.get_barrier_semaphore()
        others = [self.across_core(), self.across_x(), self.partner()]
        others += [self.along_z(step) for step in (1, 2, 3)]
        for other in others:
            pl.semaphore_signal(
                barrier, inc=1, device_id=other, device_id_type=pl.DeviceIdType.MESH
            )
        pl.semaphore_wait(barrier, len(others))


def send_to(source, target, send, recv, device):
    return pltpu.make_async_remote_copy(
        src_ref=source,
        dst_ref=target,
        send_sem=send,
        recv_sem=recv,
        device_id=device,
        device_id_type=pl.DeviceIdType.MESH,
    )


def part(ref, start, count):
    return ref.at[pl.ds(pl.multiple_of(start, 16), count)]


def add_rows(target, start, count, terms):
    tile = 48 if count % 48 == 0 else 32

    def body(i, _):
        at = pl.multiple_of(i * tile, 16)
        here = pl.ds(pl.multiple_of(start + at, 16), tile)
        total = target[here, :].astype(F32)
        for term in terms:
            total = total + term[pl.ds(at, tile), :].astype(F32)
        target[here, :] = total.astype(BF16)
        return 0

    lax.fori_loop(0, count // tile, body, 0)


class PlaneSum:
    def __init__(self, place, own, seen, out, refs):
        self.place, self.own, self.seen, self.out = place, own, seen, out
        (self.acc, self.seen_here, self.from_core, self.from_x, self.from_z, self.whole,
         self.send, self.recv, self.local) = refs
        self.rows = own.shape[0]

    @staticmethod
    def buffers(rows, width):
        return [
            pltpu.VMEM((rows // 2, width), BF16),
            pltpu.VMEM((rows // 2, width), BF16),
            pltpu.VMEM((rows // 2, width), BF16),
            pltpu.VMEM((rows // 4, width), BF16),
            pltpu.VMEM((3, rows // 16, width), BF16),
            pltpu.VMEM((rows // 2, width), BF16),
            pltpu.SemaphoreType.DMA((10,)),
            pltpu.SemaphoreType.DMA((10,)),
            pltpu.SemaphoreType.DMA((4,)),
        ]

    def copy(self, source, target, place, device):
        return send_to(source, target, self.send.at[place], self.recv.at[place], device)

    def core_copy(self):
        half = self.rows // 2
        source = part(self.own, (1 - self.place.core) * half, half)
        return self.copy(source, self.from_core, 0, self.place.across_core())

    def local_copies(self):
        half = self.rows // 2
        source = part(self.own, self.place.core * half, half)
        copies = [pltpu.make_async_copy(source, self.acc, self.local.at[0])]
        if self.seen is not None:
            copies.append(pltpu.make_async_copy(self.seen, self.seen_here, self.local.at[1]))
        return copies

    def x_copy(self):
        count = self.rows // 4
        source = part(self.acc, (1 - self.place.x) * count, count)
        return self.copy(source, self.from_x, 1, self.place.across_x())

    def z_copies(self):
        count = self.rows // 16
        copies = []
        for step in (1, 2, 3):
            there = (self.place.z + step) % 4
            source = part(self.acc, self.place.x * 4 * count + there * count, count)
            target = self.from_z.at[step - 1]
            copies.append(self.copy(source, target, 1 + step, self.place.along_z(step)))
        return copies

    def piece(self):
        count = self.rows // 16
        inside = self.place.x * 4 * count + self.place.z * count
        return part(self.acc, inside, count), part(self.whole, inside, count)

    def keep_copy(self):
        mine, there = self.piece()
        return pltpu.make_async_copy(mine, there, self.local.at[2])

    def back_z_copies(self):
        mine, there = self.piece()
        return [
            self.copy(mine, there, 4 + step, self.place.along_z(step)) for step in (1, 2, 3)
        ]

    def back_x_copy(self):
        count = self.rows // 4
        there = part(self.whole, self.place.x * count, count)
        return self.copy(there, there, 8, self.place.across_x())

    def back_core_copy(self):
        count = self.rows // 2
        there = part(self.out, self.place.core * count, count)
        return self.copy(self.whole, there, 9, self.place.across_core())

    def store_copy(self):
        count = self.rows // 2
        there = part(self.out, self.place.core * count, count)
        return pltpu.make_async_copy(self.whole, there, self.local.at[3])

    def begin_own(self):
        self.core_copy().start()
        self.local_copies()[0].start()

    def begin_seen(self):
        for copy in self.local_copies()[1:]:
            copy.start()

    def begin(self):
        self.begin_own()
        self.begin_seen()

    def along_x(self):
        self.core_copy().wait()
        for copy in self.local_copies():
            copy.wait()
        add_rows(self.acc, 0, self.rows // 2, [self.from_core, self.seen_here])
        self.x_copy().start()

    def along_z(self):
        self.x_copy().wait()
        count = self.rows // 4
        add_rows(self.acc, self.place.x * count, count, [self.from_x])
        for copy in self.z_copies():
            copy.start()

    def back_along_z(self):
        for copy in self.z_copies():
            copy.wait()
        count = self.rows // 16
        inside = self.place.x * 4 * count + self.place.z * count
        add_rows(self.acc, inside, count, [self.from_z.at[i] for i in range(3)])
        self.keep_copy().start()
        for copy in self.back_z_copies():
            copy.start()

    def back_along_x(self):
        self.keep_copy().wait()
        for copy in self.back_z_copies():
            copy.wait()
        self.back_x_copy().start()

    def back_to_core(self):
        self.back_x_copy().wait()
        self.back_core_copy().start()
        self.store_copy().start()

    def end(self):
        self.back_core_copy().wait()
        self.store_copy().wait()


class PartnerTerm:
    def __init__(self, place, other, seen, refs):
        self.place, self.other, self.seen = place, other, seen
        self.from_core, self.send, self.recv = refs
        self.half = other.shape[0] // 2

    @staticmethod
    def buffers(rows, width):
        return [
            pltpu.VMEM((rows // 2, width), BF16),
            pltpu.SemaphoreType.DMA((2,)),
            pltpu.SemaphoreType.DMA((2,)),
        ]

    def core_copy(self):
        source = part(self.other, (1 - self.place.core) * self.half, self.half)
        return send_to(
            source, self.from_core, self.send.at[0], self.recv.at[0], self.place.across_core()
        )

    def partner_copy(self):
        return send_to(
            self.from_core, self.seen, self.send.at[1], self.recv.at[1], self.place.partner()
        )

    def begin(self):
        self.core_copy().start()

    def to_partner(self):
        self.core_copy().wait()
        mine = part(self.other, self.place.core * self.half, self.half)
        add_rows(self.from_core, 0, self.half, [mine])
        self.partner_copy().start()

    def end(self):
        self.partner_copy().wait()


class SmallSum:
    ROWS = 16

    def __init__(self, place, pair, refs):
        self.place, self.pair = place, pair
        self.sums, self.got, self.got_own, self.send, self.recv = refs

    @staticmethod
    def buffers(width):
        rows = SmallSum.ROWS
        return [
            pltpu.VMEM((3, 2, rows, width), F32),
            pltpu.VMEM((5, 2, rows, width), F32),
            pltpu.VMEM((rows, width), F32),
            pltpu.SemaphoreType.DMA((6,)),
            pltpu.SemaphoreType.DMA((6,)),
        ]

    def copy(self, source, place, device):
        return send_to(source, self.got.at[place], self.send.at[place], self.recv.at[place], device)

    def core_copy(self):
        return self.copy(self.pair, 0, self.place.across_core())

    def x_copy(self):
        return self.copy(self.sums.at[0], 1, self.place.across_x())

    def z_copies(self):
        return [
            self.copy(self.sums.at[1], 1 + step, self.place.along_z(step)) for step in (1, 2, 3)
        ]

    def partner_copy(self):
        return send_to(
            self.sums.at[2, 1], self.got_own, self.send.at[5], self.recv.at[5],
            self.place.partner(),
        )

    def begin(self):
        self.core_copy().start()

    def over_x(self):
        self.core_copy().wait()
        self.sums[0] = self.pair[...] + self.got[0]
        self.x_copy().start()

    def over_z(self):
        self.x_copy().wait()
        self.sums[1] = self.sums[0] + self.got[1]
        for copy in self.z_copies():
            copy.start()

    def over_tp(self):
        for copy in self.z_copies():
            copy.wait()
        self.sums[2] = self.sums[1] + self.got[2] + self.got[3] + self.got[4]
        self.partner_copy().start()

    def end(self):
        self.partner_copy().wait()
        return self.sums[2, 0] + self.got_own[...]


class Fetch:
    def __init__(self, place, own, got, refs, deep):
        self.place, self.own, self.got, self.deep = place, own, got, deep
        self.send, self.recv = refs
        self.half = own.shape[0] // 2
        self.quarter = self.half // 2
        self.count = self.quarter // 2 if deep else self.quarter
        self.core_at = place.core * self.half
        self.x_at = self.core_at + place.x * self.quarter
        odd = place.z % 2
        self.at = self.x_at + odd * self.count if deep else self.x_at
        self.z_at = self.x_at + (1 - odd) * self.count
        self.z_device = place.at(z=place.z + 1 - 2 * odd)

    @staticmethod
    def buffers():
        return [pltpu.SemaphoreType.DMA((5,)), pltpu.SemaphoreType.DMA((5,))]

    def copy(self, source, start, count, place, device):
        there = part(self.got, start, count)
        here = part(source, start, count)
        return send_to(here, there, self.send.at[place], self.recv.at[place], device)

    def partner_copy(self):
        return self.copy(self.own, self.at, self.count, 0, self.place.partner())

    def z_copy(self):
        return self.copy(self.got, self.at, self.count, 1, self.z_device)

    def x_copies(self):
        copies = [self.copy(self.got, self.at, self.count, 2, self.place.across_x())]
        if self.deep:
            copies.append(self.copy(self.got, self.z_at, self.count, 3, self.place.across_x()))
        return copies

    def core_copy(self):
        return self.copy(self.got, self.core_at, self.half, 4, self.place.across_core())

    def begin(self):
        self.partner_copy().start()

    def share(self):
        self.partner_copy().wait()
        if self.deep:
            self.z_copy().start()
        self.x_copies()[0].start()

    def more_x(self):
        self.z_copy().wait()
        self.x_copies()[1].start()

    def to_core(self):
        for copy in self.x_copies():
            copy.wait()
        self.core_copy().start()

    def end(self):
        self.core_copy().wait()


FRONT_BLOCK = 512


def front_kernel(
    mask_ref, gain_ref, shift_ref, bout_ref, gain2_ref, shift2_ref, bias_ref, tok_hbm, wq_hbm, wk_hbm, wv_hbm, wout_hbm, wup_hbm, wdown_hbm, cot_hbm,
    x_out, qkv_out, att_out, log_out, resid_out, mid_out,
    cat_hbm, wout_all_hbm, up2_hbm, down2_hbm, grads_hbm, bias2_hbm, tok_out,
    tok_ref, x_ref, qkv_ref, att_ref, cat_ref, wout_ref, bias2_ref, up2_ref, down2_ref, grads_ref,
    load_sem, out_sem, swap_send, swap_recv, *scratch, heads, block,
):
    step = pl.program_id(0)
    place = Place()
    half = heads * HEAD_DIM
    rows = tok_ref.shape[0]
    blocks = rows // FRONT_BLOCK
    pairs = heads // HEAD_GROUP
    base = [0, blocks, blocks + pairs, 2 * blocks + pairs, 2 * blocks + 2 * pairs]

    sems = [scratch[2 * i : 2 * i + 2] for i in range(6)]
    mine = [wq_hbm, wk_hbm, wv_hbm]
    projections = [
        Fetch(place, own, cat_ref.at[1, :, pl.ds(i * half, half)], sems[i], True)
        for i, own in enumerate(mine)
    ]
    fetch_out = Fetch(place, wout_hbm, wout_ref.at[pl.ds(half, half)], sems[3], True)
    fetch_up = Fetch(place, wup_hbm, up2_ref, sems[4], True)
    fetch_down = Fetch(place, wdown_hbm, down2_ref, sems[5], True)
    bias_copy = send_to(
        bias_ref, bias2_ref, swap_send.at[0], swap_recv.at[0], place.partner()
    )
    here = pl.ds(pl.multiple_of(place.rank * LEN_L, LEN_L), LEN_L)
    theirs = pl.ds(pl.multiple_of((1 - place.rank) * LEN_L, LEN_L), LEN_L)
    cot_copy = send_to(
        cot_hbm.at[theirs], grads_ref.at[here], swap_send.at[1], swap_recv.at[1], place.partner()
    )

    def token_rows(i):
        start = pl.multiple_of(i * 2 * LEN_L + place.rank * LEN_L, LEN_L)
        return tok_hbm.at[pl.ds(start, LEN_L)]

    token_loads = [
        pltpu.make_async_copy(token_rows(i), tok_ref.at[pl.ds(i * LEN_L, LEN_L)], load_sem.at[i])
        for i in (0, 1)
    ]
    weight_loads = [
        pltpu.make_async_copy(
            own, cat_ref.at[0, :, pl.ds(i * half, half)], load_sem.at[2 + i]
        )
        for i, own in enumerate(mine)
    ]
    out_load = pltpu.make_async_copy(wout_hbm, wout_ref.at[pl.ds(0, half)], load_sem.at[5])
    kept_copy = pltpu.make_async_copy(cot_hbm.at[here], grads_ref.at[here], out_sem.at[0])
    stores = [
        pltpu.make_async_copy(cat_ref, cat_hbm, out_sem.at[1]),
        pltpu.make_async_copy(wout_ref, wout_all_hbm, out_sem.at[2]),
        pltpu.make_async_copy(bias2_ref, bias2_hbm, out_sem.at[3]),
        pltpu.make_async_copy(tok_ref, tok_out, out_sem.at[4]),
    ]
    last_stores = [
        pltpu.make_async_copy(grads_ref, grads_hbm, out_sem.at[5]),
        pltpu.make_async_copy(up2_ref, up2_hbm, out_sem.at[6]),
        pltpu.make_async_copy(down2_ref, down2_hbm, out_sem.at[7]),
    ]

    @pl.when(step == 0)
    def _():
        for copy in (*token_loads, *weight_loads, out_load):
            copy.start()
        place.greet()
        for one in projections:
            one.begin()
        bias_copy.start()
        fetch_out.begin()
        for copy in token_loads:
            copy.wait()
        for copy in weight_loads:
            copy.wait()

    def at_step(when):
        return pl.when(step == when)

    @at_step(base[1] - 2)
    def _():
        fetch_up.begin()
        fetch_down.begin()

    @at_step(base[1])
    def _():
        for one in (*projections, fetch_out):
            one.share()

    @at_step(base[1] + 1)
    def _():
        for one in (*projections, fetch_out):
            one.more_x()

    @at_step(base[2] - 1)
    def _():
        for one in (*projections, fetch_out):
            one.to_core()
        kept_copy.start()
        fetch_up.share()
        fetch_down.share()
        cot_copy.start()

    @at_step(base[2])
    def _():
        for one in (*projections, fetch_out):
            one.end()
        bias_copy.wait()
        out_load.wait()
        for copy in stores:
            copy.start()

    @at_step(base[3] + 1)
    def _():
        fetch_up.more_x()
        fetch_down.more_x()

    @at_step(base[4] + 1)
    def _():
        fetch_up.to_core()
        fetch_down.to_core()

    @at_step(base[4] + blocks - 1)
    def _():
        for one in (fetch_up, fetch_down):
            one.end()
        kept_copy.wait()
        cot_copy.wait()
        for copy in last_stores:
            copy.start()

    def project(which, i, bias):
        at = pl.ds(pl.multiple_of(i * FRONT_BLOCK, FRONT_BLOCK), FRONT_BLOCK)
        column = jnp.transpose(bias[:, : 3 * half])[:, :1]
        value = (contract(cat_ref[which], x_ref[at, :], 0, 1) + column).astype(BF16)
        qkv_ref[:, at] = value
        qkv_out[0] = value

    @pl.when(step < base[1])
    def _():
        at = pl.ds(pl.multiple_of(step * FRONT_BLOCK, FRONT_BLOCK), FRONT_BLOCK)
        hat, _ = norm_parts(tok_ref[at, :].astype(F32))
        normed = (hat * row(gain_ref) + row(shift_ref)).astype(BF16)
        x_ref[at, :] = normed
        x_out[...] = normed
        project(0, step, bias_ref[...])

    @pl.when(jnp.logical_and(step >= base[2], step < base[3]))
    def _():
        project(1, step - base[2], bias2_ref[...])

    own_part = jnp.logical_and(step >= base[1], step < base[2])
    other_part = jnp.logical_and(step >= base[3], step < base[4])

    @pl.when(jnp.logical_or(own_part, other_part))
    def _():
        second = (step >= base[3]).astype(jnp.int32)
        pair = step - base[1] - second * (base[3] - base[1])
        attend_pair(mask_ref, qkv_ref, att_ref, att_out, log_out, pair, second, heads, block)

    @pl.when(step >= base[4])
    def _():
        i = step - base[4]
        at = pl.ds(pl.multiple_of(i * FRONT_BLOCK, FRONT_BLOCK), FRONT_BLOCK)
        product = contract(att_ref[:, at], wout_ref[...], 0, 0)
        resid = tok_ref[at, :].astype(F32) + product + row(bout_ref)
        resid_out[...] = resid
        hat, _ = norm_parts(resid)
        mid_out[...] = (hat * row(gain2_ref) + row(shift2_ref)).astype(BF16)

    @pl.when(step == base[4] + blocks - 1)
    def _():
        for copy in (*stores, *last_stores):
            copy.wait()


def attend_pair(mask_ref, qkv_ref, att_ref, att_out, log_out, pair, second, heads, block):
    rows = qkv_ref.shape[1]
    half = heads * HEAD_DIM
    first = pair * HEAD_GROUP
    work = []
    for head in range(HEAD_GROUP):
        work += [(head, 0, LEN_L, at, block) for at in range(0, LEN_L, block)]
        work += [(head, start, LEN_S, 0, LEN_S) for start in range(LEN_L, rows, LEN_S)]

    def load(which, head, columns):
        start = pl.multiple_of(which * half + (first + head) * HEAD_DIM, HEAD_DIM)
        return qkv_ref[pl.ds(start, HEAD_DIM), columns]

    def scores(item):
        head, start, count, at, size = item
        every = slice(start, start + count)
        keys = load(1, head, every)
        key_rows = jnp.concatenate([keys, keys, extra_rows([mask_ref[:, every]], count)], 0)
        query = scaled_query(load(0, head, slice(start + at, start + at + size)))
        query_rows = jnp.concatenate([*query, jnp.ones((16, size), BF16)], 0)
        return contract(key_rows, query_rows, 0, 0)

    def finish(item, score):
        head, start, count, at, size = item
        here = slice(start + at, start + at + size)
        values = load(2, head, slice(start, start + count))
        value_rows = jnp.concatenate([values, jnp.ones((16, count), BF16)], 0)
        top = jnp.max(score, axis=0, keepdims=True)
        weights = jnp.exp2(score - top).astype(BF16)
        mixed = contract(value_rows, weights, 1, 0)
        total = mixed[HEAD_DIM : HEAD_DIM + 1]
        result = (mixed[:HEAD_DIM] * (1.0 / total)).astype(BF16)
        att_out[0, head, :, here] = result
        start = pl.multiple_of(second * half + (first + head) * HEAD_DIM, HEAD_DIM)
        att_ref[pl.ds(start, HEAD_DIM), here] = result
        log_out[0, head, :, here] = top + jnp.log2(total)

    score = scores(work[0])
    for place, item in enumerate(work):
        later = scores(work[place + 1]) if place + 1 < len(work) else None
        finish(item, score)
        score = later


def front(
    mask, vectors, bias, tokens, w_query, w_key, w_value, w_out, w_up, w_down, cotangent, heads,
    block=1024,
):
    width = tokens.shape[1]
    rows = tokens.shape[0] // 2
    half = heads * HEAD_DIM
    hidden = w_up.shape[1]
    blocks, pairs = rows // FRONT_BLOCK, heads // HEAD_GROUP
    base = [0, blocks, blocks + pairs, 2 * blocks + pairs, 2 * blocks + 2 * pairs]
    anywhere = pl.BlockSpec(memory_space=pl.ANY)

    def row_block(first):
        return lambda s: (jnp.clip(s - first, 0, blocks - 1), 0)

    def qkv_block(s):
        late = (s >= base[2]).astype(jnp.int32)
        return late, 0, jnp.clip(s - late * base[2], 0, blocks - 1)

    def head_block(s):
        late = (s >= base[3]).astype(jnp.int32)
        return late, jnp.clip(s - base[1] - late * (base[3] - base[1]), 0, pairs - 1), 0, 0

    by_row = lambda first: pl.BlockSpec((FRONT_BLOCK, width), row_block(first))
    bias_rows, bias_width = bias.shape
    pair_total = pair_count(2 * heads, rows)
    return pl.pallas_call(
        functools.partial(front_kernel, heads=heads, block=block),
        grid=(base[4] + blocks,),
        in_specs=[
            whole((1, rows)),
            *(whole((width,)) for _ in range(5)),
            whole(bias.shape),
        ]
        + [anywhere] * 8,
        out_specs=[
            by_row(0),
            pl.BlockSpec((1, 3 * half, FRONT_BLOCK), qkv_block),
            pl.BlockSpec((1, HEAD_GROUP, HEAD_DIM, rows), head_block),
            pl.BlockSpec((1, HEAD_GROUP, 1, rows), head_block),
            by_row(base[4]),
            by_row(base[4]),
        ]
        + [anywhere] * 7,
        out_shape=[
            jax.ShapeDtypeStruct((rows, width), BF16),
            jax.ShapeDtypeStruct((2, 3 * half, rows), BF16),
            jax.ShapeDtypeStruct((2, heads, HEAD_DIM, rows), BF16),
            jax.ShapeDtypeStruct((2, heads, 1, rows), F32),
            jax.ShapeDtypeStruct((rows, width), F32),
            jax.ShapeDtypeStruct((rows, width), BF16),
            jax.ShapeDtypeStruct((2, width, 3 * half), BF16),
            jax.ShapeDtypeStruct((2 * half, width), BF16),
            jax.ShapeDtypeStruct((width, hidden), BF16),
            jax.ShapeDtypeStruct((hidden, width), BF16),
            jax.ShapeDtypeStruct((rows, width), BF16),
            jax.ShapeDtypeStruct((bias_rows, bias_width), F32),
            jax.ShapeDtypeStruct((rows, width), BF16),
        ],
        scratch_shapes=[
            pltpu.VMEM((rows, width), BF16),
            pltpu.VMEM((rows, width), BF16),
            pltpu.VMEM((3 * half, rows), BF16),
            pltpu.VMEM((2 * half, rows), BF16),
            pltpu.VMEM((2, width, 3 * half), BF16),
            pltpu.VMEM((2 * half, width), BF16),
            pltpu.VMEM((bias_rows, bias_width), F32),
            pltpu.VMEM((width, hidden), BF16),
            pltpu.VMEM((hidden, width), BF16),
            pltpu.VMEM((rows, width), BF16),
            pltpu.SemaphoreType.DMA((6,)),
            pltpu.SemaphoreType.DMA((8,)),
            pltpu.SemaphoreType.DMA((2,)),
            pltpu.SemaphoreType.DMA((2,)),
        ]
        + [ref for _ in range(6) for ref in Fetch.buffers()],
        compiler_params=pltpu.CompilerParams(
            vmem_limit_bytes=VMEM_LIMIT, collective_id=1, has_side_effects=True
        ),
        cost_estimate=cost(
            pair_total * 2 * 512 + 14 * rows * width * half, 40 * rows * width, pair_total
        ),
        name="front",
    )(
        mask, *vectors, bias, tokens, w_query, w_key, w_value, w_out, w_up, w_down, cotangent,
    )


ERFC_TERMS = (0.254829592, -0.284496736, 1.421413741, -1.453152027, 1.061405429)
ERFC_SLOPE = 0.3275911


def gelu_and_slope(value):
    bell = jnp.exp2(value * value * (-0.5 * LOG2E))
    base = 1.0 + jnp.abs(value) * (ERFC_SLOPE * math.sqrt(0.5))
    ratio = 1.0 / base
    poly = ERFC_TERMS[4] * 0.5
    for term in ERFC_TERMS[3::-1]:
        poly = poly * ratio + term * 0.5
    tail = poly * ratio * bell
    below = jnp.where(value < 0.0, tail, 1.0 - tail)
    return value * below, below + value * bell * (1.0 / math.sqrt(2.0 * math.pi))


HIDDEN_BLOCK = 512
MID_BLOCK = 512
HIDDEN_ORDER = ((1, 0), (0, 0), (1, 1), (1, 2), (0, 1), (0, 2))
SLOTS = 4
MID_CHUNK = 512


def mid_kernel(
    mid_ref, grad_ref, bias_ref, resid_ref, gain_ref, bdown_ref, w_ref, att_ref,
    up2_hbm, up_hbm, down2_hbm, down_hbm,
    out_ref, gresid_ref, gatt_ref, dw_own_ref, dw_other_ref, small_ref, db_ref,
    dup_hbm, ddown_hbm, seen_up, seen_down, gup_hbm, gdown_hbm,
    sum_ref, gmid_ref, act_ref, gpre_ref, up_ref, down_ref, dup_ref, ddown_ref, acc_ref,
    load_sem, store_sem, *scratch, blocks,
):
    step = pl.program_id(0)
    place = Place()
    rows, width = mid_ref.shape
    cut = lambda ref, i: ref.at[:, pl.ds(i * HIDDEN_BLOCK, HIDDEN_BLOCK)]
    take = lambda ref, i, count: ref.at[pl.ds(i * count, count)]
    terms = []
    for i in range(blocks):
        refs = [scratch[6 * i : 6 * i + 3], scratch[6 * i + 3 : 6 * i + 6]]
        slot = HIDDEN_ORDER.index((1, i)) % SLOTS
        terms.append(
            (
                PartnerTerm(place, dup_ref.at[slot], cut(seen_up, i), refs[0]),
                PartnerTerm(
                    place, ddown_ref.at[slot], take(seen_down, i, HIDDEN_BLOCK // 2), refs[1]
                ),
            )
        )

    first_sums = [
        PlaneSum(
            place, dup_ref.at[1], cut(seen_up, 0), gup_hbm, scratch[6 * blocks : 6 * blocks + 9]
        ),
        PlaneSum(
            place, ddown_ref.at[1], take(seen_down, 0, HIDDEN_BLOCK // 2), gdown_hbm,
            scratch[6 * blocks + 9 :],
        ),
    ]

    def loads(at):
        side, i = HIDDEN_ORDER[at]
        up, down = (up2_hbm, down2_hbm) if side else (up_hbm, down_hbm)
        slot = at % 2
        return [
            pltpu.make_async_copy(cut(up, i), up_ref.at[slot], load_sem.at[slot, 0]),
            pltpu.make_async_copy(
                take(down, i, HIDDEN_BLOCK), down_ref.at[slot], load_sem.at[slot, 1]
            ),
        ]

    def stores(i):
        slot = HIDDEN_ORDER.index((0, i)) % SLOTS
        return [
            pltpu.make_async_copy(dup_ref.at[slot], cut(dup_hbm, i), store_sem.at[i, 0]),
            pltpu.make_async_copy(
                ddown_ref.at[slot], take(ddown_hbm, i, HIDDEN_BLOCK), store_sem.at[i, 1]
            ),
        ]

    to_core = {3: terms[1], 4: terms[2]}
    to_partner = {1: terms[0], 4: terms[1], 5: terms[2]}

    for at in range(2 * blocks + 1):

        @pl.when(step == at)
        def _(at=at):
            if at == 0:
                for copy in loads(0):
                    copy.start()
                place.greet()
                sum_ref[...] = jnp.zeros_like(sum_ref)
                gmid_ref[...] = jnp.zeros_like(gmid_ref)
            if at < 2 * blocks:
                for copy in loads(at):
                    copy.wait()
            if at + 1 < 2 * blocks:
                for copy in loads(at + 1):
                    copy.start()
            for one in to_partner.get(at, ()):
                one.to_partner()
            for one in to_core.get(at, ()):
                one.begin()
            if at >= 1 and HIDDEN_ORDER[at - 1] in ((0, 1), (0, 2)):
                for copy in stores(HIDDEN_ORDER[at - 1][1]):
                    copy.start()
            if at == 2:
                for one in first_sums:
                    one.begin_own()
            if at == 3:
                for one in terms[0]:
                    one.end()
                for one in first_sums:
                    one.begin_seen()
                for one in first_sums:
                    one.along_x()
            if at == 4:
                for one in first_sums:
                    one.along_z()
            if at == 5:
                for one in first_sums:
                    one.back_along_z()
            if at == 6:
                for one in first_sums:
                    one.back_along_x()
            if at == 2 * blocks:
                acc_ref[...] = jnp.zeros_like(acc_ref)
                small_ref[...] = jnp.zeros_like(small_ref)

    @pl.when(step < 2 * blocks)
    def _():
        up, down, bias = up_ref[step % 2], down_ref[step % 2], bias_ref[0]

        def products(at):
            here = slice(at, at + MID_CHUNK)
            return (
                contract(mid_ref[here], up, 1, 0) + bias,
                contract(grad_ref[here], down, 1, 1),
            )

        now = products(0)
        db = None
        for at in range(0, rows, MID_CHUNK):
            here = slice(at, at + MID_CHUNK)
            later = products(at + MID_CHUNK) if at + MID_CHUNK < rows else None
            value, slope = gelu_and_slope(now[0])
            act = value.astype(BF16)
            gpre = (slope * now[1]).astype(BF16)
            act_ref[here] = act
            gpre_ref[here] = gpre
            term = jnp.sum(gpre.astype(F32), axis=0, keepdims=True)
            db = term if db is None else db + term
            sum_ref[here] += contract(act, down, 1, 0)
            gmid_ref[here] += contract(gpre, up, 1, 1)
            now = later
        db_ref[0] = db
        slot = lax.rem(step, SLOTS)
        ddown_ref[slot] = contract(act_ref[...], grad_ref[...], 0, 0).astype(BF16)
        dup_ref[slot] = contract(mid_ref[...], gpre_ref[...], 0, 0).astype(BF16)

    @pl.when(step == 0)
    def _():
        for one in terms[0]:
            one.begin()

    @pl.when(step >= 2 * blocks)
    def _():
        start = (step - 2 * blocks) * MID_BLOCK
        here = pl.ds(pl.multiple_of(start, MID_BLOCK), MID_BLOCK)
        resid = resid_ref[...]
        grads = grad_ref[here, :].astype(F32)
        out_ref[...] = (resid + sum_ref[here, :] + row(bdown_ref)).astype(BF16)
        gmid = gmid_ref[here, :]
        hat, inv = norm_parts(resid)
        gresid = grads + norm_back(hat, inv, gmid * row(gain_ref))
        gresid_ref[...] = gresid
        branch = gresid.astype(BF16)
        gatt_ref[...] = contract(w_ref[...], branch, 1, 1).astype(BF16)
        acc_ref[...] += contract(branch, att_ref[...], 0, 1)
        small_ref[0:1] += jnp.sum(gmid * hat, axis=0, keepdims=True)
        small_ref[1:2] += jnp.sum(gmid, axis=0, keepdims=True)
        small_ref[2:3] += jnp.sum(gresid, axis=0, keepdims=True)
        small_ref[3:4] += jnp.sum(grads, axis=0, keepdims=True)

    @pl.when(step == pl.num_programs(0) - 1)
    def _():
        for one in first_sums:
            one.back_to_core()
        half = dw_own_ref.shape[1]
        dw_own_ref[...] = acc_ref[:, :half].astype(BF16)
        dw_other_ref[...] = acc_ref[:, half:].astype(BF16)
        for i in range(1, blocks):
            for copy in stores(i):
                copy.wait()
            for one in terms[i]:
                one.end()
        for one in first_sums:
            one.end()


def mid_part(mid, grads, biases, resid, gain, b_down, w_out, attended, up2, up, down2, down):
    rows, width = mid.shape
    hidden = up.shape[1]
    blocks = hidden // HIDDEN_BLOCK
    first = 2 * blocks
    heads_width = attended.shape[0]
    anywhere = pl.BlockSpec(memory_space=pl.ANY)
    once = lambda shape: pl.BlockSpec(
        shape, lambda *_: (0,) * len(shape), pipeline_mode=pl.Buffered(1)
    )
    row_step = lambda s: jnp.maximum(s - first, 0)
    by_row = pl.BlockSpec((MID_BLOCK, width), lambda s: (row_step(s), 0))
    columns = pl.BlockSpec((heads_width, MID_BLOCK), lambda s: (0, row_step(s)))
    by_hidden = pl.BlockSpec((1, 1, HIDDEN_BLOCK), lambda s: (jnp.minimum(s, first - 1), 0, 0))
    half = (width, heads_width // 2)
    scratch = [
        pltpu.VMEM((rows, width), F32),
        pltpu.VMEM((rows, width), F32),
        pltpu.VMEM((rows, HIDDEN_BLOCK), BF16),
        pltpu.VMEM((rows, HIDDEN_BLOCK), BF16),
        pltpu.VMEM((2, width, HIDDEN_BLOCK), BF16),
        pltpu.VMEM((2, HIDDEN_BLOCK, width), BF16),
        pltpu.VMEM((SLOTS, width, HIDDEN_BLOCK), BF16),
        pltpu.VMEM((SLOTS, HIDDEN_BLOCK, width), BF16),
        pltpu.VMEM((width, heads_width), F32),
        pltpu.SemaphoreType.DMA((2, 2)),
        pltpu.SemaphoreType.DMA((blocks, 2)),
    ]
    for _ in range(blocks):
        scratch += PartnerTerm.buffers(width, HIDDEN_BLOCK)
        scratch += PartnerTerm.buffers(HIDDEN_BLOCK, width)
    scratch += PlaneSum.buffers(width, HIDDEN_BLOCK) + PlaneSum.buffers(HIDDEN_BLOCK, width)
    return pl.pallas_call(
        functools.partial(mid_kernel, blocks=blocks),
        grid=(first + rows // MID_BLOCK,),
        in_specs=[
            once((rows, width)), once((rows, width)), by_hidden, by_row, whole((width,)),
            whole((width,)), once((heads_width, width)), columns,
        ]
        + [anywhere] * 4,
        out_specs=[
            by_row, by_row, columns, whole(half), whole(half), whole((8, width)), by_hidden,
        ]
        + [anywhere] * 6,
        out_shape=[
            jax.ShapeDtypeStruct((rows, width), BF16),
            jax.ShapeDtypeStruct((rows, width), F32),
            jax.ShapeDtypeStruct((heads_width, rows), BF16),
            jax.ShapeDtypeStruct(half, BF16),
            jax.ShapeDtypeStruct(half, BF16),
            jax.ShapeDtypeStruct((8, width), F32),
            jax.ShapeDtypeStruct((first, 1, HIDDEN_BLOCK), F32),
            jax.ShapeDtypeStruct((width, hidden), BF16),
            jax.ShapeDtypeStruct((hidden, width), BF16),
            jax.ShapeDtypeStruct((width // 2, hidden), BF16),
            jax.ShapeDtypeStruct((hidden // 2, width), BF16),
            jax.ShapeDtypeStruct((width, HIDDEN_BLOCK), BF16),
            jax.ShapeDtypeStruct((HIDDEN_BLOCK, width), BF16),
        ],
        scratch_shapes=scratch,
        compiler_params=pltpu.CompilerParams(
            vmem_limit_bytes=VMEM_LIMIT, collective_id=2, has_side_effects=True
        ),
        cost_estimate=cost(
            24 * rows * width * hidden + 4 * rows * width * heads_width, 60 * rows * width,
            4 * rows * hidden,
        ),
        name="mid",
    )(mid, grads, biases, resid, gain, b_down, w_out, attended, up2, up, down2, down)


TAIL_BLOCK = 512
SUM_ACTIONS = ("begin", "along_x", "along_z", "back_along_z", "back_along_x", "back_to_core")
SUM_STEPS = (
    (0, 1, 3, 6, 9, 11),
    (0, 2, 5, 8, 11, 13),
    (0, 4, 6, 10, 13, 15),
    (0, 5, 8, 12, 14, 16),
    (0, 8, 10, 13, 15, 17),
    (None, 17, 18, 20),
    (None, 17, 19),
    (None, 17, 20),
)
LAST_ACTIONS = (
    0, (6, "back_along_z"), (5, "back_along_x"), 1, (7, "back_along_z"), (6, "back_along_x"),
    (5, "back_to_core"), 2, (7, "back_along_x"), (6, "back_to_core"), (7, "back_to_core"),
)


def tail_kernel(
    mask_ref, qkv_ref, att_ref, log_ref, gatt_ref, gain_ref, small2_ref, dbup1_ref, dbup2_ref,
    wout2_ref, x_hbm, w_hbm, tok_hbm, gresid_hbm, up_hbm, down_hbm, wout_hbm, seen_up,
    seen_down, out_hbm,
    gtok_ref, small_ref, got_hbm, gup_hbm, gdown_hbm, gout_hbm, gcat_hbm, got_out,
    d_ref, x_ref, w_ref, tok_ref, gresid_ref, dw_ref, dw2_ref, seen_cat, sent_ref, pair_ref,
    load_sem, row_sem, tok_send, tok_recv, *scratch, heads, block,
):
    step = pl.program_id(0)
    place = Place()
    first_rows = 2 * heads + 1
    last_step = first_rows + 3
    width = x_ref.shape[1]
    half = heads * HEAD_DIM

    groups = []
    at = 0
    for count in [9] * 5 + [0] + [9] * 3 + [3, 3, 5]:
        groups.append(scratch[at : at + count])
        at += count
    columns = lambda ref, i: ref.at[:, pl.ds(i * HIDDEN_BLOCK, HIDDEN_BLOCK)]
    rows_of = lambda ref, i, count: ref.at[pl.ds(i * count, count)]
    sums = [
        PlaneSum(place, columns(up_hbm, i), columns(seen_up, i), columns(gup_hbm, i - 1), groups[i])
        for i in (1, 2)
    ]
    sums += [
        PlaneSum(
            place,
            rows_of(down_hbm, i, HIDDEN_BLOCK),
            rows_of(seen_down, i, HIDDEN_BLOCK // 2),
            rows_of(gdown_hbm, i - 1, HIDDEN_BLOCK),
            groups[2 + i],
        )
        for i in (1, 2)
    ]
    sums.append(PlaneSum(place, wout_hbm, None, gout_hbm, groups[0]))
    third = lambda ref, i: ref.at[:, pl.ds(i * half, half)]
    cat_sums = [
        PlaneSum(
            place, third(dw_ref, i), None, third(gcat_hbm, i),
            (groups[6 + i][0], third(seen_cat, i), *groups[6 + i][2:]),
        )
        for i in range(3)
    ]
    cat_term = PartnerTerm(place, dw2_ref, seen_cat, groups[9])
    out_term = PartnerTerm(place, wout2_ref, groups[0][1], groups[10])
    own_small, other_small = pair_ref.at[0], pair_ref.at[1]
    small = SmallSum(place, pair_ref, groups[11])
    theirs = pl.ds(pl.multiple_of((1 - place.rank) * LEN_L, LEN_L), LEN_L)
    out_load = pltpu.make_async_copy(out_hbm.at[theirs], sent_ref, load_sem.at[2])
    piece = LEN_L // 4
    out_copies = [
        send_to(
            sent_ref.at[pl.ds(i * piece, piece)], got_out.at[pl.ds(i * piece, piece)],
            tok_send.at[2 + i], tok_recv.at[2 + i], place.partner(),
        )
        for i in range(4)
    ]

    loads = [
        pltpu.make_async_copy(x_hbm, x_ref, load_sem.at[0]),
        pltpu.make_async_copy(w_hbm, w_ref, load_sem.at[1]),
    ]

    def row_start(i):
        mine = i // 2
        return ((1 - mine) * (1 - place.rank) + mine * place.rank) * LEN_L + (i % 2) * TAIL_BLOCK

    def row_loads(i):
        start = pl.ds(pl.multiple_of(row_start(i), TAIL_BLOCK), TAIL_BLOCK)
        slot = i % 2
        return [
            pltpu.make_async_copy(tok_hbm.at[start], tok_ref.at[slot], row_sem.at[slot, 0]),
            pltpu.make_async_copy(gresid_hbm.at[start], gresid_ref.at[slot], row_sem.at[slot, 1]),
        ]

    def token_copy(i):
        there = pl.ds(i * TAIL_BLOCK, TAIL_BLOCK)
        return send_to(
            sent_ref.at[there], got_hbm.at[there], tok_send.at[i], tok_recv.at[i], place.partner()
        )

    def weight_gradient(source, target, i):
        here = pl.ds(i * half, half)
        product = contract(x_ref[...], d_ref[source, here, :], 0, 1)
        target[:, here] = product.astype(BF16)

    def bias_rows(source, target):
        ones = jnp.ones((16, d_ref.shape[2]), BF16)
        for i, which in ((0, 0), (1, 2)):
            row = contract(ones, d_ref[source, pl.ds(which * half, half), :], 1, 1)
            target[8:9, pl.ds(i * half, half)] = row[:1]

    events = {}
    sums += cat_sums
    for one, times in zip(sums, SUM_STEPS):
        for when, action in zip(times, SUM_ACTIONS):
            if when is None:
                continue
            events.setdefault(when, []).append(getattr(one, action))

    for when in sorted(events):

        @pl.when(step == when)
        def _(when=when):
            if when == 0:
                out_load.start()
                place.greet()
                out_term.begin()
            if when == 1:
                out_term.to_partner()
                out_load.wait()
                out_copies[0].start()
                out_copies[1].start()
            if when == 3:
                out_copies[2].start()
            if when == 13:
                out_copies[3].start()
            if when == 8:
                out_term.end()
            for action in events[when]:
                action()

    @pl.when(step == 2)
    def _():
        for copy in loads:
            copy.start()

    @pl.when(step == heads)
    def _():
        for copy in loads:
            copy.wait()
        for i in range(3):
            weight_gradient(1, dw2_ref, i)
        cat_term.begin()

    @pl.when(step == heads + 1)
    def _():
        cat_term.to_partner()
        own_small[...] = jnp.zeros_like(own_small)
        other_small[...] = jnp.zeros_like(other_small)
        bias_rows(1, other_small)

    @pl.when(step < 2 * heads)
    def _():
        back_one_head(mask_ref, qkv_ref, att_ref, log_ref, gatt_ref, d_ref, step, heads, block)

    @pl.when(step == 2 * heads)
    def _():
        for copy in row_loads(0):
            copy.start()
        cat_term.end()
        for i in range(3):
            weight_gradient(0, dw_ref, i)
            cat_sums[i].begin()
        bias_rows(0, own_small)


    for i in range(4):

        @pl.when(step == first_rows + i)
        def _(i=i):
            for copy in row_loads(i):
                copy.wait()
            if i == 0:
                for copy in out_copies:
                    copy.wait()
            if i < 3:
                for copy in row_loads(i + 1):
                    copy.start()
            here = pl.ds(pl.multiple_of(row_start(i), TAIL_BLOCK), TAIL_BLOCK)
            gin = contract(d_ref[0, :, here], w_ref[0], 0, 1)
            gin += contract(d_ref[1, :, here], w_ref[1], 0, 1)
            hat, inv = norm_parts(tok_ref[i % 2].astype(F32))
            gtok = gresid_ref[i % 2] + norm_back(hat, inv, gin * row(gain_ref))
            own_small[0:1] += jnp.sum(gin * hat, axis=0, keepdims=True)
            own_small[1:2] += jnp.sum(gin, axis=0, keepdims=True)
            if i < 2:
                sent_ref[pl.ds(i * TAIL_BLOCK, TAIL_BLOCK), :] = gtok.astype(BF16)
                token_copy(i).start()
            else:
                gtok_ref[...] = gtok

    @pl.when(step == last_step)
    def _():
        own_small[2:6] = small2_ref[0:4]
        other_small[0:2] = own_small[0:2]
        other_small[2:6] = small2_ref[0:4]
        for i in (0, 1):
            own_small[6 + i : 7 + i] = dbup1_ref[:, pl.ds(i * width, width)]
            other_small[6 + i : 7 + i] = dbup2_ref[:, pl.ds(i * width, width)]
        small.begin()
        small_actions = (small.over_x, small.over_z, small.over_tp)
        for item in LAST_ACTIONS:
            if isinstance(item, int):
                small_actions[item]()
            else:
                getattr(sums[item[0]], item[1])()
        small_ref[...] = small.end()
        for i in (0, 1):
            token_copy(i).wait()
        for one in sums:
            one.end()


def back_one_head(mask_ref, qkv_ref, att_ref, log_ref, gatt_ref, d_ref, step, heads, block):
    rows = qkv_ref.shape[4]
    half = heads * HEAD_DIM
    source = 1 - step // heads
    head_at = pl.multiple_of((step % heads) * HEAD_DIM, HEAD_DIM)

    def store(which, columns, value):
        d_ref[source, pl.ds(which * half + head_at, HEAD_DIM), columns] = value.astype(BF16)

    work = []
    images = [(0, LEN_L, block)] + [(at, LEN_S, LEN_S) for at in range(LEN_L, rows, LEN_S)]
    for start, count, size in images:
        work += [(start, count, at, size) for at in range(start, start + count, size)]
    kept = {}

    def operands(start, count):
        if start not in kept:
            every = slice(start, start + count)
            keys = qkv_ref[0, 1, 0, :, every]
            values = qkv_ref[0, 2, 0, :, every]
            ones = jnp.ones((1, count), F32)
            key_rows = jnp.concatenate(
                [keys, keys, extra_rows([ones, ones, ones, mask_ref[:, every]], count)], 0
            )
            value_rows = jnp.concatenate([values, extra_rows([ones, ones, ones], count)], 0)
            kept[start] = keys, key_rows, value_rows
        return kept[start]

    def products(item):
        start, count, at, size = item
        here = slice(at, at + size)
        _, key_rows, value_rows = operands(start, count)
        query = qkv_ref[0, 0, 0, :, here]
        grads = gatt_ref[0, 0, :, here]
        inner = jnp.sum(
            grads.astype(F32) * att_ref[0, 0, :, here].astype(F32), axis=0, keepdims=True
        )
        terms = three_terms(-log_ref[0, 0, :, here]) + [jnp.ones((1, size), F32)]
        query_rows = jnp.concatenate([*scaled_query(query), extra_rows(terms, size)], 0)
        grad_rows = jnp.concatenate([grads, extra_rows(three_terms(-inner), size)], 0)
        return contract(query_rows, key_rows, 0, 0), contract(grad_rows, value_rows, 0, 0)

    sums = {}
    now = products(work[0])
    for place, item in enumerate(work):
        later = products(work[place + 1]) if place + 1 < len(work) else None
        start, count, at, size = item
        here = slice(at, at + size)
        keys = operands(start, count)[0]
        query = qkv_ref[0, 0, 0, :, here]
        grads = gatt_ref[0, 0, :, here]
        score, grad_probs = now
        probs = jnp.exp2(score)
        grad_score = (probs * grad_probs).astype(BF16)
        part_values = contract(grads, probs.astype(BF16), 1, 0)
        part_keys = contract(query, grad_score, 1, 0)
        store(0, here, contract(keys, grad_score, 1, 1) * SCALE)
        if start in sums:
            part_keys, part_values = sums[start][0] + part_keys, sums[start][1] + part_values
        sums[start] = part_keys, part_values
        if at + size == start + count:
            every = slice(start, start + count)
            store(1, every, part_keys * SCALE)
            store(2, every, part_values)
        now = later


def tail(
    mask, qkv, att, log_total, gatt, gain, small2, dbup1, dbup2, dwout2, normed, w_cat,
    tokens, gresid, dup, ddown, dwout, seen_up, seen_down, out_rows, block=256,
):
    _, _, heads, _, rows = qkv.shape
    _, width, out = w_cat.shape
    anywhere = pl.BlockSpec(memory_space=pl.ANY)
    last = 2 * heads - 1

    def head(h):
        h = jnp.minimum(h, last)
        return 1 - h // heads, h % heads

    all_three = pl.BlockSpec(
        (1, 3, 1, HEAD_DIM, rows), lambda h: (head(h)[0], 0, head(h)[1], 0, 0)
    )
    one = pl.BlockSpec((1, 1, HEAD_DIM, rows), lambda h: (*head(h), 0, 0))
    per_head = pl.BlockSpec((1, 1, 1, rows), lambda h: (*head(h), 0, 0))
    sum_shapes = [dwout.shape] + [(width, HIDDEN_BLOCK)] * 2 + [(HIDDEN_BLOCK, width)] * 2 + [(width, out // 3)] * 3
    scratch = [
        pltpu.VMEM((2, out, rows), BF16),
        pltpu.VMEM((rows, width), BF16),
        pltpu.VMEM((2, width, out), BF16),
        pltpu.VMEM((2, TAIL_BLOCK, width), BF16),
        pltpu.VMEM((2, TAIL_BLOCK, width), F32),
        pltpu.VMEM((width, out), BF16),
        pltpu.VMEM((width, out), BF16),
        pltpu.VMEM((width // 2, out), BF16),
        pltpu.VMEM((rows // 2, width), BF16),
        pltpu.VMEM((2, SmallSum.ROWS, width), F32),
        pltpu.SemaphoreType.DMA((3,)),
        pltpu.SemaphoreType.DMA((2, 2)),
        pltpu.SemaphoreType.DMA((6,)),
        pltpu.SemaphoreType.DMA((6,)),
    ]
    for shape in sum_shapes:
        scratch += PlaneSum.buffers(*shape)
    scratch += PartnerTerm.buffers(width, out) + PartnerTerm.buffers(*dwout.shape)
    scratch += SmallSum.buffers(width)
    pairs = pair_count(2 * heads, rows)
    first_rows = 2 * heads + 1
    return pl.pallas_call(
        functools.partial(tail_kernel, heads=heads, block=block),
        grid=(first_rows + 4,),
        in_specs=[
            whole((1, rows)), all_three, one, per_head, one, whole((width,)), whole((8, width)),
            whole((1, 2 * width)), whole((1, 2 * width)), whole(dwout.shape),
        ]
        + [anywhere] * 10,
        out_specs=[
            pl.BlockSpec(
                (TAIL_BLOCK, width), lambda h: (jnp.maximum(h - first_rows - 2, 0), 0)
            ),
            whole((SmallSum.ROWS, width)),
        ]
        + [anywhere] * 6,
        out_shape=[
            jax.ShapeDtypeStruct((rows // 2, width), F32),
            jax.ShapeDtypeStruct((SmallSum.ROWS, width), F32),
            jax.ShapeDtypeStruct((rows // 2, width), BF16),
            jax.ShapeDtypeStruct((width, dup.shape[1] - HIDDEN_BLOCK), BF16),
            jax.ShapeDtypeStruct((ddown.shape[0] - HIDDEN_BLOCK, width), BF16),
            jax.ShapeDtypeStruct(dwout.shape, BF16),
            jax.ShapeDtypeStruct((width, out), BF16),
            jax.ShapeDtypeStruct((rows // 2, width), BF16),
        ],
        scratch_shapes=scratch,
        compiler_params=pltpu.CompilerParams(
            vmem_limit_bytes=VMEM_LIMIT, collective_id=0, has_side_effects=True
        ),
        cost_estimate=cost(pairs * 5 * 512, 32 * heads * HEAD_DIM * rows, pairs),
        name="tail",
    )(
        mask, qkv, att, log_total, gatt, gain, small2, dbup1, dbup2, dwout2, normed, w_cat,
        tokens, gresid, dup, ddown, dwout, seen_up, seen_down, out_rows,
    )


def joined(mine, theirs, second):
    return jnp.where(second, jnp.concatenate([theirs, mine], 0), jnp.concatenate([mine, theirs], 0))


def half_of(array, second):
    size = array.shape[0] // 2
    return lax.dynamic_slice_in_dim(array, jnp.where(second, size, 0), size, 0)


def by_images(
    tokens, long_lengths, short_lengths, ln1_gain, ln1_bias, w_query, b_query, w_key, w_value,
    b_value, w_out, b_out, ln2_gain, ln2_bias, w_up, b_up, w_down, b_down, cotangent,
):
    rank = lax.axis_index("tp")
    rank_arr = jnp.reshape(rank, (1,)).astype(jnp.int32)
    second = rank == 1
    rows = tokens.shape[0] // 2
    width = tokens.shape[1]
    half = w_query.shape[1]
    heads = half // HEAD_DIM
    long_len = lax.dynamic_slice_in_dim(long_lengths, rank, 1, 0)
    shorts = short_lengths.shape[0] // 2
    short_len = lax.dynamic_slice_in_dim(short_lengths, rank * shorts, shorts, 0)
    valid = jnp.concatenate(
        [
            jnp.arange(LEN_L) < long_len[0],
            (jnp.arange(LEN_S)[None, :] < short_len[:, None]).reshape(-1),
        ]
    )
    mask = jnp.where(valid, 0.0, -1e30).astype(F32).reshape(1, -1)
    biases = jnp.concatenate([b_query, jnp.zeros_like(b_query), b_value, b_up]).astype(F32)
    bias = jnp.broadcast_to(biases.reshape(1, -1), (8, biases.shape[0]))

    (normed, qkv, att, log_total, resid, mid, w_cat, w_out_all, w_up2, w_down2, grads, bias2,
     own_tokens) = front(
        mask, (ln1_gain, ln1_bias, b_out, ln2_gain, ln2_bias), bias,
        tokens, w_query, w_key, w_value, w_out, w_up, w_down, cotangent, heads,
    )
    qkv = qkv.reshape(2, 3, heads, HEAD_DIM, rows)
    attended = att.reshape(2 * half, rows)
    up_bias = [
        rows_of.reshape(-1, 1, HIDDEN_BLOCK)
        for rows_of in (bias[0, 3 * half :], bias2[0, 3 * half :])
    ]
    up_bias = jnp.stack([up_bias[side][i] for side, i in HIDDEN_ORDER])
    (out, gresid, gatt, dwout1, dwout2, small2, db_up, dup1, ddown1, seen_up, seen_down,
     first_up, first_down) = mid_part(
        mid, grads, up_bias, resid, ln2_gain, b_down, w_out_all,
        attended, w_up2, w_up, w_down2, w_down,
    )
    dbup1, dbup2 = (
        jnp.concatenate([db_up[at] for at, (own, _) in enumerate(HIDDEN_ORDER) if own == side], 1)
        for side in (0, 1)
    )
    gtok, small, got_tok, grad_up, grad_down, grad_out_t, grad_cat, got_out = tail(
        mask, qkv, att, log_total, gatt.reshape(2, heads, HEAD_DIM, rows), ln1_gain, small2,
        dbup1, dbup2, dwout2, normed, w_cat, own_tokens, gresid, dup1, ddown1, dwout1,
        seen_up, seen_down, out,
    )
    result = joined(half_of(out, second), got_out, second)
    grad_tokens = joined(gtok, got_tok.astype(F32), second)
    grad_cat = grad_cat.astype(F32)
    return (
        result,
        grad_tokens,
        small[0],
        small[1],
        grad_cat[:, :half],
        small[8, :half],
        grad_cat[:, half : 2 * half],
        grad_cat[:, 2 * half :],
        small[8, half:],
        grad_out_t.T.astype(F32),
        small[4],
        small[2],
        small[3],
        jnp.concatenate([first_up, grad_up], 1).astype(F32),
        small[6:8].reshape(-1),
        jnp.concatenate([first_down, grad_down], 0).astype(F32),
        small[5],
    )


def layer_norm(values, gain, shift):
    center = values - jnp.mean(values, axis=-1, keepdims=True)
    spread = jnp.mean(center * center, axis=-1, keepdims=True)
    return center * lax.rsqrt(spread + 1e-06) * gain + shift


def dot_plain(left, right):
    return jnp.dot(left, right, preferred_element_type=jnp.float32)


def dot_rows(left, right):
    return lax.dot_general(
        left, right, (((0,), (0,)), ((), ())), preferred_element_type=jnp.float32
    )


def dot_back(left, right):
    return lax.dot_general(
        left, right, (((1,), (1,)), ((), ())), preferred_element_type=jnp.float32
    )


def group_shape(image_count, seq_len, head_count):
    per_step = math.gcd(image_count, max(1, 512 // seq_len))
    return (image_count // per_step, per_step, seq_len, head_count, HEAD_DIM)


def masked_scores(query_blk, key_blk, length_blk):
    seq_len = query_blk.shape[1]
    raw = jnp.einsum(
        "bqhd,bkhd->bhqk", query_blk, key_blk, preferred_element_type=jnp.float32
    ) * HEAD_DIM ** (-0.5)
    keep = jnp.arange(seq_len, dtype=jnp.int32)[None, :] < length_blk[:, None]
    return jnp.where(keep[:, None, None, :], raw, -1e30)


def attention_forward(queries, key_rows, value_rows, lengths, seq_len):
    image_count = lengths.shape[0]
    head_count = queries.shape[1] // HEAD_DIM
    block_shape = group_shape(image_count, seq_len, head_count)

    def one_step(block):
        query_blk, key_blk, value_blk, length_blk = block
        scores = masked_scores(query_blk, key_blk, length_blk)
        row_top = jnp.max(scores, axis=-1, keepdims=True)
        exp_terms = jnp.exp(scores - row_top)
        row_total = jnp.sum(exp_terms, axis=-1, keepdims=True)
        weights = (exp_terms / row_total).astype(jnp.bfloat16)
        mixed = jnp.einsum(
            "bhqk,bkhd->bqhd", weights, value_blk, preferred_element_type=jnp.float32
        )
        return (mixed, (row_top + jnp.log(row_total))[..., 0])

    mixed, log_total = lax.map(
        one_step,
        (
            queries.reshape(block_shape),
            key_rows.reshape(block_shape),
            value_rows.reshape(block_shape),
            lengths.reshape(block_shape[:2]),
        ),
    )
    return (mixed.reshape(image_count * seq_len, head_count * HEAD_DIM), log_total)


def attention_backward(queries, key_rows, value_rows, grads, lengths, log_total, seq_len):
    image_count = lengths.shape[0]
    head_count = queries.shape[1] // HEAD_DIM
    block_shape = group_shape(image_count, seq_len, head_count)
    scale = HEAD_DIM ** (-0.5)

    def one_step(block):
        query_blk, key_blk, value_blk, grad_blk, length_blk, total_blk = block
        scores = masked_scores(query_blk, key_blk, length_blk)
        probs = jnp.exp(scores - total_blk[..., None])
        grad_values = jnp.einsum(
            "bhqk,bqhd->bkhd",
            probs.astype(jnp.bfloat16),
            grad_blk,
            preferred_element_type=jnp.float32,
        )
        grad_probs = jnp.einsum(
            "bqhd,bkhd->bhqk", grad_blk, value_blk, preferred_element_type=jnp.float32
        )
        inner = jnp.sum(probs * grad_probs, axis=-1, keepdims=True)
        grad_scores = (probs * (grad_probs - inner)).astype(jnp.bfloat16)
        grad_queries = (
            jnp.einsum("bhqk,bkhd->bqhd", grad_scores, key_blk, preferred_element_type=jnp.float32)
            * scale
        )
        grad_keys = (
            jnp.einsum(
                "bhqk,bqhd->bkhd", grad_scores, query_blk, preferred_element_type=jnp.float32
            )
            * scale
        )
        return (grad_queries, grad_keys, grad_values)

    results = lax.map(
        one_step,
        (
            queries.reshape(block_shape),
            key_rows.reshape(block_shape),
            value_rows.reshape(block_shape),
            grads.reshape(block_shape),
            lengths.reshape(block_shape[:2]),
            log_total,
        ),
    )
    flat = (image_count * seq_len, head_count * HEAD_DIM)
    return tuple((item.reshape(flat) for item in results))


def local(
    tokens,
    long_lengths,
    short_lengths,
    ln1_gain,
    ln1_bias,
    w_query,
    b_query,
    w_key,
    w_value,
    b_value,
    w_out,
    b_out,
    ln2_gain,
    ln2_bias,
    w_up,
    b_up,
    w_down,
    b_down,
    cotangent,
):
    tp_count = lax.axis_size("tp")
    tp_rank = lax.axis_index("tp")
    row_count = tokens.shape[0]
    share = row_count // tp_count
    split = long_lengths.shape[0] * LEN_L
    gain_one = ln1_gain.astype(jnp.float32)
    shift_one = ln1_bias.astype(jnp.float32)
    gain_two = ln2_gain.astype(jnp.float32)
    shift_two = ln2_bias.astype(jnp.float32)
    normed_in = layer_norm(tokens.astype(jnp.float32), gain_one, shift_one).astype(jnp.bfloat16)
    queries = (dot_plain(normed_in, w_query) + b_query.astype(jnp.float32)).astype(jnp.bfloat16)
    key_rows = dot_plain(normed_in, w_key).astype(jnp.bfloat16)
    value_rows = (dot_plain(normed_in, w_value) + b_value.astype(jnp.float32)).astype(jnp.bfloat16)
    long_mixed, long_total = attention_forward(
        queries[:split], key_rows[:split], value_rows[:split], long_lengths, LEN_L
    )
    short_mixed, short_total = attention_forward(
        queries[split:], key_rows[split:], value_rows[split:], short_lengths, LEN_S
    )
    attended = jnp.concatenate([long_mixed, short_mixed], axis=0).astype(jnp.bfloat16)
    attn_sum = lax.psum_scatter(dot_plain(attended, w_out), "tp", scatter_dimension=0, tiled=True)
    own_tokens = lax.dynamic_slice_in_dim(tokens, tp_rank * share, share, 0).astype(jnp.float32)
    resid = own_tokens + attn_sum + b_out.astype(jnp.float32)
    normed_mid = layer_norm(resid, gain_two, shift_two).astype(jnp.bfloat16)
    grad_out = cotangent.astype(jnp.float32)
    mid_rows = lax.all_gather(normed_mid, "tp", axis=0, tiled=True)
    pre_up = dot_plain(mid_rows, w_up) + b_up.astype(jnp.float32)
    activ = jax.nn.gelu(pre_up, approximate=False).astype(jnp.bfloat16)
    ffn_sum = lax.psum_scatter(
        dot_plain(activ, w_down).astype(jnp.bfloat16), "tp", scatter_dimension=0, tiled=True
    ).astype(jnp.float32)
    result = resid + ffn_sum + b_down.astype(jnp.float32)
    grad_rows = lax.all_gather(cotangent, "tp", axis=0, tiled=True)
    grad_w_down = dot_rows(activ, grad_rows)
    grad_activ = dot_back(grad_rows, w_down)
    _, gelu_back = jax.vjp(lambda inner: jax.nn.gelu(inner, approximate=False), pre_up)
    grad_pre = gelu_back(grad_activ)[0].astype(jnp.bfloat16)
    grad_w_up = dot_rows(mid_rows, grad_pre)
    grad_b_up = jnp.sum(grad_pre.astype(jnp.float32), axis=0)
    grad_mid = lax.psum_scatter(dot_back(grad_pre, w_up), "tp", scatter_dimension=0, tiled=True)
    _, norm_two_back = jax.vjp(layer_norm, resid, gain_two, shift_two)
    grad_resid_norm, grad_gain_two, grad_shift_two = norm_two_back(grad_mid)
    grad_resid = grad_out + grad_resid_norm
    grad_b_down = jnp.sum(grad_out, axis=0)
    grad_b_out = jnp.sum(grad_resid, axis=0)
    grad_branch = lax.all_gather(grad_resid.astype(jnp.bfloat16), "tp", axis=0, tiled=True)
    grad_w_out = dot_rows(attended, grad_branch)
    grad_attended = dot_back(grad_branch, w_out).astype(jnp.bfloat16)
    long_grads = attention_backward(
        queries[:split],
        key_rows[:split],
        value_rows[:split],
        grad_attended[:split],
        long_lengths,
        long_total,
        LEN_L,
    )
    short_grads = attention_backward(
        queries[split:],
        key_rows[split:],
        value_rows[split:],
        grad_attended[split:],
        short_lengths,
        short_total,
        LEN_S,
    )
    grad_queries = jnp.concatenate([long_grads[0], short_grads[0]], axis=0).astype(jnp.bfloat16)
    grad_keys = jnp.concatenate([long_grads[1], short_grads[1]], axis=0).astype(jnp.bfloat16)
    grad_values = jnp.concatenate([long_grads[2], short_grads[2]], axis=0).astype(jnp.bfloat16)
    grad_w_query = dot_rows(normed_in, grad_queries)
    grad_b_query = jnp.sum(grad_queries.astype(jnp.float32), axis=0)
    grad_w_key = dot_rows(normed_in, grad_keys)
    grad_w_value = dot_rows(normed_in, grad_values)
    grad_b_value = jnp.sum(grad_values.astype(jnp.float32), axis=0)
    grad_in = lax.psum_scatter(
        dot_back(grad_queries, w_query)
        + dot_back(grad_keys, w_key)
        + dot_back(grad_values, w_value),
        "tp",
        scatter_dimension=0,
        tiled=True,
    )
    _, norm_one_back = jax.vjp(layer_norm, own_tokens, gain_one, shift_one)
    grad_tokens_norm, grad_gain_one, grad_shift_one = norm_one_back(grad_in)
    grad_tokens = grad_resid + grad_tokens_norm
    summed = lax.psum(
        (
            grad_w_query,
            grad_b_query,
            grad_w_key,
            grad_w_value,
            grad_b_value,
            grad_w_out,
            grad_w_up,
            grad_b_up,
            grad_w_down,
        ),
        "dp",
    )
    shared = lax.psum(
        (grad_gain_one, grad_shift_one, grad_b_out, grad_gain_two, grad_shift_two, grad_b_down),
        ("dp", "tp"),
    )
    return (
        result.astype(jnp.bfloat16),
        grad_tokens,
        shared[0],
        shared[1],
        summed[0],
        summed[1],
        summed[2],
        summed[3],
        summed[4],
        summed[5],
        shared[2],
        shared[3],
        shared[4],
        summed[6],
        summed[7],
        summed[8],
        shared[5],
    )


def pick(*arrays):
    tokens, long_lengths, short_lengths, w_query, w_up = (arrays[i] for i in (0, 1, 2, 5, 14))
    fits = (
        lax.axis_size("tp") == 2
        and lax.axis_size("dp") == 16
        and long_lengths.shape[0] == 2
        and short_lengths.shape[0] == 8
        and tokens.shape == (2 * LEN_L + 8 * LEN_S, 768)
        and w_query.shape[1] == 8 * HEAD_DIM
        and w_up.shape[1] == 1536
    )
    return by_images(*arrays) if fits else local(*arrays)


def solution(mesh):
    placed = (
        P("dp", None),
        P("dp"),
        P("dp"),
        P(),
        P(),
        P(None, "tp"),
        P("tp"),
        P(None, "tp"),
        P(None, "tp"),
        P("tp"),
        P("tp", None),
        P(),
        P(),
        P(),
        P(None, "tp"),
        P("tp"),
        P("tp", None),
        P(),
        P(("dp", "tp"), None),
    )
    return jax.shard_map(
        pick,
        mesh=mesh,
        in_specs=placed,
        out_specs=(
            P(("dp", "tp"), None),
            P(("dp", "tp"), None),
            P(),
            P(),
            P(None, "tp"),
            P("tp"),
            P(None, "tp"),
            P(None, "tp"),
            P("tp"),
            P("tp", None),
            P(),
            P(),
            P(),
            P(None, "tp"),
            P("tp"),
            P("tp", None),
            P(),
        ),
        check_vma=False,
    )
```
